32 devices in a mesh: lon: 8 (over z, x), lat: 4 (over y, core).
Axes of the slice: x: 2, y: 2, z: 4, core: 2. Of those that a mesh axis runs over, the one named last changes fastest.
Arguments:
- warmth_deviation: float32 [10, 256, 1024], P(None, 'lat', 'lon'), may hold values from -6 to 6
- saltiness_deviation: float32 [10, 256, 1024], P(None, 'lat', 'lon'), may hold values from -6 to 6
- easterly_speed: float32 [10, 256, 1024], P(None, 'lat', 'lon'), may hold values from -6 to 6
- poleward_speed: float32 [10, 256, 1024], P(None, 'lat', 'lon'), may hold values from -6 to 6
- stratum_spans: float32 [10], replicated, may hold values from 0.5 to 2
- water_indicator: int32 [256, 1024], P('lat', 'lon'), may hold values 0 or 1
- opposite_counterpart: int32 [1024], P('lon'), may hold values from 0 to 1023, as said below
- elevation_weights: float32 [256, 1024], P('lat', 'lon'), may hold values from 0.2 to 2
- elevation_anomaly: float32 [256, 1024], P('lat', 'lon'), may hold values from -3 to 17
Outputs:
- new_temperature: float32 [10, 256, 1024], P(None, 'lat', 'lon')
- new_salinity: float32 [10, 256, 1024], P(None, 'lat', 'lon')
- new_zonal: float32 [10, 256, 1024], P(None, 'lat', 'lon')
- new_meridional: float32 [10, 256, 1024], P(None, 'lat', 'lon')
- new_surface: float32 [256, 1024], P('lat', 'lon')
The draws below stay inside these ranges and needn't reach their ends.
Inputs may be any that keep to these rules, and one draw needn't show every extreme that they name: opposite_counterpart[x] = (h - 1 - x) mod 1024 for a hinge column h chosen by the draw, so opposite_counterpart[opposite_counterpart[x]] = x.
All inputs are finite; a program needn't handle non-finite values. No bound on the sum of `water_indicator` on one device may be relied on, other than what follows from the above.
Results may differ from the reference program's by a relative error of at most 0.0001.
Values sent between devices are 32-bit elements; how exact they have to be, the bound alone decides.
No kernel may reach another device: no remote copies, remote signals or barrier semaphores. Data moves between devices by JAX's collectives and lax.ppermute only.
A program may use at most 64 MiB of HBM per device.

```python
import math
import jax
import jax.numpy as jnp

STRATA_COUNT = 10
ITERS = 3
EASTWARD_CELLS = 1024
POLEWARD_CELLS = 256


def draw_opposite_counterpart(key, part):
    key = jax.random.fold_in(key, 11)
    hinge = jax.random.randint(key, (), 0, EASTWARD_CELLS)
    return jnp.mod(hinge - 1 - jnp.arange(EASTWARD_CELLS, dtype=jnp.int32), EASTWARD_CELLS).astype(jnp.int32)


def draw_elevation_anomaly(key, part):
    key = jax.random.fold_in(key, 23)
    rough = jnp.clip(jax.random.normal(key, (POLEWARD_CELLS, EASTWARD_CELLS), jnp.float32), -3.0, 3.0)
    return rough.astype(jnp.float32)


def place_ends(drawn, rng, least, largest):
    place = [jax.random.randint(jax.random.fold_in(rng, axis), (), 0, length) for axis, length in enumerate(drawn.shape)]
    main_axis = drawn.shape.index(max(drawn.shape))
    beside = place[:main_axis] + [(place[main_axis] + 1) % drawn.shape[main_axis]] + place[main_axis + 1:]
    return drawn.at[tuple(place)].set(least).at[tuple(beside)].set(largest)


def block_levels(own_key, extent, split, low, top_value):
    level = 1.0
    for dim, parts in split:
        steps = jax.random.uniform(jax.random.fold_in(jax.random.fold_in(own_key, 6), dim), (parts,), jnp.float32, low / len(split), top_value / len(split))
        level = level * jnp.repeat(jnp.exp(steps), extent[dim] // parts).reshape((-1,) + (1,) * (len(extent) - 1 - dim))
    return level


def noise(own_key, extent, scale, bound, shards=(), kind=jnp.bfloat16):
    drawn = scale * jax.random.normal(own_key, extent, jnp.float32)
    if shards:
        drawn = drawn * block_levels(own_key, extent, shards, -0.22, 0.18)
    return jnp.clip(drawn, -bound, bound).astype(kind)


def setup_inputs(seed: int = 0) -> dict:
    key_list = jax.random.split(jax.random.key(seed), 10)
    warmth_deviation = noise(key_list[0], (STRATA_COUNT, POLEWARD_CELLS, EASTWARD_CELLS), 1.0, 6.0, ((1, 4), (2, 8)), jnp.float32)
    saltiness_deviation = noise(key_list[1], (STRATA_COUNT, POLEWARD_CELLS, EASTWARD_CELLS), 1.0, 6.0, ((1, 4), (2, 8)), jnp.float32)
    easterly_speed = noise(key_list[2], (STRATA_COUNT, POLEWARD_CELLS, EASTWARD_CELLS), 1.0, 6.0, ((1, 4), (2, 8)), jnp.float32)
    poleward_speed = noise(key_list[3], (STRATA_COUNT, POLEWARD_CELLS, EASTWARD_CELLS), 1.0, 6.0, ((1, 4), (2, 8)), jnp.float32)
    stratum_spans = jnp.clip(jnp.exp(jax.random.uniform(key_list[4], (STRATA_COUNT,), jnp.float32, math.log(0.5), math.log(2.0))), 0.5, 2.0)
    water_indicator = place_ends((jax.random.randint(key_list[5], (POLEWARD_CELLS, EASTWARD_CELLS), 0, 4) < 3).astype(jnp.int32), jax.random.fold_in(key_list[5], 1), 0, 1)
    opposite_counterpart = draw_opposite_counterpart(jax.random.fold_in(key_list[9], 71), 0)
    elevation_weights = jnp.clip(jnp.exp(math.log(2.0) - 2.3025851 * jax.random.uniform(key_list[7], (POLEWARD_CELLS, EASTWARD_CELLS), jnp.float32) ** block_levels(key_list[7], (POLEWARD_CELLS, EASTWARD_CELLS), ((0, 4), (1, 8)), -0.2, 0.2)), 0.2, 2.0)
    elevation_anomaly = draw_elevation_anomaly(jax.random.fold_in(key_list[9], 71), 0)
    return dict(warmth_deviation=warmth_deviation, saltiness_deviation=saltiness_deviation, easterly_speed=easterly_speed, poleward_speed=poleward_speed, stratum_spans=stratum_spans, water_indicator=water_indicator, opposite_counterpart=opposite_counterpart, elevation_weights=elevation_weights, elevation_anomaly=elevation_anomaly)


LINEAR_HEAT = 1.0
SQUARE_HEAT = 0.3
SALT_COEF = 0.8
CROSS_COEF = 0.2
TIME_STEP = 0.1
MIXING = 0.1


def periodic(field, width):
    return jnp.concatenate([field[..., -width:], field, field[..., :width]], axis=-1)


def northward(field, opposite_counterpart, width, sign):
    rows = field.shape[-2]
    south = jnp.zeros(field.shape[:-2] + (width, field.shape[-1]), jnp.float32)
    folded = [sign * jnp.take(field[..., rows - 1 - offset, :], opposite_counterpart, axis=-1) for offset in range(width)]
    north = jnp.stack(folded, axis=-2)
    return jnp.concatenate([south, field, north], axis=-2)


def density(heat_part, salt_part):
    return -LINEAR_HEAT * heat_part - 0.5 * SQUARE_HEAT * heat_part * heat_part + SALT_COEF * salt_part - CROSS_COEF * heat_part * salt_part


def pressure(heat_part, salt_part, stratum_spans):
    layers = density(heat_part, salt_part) * stratum_spans[:, None, None]
    return jnp.cumsum(layers, axis=0) - 0.5 * layers


def reference(warmth_deviation, saltiness_deviation, easterly_speed, poleward_speed, stratum_spans, water_indicator, opposite_counterpart, elevation_weights, elevation_anomaly):
    wetness = water_indicator.astype(jnp.float32)
    advected_quantities = jnp.stack([warmth_deviation, saltiness_deviation])
    along = periodic(advected_quantities, 2)
    across = northward(advected_quantities, opposite_counterpart, 2, 1.0)
    east_one = along[..., 3:-1]
    west_one = along[..., 1:-3]
    east_two = along[..., 4:]
    west_two = along[..., :-4]
    north_one = across[..., 3:-1, :]
    south_one = across[..., 1:-3, :]
    north_two = across[..., 4:, :]
    south_two = across[..., :-4, :]
    grad_east = (8.0 * (east_one - west_one) - (east_two - west_two)) / 12.0
    grad_north = (8.0 * (north_one - south_one) - (north_two - south_two)) / 12.0
    laplace = east_one + west_one + north_one + south_one - 4.0 * advected_quantities
    tendency = -TIME_STEP * (easterly_speed * grad_east + poleward_speed * grad_north) + MIXING * laplace
    updated = advected_quantities + wetness * tendency
    press_east = pressure(along[0][..., 1:-1], along[1][..., 1:-1], stratum_spans)
    press_north = pressure(across[0][:, 1:-1, :], across[1][:, 1:-1, :], stratum_spans)
    slope_east = 0.5 * (press_east[..., 2:] - press_east[..., :-2])
    slope_north = 0.5 * (press_north[:, 2:, :] - press_north[:, :-2, :])
    new_zonal = wetness * (easterly_speed - TIME_STEP * slope_east)
    new_meridional = wetness * (poleward_speed - TIME_STEP * slope_north)
    east_flow = jnp.sum(stratum_spans[:, None, None] * new_zonal, axis=0)
    north_flow = jnp.sum(stratum_spans[:, None, None] * new_meridional, axis=0)
    transports = jnp.stack([east_flow, north_flow])
    flow_along = periodic(transports, 1)
    flow_across = northward(transports, opposite_counterpart, 1, -1.0)
    divergence = 0.5 * (flow_along[0][:, 2:] - flow_along[0][:, :-2] + flow_across[1][2:, :] - flow_across[1][:-2, :])
    right_side = wetness * (elevation_weights * elevation_anomaly - divergence)
    diagonal = 4.0 + elevation_weights

    def operate(field):
        cycle_ext = periodic(field, 1)
        row_ext = northward(field, opposite_counterpart, 1, 1.0)
        neighbours = cycle_ext[:, 2:] + cycle_ext[:, :-2] + row_ext[2:, :] + row_ext[:-2, :]
        return diagonal * field - wetness * neighbours

    solution = jnp.zeros_like(right_side)
    residual = right_side
    precond = residual / diagonal
    direction = precond
    norm_now = jnp.sum(residual * precond)
    for step in range(ITERS):
        image = operate(direction)
        alpha = norm_now / jnp.sum(direction * image)
        solution = solution + alpha * direction
        residual = residual - alpha * image
        precond = residual / diagonal
        norm_next = jnp.sum(residual * precond)
        direction = precond + (norm_next / norm_now) * direction
        norm_now = norm_next
    return updated[0], updated[1], new_zonal, new_meridional, solution
```

```python
import functools

import jax
import jax.numpy as jnp
from jax import lax
from jax.experimental import pallas as pl
from jax.experimental.pallas import tpu as pltpu
from jax.sharding import PartitionSpec as P

TIME_STEP = 0.1
MIXING = 0.1

DEEP = 5
FIELDS = 6
VMEM_LIMIT = 32 * 1024 * 1024


def density(heat, salt):
    return heat * (-1.0 - 0.15 * heat - 0.2 * salt) + 0.8 * salt


def iota(shape, axis):
    return lax.broadcasted_iota(jnp.int32, shape, axis)


def packet_rows(levels):
    return -(-(4 * levels + FIELDS * DEEP) // 8) * 8


def pack_kernel(meta, spans, heat, salt, zonal, merid, water, weights, anomaly, fields, first, second, columns):
    levels, rows, cols = heat.shape
    span = [spans[k] for k in range(levels)]
    below = [None] * levels
    total = 0.0
    for k in reversed(range(levels)):
        below[k] = span[k] * (0.5 * span[k] + total)
        total = total + span[k]
    press = jnp.zeros((rows, cols), jnp.float32)
    east = jnp.zeros((rows, cols), jnp.float32)
    north = jnp.zeros((rows, cols), jnp.float32)
    for k in range(levels):
        press = press + below[k] * density(heat[k], salt[k])
        east = east + span[k] * zonal[k]
        north = north + span[k] * merid[k]
    fields[0] = press
    fields[1] = east
    fields[2] = north
    fields[3] = water[...].astype(jnp.float32)
    fields[4] = weights[...]
    fields[5] = anomaly[...]
    odd = meta[0]
    for packet, at_top in ((first, odd == 0), (second, odd == 1)):
        for j in range(DEEP):
            row = jnp.where(at_top, rows - 1 - j, j)
            if j < 2:
                for place, source in ((0, heat), (2 * levels, salt)):
                    for k in range(levels):
                        at = place + j * levels + k
                        packet[at : at + 1, :] = source[k, pl.ds(row, 1), :]
            for f in range(FIELDS):
                at = 4 * levels + FIELDS * j + f
                packet[at : at + 1, :] = fields[f, pl.ds(row, 1), :]
        used = 4 * levels + FIELDS * DEEP
        if used < packet.shape[0]:
            packet[used:, :] = jnp.zeros((packet.shape[0] - used, cols), jnp.float32)
    group = iota((rows, cols), 1) // 4
    edge = jnp.zeros((rows, cols), jnp.float32)
    for q in range(2 * levels):
        layer = heat[q] if q < levels else salt[q - levels]
        edge = jnp.where(group == q, pltpu.roll(layer, (4 * q + 2) % cols, 1), edge)
    columns[...] = edge


def turn_kernel(meta, fields, first, second, third, columns, ext, north_rows, south_rows, to_east, to_west):
    high, cols = first.shape
    rows = fields.shape[1]
    tall = ext.shape[1]
    levels = north_rows.shape[0] // 4
    odd, offset, top = meta[0], meta[1], meta[2]
    lane = iota((high, cols), 1)
    place = iota((high, cols), 0) - 4 * levels
    kind = lax.rem(jnp.maximum(place, 0), FIELDS)
    flips = (place >= 0) & ((kind == 1) | (kind == 2))
    from_first = first[...]
    from_second = second[...]
    facing = jnp.where(lane < offset, third[...], from_second)
    source = offset - 1 - lane
    source = jnp.where(source < 0, source + cols, source)
    facing = jnp.take_along_axis(facing, source, axis=1)
    facing = jnp.where(flips, -facing, facing)
    beyond = jnp.where(top == 1, facing, from_second)
    north = jnp.where(odd == 1, beyond, from_first)
    south = jnp.where(odd == 1, from_first, from_second)
    north_rows[...] = north[: 4 * levels]
    south_rows[...] = south[: 4 * levels]
    for f in range(FIELDS):
        ext[f, :rows, :] = fields[f]
        ext[f, rows + DEEP : tall - DEEP, :] = jnp.zeros((tall - rows - 2 * DEEP, cols), jnp.float32)
        for j in range(DEEP):
            at = 4 * levels + FIELDS * j + f
            ext[f, rows + j : rows + j + 1, :] = north[at : at + 1]
            ext[f, tall - 1 - j : tall - j, :] = south[at : at + 1]
    used = 8 * levels
    lane = iota((tall, cols), 1)
    base = jnp.concatenate([columns[...], jnp.zeros((tall - rows, cols), jnp.float32)], axis=0)
    east, west = base, base
    for f in range(FIELDS):
        here = (lane >= used + DEEP * f) & (lane < used + DEEP * (f + 1))
        layer = ext[f]
        east = jnp.where(here, pltpu.roll(layer, (used + DEEP * f + DEEP) % cols, 1), east)
        west = jnp.where(here, pltpu.roll(layer, used + DEEP * f, 1), west)
    to_east[...] = east
    to_west[...] = west


def krylov_kernel(used, ext, from_west, from_east, base, moments):
    tall, cols = ext.shape[1], ext.shape[2]
    rows = base.shape[1]
    lane = iota((tall, cols), 1)
    west = from_west[...]
    east = from_east[...]
    first = lane == 0
    last = lane == cols - 1

    def load(f):
        a = pltpu.roll(west, (2 * cols - DEEP - used - DEEP * f) % cols, 1)
        b = pltpu.roll(east, (2 * cols - used - DEEP * f) % cols, 1)
        side = jnp.where(lane >= cols - DEEP, a, jnp.where(lane < DEEP, b, 0.0))
        return ext[f], side

    def plus_x(pair):
        a, b = (pltpu.roll(part, cols - 1, 1) for part in pair)
        return jnp.where(last, b, a), jnp.where(last, a, b)

    def minus_x(pair):
        a, b = (pltpu.roll(part, 1, 1) for part in pair)
        return jnp.where(first, b, a), jnp.where(first, a, b)

    def plus_y(pair):
        return tuple(pltpu.roll(part, tall - 1, 0) for part in pair)

    def minus_y(pair):
        return tuple(pltpu.roll(part, 1, 0) for part in pair)

    def each(function, *pairs):
        return tuple(function(*parts) for parts in zip(*pairs))

    def neighbours(pair):
        return each(
            lambda a, b, c, d: (a + b) + (c + d), plus_x(pair), minus_x(pair), plus_y(pair), minus_y(pair)
        )

    press, zonal, merid, wet, weights, anomaly = (load(f) for f in range(FIELDS))
    half = 0.5 * TIME_STEP
    flow = lambda w, speed, a, b: w * (speed - half * (a - b))
    east_flow = each(flow, wet, zonal, plus_x(press), minus_x(press))
    north_flow = each(flow, wet, merid, plus_y(press), minus_y(press))
    right = each(
        lambda w, g, n, a, b, c, d: w * (g * n - 0.5 * (a - b + c - d)),
        wet,
        weights,
        anomaly,
        plus_x(east_flow),
        minus_x(east_flow),
        plus_y(north_flow),
        minus_y(north_flow),
    )
    diagonal = each(lambda g: 4.0 + g, weights)
    inverse = each(lambda m: 1.0 / m, diagonal)
    scale = each(lambda w, i: w * i, wet, inverse)
    zero = each(lambda r, i: r * i, right, inverse)
    one = each(lambda a, n: a * n, scale, neighbours(zero))
    two = each(lambda a, n: a * n, scale, neighbours(one))
    last_sum = neighbours(two)[0][:rows]
    right, middle = right[0][:rows], diagonal[0][:rows]
    zero, one, two = zero[0][:rows], one[0][:rows], two[0][:rows]
    base[0] = zero
    base[1] = one
    base[2] = two
    weighted = middle * one
    products = (
        right * zero,
        right * one,
        weighted * one,
        weighted * two,
        middle * two * two,
        last_sum * two,
    )
    for k, product in enumerate(products):
        moments[k : k + 1, :] = jnp.sum(product, axis=0, keepdims=True)
    moments[len(products) :, :] = jnp.zeros((moments.shape[0] - len(products), cols), jnp.float32)


def step_kernel(
    spans, heat, salt, zonal, merid, water, north_rows, south_rows, from_west, from_east,
    new_heat, new_salt, new_zonal, new_merid,
):
    levels, rows, cols = heat.shape
    wet = water[...].astype(jnp.float32)
    lane = iota((rows, cols), 1)
    row = iota((rows, cols), 0)
    sides = jnp.where((lane & 3) < 2, from_west[:rows, :], from_east[:rows, :])

    def around(cells, q, k, place):
        side = pltpu.roll(sides, (2 * cols - (4 * q + 2)) % cols, 1)

        def shift_x(by):
            a = pltpu.roll(cells, by % cols, 1)
            b = pltpu.roll(side, by % cols, 1)
            own = lane >= by if by > 0 else lane < cols + by
            return jnp.where(own, a, b)

        n0 = north_rows[place + k : place + k + 1, :]
        n1 = north_rows[place + levels + k : place + levels + k + 1, :]
        s0 = south_rows[place + k : place + k + 1, :]
        s1 = south_rows[place + levels + k : place + levels + k + 1, :]
        north_one = jnp.where(row == rows - 1, n0, pltpu.roll(cells, rows - 1, 0))
        north_two = jnp.where(row == rows - 1, n1, jnp.where(row == rows - 2, n0, pltpu.roll(cells, rows - 2, 0)))
        south_one = jnp.where(row == 0, s0, pltpu.roll(cells, 1, 0))
        south_two = jnp.where(row == 0, s1, jnp.where(row == 1, s0, pltpu.roll(cells, 2, 0)))
        return (shift_x(-1), shift_x(1), shift_x(-2), shift_x(2), north_one, south_one, north_two, south_two)

    def advance(cells, parts, speed_x, speed_y):
        e1, w1, e2, w2, n1, s1, n2, s2 = parts
        grad_east = 8.0 * (e1 - w1) - (e2 - w2)
        grad_north = 8.0 * (n1 - s1) - (n2 - s2)
        laplace = (e1 + w1) + (n1 + s1) - 4.0 * cells
        tendency = (-TIME_STEP / 12.0) * (speed_x * grad_east + speed_y * grad_north) + MIXING * laplace
        return cells + wet * tendency

    half = 0.5 * TIME_STEP
    above_x = jnp.zeros((rows, cols), jnp.float32)
    above_y = jnp.zeros((rows, cols), jnp.float32)
    for k in range(levels):
        t, s, u, v = heat[k], salt[k], zonal[k], merid[k]
        around_t = around(t, k, k, 0)
        around_s = around(s, levels + k, k, 2 * levels)
        new_heat[k] = advance(t, around_t, u, v)
        new_salt[k] = advance(s, around_s, u, v)
        layer_x = spans[k] * (density(around_t[0], around_s[0]) - density(around_t[1], around_s[1]))
        layer_y = spans[k] * (density(around_t[4], around_s[4]) - density(around_t[5], around_s[5]))
        new_zonal[k] = wet * (u - half * (above_x + 0.5 * layer_x))
        new_merid[k] = wet * (v - half * (above_y + 0.5 * layer_y))
        above_x = above_x + layer_x
        above_y = above_y + layer_y


def surface_kernel(mine, theirs, base, surface):
    sums = jnp.sum(mine[...] + theirs[...], axis=1, keepdims=True)
    nu = [sums[k : k + 1, :] for k in range(6)]

    def ratio(a, b):
        good = b > 0.0
        return jnp.where(good, a / jnp.where(good, b, 1.0), 0.0)

    def form(p, h):
        total = 0.0
        for i, a in enumerate(p):
            for j in range(i, len(p)):
                term = a * p[j] * h[i + j]
                total = total + (term if i == j else 2.0 * term)
        return total

    gap = [nu[k] - nu[k + 1] for k in range(5)]
    rz = nu[0]
    alpha = ratio(rz, gap[0])
    one = jnp.ones_like(rz)
    y = [one - alpha, alpha]
    x = [alpha, 0.0, 0.0]
    new = form(y, nu)
    beta = ratio(new, rz)
    rz = new
    p = [y[0] + beta, y[1]]
    alpha = ratio(rz, form(p, gap))
    x = [x[0] + alpha * p[0], alpha * p[1], 0.0]
    y = [y[0] - alpha * p[0], y[1] - alpha * (p[1] - p[0]), alpha * p[1]]
    new = form(y, nu)
    beta = ratio(new, rz)
    rz = new
    p = [y[0] + beta * p[0], y[1] + beta * p[1], y[2]]
    alpha = ratio(rz, form(p, gap))
    x = [x[0] + alpha * p[0], x[1] + alpha * p[1], alpha * p[2]]
    surface[...] = x[0] * base[0] + x[1] * base[1] + x[2] * base[2]


def call(kernel, outs, smem, flops, moved, **named):
    specs = lambda count: [pl.BlockSpec(memory_space=pltpu.VMEM)] * count

    def run(*args):
        return pl.pallas_call(
            kernel,
            out_shape=[jax.ShapeDtypeStruct(shape, jnp.float32) for shape in outs],
            in_specs=[pl.BlockSpec(memory_space=pltpu.SMEM)] * smem + specs(len(args) - smem),
            out_specs=specs(len(outs)),
            cost_estimate=pl.CostEstimate(flops=flops, bytes_accessed=moved, transcendentals=0),
            compiler_params=pltpu.CompilerParams(vmem_limit_bytes=VMEM_LIMIT),
            **named,
        )(*args)

    return run


def body(
    warmth_deviation,
    saltiness_deviation,
    easterly_speed,
    poleward_speed,
    stratum_spans,
    water_indicator,
    opposite_counterpart,
    elevation_weights,
    elevation_anomaly,
):
    lons, lats = lax.axis_size("lon"), lax.axis_size("lat")
    lon, lat = lax.axis_index("lon"), lax.axis_index("lat")
    levels, rows, cols = warmth_deviation.shape
    high = packet_rows(levels)
    tall = rows + 16
    width = cols * lons
    flat = lambda i, j: (i % lons) * lats + j

    hinge = lax.rem(opposite_counterpart[0] + 1 + cols * lon, width)
    block = hinge // cols
    meta = jnp.stack([lax.rem(lat, 2), lax.rem(hinge, cols), (lat == lats - 1).astype(jnp.int32)]).astype(jnp.int32)

    state = (warmth_deviation, saltiness_deviation, easterly_speed, poleward_speed)
    cells = levels * rows * cols
    fields, first, second, columns = call(
        pack_kernel,
        [(FIELDS, rows, cols), (high, cols), (high, cols), (rows, cols)],
        2,
        12 * cells,
        16 * cells,
        name="level_sums",
    )(meta, stratum_spans, *state, water_indicator, elevation_weights, elevation_anomaly)

    pairs_first = [(flat(i, j), flat(i, j ^ 1)) for i in range(lons) for j in range(lats)]
    pairs_inner = [
        (flat(i, a), flat(i, b))
        for i in range(lons)
        for j in range(1, lats - 1, 2)
        for a, b in ((j, j + 1), (j + 1, j))
    ]
    axes = ("lon", "lat")
    got_first = lax.ppermute(first, axes, pairs_first)

    def facing(shift, packet):
        near = [(flat(shift - 1 - i, lats - 1), flat(i, lats - 1)) for i in range(lons)]
        far = [(flat(shift - i, lats - 1), flat(i, lats - 1)) for i in range(lons)]
        return lax.ppermute(packet, axes, pairs_inner + near), lax.ppermute(packet, axes, far)

    got_second, got_third = lax.switch(block, [functools.partial(facing, s) for s in range(lons)], second)

    ext, north_rows, south_rows, to_east, to_west = call(
        turn_kernel,
        [(FIELDS, tall, cols), (4 * levels, cols), (4 * levels, cols), (tall, cols), (tall, cols)],
        1,
        FIELDS * tall * cols,
        4 * 4 * FIELDS * tall * cols,
        name="row_halos",
    )(meta, fields, got_first, got_second, got_third, columns)

    from_west = lax.ppermute(to_east, "lon", [(i, (i + 1) % lons) for i in range(lons)])
    from_east = lax.ppermute(to_west, "lon", [((i + 1) % lons, i) for i in range(lons)])

    base, moments = call(
        functools.partial(krylov_kernel, 8 * levels),
        [(3, rows, cols), (8, cols)],
        0,
        200 * tall * cols,
        4 * 12 * tall * cols,
        name="krylov",
    )(ext, from_west, from_east)

    new_heat, new_salt, new_zonal, new_merid = call(
        step_kernel,
        [(levels, rows, cols)] * 4,
        1,
        120 * cells,
        32 * cells,
        name="levels_step",
    )(stratum_spans, *state, water_indicator, north_rows, south_rows, from_west, from_east)

    count = lons * lats
    bit = 1
    theirs = None
    while bit < count:
        if theirs is not None:
            moments = moments + theirs
        theirs = lax.ppermute(moments, axes, [(i, i ^ bit) for i in range(count)])
        bit *= 2
    (surface,) = call(
        surface_kernel, [(rows, cols)], 0, 6 * rows * cols, 16 * rows * cols, name="surface"
    )(moments, theirs, base)
    return (new_heat, new_salt, new_zonal, new_merid, surface)


def solution(mesh):
    for axis in mesh.shape.values():
        assert axis > 1 and axis & (axis - 1) == 0
    levels = P(None, "lat", "lon")
    flat = P("lat", "lon")
    return jax.shard_map(
        body,
        mesh=mesh,
        in_specs=(levels, levels, levels, levels, P(), flat, P("lon"), flat, flat),
        out_specs=(levels, levels, levels, levels, flat),
        check_vma=False,
    )
```

```python
import functools

import jax
import jax.numpy as jnp
from jax import lax
from jax.experimental import pallas as pl
from jax.experimental.pallas import tpu as pltpu
from jax.sharding import PartitionSpec as P

TIME_STEP = 0.1
MIXING = 0.1

DEEP = 5
FIELDS = 6
VMEM_LIMIT = 32 * 1024 * 1024


def density(heat, salt):
    return heat * (-1.0 - 0.15 * heat - 0.2 * salt) + 0.8 * salt


def iota(shape, axis):
    return lax.broadcasted_iota(jnp.int32, shape, axis)


def packet_rows(levels):
    return -(-(4 * levels + FIELDS * DEEP) // 8) * 8


def pack_kernel(meta, spans, heat, salt, zonal, merid, water, weights, anomaly, fields, first, second, columns):
    levels, rows, cols = heat.shape
    span = [spans[k] for k in range(levels)]
    below = [None] * levels
    total = 0.0
    for k in reversed(range(levels)):
        below[k] = span[k] * (0.5 * span[k] + total)
        total = total + span[k]
    press = jnp.zeros((rows, cols), jnp.float32)
    east = jnp.zeros((rows, cols), jnp.float32)
    north = jnp.zeros((rows, cols), jnp.float32)
    for k in range(levels):
        press = press + below[k] * density(heat[k], salt[k])
        east = east + span[k] * zonal[k]
        north = north + span[k] * merid[k]
    fields[0] = press
    fields[1] = east
    fields[2] = north
    fields[3] = water[...].astype(jnp.float32)
    fields[4] = weights[...]
    fields[5] = anomaly[...]
    odd = meta[0]
    for packet, at_top in ((first, odd == 0), (second, odd == 1)):
        for j in range(DEEP):
            row = jnp.where(at_top, rows - 1 - j, j)
            if j < 2:
                for place, source in ((0, heat), (2 * levels, salt)):
                    for k in range(levels):
                        at = place + j * levels + k
                        packet[at : at + 1, :] = source[k, pl.ds(row, 1), :]
            for f in range(FIELDS):
                at = 4 * levels + FIELDS * j + f
                packet[at : at + 1, :] = fields[f, pl.ds(row, 1), :]
        used = 4 * levels + FIELDS * DEEP
        if used < packet.shape[0]:
            packet[used:, :] = jnp.zeros((packet.shape[0] - used, cols), jnp.float32)
    group = iota((rows, cols), 1) // 4
    edge = jnp.zeros((rows, cols), jnp.float32)
    for q in range(2 * levels):
        layer = heat[q] if q < levels else salt[q - levels]
        edge = jnp.where(group == q, pltpu.roll(layer, (4 * q + 2) % cols, 1), edge)
    columns[...] = edge


def turn_kernel(meta, fields, first, second, third, columns, ext, north_rows, south_rows, to_east, to_west):
    high, cols = first.shape
    rows = fields.shape[1]
    tall = ext.shape[1]
    levels = north_rows.shape[0] // 4
    odd, offset, top = meta[0], meta[1], meta[2]
    lane = iota((high, cols), 1)
    place = iota((high, cols), 0) - 4 * levels
    kind = lax.rem(jnp.maximum(place, 0), FIELDS)
    flips = (place >= 0) & ((kind == 1) | (kind == 2))
    from_first = first[...]
    from_second = second[...]
    facing = jnp.where(lane < offset, third[...], from_second)
    source = offset - 1 - lane
    source = jnp.where(source < 0, source + cols, source)
    facing = jnp.take_along_axis(facing, source, axis=1)
    facing = jnp.where(flips, -facing, facing)
    beyond = jnp.where(top == 1, facing, from_second)
    north = jnp.where(odd == 1, beyond, from_first)
    south = jnp.where(odd == 1, from_first, from_second)
    north_rows[...] = north[: 4 * levels]
    south_rows[...] = south[: 4 * levels]
    for f in range(FIELDS):
        ext[f, :rows, :] = fields[f]
        ext[f, rows + DEEP : tall - DEEP, :] = jnp.zeros((tall - rows - 2 * DEEP, cols), jnp.float32)
        for j in range(DEEP):
            at = 4 * levels + FIELDS * j + f
            ext[f, rows + j : rows + j + 1, :] = north[at : at + 1]
            ext[f, tall - 1 - j : tall - j, :] = south[at : at + 1]
    used = 8 * levels
    lane = iota((tall, cols), 1)
    base = jnp.concatenate([columns[...], jnp.zeros((tall - rows, cols), jnp.float32)], axis=0)
    east, west = base, base
    for f in range(FIELDS):
        here = (lane >= used + DEEP * f) & (lane < used + DEEP * (f + 1))
        layer = ext[f]
        east = jnp.where(here, pltpu.roll(layer, (used + DEEP * f + DEEP) % cols, 1), east)
        west = jnp.where(here, pltpu.roll(layer, used + DEEP * f, 1), west)
    to_east[...] = east
    to_west[...] = west


def krylov_kernel(used, ext, from_west, from_east, base, moments):
    tall, cols = ext.shape[1], ext.shape[2]
    rows = base.shape[1]
    lane = iota((tall, cols), 1)
    west = from_west[...]
    east = from_east[...]
    first = lane == 0
    last = lane == cols - 1

    def load(f):
        a = pltpu.roll(west, (2 * cols - DEEP - used - DEEP * f) % cols, 1)
        b = pltpu.roll(east, (2 * cols - used - DEEP * f) % cols, 1)
        side = jnp.where(lane >= cols - DEEP, a, jnp.where(lane < DEEP, b, 0.0))
        return ext[f], side

    def plus_x(pair):
        a, b = (pltpu.roll(part, cols - 1, 1) for part in pair)
        return jnp.where(last, b, a), jnp.where(last, a, b)

    def minus_x(pair):
        a, b = (pltpu.roll(part, 1, 1) for part in pair)
        return jnp.where(first, b, a), jnp.where(first, a, b)

    def plus_y(pair):
        return tuple(pltpu.roll(part, tall - 1, 0) for part in pair)

    def minus_y(pair):
        return tuple(pltpu.roll(part, 1, 0) for part in pair)

    def each(function, *pairs):
        return tuple(function(*parts) for parts in zip(*pairs))

    def neighbours(pair):
        return each(
            lambda a, b, c, d: (a + b) + (c + d), plus_x(pair), minus_x(pair), plus_y(pair), minus_y(pair)
        )

    press, zonal, merid, wet, weights, anomaly = (load(f) for f in range(FIELDS))
    half = 0.5 * TIME_STEP
    flow = lambda w, speed, a, b: w * (speed - half * (a - b))
    east_flow = each(flow, wet, zonal, plus_x(press), minus_x(press))
    north_flow = each(flow, wet, merid, plus_y(press), minus_y(press))
    right = each(
        lambda w, g, n, a, b, c, d: w * (g * n - 0.5 * (a - b + c - d)),
        wet,
        weights,
        anomaly,
        plus_x(east_flow),
        minus_x(east_flow),
        plus_y(north_flow),
        minus_y(north_flow),
    )
    diagonal = each(lambda g: 4.0 + g, weights)
    inverse = each(lambda m: 1.0 / m, diagonal)
    scale = each(lambda w, i: w * i, wet, inverse)
    zero = each(lambda r, i: r * i, right, inverse)
    one = each(lambda a, n: a * n, scale, neighbours(zero))
    two = each(lambda a, n: a * n, scale, neighbours(one))
    last_sum = neighbours(two)[0][:rows]
    right, middle = right[0][:rows], diagonal[0][:rows]
    zero, one, two = zero[0][:rows], one[0][:rows], two[0][:rows]
    base[0] = zero
    base[1] = one
    base[2] = two
    weighted = middle * one
    products = (
        right * zero,
        right * one,
        weighted * one,
        weighted * two,
        middle * two * two,
        last_sum * two,
    )
    for k, product in enumerate(products):
        moments[k : k + 1, :] = jnp.sum(product, axis=0, keepdims=True)
    moments[len(products) :, :] = jnp.zeros((moments.shape[0] - len(products), cols), jnp.float32)


def step_kernel(
    spans, heat, salt, zonal, merid, water, north_rows, south_rows, from_west, from_east,
    new_heat, new_salt, new_zonal, new_merid,
):
    levels, rows, cols = heat.shape
    wet = water[...].astype(jnp.float32)
    lane = iota((rows, cols), 1)
    row = iota((rows, cols), 0)
    sides = jnp.where((lane & 3) < 2, from_west[:rows, :], from_east[:rows, :])

    def around(cells, q, k, place):
        side = pltpu.roll(sides, (2 * cols - (4 * q + 2)) % cols, 1)

        def shift_x(by):
            a = pltpu.roll(cells, by % cols, 1)
            b = pltpu.roll(side, by % cols, 1)
            own = lane >= by if by > 0 else lane < cols + by
            return jnp.where(own, a, b)

        n0 = north_rows[place + k : place + k + 1, :]
        n1 = north_rows[place + levels + k : place + levels + k + 1, :]
        s0 = south_rows[place + k : place + k + 1, :]
        s1 = south_rows[place + levels + k : place + levels + k + 1, :]
        north_one = jnp.where(row == rows - 1, n0, pltpu.roll(cells, rows - 1, 0))
        north_two = jnp.where(row == rows - 1, n1, jnp.where(row == rows - 2, n0, pltpu.roll(cells, rows - 2, 0)))
        south_one = jnp.where(row == 0, s0, pltpu.roll(cells, 1, 0))
        south_two = jnp.where(row == 0, s1, jnp.where(row == 1, s0, pltpu.roll(cells, 2, 0)))
        return (shift_x(-1), shift_x(1), shift_x(-2), shift_x(2), north_one, south_one, north_two, south_two)

    def advance(cells, parts, speed_x, speed_y):
        e1, w1, e2, w2, n1, s1, n2, s2 = parts
        grad_east = 8.0 * (e1 - w1) - (e2 - w2)
        grad_north = 8.0 * (n1 - s1) - (n2 - s2)
        laplace = (e1 + w1) + (n1 + s1) - 4.0 * cells
        tendency = (-TIME_STEP / 12.0) * (speed_x * grad_east + speed_y * grad_north) + MIXING * laplace
        return cells + wet * tendency

    half = 0.5 * TIME_STEP
    above_x = jnp.zeros((rows, cols), jnp.float32)
    above_y = jnp.zeros((rows, cols), jnp.float32)
    for k in range(levels):
        t, s, u, v = heat[k], salt[k], zonal[k], merid[k]
        around_t = around(t, k, k, 0)
        around_s = around(s, levels + k, k, 2 * levels)
        new_heat[k] = advance(t, around_t, u, v)
        new_salt[k] = advance(s, around_s, u, v)
        layer_x = spans[k] * (density(around_t[0], around_s[0]) - density(around_t[1], around_s[1]))
        layer_y = spans[k] * (density(around_t[4], around_s[4]) - density(around_t[5], around_s[5]))
        new_zonal[k] = wet * (u - half * (above_x + 0.5 * layer_x))
        new_merid[k] = wet * (v - half * (above_y + 0.5 * layer_y))
        above_x = above_x + layer_x
        above_y = above_y + layer_y


def surface_kernel(shares, base, surface):
    sums = jnp.sum(jnp.sum(shares[...], axis=0), axis=1, keepdims=True)
    nu = [sums[k : k + 1, :] for k in range(6)]

    def ratio(a, b):
        good = b > 0.0
        return jnp.where(good, a / jnp.where(good, b, 1.0), 0.0)

    def form(p, h):
        total = 0.0
        for i, a in enumerate(p):
            for j in range(i, len(p)):
                term = a * p[j] * h[i + j]
                total = total + (term if i == j else 2.0 * term)
        return total

    gap = [nu[k] - nu[k + 1] for k in range(5)]
    rz = nu[0]
    alpha = ratio(rz, gap[0])
    one = jnp.ones_like(rz)
    y = [one - alpha, alpha]
    x = [alpha, 0.0, 0.0]
    new = form(y, nu)
    beta = ratio(new, rz)
    rz = new
    p = [y[0] + beta, y[1]]
    alpha = ratio(rz, form(p, gap))
    x = [x[0] + alpha * p[0], alpha * p[1], 0.0]
    y = [y[0] - alpha * p[0], y[1] - alpha * (p[1] - p[0]), alpha * p[1]]
    new = form(y, nu)
    beta = ratio(new, rz)
    rz = new
    p = [y[0] + beta * p[0], y[1] + beta * p[1], y[2]]
    alpha = ratio(rz, form(p, gap))
    x = [x[0] + alpha * p[0], x[1] + alpha * p[1], alpha * p[2]]
    surface[...] = x[0] * base[0] + x[1] * base[1] + x[2] * base[2]


def call(kernel, outs, smem, flops, moved, **named):
    specs = lambda count: [pl.BlockSpec(memory_space=pltpu.VMEM)] * count

    def run(*args):
        return pl.pallas_call(
            kernel,
            out_shape=[jax.ShapeDtypeStruct(shape, jnp.float32) for shape in outs],
            in_specs=[pl.BlockSpec(memory_space=pltpu.SMEM)] * smem + specs(len(args) - smem),
            out_specs=specs(len(outs)),
            cost_estimate=pl.CostEstimate(flops=flops, bytes_accessed=moved, transcendentals=0),
            compiler_params=pltpu.CompilerParams(vmem_limit_bytes=VMEM_LIMIT),
            **named,
        )(*args)

    return run


def body(
    warmth_deviation,
    saltiness_deviation,
    easterly_speed,
    poleward_speed,
    stratum_spans,
    water_indicator,
    opposite_counterpart,
    elevation_weights,
    elevation_anomaly,
):
    lons, lats = lax.axis_size("lon"), lax.axis_size("lat")
    lon, lat = lax.axis_index("lon"), lax.axis_index("lat")
    levels, rows, cols = warmth_deviation.shape
    high = packet_rows(levels)
    tall = rows + 16
    width = cols * lons
    flat = lambda i, j: (i % lons) * lats + j

    hinge = lax.rem(opposite_counterpart[0] + 1 + cols * lon, width)
    block = hinge // cols
    meta = jnp.stack([lax.rem(lat, 2), lax.rem(hinge, cols), (lat == lats - 1).astype(jnp.int32)]).astype(jnp.int32)

    state = (warmth_deviation, saltiness_deviation, easterly_speed, poleward_speed)
    cells = levels * rows * cols
    fields, first, second, columns = call(
        pack_kernel,
        [(FIELDS, rows, cols), (high, cols), (high, cols), (rows, cols)],
        2,
        12 * cells,
        16 * cells,
        name="level_sums",
    )(meta, stratum_spans, *state, water_indicator, elevation_weights, elevation_anomaly)

    pairs_first = [(flat(i, j), flat(i, j ^ 1)) for i in range(lons) for j in range(lats)]
    pairs_inner = [
        (flat(i, a), flat(i, b))
        for i in range(lons)
        for j in range(1, lats - 1, 2)
        for a, b in ((j, j + 1), (j + 1, j))
    ]
    axes = ("lon", "lat")
    got_first = lax.ppermute(first, axes, pairs_first)

    def facing(shift, packet):
        near = [(flat(shift - 1 - i, lats - 1), flat(i, lats - 1)) for i in range(lons)]
        far = [(flat(shift - i, lats - 1), flat(i, lats - 1)) for i in range(lons)]
        return lax.ppermute(packet, axes, pairs_inner + near), lax.ppermute(packet, axes, far)

    got_second, got_third = lax.switch(block, [functools.partial(facing, s) for s in range(lons)], second)

    ext, north_rows, south_rows, to_east, to_west = call(
        turn_kernel,
        [(FIELDS, tall, cols), (4 * levels, cols), (4 * levels, cols), (tall, cols), (tall, cols)],
        1,
        FIELDS * tall * cols,
        4 * 4 * FIELDS * tall * cols,
        name="row_halos",
    )(meta, fields, got_first, got_second, got_third, columns)

    from_west = lax.ppermute(to_east, "lon", [(i, (i + 1) % lons) for i in range(lons)])
    from_east = lax.ppermute(to_west, "lon", [((i + 1) % lons, i) for i in range(lons)])

    base, moments = call(
        functools.partial(krylov_kernel, 8 * levels),
        [(3, rows, cols), (8, cols)],
        0,
        200 * tall * cols,
        4 * 12 * tall * cols,
        name="krylov",
    )(ext, from_west, from_east)

    new_heat, new_salt, new_zonal, new_merid = call(
        step_kernel,
        [(levels, rows, cols)] * 4,
        1,
        120 * cells,
        32 * cells,
        name="levels_step",
    )(stratum_spans, *state, water_indicator, north_rows, south_rows, from_west, from_east)

    count = lons * lats
    shares = lax.all_to_all(jnp.broadcast_to(moments, (count,) + moments.shape), axes, 0, 0)
    (surface,) = call(
        surface_kernel, [(rows, cols)], 0, 6 * rows * cols, 16 * rows * cols, name="surface"
    )(shares, base)
    return (new_heat, new_salt, new_zonal, new_merid, surface)


def solution(mesh):
    for axis in mesh.shape.values():
        assert axis > 1 and axis & (axis - 1) == 0
    levels = P(None, "lat", "lon")
    flat = P("lat", "lon")
    return jax.shard_map(
        body,
        mesh=mesh,
        in_specs=(levels, levels, levels, levels, P(), flat, P("lon"), flat, flat),
        out_specs=(levels, levels, levels, levels, flat),
        check_vma=False,
    )
```

```python
import functools

import jax
import jax.numpy as jnp
from jax import lax
from jax.experimental import pallas as pl
from jax.experimental.pallas import tpu as pltpu
from jax.sharding import PartitionSpec as P

TIME_STEP = 0.1
MIXING = 0.1

DEEP = 5
FIELDS = 6
VMEM_LIMIT = 32 * 1024 * 1024
LOAD_FLOPS = 10**10


def density(heat, salt):
    return heat * (-1.0 - 0.15 * heat - 0.2 * salt) + 0.8 * salt


def iota(shape, axis):
    return lax.broadcasted_iota(jnp.int32, shape, axis)


def packet_rows(levels):
    return -(-(4 * levels + FIELDS * DEEP) // 8) * 8


def place_kernel(meta, placed):
    for i in range(4):
        placed[i] = meta[i]


def pack_kernel(
    meta, spans, facing_of, heat, salt, zonal, merid, water, weights, anomaly, sums, first, second, columns
):
    levels, rows, cols = heat.shape
    span = [spans[k] for k in range(levels)]
    below = [None] * levels
    total = 0.0
    for k in reversed(range(levels)):
        below[k] = span[k] * (0.5 * span[k] + total)
        total = total + span[k]
    odd = meta[0]
    packets = ((first, odd == 0), (second, odd == 1))
    near_row = [[jnp.where(at_top, rows - 1 - j, j) for j in range(DEEP)] for _, at_top in packets]
    group = iota((rows, cols), 1) // 4
    press = jnp.zeros((rows, cols), jnp.float32)
    east = jnp.zeros((rows, cols), jnp.float32)
    north = jnp.zeros((rows, cols), jnp.float32)
    edge = jnp.zeros((rows, cols), jnp.float32)
    for k in range(levels):
        press = press + below[k] * density(heat[k], salt[k])
        east = east + span[k] * zonal[k]
        north = north + span[k] * merid[k]
        for q, source in ((k, heat), (levels + k, salt)):
            edge = jnp.where(group == q, pltpu.roll(source[k], (4 * q + 2) % cols, 1), edge)
            for (packet, _), near in zip(packets, near_row):
                for j in range(2):
                    at = q + j * levels if q < levels else q + (j + 1) * levels
                    packet[at : at + 1, :] = source[k, pl.ds(near[j], 1), :]
    columns[...] = edge
    sums[0] = press
    sums[1] = east
    sums[2] = north
    fields = (sums.at[0], sums.at[1], sums.at[2], water, weights, anomaly)
    for (packet, _), near in zip(packets, near_row):
        for j in range(DEEP):
            for f, field in enumerate(fields):
                at = 4 * levels + FIELDS * j + f
                packet[at : at + 1, :] = field[pl.ds(near[j], 1), :].astype(jnp.float32)
        used = 4 * levels + FIELDS * DEEP
        if used < packet.shape[0]:
            packet[used:, :] = jnp.zeros((packet.shape[0] - used, cols), jnp.float32)


def turn_kernel(
    meta, facing_of, sums, water, weights, anomaly, first, second, third, columns,
    ext, north_rows, south_rows, to_near, to_far,
):
    high, cols = first.shape
    rows = sums.shape[1]
    tall = ext.shape[1]
    levels = north_rows.shape[0] // 4
    odd, top, lon_odd, lon = meta[0], meta[1], meta[2], meta[3]
    offset = lax.rem(facing_of[0] + 1 + cols * lon, cols)
    lane = iota((high, cols), 1)
    place = iota((high, cols), 0) - 4 * levels
    kind = lax.rem(jnp.maximum(place, 0), FIELDS)
    flips = (place >= 0) & ((kind == 1) | (kind == 2))
    from_first = first[...]
    from_second = second[...]
    facing = jnp.where(lane < offset, third[...], from_second)
    source = offset - 1 - lane
    source = jnp.where(source < 0, source + cols, source)
    facing = jnp.take_along_axis(facing, source, axis=1)
    facing = jnp.where(flips, -facing, facing)
    beyond = jnp.where(top == 1, facing, from_second)
    north = jnp.where(odd == 1, beyond, from_first)
    south = jnp.where(odd == 1, from_first, from_second)
    north_rows[...] = north[: 4 * levels]
    south_rows[...] = south[: 4 * levels]
    fields = (sums.at[0], sums.at[1], sums.at[2], water, weights, anomaly)
    for f in range(FIELDS):
        ext[f, :rows, :] = fields[f][...].astype(jnp.float32)
        ext[f, rows + DEEP : tall - DEEP, :] = jnp.zeros((tall - rows - 2 * DEEP, cols), jnp.float32)
        for j in range(DEEP):
            at = 4 * levels + FIELDS * j + f
            ext[f, rows + j : rows + j + 1, :] = north[at : at + 1]
            ext[f, tall - 1 - j : tall - j, :] = south[at : at + 1]
    used = 8 * levels
    lane = iota((tall, cols), 1)
    base = jnp.concatenate([columns[...], jnp.zeros((tall - rows, cols), jnp.float32)], axis=0)
    east, west = base, base
    for f in range(FIELDS):
        here = (lane >= used + DEEP * f) & (lane < used + DEEP * (f + 1))
        layer = ext[f]
        east = jnp.where(here, pltpu.roll(layer, (used + DEEP * f + DEEP) % cols, 1), east)
        west = jnp.where(here, pltpu.roll(layer, used + DEEP * f, 1), west)
    to_near[...] = jnp.where(lon_odd == 1, west, east)
    to_far[...] = jnp.where(lon_odd == 1, east, west)


def krylov_kernel(used, meta, ext, from_near, from_far, base, moments):
    tall, cols = ext.shape[1], ext.shape[2]
    rows = base.shape[1]
    lane = iota((tall, cols), 1)
    west = jnp.where(meta[2] == 1, from_near[...], from_far[...])
    east = jnp.where(meta[2] == 1, from_far[...], from_near[...])
    first = lane == 0
    last = lane == cols - 1

    def load(f):
        a = pltpu.roll(west, (2 * cols - DEEP - used - DEEP * f) % cols, 1)
        b = pltpu.roll(east, (2 * cols - used - DEEP * f) % cols, 1)
        side = jnp.where(lane >= cols - DEEP, a, jnp.where(lane < DEEP, b, 0.0))
        return ext[f], side

    def plus_x(pair):
        a, b = (pltpu.roll(part, cols - 1, 1) for part in pair)
        return jnp.where(last, b, a), jnp.where(last, a, b)

    def minus_x(pair):
        a, b = (pltpu.roll(part, 1, 1) for part in pair)
        return jnp.where(first, b, a), jnp.where(first, a, b)

    def plus_y(pair):
        return tuple(pltpu.roll(part, tall - 1, 0) for part in pair)

    def minus_y(pair):
        return tuple(pltpu.roll(part, 1, 0) for part in pair)

    def each(function, *pairs):
        return tuple(function(*parts) for parts in zip(*pairs))

    def neighbours(pair):
        return each(
            lambda a, b, c, d: (a + b) + (c + d), plus_x(pair), minus_x(pair), plus_y(pair), minus_y(pair)
        )

    press, zonal, merid, wet, weights, anomaly = (load(f) for f in range(FIELDS))
    half = 0.5 * TIME_STEP
    flow = lambda w, speed, a, b: w * (speed - half * (a - b))
    east_flow = each(flow, wet, zonal, plus_x(press), minus_x(press))
    north_flow = each(flow, wet, merid, plus_y(press), minus_y(press))
    right = each(
        lambda w, g, n, a, b, c, d: w * (g * n - 0.5 * (a - b + c - d)),
        wet,
        weights,
        anomaly,
        plus_x(east_flow),
        minus_x(east_flow),
        plus_y(north_flow),
        minus_y(north_flow),
    )
    diagonal = each(lambda g: 4.0 + g, weights)
    inverse = each(lambda m: 1.0 / m, diagonal)
    scale = each(lambda w, i: w * i, wet, inverse)
    zero = each(lambda r, i: r * i, right, inverse)
    one = each(lambda a, n: a * n, scale, neighbours(zero))
    two = each(lambda a, n: a * n, scale, neighbours(one))
    last_sum = neighbours(two)[0][:rows]
    right, middle = right[0][:rows], diagonal[0][:rows]
    zero, one, two = zero[0][:rows], one[0][:rows], two[0][:rows]
    base[0] = zero
    base[1] = one
    base[2] = two
    weighted = middle * one
    products = (
        right * zero,
        right * one,
        weighted * one,
        weighted * two,
        middle * two * two,
        last_sum * two,
    )
    which = iota((8, cols), 0)
    sums = jnp.zeros((8, cols), jnp.float32)
    for k, product in enumerate(products):
        sums = jnp.where(which == k, jnp.sum(product, axis=0, keepdims=True), sums)
    sums = jnp.sum(sums, axis=1, keepdims=True)
    sums = jnp.sum(jnp.where(which == iota((8, cols), 1), sums, 0.0), axis=0, keepdims=True)
    moments[...] = jnp.broadcast_to(sums, moments.shape)


def step_kernel(
    meta, spans, heat, salt, zonal, merid, water, north_rows, south_rows, from_near, from_far,
    heat_out, salt_out, zonal_out, merid_out,
    new_heat, new_salt, new_zonal, new_merid, sems,
):
    levels, rows, cols = heat.shape
    wet = water[...].astype(jnp.float32)
    lane = iota((rows, cols), 1)
    row = iota((rows, cols), 0)
    near = ((lane & 3) < 2) == (meta[2] == 1)
    sides = jnp.where(near, from_near[:rows, :], from_far[:rows, :])

    def around(cells, q, k, place):
        side = pltpu.roll(sides, (2 * cols - (4 * q + 2)) % cols, 1)

        def shift_x(by):
            a = pltpu.roll(cells, by % cols, 1)
            b = pltpu.roll(side, by % cols, 1)
            own = lane >= by if by > 0 else lane < cols + by
            return jnp.where(own, a, b)

        n0 = north_rows[place + k : place + k + 1, :]
        n1 = north_rows[place + levels + k : place + levels + k + 1, :]
        s0 = south_rows[place + k : place + k + 1, :]
        s1 = south_rows[place + levels + k : place + levels + k + 1, :]
        north_one = jnp.where(row == rows - 1, n0, pltpu.roll(cells, rows - 1, 0))
        north_two = jnp.where(row == rows - 1, n1, jnp.where(row == rows - 2, n0, pltpu.roll(cells, rows - 2, 0)))
        south_one = jnp.where(row == 0, s0, pltpu.roll(cells, 1, 0))
        south_two = jnp.where(row == 0, s1, jnp.where(row == 1, s0, pltpu.roll(cells, 2, 0)))
        return (shift_x(-1), shift_x(1), shift_x(-2), shift_x(2), north_one, south_one, north_two, south_two)

    def advance(cells, parts, speed_x, speed_y):
        e1, w1, e2, w2, n1, s1, n2, s2 = parts
        grad_east = 8.0 * (e1 - w1) - (e2 - w2)
        grad_north = 8.0 * (n1 - s1) - (n2 - s2)
        laplace = (e1 + w1) + (n1 + s1) - 4.0 * cells
        tendency = (-TIME_STEP / 12.0) * (speed_x * grad_east + speed_y * grad_north) + MIXING * laplace
        return cells + wet * tendency

    stores = ((new_heat, heat_out), (new_salt, salt_out), (new_zonal, zonal_out), (new_merid, merid_out))
    size = levels // sems.shape[1]
    copies = []
    half = 0.5 * TIME_STEP
    above_x = jnp.zeros((rows, cols), jnp.float32)
    above_y = jnp.zeros((rows, cols), jnp.float32)
    for k in range(levels):
        t, s, u, v = heat[k], salt[k], zonal[k], merid[k]
        around_t = around(t, k, k, 0)
        around_s = around(s, levels + k, k, 2 * levels)
        new_heat[k] = advance(t, around_t, u, v)
        new_salt[k] = advance(s, around_s, u, v)
        layer_x = spans[k] * (density(around_t[0], around_s[0]) - density(around_t[1], around_s[1]))
        layer_y = spans[k] * (density(around_t[4], around_s[4]) - density(around_t[5], around_s[5]))
        new_zonal[k] = wet * (u - half * (above_x + 0.5 * layer_x))
        new_merid[k] = wet * (v - half * (above_y + 0.5 * layer_y))
        above_x = above_x + layer_x
        above_y = above_y + layer_y
        if (k + 1) % size == 0:
            piece = pl.ds(k + 1 - size, size)
            for i, (near_ref, far_ref) in enumerate(stores):
                copies.append(pltpu.make_async_copy(near_ref.at[piece], far_ref.at[piece], sems.at[i, k // size]))
                copies[-1].start()
    for copy in copies:
        copy.wait()


def surface_kernel(shares, base, surface):
    sums = jnp.sum(shares[...], axis=0, keepdims=True)
    lane = iota(sums.shape, 1)
    nu = [jnp.sum(jnp.where(lane == k, sums, 0.0), axis=1, keepdims=True) for k in range(6)]

    def ratio(a, b):
        good = b > 0.0
        return jnp.where(good, a / jnp.where(good, b, 1.0), 0.0)

    def form(p, h):
        total = 0.0
        for i, a in enumerate(p):
            for j in range(i, len(p)):
                term = a * p[j] * h[i + j]
                total = total + (term if i == j else 2.0 * term)
        return total

    gap = [nu[k] - nu[k + 1] for k in range(5)]
    rz = nu[0]
    alpha = ratio(rz, gap[0])
    one = jnp.ones_like(rz)
    y = [one - alpha, alpha]
    x = [alpha, 0.0, 0.0]
    new = form(y, nu)
    beta = ratio(new, rz)
    rz = new
    p = [y[0] + beta, y[1]]
    alpha = ratio(rz, form(p, gap))
    x = [x[0] + alpha * p[0], alpha * p[1], 0.0]
    y = [y[0] - alpha * p[0], y[1] - alpha * (p[1] - p[0]), alpha * p[1]]
    new = form(y, nu)
    beta = ratio(new, rz)
    rz = new
    p = [y[0] + beta * p[0], y[1] + beta * p[1], y[2]]
    alpha = ratio(rz, form(p, gap))
    x = [x[0] + alpha * p[0], x[1] + alpha * p[1], alpha * p[2]]
    surface[...] = x[0] * base[0] + x[1] * base[1] + x[2] * base[2]


def call(kernel, outs, ins, flops, moved, name, out_space=pltpu.VMEM, scratch=(), types=jnp.float32):
    space = {"s": pltpu.SMEM, "v": pltpu.VMEM, "h": pltpu.HBM}
    return pl.pallas_call(
        kernel,
        out_shape=[jax.ShapeDtypeStruct(shape, types) for shape in outs],
        in_specs=[pl.BlockSpec(memory_space=space[letter]) for letter in ins],
        out_specs=[pl.BlockSpec(memory_space=out_space)] * len(outs),
        scratch_shapes=list(scratch),
        cost_estimate=pl.CostEstimate(flops=flops, bytes_accessed=moved, transcendentals=0),
        compiler_params=pltpu.CompilerParams(vmem_limit_bytes=VMEM_LIMIT),
        name=name,
    )


def body(
    warmth_deviation,
    saltiness_deviation,
    easterly_speed,
    poleward_speed,
    stratum_spans,
    water_indicator,
    opposite_counterpart,
    elevation_weights,
    elevation_anomaly,
):
    lons, lats = lax.axis_size("lon"), lax.axis_size("lat")
    lon, lat = lax.axis_index("lon"), lax.axis_index("lat")
    levels, rows, cols = warmth_deviation.shape
    high = packet_rows(levels)
    tall = rows + 16
    width = cols * lons
    flat = lambda i, j: (i % lons) * lats + j

    hinge = lax.rem(opposite_counterpart[0] + 1 + cols * lon, width)
    block = hinge // cols
    meta = jnp.stack([lax.rem(lat, 2), (lat == lats - 1).astype(jnp.int32), lax.rem(lon, 2), lon]).astype(jnp.int32)

    (meta,) = call(place_kernel, [(4,)], "s", LOAD_FLOPS, 16, "place", out_space=pltpu.SMEM, types=jnp.int32)(meta)

    state = (warmth_deviation, saltiness_deviation, easterly_speed, poleward_speed)
    cells = levels * rows * cols
    chunks = 5 if levels % 5 == 0 else 1
    level_buffers = [pltpu.VMEM((levels, rows, cols), jnp.float32)] * 4
    sums, first, second, columns = call(
        pack_kernel,
        [(3, rows, cols), (high, cols), (high, cols), (rows, cols)],
        "sssvvvvvvv",
        12 * cells,
        16 * cells,
        "level_sums",
    )(
        meta, stratum_spans, opposite_counterpart, *state,
        water_indicator, elevation_weights, elevation_anomaly,
    )

    pairs_first = [(flat(i, j), flat(i, j ^ 1)) for i in range(lons) for j in range(lats)]
    pairs_inner = [
        (flat(i, a), flat(i, b))
        for i in range(lons)
        for j in range(1, lats - 1, 2)
        for a, b in ((j, j + 1), (j + 1, j))
    ]
    axes = ("lon", "lat")
    got_first = lax.ppermute(first, axes, pairs_first)

    def facing(shift, packet):
        near = [(flat(shift - 1 - i, lats - 1), flat(i, lats - 1)) for i in range(lons)]
        far = [(flat(shift - i, lats - 1), flat(i, lats - 1)) for i in range(lons)]
        return lax.ppermute(packet, axes, pairs_inner + near), lax.ppermute(packet, axes, far)

    got_second, got_third = lax.switch(block, [functools.partial(facing, s) for s in range(lons)], second)

    ext, north_rows, south_rows, to_near, to_far = call(
        turn_kernel,
        [(FIELDS, tall, cols), (4 * levels, cols), (4 * levels, cols), (tall, cols), (tall, cols)],
        "ssvvvvvvvv",
        FIELDS * tall * cols,
        4 * 4 * FIELDS * tall * cols,
        "row_halos",
    )(
        meta, opposite_counterpart, sums, water_indicator, elevation_weights, elevation_anomaly,
        got_first, got_second, got_third, columns,
    )

    from_near = lax.ppermute(to_near, "lon", [(i, i ^ 1) for i in range(lons)])
    from_far = lax.ppermute(to_far, "lon", [(i, (i + 1 if i % 2 else i - 1) % lons) for i in range(lons)])

    count = lons * lats
    base, moments = call(
        functools.partial(krylov_kernel, 8 * levels),
        [(3, rows, cols), (count, cols)],
        "svvv",
        200 * tall * cols,
        4 * 12 * tall * cols,
        "krylov",
    )(meta, ext, from_near, from_far)

    new_heat, new_salt, new_zonal, new_merid = call(
        step_kernel,
        [(levels, rows, cols)] * 4,
        "ssvvvvvvvvv",
        120 * cells,
        32 * cells,
        "levels_step",
        out_space=pltpu.HBM,
        scratch=[*level_buffers, pltpu.SemaphoreType.DMA((4, chunks))],
    )(meta, stratum_spans, *state, water_indicator, north_rows, south_rows, from_near, from_far)

    shares = lax.all_to_all(moments, axes, 0, 0, tiled=True)
    (surface,) = call(surface_kernel, [(rows, cols)], "vv", 6 * rows * cols, 16 * rows * cols, "surface")(shares, base)
    return (new_heat, new_salt, new_zonal, new_merid, surface)


def solution(mesh):
    for axis in mesh.shape.values():
        assert axis > 1 and axis & (axis - 1) == 0
    levels = P(None, "lat", "lon")
    flat = P("lat", "lon")
    return jax.shard_map(
        body,
        mesh=mesh,
        in_specs=(levels, levels, levels, levels, P(), flat, P("lon"), flat, flat),
        out_specs=(levels, levels, levels, levels, flat),
        check_vma=False,
    )
```

```python
import functools

import jax
import jax.numpy as jnp
from jax import lax
from jax.experimental import pallas as pl
from jax.experimental.pallas import tpu as pltpu
from jax.sharding import PartitionSpec as P

TIME_STEP = 0.1
MIXING = 0.1

DEEP = 5
SIDE = (5, 4, 3, 4, 3, 3)
FIELDS = len(SIDE)
START = tuple(sum(SIDE[:f]) for f in range(FIELDS))
FLIPPED = (1, 2)
VMEM_LIMIT = 32 * 1024 * 1024
LOAD_FLOPS = 10**10


def density(heat, salt):
    return heat * (-1.0 - 0.15 * heat - 0.2 * salt) + 0.8 * salt


def iota(shape, axis):
    return lax.broadcasted_iota(jnp.int32, shape, axis)


def packet_rows(levels):
    return -(-(4 * levels + FIELDS * DEEP) // 8) * 8


def flags(meta):
    return meta[0:1, :] == 1, meta[1:2, :] == 1, meta[2:3, :] == 1


def place_kernel(meta, placed):
    for i in range(3):
        placed[i : i + 1, :] = jnp.broadcast_to(meta[0:1, i : i + 1], (1, placed.shape[1]))
    placed[3:, :] = jnp.zeros((placed.shape[0] - 3, placed.shape[1]), jnp.int32)


def pack_kernel(
    meta, spans, facing, heat, salt, zonal, merid, water, weights, anomaly,
    sums, first, second, east_columns, west_columns,
    top, bottom, back,
):
    levels, rows, cols = heat.shape
    span = [spans[0:1, k : k + 1] for k in range(levels)]
    below = [None] * levels
    total = jnp.zeros((1, 1), jnp.float32)
    for k in reversed(range(levels)):
        below[k] = span[k] * (0.5 * span[k] + total)
        total = total + span[k]
    pair = iota((rows, cols), 1) // 2
    zero = jnp.zeros((rows, cols), jnp.float32)
    press, east, north, east_edge, west_edge = zero, zero, zero, zero, zero
    for k in range(levels):
        press = press + below[k] * density(heat[k], salt[k])
        east = east + span[k] * zonal[k]
        north = north + span[k] * merid[k]
        for q, source in ((k, heat), (levels + k, salt)):
            cells = source[k]
            here = pair == q
            east_edge = jnp.where(here, pltpu.roll(cells, (2 * q + 2) % cols, 1), east_edge)
            west_edge = jnp.where(here, pltpu.roll(cells, 2 * q, 1), west_edge)
            top[2 * q : 2 * q + 2, :] = source[k, rows - 2 :, :]
            bottom[2 * q : 2 * q + 2, :] = source[k, :2, :]
            for i in range(2):
                back[2 * q + i : 2 * q + i + 1, :] = source[k, rows - 1 - i : rows - i, :]
    east_columns[...] = east_edge
    west_columns[...] = west_edge
    sums[0] = press
    sums[1] = east
    sums[2] = north
    fields = (sums.at[0], sums.at[1], sums.at[2], water, weights, anomaly)
    for f, field in enumerate(fields):
        at = 4 * levels + DEEP * f
        top[at : at + DEEP, :] = field[rows - DEEP :, :].astype(jnp.float32)
        bottom[at : at + DEEP, :] = field[:DEEP, :].astype(jnp.float32)
        for j in range(DEEP):
            back[at + j : at + j + 1, :] = field[rows - 1 - j : rows - j, :].astype(jnp.float32)
    used = 4 * levels + DEEP * FIELDS
    high = first.shape[0]
    if used < high:
        for packet in (top, bottom, back):
            packet[used:, :] = jnp.zeros((high - used, cols), jnp.float32)
    odd, last, _ = flags(meta)
    first[...] = jnp.where(odd, bottom[...], top[...])
    second[...] = jnp.where(last, back[...], jnp.where(odd, top[...], bottom[...]))


def turn_kernel(
    meta, sums, water, weights, anomaly, first, second, east_columns, west_columns,
    ext, to_near, to_far,
):
    rows, cols = sums.shape[1], sums.shape[2]
    tall = ext.shape[1]
    high = first.shape[0]
    deep = high - to_near.shape[0] + tall
    odd, _, lon_odd = flags(meta)
    from_first = first[...]
    from_second = second[...]
    north = jnp.where(odd, from_second, from_first)
    south = jnp.where(odd, from_first, from_second)
    fields = (sums.at[0], sums.at[1], sums.at[2], water, weights, anomaly)
    for f in range(FIELDS):
        at = deep + DEEP * f
        ext[f, :rows, :] = fields[f][...].astype(jnp.float32)
        ext[f, rows : rows + DEEP, :] = north[at : at + DEEP]
        ext[f, rows + DEEP : tall - DEEP, :] = jnp.zeros((tall - rows - 2 * DEEP, cols), jnp.float32)
        ext[f, tall - DEEP :, :] = south[at : at + DEEP]
    lane = iota((tall, cols), 1)
    spare = jnp.zeros((tall - rows, cols), jnp.float32)
    passed = from_second[:deep]
    fill = jnp.zeros((tall - deep, cols), jnp.float32)
    half = lane >= cols // 2
    east = jnp.where(half, jnp.concatenate([pltpu.roll(passed, cols // 2, 1), fill], axis=0),
                     jnp.concatenate([east_columns[...], spare], axis=0))
    west = jnp.where(half, jnp.concatenate([passed, fill], axis=0),
                     jnp.concatenate([west_columns[...], spare], axis=0))
    for f in range(FIELDS):
        at = deep + START[f]
        here = (lane >= at) & (lane < at + SIDE[f])
        layer = ext[f]
        east = jnp.where(here, pltpu.roll(layer, (at + SIDE[f]) % cols, 1), east)
        west = jnp.where(here, pltpu.roll(layer, at, 1), west)
    to_near[:tall, :] = jnp.where(lon_odd, west, east)
    to_far[:tall, :] = jnp.where(lon_odd, east, west)
    to_near[tall:, :] = from_second[deep:]
    to_far[tall:, :] = from_second[deep:]


def fold_shift(facing):
    cols = facing.shape[1]
    offset = (facing[0:1, 0:1] + 1) & (cols - 1)
    return jnp.where(offset >= cols // 2, offset - cols, offset)


def fold(shift, west, own, east, beside):
    rows, cols = own.shape
    lane = iota((rows, cols), 1)
    source = cols - 1 - lane
    if beside:
        place = (source + shift) & (cols - 1)
        low = jnp.where(place - cols < shift, west, own)
        merged = jnp.where(place >= cols // 2, low, jnp.where(place >= shift, east, own))
    else:
        merged = jnp.where(source >= cols - shift, west, jnp.where(source < -shift, east, own))
    return jnp.take_along_axis(merged, cols - 1 - ((lane - shift) & (cols - 1)), axis=1)


def krylov_kernel(used, meta, facing, ext, second, from_near, from_far, base, moments, folded):
    tall, cols = ext.shape[1], ext.shape[2]
    rows = base.shape[1]
    size = from_near.shape[0] - tall
    _, top, lon_odd = flags(meta)
    west = jnp.where(lon_odd, from_near[...], from_far[...])
    east = jnp.where(lon_odd, from_far[...], from_near[...])
    shift = fold_shift(facing)
    row = iota((size, cols), 0)
    flips = (row >= DEEP * FLIPPED[0]) & (row < DEEP * (FLIPPED[-1] + 1))
    for side in range(2):
        cells = fold(shift, west[tall:], second[used:, :], east[tall:], side == 1)
        folded[side, :size, :] = jnp.where(flips, -cells, cells)
    folded[:, size:, :] = jnp.zeros((2, folded.shape[1] - size, cols), jnp.float32)
    lane = iota((tall, cols), 1)
    first = lane == 0
    last = lane == cols - 1
    kept = iota((8, cols), 0) < DEEP

    def load(f):
        at = used + START[f]
        a = pltpu.roll(west[:tall], (2 * cols - SIDE[f] - at) % cols, 1)
        b = pltpu.roll(east[:tall], (cols - at) % cols, 1)
        beside = jnp.where(lane >= cols - SIDE[f], a, jnp.where(lane < SIDE[f], b, 0.0))

        def put(cells, side):
            new = folded[side, DEEP * f : DEEP * f + 8, :]
            new = jnp.where(kept, jnp.where(top, new, cells[rows : rows + 8]), 0.0)
            return jnp.concatenate([cells[:rows], new, cells[rows + 8 :]], axis=0)

        return put(ext[f], 0), put(beside, 1)

    def plus_x(pair):
        a, b = (pltpu.roll(part, cols - 1, 1) for part in pair)
        return jnp.where(last, b, a), jnp.where(last, a, b)

    def minus_x(pair):
        a, b = (pltpu.roll(part, 1, 1) for part in pair)
        return jnp.where(first, b, a), jnp.where(first, a, b)

    def plus_y(pair):
        return tuple(pltpu.roll(part, tall - 1, 0) for part in pair)

    def minus_y(pair):
        return tuple(pltpu.roll(part, 1, 0) for part in pair)

    def each(function, *pairs):
        return tuple(function(*parts) for parts in zip(*pairs))

    def neighbours(pair):
        return each(
            lambda a, b, c, d: (a + b) + (c + d), plus_x(pair), minus_x(pair), plus_y(pair), minus_y(pair)
        )

    press, zonal, merid, wet, weights, anomaly = (load(f) for f in range(FIELDS))
    half = 0.5 * TIME_STEP
    flow = lambda w, speed, a, b: w * (speed - half * (a - b))
    east_flow = each(flow, wet, zonal, plus_x(press), minus_x(press))
    north_flow = each(flow, wet, merid, plus_y(press), minus_y(press))
    right = each(
        lambda w, g, n, a, b, c, d: w * (g * n - 0.5 * (a - b + c - d)),
        wet,
        weights,
        anomaly,
        plus_x(east_flow),
        minus_x(east_flow),
        plus_y(north_flow),
        minus_y(north_flow),
    )
    diagonal = each(lambda g: 4.0 + g, weights)
    inverse = each(lambda m: 1.0 / m, diagonal)
    scale = each(lambda w, i: w * i, wet, inverse)
    zero = each(lambda r, i: r * i, right, inverse)
    one = each(lambda a, n: a * n, scale, neighbours(zero))
    two = each(lambda a, n: a * n, scale, neighbours(one))
    last_sum = neighbours(two)[0][:rows]
    right, middle = right[0][:rows], diagonal[0][:rows]
    zero, one, two = zero[0][:rows], one[0][:rows], two[0][:rows]
    base[0] = zero
    base[1] = one
    base[2] = two
    weighted = middle * one
    products = (
        right * zero,
        right * one,
        weighted * one,
        weighted * two,
        middle * two * two,
        last_sum * two,
    )
    which = iota((8, cols), 0)
    sums = jnp.zeros((8, cols), jnp.float32)
    for k, product in enumerate(products):
        sums = jnp.where(which == k, jnp.sum(product, axis=0, keepdims=True), sums)
    sums = jnp.sum(sums, axis=1, keepdims=True)
    sums = jnp.sum(jnp.where(which == iota((8, cols), 1), sums, 0.0), axis=0, keepdims=True)
    moments[...] = jnp.broadcast_to(sums, moments.shape)


def step_kernel(
    meta, spans, facing, heat, salt, zonal, merid, water, first, second, from_near, from_far,
    heat_out, salt_out, zonal_out, merid_out,
    new_heat, new_salt, new_zonal, new_merid, north_rows, south_rows, sems,
):
    levels, rows, cols = heat.shape
    deep = 4 * levels
    odd, top, lon_odd = flags(meta)
    wet = water[...].astype(jnp.float32)
    lane = iota((rows, cols), 1)
    row = iota((rows, cols), 0)
    east = jnp.where(lon_odd, from_far[:rows, :], from_near[:rows, :])
    west = jnp.where(lon_odd, from_near[:rows, :], from_far[:rows, :])
    from_second = second[:deep, :]
    across = fold(fold_shift(facing), pltpu.roll(west[:deep], cols // 2, 1), from_second, east[:deep], False)
    north_rows[...] = jnp.where(odd, jnp.where(top, across, from_second), first[:deep, :])
    south_rows[...] = jnp.where(odd, first[:deep, :], from_second)

    def around(cells, q):
        a = pltpu.roll(east, (cols - 2 * q) % cols, 1)
        b = pltpu.roll(west, (2 * cols - 2 - 2 * q) % cols, 1)
        side = jnp.where(lane < 2, a, b)

        def shift_x(by):
            a = pltpu.roll(cells, by % cols, 1)
            b = pltpu.roll(side, by % cols, 1)
            own = lane >= by if by > 0 else lane < cols + by
            return jnp.where(own, a, b)

        n0 = north_rows[2 * q : 2 * q + 1, :]
        n1 = north_rows[2 * q + 1 : 2 * q + 2, :]
        s0 = south_rows[2 * q + 1 : 2 * q + 2, :]
        s1 = south_rows[2 * q : 2 * q + 1, :]
        north_one = jnp.where(row == rows - 1, n0, pltpu.roll(cells, rows - 1, 0))
        north_two = jnp.where(row == rows - 1, n1, jnp.where(row == rows - 2, n0, pltpu.roll(cells, rows - 2, 0)))
        south_one = jnp.where(row == 0, s0, pltpu.roll(cells, 1, 0))
        south_two = jnp.where(row == 0, s1, jnp.where(row == 1, s0, pltpu.roll(cells, 2, 0)))
        return (shift_x(-1), shift_x(1), shift_x(-2), shift_x(2), north_one, south_one, north_two, south_two)

    def advance(cells, parts, speed_x, speed_y):
        e1, w1, e2, w2, n1, s1, n2, s2 = parts
        grad_east = 8.0 * (e1 - w1) - (e2 - w2)
        grad_north = 8.0 * (n1 - s1) - (n2 - s2)
        laplace = (e1 + w1) + (n1 + s1) - 4.0 * cells
        tendency = (-TIME_STEP / 12.0) * (speed_x * grad_east + speed_y * grad_north) + MIXING * laplace
        return cells + wet * tendency

    stores = ((new_heat, heat_out), (new_salt, salt_out), (new_zonal, zonal_out), (new_merid, merid_out))
    size = levels // sems.shape[1]
    copies = []
    half = 0.5 * TIME_STEP
    above_x = jnp.zeros((rows, cols), jnp.float32)
    above_y = jnp.zeros((rows, cols), jnp.float32)
    for k in range(levels):
        t, s, u, v = heat[k], salt[k], zonal[k], merid[k]
        around_t = around(t, k)
        around_s = around(s, levels + k)
        new_heat[k] = advance(t, around_t, u, v)
        new_salt[k] = advance(s, around_s, u, v)
        span = spans[0:1, k : k + 1]
        layer_x = span * (density(around_t[0], around_s[0]) - density(around_t[1], around_s[1]))
        layer_y = span * (density(around_t[4], around_s[4]) - density(around_t[5], around_s[5]))
        new_zonal[k] = wet * (u - half * (above_x + 0.5 * layer_x))
        new_merid[k] = wet * (v - half * (above_y + 0.5 * layer_y))
        above_x = above_x + layer_x
        above_y = above_y + layer_y
        if (k + 1) % size == 0:
            piece = pl.ds(k + 1 - size, size)
            for i, (near_ref, far_ref) in enumerate(stores):
                copies.append(pltpu.make_async_copy(near_ref.at[piece], far_ref.at[piece], sems.at[i, k // size]))
                copies[-1].start()
    for copy in copies:
        copy.wait()


def surface_kernel(shares, base, surface):
    sums = jnp.sum(shares[...], axis=0, keepdims=True)
    lane = iota(sums.shape, 1)
    nu = [jnp.sum(jnp.where(lane == k, sums, 0.0), axis=1, keepdims=True) for k in range(6)]

    def ratio(a, b):
        good = b > 0.0
        return jnp.where(good, a / jnp.where(good, b, 1.0), 0.0)

    def form(p, h):
        total = 0.0
        for i, a in enumerate(p):
            for j in range(i, len(p)):
                term = a * p[j] * h[i + j]
                total = total + (term if i == j else 2.0 * term)
        return total

    gap = [nu[k] - nu[k + 1] for k in range(5)]
    rz = nu[0]
    alpha = ratio(rz, gap[0])
    one = jnp.ones_like(rz)
    y = [one - alpha, alpha]
    x = [alpha, 0.0, 0.0]
    new = form(y, nu)
    beta = ratio(new, rz)
    rz = new
    p = [y[0] + beta, y[1]]
    alpha = ratio(rz, form(p, gap))
    x = [x[0] + alpha * p[0], alpha * p[1], 0.0]
    y = [y[0] - alpha * p[0], y[1] - alpha * (p[1] - p[0]), alpha * p[1]]
    new = form(y, nu)
    beta = ratio(new, rz)
    rz = new
    p = [y[0] + beta * p[0], y[1] + beta * p[1], y[2]]
    alpha = ratio(rz, form(p, gap))
    x = [x[0] + alpha * p[0], x[1] + alpha * p[1], alpha * p[2]]
    surface[...] = x[0] * base[0] + x[1] * base[1] + x[2] * base[2]


def call(kernel, outs, flops, moved, name, out_space=pltpu.VMEM, scratch=(), types=jnp.float32):
    def run(*args):
        return pl.pallas_call(
            kernel,
            out_shape=[jax.ShapeDtypeStruct(shape, types) for shape in outs],
            in_specs=[pl.BlockSpec(memory_space=pltpu.VMEM)] * len(args),
            out_specs=[pl.BlockSpec(memory_space=out_space)] * len(outs),
            scratch_shapes=list(scratch),
            cost_estimate=pl.CostEstimate(flops=flops, bytes_accessed=moved, transcendentals=0),
            compiler_params=pltpu.CompilerParams(vmem_limit_bytes=VMEM_LIMIT),
            name=name,
        )(*args)

    return run


def body(
    warmth_deviation,
    saltiness_deviation,
    easterly_speed,
    poleward_speed,
    stratum_spans,
    water_indicator,
    opposite_counterpart,
    elevation_weights,
    elevation_anomaly,
):
    lons, lats = lax.axis_size("lon"), lax.axis_size("lat")
    lon, lat = lax.axis_index("lon"), lax.axis_index("lat")
    levels, rows, cols = warmth_deviation.shape
    assert cols & (cols - 1) == 0 and 4 * levels + sum(SIDE) <= cols // 2
    high = packet_rows(levels)
    tall = rows + 16
    long = tall + high - 4 * levels
    width = cols * lons
    flat = lambda i, j: (i % lons) * lats + j

    place = (lax.rem(lat, 2), (lat == lats - 1).astype(jnp.int32), lax.rem(lon, 2))
    meta = jnp.stack(place).astype(jnp.int32).reshape(1, 3)
    (meta,) = call(place_kernel, [(8, cols)], LOAD_FLOPS, 16, "place", types=jnp.int32)(meta)

    spans = stratum_spans.reshape(1, levels)
    facing = opposite_counterpart.reshape(1, cols)
    state = (warmth_deviation, saltiness_deviation, easterly_speed, poleward_speed)
    flat_state = (water_indicator, elevation_weights, elevation_anomaly)
    cells = levels * rows * cols
    sums, first, second, east_columns, west_columns = call(
        pack_kernel,
        [(3, rows, cols), (high, cols), (high, cols), (rows, cols), (rows, cols)],
        12 * cells,
        16 * cells,
        "level_sums",
        scratch=[pltpu.VMEM((high, cols), jnp.float32)] * 3,
    )(meta, spans, facing, *state, *flat_state)

    axes = ("lon", "lat")
    pairs_first = [(flat(i, j), flat(i, j ^ 1)) for i in range(lons) for j in range(lats)]
    pairs_inner = [
        (flat(i, a), flat(i, b))
        for i in range(lons)
        for j in range(1, lats - 1, 2)
        for a, b in ((j, j + 1), (j + 1, j))
    ]

    counterpart, first = lax.optimization_barrier((opposite_counterpart, first))
    hinge = lax.rem(counterpart[0] + 1 + cols * lon, width)
    block = lax.rem((hinge + cols // 2) // cols, lons)

    def exchange(shift, first, second):
        pairs_fold = [(flat(shift - 1 - i, lats - 1), flat(i, lats - 1)) for i in range(lons)]
        second = lax.ppermute(second, axes, pairs_inner + pairs_fold)
        return lax.ppermute(first, axes, pairs_first), second

    first, second = lax.switch(block, [functools.partial(exchange, s) for s in range(lons)], first, second)

    ext, to_near, to_far = call(
        turn_kernel,
        [(FIELDS, tall, cols), (long, cols), (long, cols)],
        FIELDS * tall * cols,
        4 * 4 * FIELDS * tall * cols,
        "row_halos",
    )(meta, sums, *flat_state, first, second, east_columns, west_columns)

    from_far = lax.ppermute(to_far, "lon", [(i, (i + 1 if i % 2 else i - 1) % lons) for i in range(lons)])
    from_near = lax.ppermute(to_near, "lon", [(i, i ^ 1) for i in range(lons)])

    count = lons * lats
    base, moments = call(
        functools.partial(krylov_kernel, 4 * levels),
        [(3, rows, cols), (count, cols)],
        200 * tall * cols,
        4 * 12 * tall * cols,
        "krylov",
        scratch=[pltpu.VMEM((2, high - 4 * levels + 8, cols), jnp.float32)],
    )(meta, facing, ext, second, from_near, from_far)

    chunks = 5 if levels % 5 == 0 else 1
    new_heat, new_salt, new_zonal, new_merid = call(
        step_kernel,
        [(levels, rows, cols)] * 4,
        120 * cells,
        32 * cells,
        "levels_step",
        out_space=pltpu.HBM,
        scratch=[
            *[pltpu.VMEM((levels, rows, cols), jnp.float32)] * 4,
            *[pltpu.VMEM((4 * levels, cols), jnp.float32)] * 2,
            pltpu.SemaphoreType.DMA((4, chunks)),
        ],
    )(meta, spans, facing, *state, water_indicator, first, second, from_near, from_far)

    shares = lax.all_to_all(moments, axes, 0, 0, tiled=True)
    (surface,) = call(surface_kernel, [(rows, cols)], 6 * rows * cols, 16 * rows * cols, "surface")(shares, base)
    return (new_heat, new_salt, new_zonal, new_merid, surface)


def solution(mesh):
    for axis in mesh.shape.values():
        assert axis > 1 and axis & (axis - 1) == 0
    levels = P(None, "lat", "lon")
    flat = P("lat", "lon")
    return jax.shard_map(
        body,
        mesh=mesh,
        in_specs=(levels, levels, levels, levels, P(), flat, P("lon"), flat, flat),
        out_specs=(levels, levels, levels, levels, flat),
        check_vma=False,
    )
```

```python
import functools

import jax
import jax.numpy as jnp
from jax import lax
from jax.experimental import pallas as pl
from jax.experimental.pallas import tpu as pltpu
from jax.sharding import PartitionSpec as P

TIME_STEP = 0.1
MIXING = 0.1

DEEP = 5
SIDE = (5, 4, 3, 4, 3, 3)
FIELDS = len(SIDE)
START = tuple(sum(SIDE[:f]) for f in range(FIELDS))
FLIPPED = (1, 2)
VMEM_LIMIT = 32 * 1024 * 1024
LOAD_FLOPS = 10**10


def density(heat, salt):
    return heat * (-1.0 - 0.15 * heat - 0.2 * salt) + 0.8 * salt


def iota(shape, axis):
    return lax.broadcasted_iota(jnp.int32, shape, axis)


def packet_rows(levels):
    return -(-(4 * levels + FIELDS * DEEP) // 8) * 8


def flags(meta):
    return meta[0:1, :] == 1, meta[1:2, :] == 1, meta[2:3, :] == 1


def place_kernel(meta, placed):
    for i in range(3):
        placed[i : i + 1, :] = jnp.broadcast_to(meta[0:1, i : i + 1], (1, placed.shape[1]))
    placed[3:, :] = jnp.zeros((placed.shape[0] - 3, placed.shape[1]), jnp.int32)


def pack_kernel(
    meta, spans, facing, heat, salt, zonal, merid, water, weights, anomaly,
    sums, first, second, east_columns, west_columns,
    top, bottom, back,
):
    levels, rows, cols = heat.shape
    span = [spans[0:1, k : k + 1] for k in range(levels)]
    below = [None] * levels
    total = jnp.zeros((1, 1), jnp.float32)
    for k in reversed(range(levels)):
        below[k] = span[k] * (0.5 * span[k] + total)
        total = total + span[k]
    pair = iota((rows, cols), 1) // 2
    zero = jnp.zeros((rows, cols), jnp.float32)
    press, east, north, east_edge, west_edge = zero, zero, zero, zero, zero
    for k in range(levels):
        press = press + below[k] * density(heat[k], salt[k])
        east = east + span[k] * zonal[k]
        north = north + span[k] * merid[k]
        for q, source in ((k, heat), (levels + k, salt)):
            cells = source[k]
            here = pair == q
            east_edge = jnp.where(here, pltpu.roll(cells, (2 * q + 2) % cols, 1), east_edge)
            west_edge = jnp.where(here, pltpu.roll(cells, 2 * q, 1), west_edge)
            top[2 * q : 2 * q + 2, :] = source[k, rows - 2 :, :]
            bottom[2 * q : 2 * q + 2, :] = source[k, :2, :]
            for i in range(2):
                back[2 * q + i : 2 * q + i + 1, :] = source[k, rows - 1 - i : rows - i, :]
    east_columns[...] = east_edge
    west_columns[...] = west_edge
    sums[0] = press
    sums[1] = east
    sums[2] = north
    fields = (sums.at[0], sums.at[1], sums.at[2], water, weights, anomaly)
    for f, field in enumerate(fields):
        at = 4 * levels + DEEP * f
        top[at : at + DEEP, :] = field[rows - DEEP :, :].astype(jnp.float32)
        bottom[at : at + DEEP, :] = field[:DEEP, :].astype(jnp.float32)
        for j in range(DEEP):
            back[at + j : at + j + 1, :] = field[rows - 1 - j : rows - j, :].astype(jnp.float32)
    used = 4 * levels + DEEP * FIELDS
    high = first.shape[0]
    if used < high:
        for packet in (top, bottom, back):
            packet[used:, :] = jnp.zeros((high - used, cols), jnp.float32)
    odd, last, _ = flags(meta)
    first[...] = jnp.where(odd, bottom[...], top[...])
    second[...] = jnp.where(last, back[...], jnp.where(odd, top[...], bottom[...]))


def turn_kernel(
    meta, sums, water, weights, anomaly, second, first, east_columns, west_columns,
    ext, to_near, to_far,
):
    rows, cols = sums.shape[1], sums.shape[2]
    tall = ext.shape[1]
    high = first.shape[0]
    deep = high - to_near.shape[0] + tall
    odd, _, lon_odd = flags(meta)
    from_first = first[...]
    from_second = second[...]
    north = jnp.where(odd, from_second, from_first)
    south = jnp.where(odd, from_first, from_second)
    fields = (sums.at[0], sums.at[1], sums.at[2], water, weights, anomaly)
    for f in range(FIELDS):
        at = deep + DEEP * f
        ext[f, :rows, :] = fields[f][...].astype(jnp.float32)
        ext[f, rows : rows + DEEP, :] = north[at : at + DEEP]
        ext[f, rows + DEEP : tall - DEEP, :] = jnp.zeros((tall - rows - 2 * DEEP, cols), jnp.float32)
        ext[f, tall - DEEP :, :] = south[at : at + DEEP]
    lane = iota((tall, cols), 1)
    spare = jnp.zeros((tall - rows, cols), jnp.float32)
    passed = from_second[:deep]
    fill = jnp.zeros((tall - deep, cols), jnp.float32)
    half = lane >= cols // 2
    east = jnp.where(half, jnp.concatenate([pltpu.roll(passed, cols // 2, 1), fill], axis=0),
                     jnp.concatenate([east_columns[...], spare], axis=0))
    west = jnp.where(half, jnp.concatenate([passed, fill], axis=0),
                     jnp.concatenate([west_columns[...], spare], axis=0))
    for f in range(FIELDS):
        at = deep + START[f]
        here = (lane >= at) & (lane < at + SIDE[f])
        layer = ext[f]
        east = jnp.where(here, pltpu.roll(layer, (at + SIDE[f]) % cols, 1), east)
        west = jnp.where(here, pltpu.roll(layer, at, 1), west)
    to_near[:tall, :] = jnp.where(lon_odd, west, east)
    to_far[:tall, :] = jnp.where(lon_odd, east, west)
    to_near[tall:, :] = from_second[deep:]
    to_far[tall:, :] = from_second[deep:]


def fold_shift(facing):
    cols = facing.shape[1]
    offset = (facing[0:1, 0:1] + 1) & (cols - 1)
    return jnp.where(offset >= cols // 2, offset - cols, offset)


def fold(shift, west, own, east, beside):
    rows, cols = own.shape
    lane = iota((rows, cols), 1)
    source = cols - 1 - lane
    if beside:
        place = (source + shift) & (cols - 1)
        low = jnp.where(place - cols < shift, west, own)
        merged = jnp.where(place >= cols // 2, low, jnp.where(place >= shift, east, own))
    else:
        merged = jnp.where(source >= cols - shift, west, jnp.where(source < -shift, east, own))
    return jnp.take_along_axis(merged, cols - 1 - ((lane - shift) & (cols - 1)), axis=1)


def krylov_kernel(used, meta, facing, ext, second, from_far, from_near, base, moments, folded):
    tall, cols = ext.shape[1], ext.shape[2]
    rows = base.shape[1]
    size = from_near.shape[0] - tall
    _, top, lon_odd = flags(meta)
    west = jnp.where(lon_odd, from_near[...], from_far[...])
    east = jnp.where(lon_odd, from_far[...], from_near[...])
    shift = fold_shift(facing)
    row = iota((size, cols), 0)
    flips = (row >= DEEP * FLIPPED[0]) & (row < DEEP * (FLIPPED[-1] + 1))
    for side in range(2):
        cells = fold(shift, west[tall:], second[used:, :], east[tall:], side == 1)
        folded[side, :size, :] = jnp.where(flips, -cells, cells)
    folded[:, size:, :] = jnp.zeros((2, folded.shape[1] - size, cols), jnp.float32)
    lane = iota((tall, cols), 1)
    first = lane == 0
    last = lane == cols - 1
    kept = iota((8, cols), 0) < DEEP

    def load(f):
        at = used + START[f]
        a = pltpu.roll(west[:tall], (2 * cols - SIDE[f] - at) % cols, 1)
        b = pltpu.roll(east[:tall], (cols - at) % cols, 1)
        beside = jnp.where(lane >= cols - SIDE[f], a, jnp.where(lane < SIDE[f], b, 0.0))

        def put(cells, side):
            new = folded[side, DEEP * f : DEEP * f + 8, :]
            new = jnp.where(kept, jnp.where(top, new, cells[rows : rows + 8]), 0.0)
            return jnp.concatenate([cells[:rows], new, cells[rows + 8 :]], axis=0)

        return put(ext[f], 0), put(beside, 1)

    def plus_x(pair):
        a, b = (pltpu.roll(part, cols - 1, 1) for part in pair)
        return jnp.where(last, b, a), jnp.where(last, a, b)

    def minus_x(pair):
        a, b = (pltpu.roll(part, 1, 1) for part in pair)
        return jnp.where(first, b, a), jnp.where(first, a, b)

    def plus_y(pair):
        return tuple(pltpu.roll(part, tall - 1, 0) for part in pair)

    def minus_y(pair):
        return tuple(pltpu.roll(part, 1, 0) for part in pair)

    def each(function, *pairs):
        return tuple(function(*parts) for parts in zip(*pairs))

    def neighbours(pair):
        return each(
            lambda a, b, c, d: (a + b) + (c + d), plus_x(pair), minus_x(pair), plus_y(pair), minus_y(pair)
        )

    press, zonal, merid, wet, weights, anomaly = (load(f) for f in range(FIELDS))
    half = 0.5 * TIME_STEP
    flow = lambda w, speed, a, b: w * (speed - half * (a - b))
    east_flow = each(flow, wet, zonal, plus_x(press), minus_x(press))
    north_flow = each(flow, wet, merid, plus_y(press), minus_y(press))
    right = each(
        lambda w, g, n, a, b, c, d: w * (g * n - 0.5 * (a - b + c - d)),
        wet,
        weights,
        anomaly,
        plus_x(east_flow),
        minus_x(east_flow),
        plus_y(north_flow),
        minus_y(north_flow),
    )
    diagonal = each(lambda g: 4.0 + g, weights)
    inverse = each(lambda m: 1.0 / m, diagonal)
    scale = each(lambda w, i: w * i, wet, inverse)
    zero = each(lambda r, i: r * i, right, inverse)
    one = each(lambda a, n: a * n, scale, neighbours(zero))
    two = each(lambda a, n: a * n, scale, neighbours(one))
    last_sum = neighbours(two)[0][:rows]
    right, middle = right[0][:rows], diagonal[0][:rows]
    zero, one, two = zero[0][:rows], one[0][:rows], two[0][:rows]
    base[0] = zero
    base[1] = one
    base[2] = two
    weighted = middle * one
    products = (
        right * zero,
        right * one,
        weighted * one,
        weighted * two,
        middle * two * two,
        last_sum * two,
    )
    which = iota((8, cols), 0)
    sums = jnp.zeros((8, cols), jnp.float32)
    for k, product in enumerate(products):
        sums = jnp.where(which == k, jnp.sum(product, axis=0, keepdims=True), sums)
    sums = jnp.sum(sums, axis=1, keepdims=True)
    sums = jnp.sum(jnp.where(which == iota((8, cols), 1), sums, 0.0), axis=0, keepdims=True)
    moments[...] = jnp.broadcast_to(sums, moments.shape)


def step_kernel(
    meta, spans, facing, heat, salt, zonal, merid, water, second, first, from_far, from_near,
    heat_out, salt_out, zonal_out, merid_out,
    new_heat, new_salt, new_zonal, new_merid, north_rows, south_rows, sems,
):
    levels, rows, cols = heat.shape
    deep = 4 * levels
    odd, top, lon_odd = flags(meta)
    wet = water[...].astype(jnp.float32)
    lane = iota((rows, cols), 1)
    row = iota((rows, cols), 0)
    east = jnp.where(lon_odd, from_far[:rows, :], from_near[:rows, :])
    west = jnp.where(lon_odd, from_near[:rows, :], from_far[:rows, :])
    from_second = second[:deep, :]
    across = fold(fold_shift(facing), pltpu.roll(west[:deep], cols // 2, 1), from_second, east[:deep], False)
    north_rows[...] = jnp.where(odd, jnp.where(top, across, from_second), first[:deep, :])
    south_rows[...] = jnp.where(odd, first[:deep, :], from_second)

    def around(cells, q):
        a = pltpu.roll(east, (cols - 2 * q) % cols, 1)
        b = pltpu.roll(west, (2 * cols - 2 - 2 * q) % cols, 1)
        side = jnp.where(lane < 2, a, b)

        def shift_x(by):
            a = pltpu.roll(cells, by % cols, 1)
            b = pltpu.roll(side, by % cols, 1)
            own = lane >= by if by > 0 else lane < cols + by
            return jnp.where(own, a, b)

        n0 = north_rows[2 * q : 2 * q + 1, :]
        n1 = north_rows[2 * q + 1 : 2 * q + 2, :]
        s0 = south_rows[2 * q + 1 : 2 * q + 2, :]
        s1 = south_rows[2 * q : 2 * q + 1, :]
        north_one = jnp.where(row == rows - 1, n0, pltpu.roll(cells, rows - 1, 0))
        north_two = jnp.where(row == rows - 1, n1, jnp.where(row == rows - 2, n0, pltpu.roll(cells, rows - 2, 0)))
        south_one = jnp.where(row == 0, s0, pltpu.roll(cells, 1, 0))
        south_two = jnp.where(row == 0, s1, jnp.where(row == 1, s0, pltpu.roll(cells, 2, 0)))
        return (shift_x(-1), shift_x(1), shift_x(-2), shift_x(2), north_one, south_one, north_two, south_two)

    def advance(cells, parts, speed_x, speed_y):
        e1, w1, e2, w2, n1, s1, n2, s2 = parts
        grad_east = 8.0 * (e1 - w1) - (e2 - w2)
        grad_north = 8.0 * (n1 - s1) - (n2 - s2)
        laplace = (e1 + w1) + (n1 + s1) - 4.0 * cells
        tendency = (-TIME_STEP / 12.0) * (speed_x * grad_east + speed_y * grad_north) + MIXING * laplace
        return cells + wet * tendency

    stores = ((new_heat, heat_out), (new_salt, salt_out), (new_zonal, zonal_out), (new_merid, merid_out))
    size = levels // sems.shape[1]
    copies = []
    half = 0.5 * TIME_STEP
    above_x = jnp.zeros((rows, cols), jnp.float32)
    above_y = jnp.zeros((rows, cols), jnp.float32)
    for k in range(levels):
        t, s, u, v = heat[k], salt[k], zonal[k], merid[k]
        around_t = around(t, k)
        around_s = around(s, levels + k)
        new_heat[k] = advance(t, around_t, u, v)
        new_salt[k] = advance(s, around_s, u, v)
        span = spans[0:1, k : k + 1]
        layer_x = span * (density(around_t[0], around_s[0]) - density(around_t[1], around_s[1]))
        layer_y = span * (density(around_t[4], around_s[4]) - density(around_t[5], around_s[5]))
        new_zonal[k] = wet * (u - half * (above_x + 0.5 * layer_x))
        new_merid[k] = wet * (v - half * (above_y + 0.5 * layer_y))
        above_x = above_x + layer_x
        above_y = above_y + layer_y
        if (k + 1) % size == 0:
            piece = pl.ds(k + 1 - size, size)
            for i, (near_ref, far_ref) in enumerate(stores):
                copies.append(pltpu.make_async_copy(near_ref.at[piece], far_ref.at[piece], sems.at[i, k // size]))
                copies[-1].start()
    for copy in copies:
        copy.wait()


def surface_kernel(shares, base, surface):
    sums = jnp.sum(shares[...], axis=0, keepdims=True)
    lane = iota(sums.shape, 1)
    nu = [jnp.sum(jnp.where(lane == k, sums, 0.0), axis=1, keepdims=True) for k in range(6)]

    def ratio(a, b):
        good = b > 0.0
        return jnp.where(good, a / jnp.where(good, b, 1.0), 0.0)

    def form(p, h):
        total = 0.0
        for i, a in enumerate(p):
            for j in range(i, len(p)):
                term = a * p[j] * h[i + j]
                total = total + (term if i == j else 2.0 * term)
        return total

    gap = [nu[k] - nu[k + 1] for k in range(5)]
    rz = nu[0]
    alpha = ratio(rz, gap[0])
    one = jnp.ones_like(rz)
    y = [one - alpha, alpha]
    x = [alpha, 0.0, 0.0]
    new = form(y, nu)
    beta = ratio(new, rz)
    rz = new
    p = [y[0] + beta, y[1]]
    alpha = ratio(rz, form(p, gap))
    x = [x[0] + alpha * p[0], alpha * p[1], 0.0]
    y = [y[0] - alpha * p[0], y[1] - alpha * (p[1] - p[0]), alpha * p[1]]
    new = form(y, nu)
    beta = ratio(new, rz)
    rz = new
    p = [y[0] + beta * p[0], y[1] + beta * p[1], y[2]]
    alpha = ratio(rz, form(p, gap))
    x = [x[0] + alpha * p[0], x[1] + alpha * p[1], alpha * p[2]]
    surface[...] = x[0] * base[0] + x[1] * base[1] + x[2] * base[2]


def call(kernel, outs, flops, moved, name, out_space=pltpu.VMEM, scratch=(), types=jnp.float32):
    def run(*args):
        return pl.pallas_call(
            kernel,
            out_shape=[jax.ShapeDtypeStruct(shape, types) for shape in outs],
            in_specs=[pl.BlockSpec(memory_space=pltpu.VMEM)] * len(args),
            out_specs=[pl.BlockSpec(memory_space=out_space)] * len(outs),
            scratch_shapes=list(scratch),
            cost_estimate=pl.CostEstimate(flops=flops, bytes_accessed=moved, transcendentals=0),
            compiler_params=pltpu.CompilerParams(vmem_limit_bytes=VMEM_LIMIT),
            name=name,
        )(*args)

    return run


def body(
    warmth_deviation,
    saltiness_deviation,
    easterly_speed,
    poleward_speed,
    stratum_spans,
    water_indicator,
    opposite_counterpart,
    elevation_weights,
    elevation_anomaly,
):
    lons, lats = lax.axis_size("lon"), lax.axis_size("lat")
    lon, lat = lax.axis_index("lon"), lax.axis_index("lat")
    levels, rows, cols = warmth_deviation.shape
    assert cols & (cols - 1) == 0 and 4 * levels + sum(SIDE) <= cols // 2
    high = packet_rows(levels)
    tall = rows + 16
    long = tall + high - 4 * levels
    width = cols * lons
    flat = lambda i, j: (i % lons) * lats + j

    place = (lax.rem(lat, 2), (lat == lats - 1).astype(jnp.int32), lax.rem(lon, 2))
    meta = jnp.stack(place).astype(jnp.int32).reshape(1, 3)
    (meta,) = call(place_kernel, [(8, cols)], LOAD_FLOPS, 16, "place", types=jnp.int32)(meta)

    spans = stratum_spans.reshape(1, levels)
    facing = opposite_counterpart.reshape(1, cols)
    state = (warmth_deviation, saltiness_deviation, easterly_speed, poleward_speed)
    flat_state = (water_indicator, elevation_weights, elevation_anomaly)
    cells = levels * rows * cols
    sums, first, second, east_columns, west_columns = call(
        pack_kernel,
        [(3, rows, cols), (high, cols), (high, cols), (rows, cols), (rows, cols)],
        12 * cells,
        16 * cells,
        "level_sums",
        scratch=[pltpu.VMEM((high, cols), jnp.float32)] * 3,
    )(meta, spans, facing, *state, *flat_state)

    axes = ("lon", "lat")
    pairs_first = [(flat(i, j), flat(i, j ^ 1)) for i in range(lons) for j in range(lats)]
    pairs_inner = [
        (flat(i, a), flat(i, b))
        for i in range(lons)
        for j in range(1, lats - 1, 2)
        for a, b in ((j, j + 1), (j + 1, j))
    ]

    counterpart, first = lax.optimization_barrier((opposite_counterpart, first))
    hinge = lax.rem(counterpart[0] + 1 + cols * lon, width)
    block = lax.rem((hinge + cols // 2) // cols, lons)

    core_groups = [[flat(i, j) for i in range(lons) for j in range(c, lats, 2)] for c in range(2)]

    def rest(shift, first, second):
        pairs_fold = [(flat(shift - 1 - i, lats - 1), flat(i, lats - 1)) for i in range(lons)]
        second = lax.ppermute(second, axes, pairs_inner + pairs_fold)
        first = lax.ppermute(first, axes, pairs_first)

        ext, to_near, to_far = call(
            turn_kernel,
            [(FIELDS, tall, cols), (long, cols), (long, cols)],
            FIELDS * tall * cols,
            4 * 4 * FIELDS * tall * cols,
            "row_halos",
        )(meta, sums, *flat_state, second, first, east_columns, west_columns)

        from_far = lax.ppermute(to_far, "lon", [(i, (i + 1 if i % 2 else i - 1) % lons) for i in range(lons)])
        from_near = lax.ppermute(to_near, "lon", [(i, i ^ 1) for i in range(lons)])

        count = lons * lats // 2
        base, moments = call(
            functools.partial(krylov_kernel, 4 * levels),
            [(3, rows, cols), (count, cols)],
            200 * tall * cols,
            4 * 12 * tall * cols,
            "krylov",
            scratch=[pltpu.VMEM((2, high - 4 * levels + 8, cols), jnp.float32)],
        )(meta, facing, ext, second, from_far, from_near)

        moments = moments + lax.ppermute(moments, axes, pairs_first)
        moments, from_far = lax.optimization_barrier((moments, from_far))

        chunks = 5 if levels % 5 == 0 else 1
        new_heat, new_salt, new_zonal, new_merid = call(
            step_kernel,
            [(levels, rows, cols)] * 4,
            120 * cells,
            32 * cells,
            "levels_step",
            out_space=pltpu.HBM,
            scratch=[
                *[pltpu.VMEM((levels, rows, cols), jnp.float32)] * 4,
                *[pltpu.VMEM((4 * levels, cols), jnp.float32)] * 2,
                pltpu.SemaphoreType.DMA((4, chunks)),
            ],
        )(meta, spans, facing, *state, water_indicator, second, first, from_far, from_near)

        shares = lax.all_to_all(moments, axes, 0, 0, tiled=True, axis_index_groups=core_groups)
        (surface,) = call(surface_kernel, [(rows, cols)], 6 * rows * cols, 16 * rows * cols, "surface")(shares, base)
        return new_heat, new_salt, new_zonal, new_merid, surface

    return lax.switch(block, [functools.partial(rest, s) for s in range(lons)], first, second)


def solution(mesh):
    for axis in mesh.shape.values():
        assert axis > 1 and axis & (axis - 1) == 0
    levels = P(None, "lat", "lon")
    flat = P("lat", "lon")
    return jax.shard_map(
        body,
        mesh=mesh,
        in_specs=(levels, levels, levels, levels, P(), flat, P("lon"), flat, flat),
        out_specs=(levels, levels, levels, levels, flat),
        check_vma=False,
    )
```

```python
import functools

import jax
import jax.numpy as jnp
from jax import lax
from jax.experimental import pallas as pl
from jax.experimental.pallas import tpu as pltpu
from jax.sharding import PartitionSpec as P

TIME_STEP = 0.1
MIXING = 0.1

DEEP = (5, 3, 4, 4, 3, 3)
SIDE = (5, 4, 3, 4, 3, 3)
FIELDS = len(SIDE)
ROW = tuple(sum(DEEP[:f]) for f in range(FIELDS + 1))
START = tuple(sum(SIDE[:f]) for f in range(FIELDS))
FLIPPED = (1, 2)
VMEM_LIMIT = 32 * 1024 * 1024
LOAD_FLOPS = 10**10


def density(heat, salt):
    return heat * (-1.0 - 0.15 * heat - 0.2 * salt) + 0.8 * salt


def iota(shape, axis):
    return lax.broadcasted_iota(jnp.int32, shape, axis)


def packet_rows(levels):
    return -(-(4 * levels + ROW[-1]) // 8) * 8


def flags(meta):
    return meta[0:1, :] == 1, meta[1:2, :] == 1, meta[2:3, :] == 1


def place_kernel(meta, placed):
    for i in range(3):
        placed[i : i + 1, :] = jnp.broadcast_to(meta[0:1, i : i + 1], (1, placed.shape[1]))
    placed[3:, :] = jnp.zeros((placed.shape[0] - 3, placed.shape[1]), jnp.int32)


def pack_kernel(
    meta, spans, facing, heat, salt, zonal, merid, water, weights, anomaly,
    sums, first, second, east_columns, west_columns,
    top, bottom, back,
):
    levels, rows, cols = heat.shape
    span = [spans[0:1, k : k + 1] for k in range(levels)]
    below = [None] * levels
    total = jnp.zeros((1, 1), jnp.float32)
    for k in reversed(range(levels)):
        below[k] = span[k] * (0.5 * span[k] + total)
        total = total + span[k]
    pair = iota((rows, cols), 1) // 2
    zero = jnp.zeros((rows, cols), jnp.float32)
    press, east, north, east_edge, west_edge = zero, zero, zero, zero, zero
    for k in range(levels):
        press = press + below[k] * density(heat[k], salt[k])
        east = east + span[k] * zonal[k]
        north = north + span[k] * merid[k]
        for q, source in ((k, heat), (levels + k, salt)):
            cells = source[k]
            here = pair == q
            east_edge = jnp.where(here, pltpu.roll(cells, (2 * q + 2) % cols, 1), east_edge)
            west_edge = jnp.where(here, pltpu.roll(cells, 2 * q, 1), west_edge)
            top[2 * q : 2 * q + 2, :] = source[k, rows - 2 :, :]
            bottom[2 * q : 2 * q + 2, :] = source[k, :2, :]
            for i in range(2):
                back[2 * q + i : 2 * q + i + 1, :] = source[k, rows - 1 - i : rows - i, :]
    east_columns[...] = east_edge
    west_columns[...] = west_edge
    sums[0] = press
    sums[1] = east
    sums[2] = north
    fields = (sums.at[0], sums.at[1], sums.at[2], water, weights, anomaly)
    for f, field in enumerate(fields):
        at = 4 * levels + ROW[f]
        deep = DEEP[f]
        top[at : at + deep, :] = field[rows - deep :, :].astype(jnp.float32)
        bottom[at : at + deep, :] = field[:deep, :].astype(jnp.float32)
        for j in range(deep):
            back[at + j : at + j + 1, :] = field[rows - 1 - j : rows - j, :].astype(jnp.float32)
    used = 4 * levels + ROW[-1]
    high = first.shape[0]
    if used < high:
        for packet in (top, bottom, back):
            packet[used:, :] = jnp.zeros((high - used, cols), jnp.float32)
    odd, last, _ = flags(meta)
    first[...] = jnp.where(odd, bottom[...], top[...])
    second[...] = jnp.where(last, back[...], jnp.where(odd, top[...], bottom[...]))


def turn_kernel(
    meta, sums, water, weights, anomaly, second, first, east_columns, west_columns,
    ext, to_far, to_near, facing_rows, north_rows, south_rows,
):
    rows, cols = sums.shape[1], sums.shape[2]
    tall = ext.shape[1]
    deep = north_rows.shape[0]
    odd, _, lon_odd = flags(meta)
    from_first = first[...]
    from_second = second[...]
    north = jnp.where(odd, from_second, from_first)
    south = jnp.where(odd, from_first, from_second)
    fields = (sums.at[0], sums.at[1], sums.at[2], water, weights, anomaly)
    for f in range(FIELDS):
        at = deep + ROW[f]
        size = DEEP[f]
        ext[f, :rows, :] = fields[f][...].astype(jnp.float32)
        ext[f, rows : rows + size, :] = north[at : at + size]
        ext[f, rows + size : tall - size, :] = jnp.zeros((tall - rows - 2 * size, cols), jnp.float32)
        ext[f, tall - size :, :] = south[at : at + size]
    lane = iota((tall, cols), 1)
    spare = jnp.zeros((tall - rows, cols), jnp.float32)
    passed = from_second[:deep]
    fill = jnp.zeros((tall - deep, cols), jnp.float32)
    half = lane >= cols // 2
    east = jnp.where(half, jnp.concatenate([pltpu.roll(passed, cols // 2, 1), fill], axis=0),
                     jnp.concatenate([east_columns[...], spare], axis=0))
    west = jnp.where(half, jnp.concatenate([passed, fill], axis=0),
                     jnp.concatenate([west_columns[...], spare], axis=0))
    for f in range(FIELDS):
        at = deep + START[f]
        here = (lane >= at) & (lane < at + SIDE[f])
        layer = ext[f]
        east = jnp.where(here, pltpu.roll(layer, (at + SIDE[f]) % cols, 1), east)
        west = jnp.where(here, pltpu.roll(layer, at, 1), west)
    to_near[:tall, :] = jnp.where(lon_odd, west, east)
    to_far[:tall, :] = jnp.where(lon_odd, east, west)
    to_near[tall:, :] = from_second[deep:]
    to_far[tall:, :] = from_second[deep:]
    facing_rows[...] = from_second[deep:]
    north_rows[...] = north[:deep]
    south_rows[...] = south[:deep]


def fold_shift(facing):
    cols = facing.shape[1]
    offset = (facing[0:1, 0:1] + 1) & (cols - 1)
    return jnp.where(offset >= cols // 2, offset - cols, offset)


def fold(shift, west, own, east, beside):
    rows, cols = own.shape
    lane = iota((rows, cols), 1)
    source = cols - 1 - lane
    if beside:
        place = (source + shift) & (cols - 1)
        low = jnp.where(place - cols < shift, west, own)
        merged = jnp.where(place >= cols // 2, low, jnp.where(place >= shift, east, own))
    else:
        merged = jnp.where(source >= cols - shift, west, jnp.where(source < -shift, east, own))
    return jnp.take_along_axis(merged, cols - 1 - ((lane - shift) & (cols - 1)), axis=1)


def krylov_kernel(used, meta, facing, ext, facing_rows, from_far, from_near, base, moments, folded):
    tall, cols = ext.shape[1], ext.shape[2]
    rows = base.shape[1]
    size = from_near.shape[0] - tall
    _, top, lon_odd = flags(meta)
    west = jnp.where(lon_odd, from_near[...], from_far[...])
    east = jnp.where(lon_odd, from_far[...], from_near[...])
    shift = fold_shift(facing)
    row = iota((size, cols), 0)
    flips = (row >= ROW[FLIPPED[0]]) & (row < ROW[FLIPPED[-1] + 1])
    for side in range(2):
        cells = fold(shift, west[tall:], facing_rows[...], east[tall:], side == 1)
        folded[side, :size, :] = jnp.where(flips, -cells, cells)
    folded[:, size:, :] = jnp.zeros((2, folded.shape[1] - size, cols), jnp.float32)
    lane = iota((tall, cols), 1)
    first = lane == 0
    last = lane == cols - 1
    eighth = iota((8, cols), 0)

    def load(f):
        at = used + START[f]
        a = pltpu.roll(west[:tall], (2 * cols - SIDE[f] - at) % cols, 1)
        b = pltpu.roll(east[:tall], (cols - at) % cols, 1)
        beside = jnp.where(lane >= cols - SIDE[f], a, jnp.where(lane < SIDE[f], b, 0.0))

        def put(cells, side):
            new = folded[side, ROW[f] : ROW[f] + 8, :]
            new = jnp.where(eighth < DEEP[f], jnp.where(top, new, cells[rows : rows + 8]), 0.0)
            return jnp.concatenate([cells[:rows], new, cells[rows + 8 :]], axis=0)

        return put(ext[f], 0), put(beside, 1)

    def plus_x(pair):
        a, b = (pltpu.roll(part, cols - 1, 1) for part in pair)
        return jnp.where(last, b, a), jnp.where(last, a, b)

    def minus_x(pair):
        a, b = (pltpu.roll(part, 1, 1) for part in pair)
        return jnp.where(first, b, a), jnp.where(first, a, b)

    def plus_y(pair):
        return tuple(pltpu.roll(part, tall - 1, 0) for part in pair)

    def minus_y(pair):
        return tuple(pltpu.roll(part, 1, 0) for part in pair)

    def each(function, *pairs):
        return tuple(function(*parts) for parts in zip(*pairs))

    def neighbours(pair):
        return each(
            lambda a, b, c, d: (a + b) + (c + d), plus_x(pair), minus_x(pair), plus_y(pair), minus_y(pair)
        )

    press, zonal, merid, wet, weights, anomaly = (load(f) for f in range(FIELDS))
    half = 0.5 * TIME_STEP
    flow = lambda w, speed, a, b: w * (speed - half * (a - b))
    east_flow = each(flow, wet, zonal, plus_x(press), minus_x(press))
    north_flow = each(flow, wet, merid, plus_y(press), minus_y(press))
    right = each(
        lambda w, g, n, a, b, c, d: w * (g * n - 0.5 * (a - b + c - d)),
        wet,
        weights,
        anomaly,
        plus_x(east_flow),
        minus_x(east_flow),
        plus_y(north_flow),
        minus_y(north_flow),
    )
    diagonal = each(lambda g: 4.0 + g, weights)
    inverse = each(lambda m: 1.0 / m, diagonal)
    scale = each(lambda w, i: w * i, wet, inverse)
    zero = each(lambda r, i: r * i, right, inverse)
    one = each(lambda a, n: a * n, scale, neighbours(zero))
    two = each(lambda a, n: a * n, scale, neighbours(one))
    last_sum = neighbours(two)[0][:rows]
    right, middle = right[0][:rows], diagonal[0][:rows]
    zero, one, two = zero[0][:rows], one[0][:rows], two[0][:rows]
    base[0] = zero
    base[1] = one
    base[2] = two
    weighted = middle * one
    products = (
        right * zero,
        right * one,
        weighted * one,
        weighted * two,
        middle * two * two,
        last_sum * two,
    )
    which = iota((8, cols), 0)
    sums = jnp.zeros((8, cols), jnp.float32)
    for k, product in enumerate(products):
        sums = jnp.where(which == k, jnp.sum(product, axis=0, keepdims=True), sums)
    sums = jnp.sum(sums, axis=1, keepdims=True)
    sums = jnp.sum(jnp.where(which == iota((8, cols), 1), sums, 0.0), axis=0, keepdims=True)
    moments[...] = jnp.broadcast_to(sums, moments.shape)


def step_kernel(
    meta, spans, facing, heat, salt, zonal, merid, water, north_came, south_rows, from_far, from_near,
    heat_out, salt_out, zonal_out, merid_out,
    new_heat, new_salt, new_zonal, new_merid, north_rows, sems,
):
    levels, rows, cols = heat.shape
    deep = 4 * levels
    _, top, lon_odd = flags(meta)
    wet = water[...].astype(jnp.float32)
    lane = iota((rows, cols), 1)
    row = iota((rows, cols), 0)
    east = jnp.where(lon_odd, from_far[:rows, :], from_near[:rows, :])
    west = jnp.where(lon_odd, from_near[:rows, :], from_far[:rows, :])
    came = north_came[...]
    across = fold(fold_shift(facing), pltpu.roll(west[:deep], cols // 2, 1), came, east[:deep], False)
    north_rows[...] = jnp.where(top, across, came)

    def around(cells, q):
        a = pltpu.roll(east, (cols - 2 * q) % cols, 1)
        b = pltpu.roll(west, (2 * cols - 2 - 2 * q) % cols, 1)
        side = jnp.where(lane < 2, a, b)

        def shift_x(by):
            a = pltpu.roll(cells, by % cols, 1)
            b = pltpu.roll(side, by % cols, 1)
            own = lane >= by if by > 0 else lane < cols + by
            return jnp.where(own, a, b)

        n0 = north_rows[2 * q : 2 * q + 1, :]
        n1 = north_rows[2 * q + 1 : 2 * q + 2, :]
        s0 = south_rows[2 * q + 1 : 2 * q + 2, :]
        s1 = south_rows[2 * q : 2 * q + 1, :]
        north_one = jnp.where(row == rows - 1, n0, pltpu.roll(cells, rows - 1, 0))
        north_two = jnp.where(row == rows - 1, n1, jnp.where(row == rows - 2, n0, pltpu.roll(cells, rows - 2, 0)))
        south_one = jnp.where(row == 0, s0, pltpu.roll(cells, 1, 0))
        south_two = jnp.where(row == 0, s1, jnp.where(row == 1, s0, pltpu.roll(cells, 2, 0)))
        return (shift_x(-1), shift_x(1), shift_x(-2), shift_x(2), north_one, south_one, north_two, south_two)

    def advance(cells, parts, speed_x, speed_y):
        e1, w1, e2, w2, n1, s1, n2, s2 = parts
        grad_east = 8.0 * (e1 - w1) - (e2 - w2)
        grad_north = 8.0 * (n1 - s1) - (n2 - s2)
        laplace = (e1 + w1) + (n1 + s1) - 4.0 * cells
        tendency = (-TIME_STEP / 12.0) * (speed_x * grad_east + speed_y * grad_north) + MIXING * laplace
        return cells + wet * tendency

    stores = ((new_heat, heat_out), (new_salt, salt_out), (new_zonal, zonal_out), (new_merid, merid_out))
    size = levels // sems.shape[1]
    copies = []
    half = 0.5 * TIME_STEP
    above_x = jnp.zeros((rows, cols), jnp.float32)
    above_y = jnp.zeros((rows, cols), jnp.float32)
    for k in range(levels):
        t, s, u, v = heat[k], salt[k], zonal[k], merid[k]
        around_t = around(t, k)
        around_s = around(s, levels + k)
        new_heat[k] = advance(t, around_t, u, v)
        new_salt[k] = advance(s, around_s, u, v)
        span = spans[0:1, k : k + 1]
        layer_x = span * (density(around_t[0], around_s[0]) - density(around_t[1], around_s[1]))
        layer_y = span * (density(around_t[4], around_s[4]) - density(around_t[5], around_s[5]))
        new_zonal[k] = wet * (u - half * (above_x + 0.5 * layer_x))
        new_merid[k] = wet * (v - half * (above_y + 0.5 * layer_y))
        above_x = above_x + layer_x
        above_y = above_y + layer_y
        if (k + 1) % size == 0:
            piece = pl.ds(k + 1 - size, size)
            for i, (near_ref, far_ref) in enumerate(stores):
                copies.append(pltpu.make_async_copy(near_ref.at[piece], far_ref.at[piece], sems.at[i, k // size]))
                copies[-1].start()
    for copy in copies:
        copy.wait()


def surface_kernel(shares, base, surface):
    sums = jnp.sum(shares[...], axis=0, keepdims=True)
    lane = iota(sums.shape, 1)
    nu = [jnp.sum(jnp.where(lane == k, sums, 0.0), axis=1, keepdims=True) for k in range(6)]

    def ratio(a, b):
        good = b > 0.0
        return jnp.where(good, a / jnp.where(good, b, 1.0), 0.0)

    def form(p, h):
        total = 0.0
        for i, a in enumerate(p):
            for j in range(i, len(p)):
                term = a * p[j] * h[i + j]
                total = total + (term if i == j else 2.0 * term)
        return total

    gap = [nu[k] - nu[k + 1] for k in range(5)]
    rz = nu[0]
    alpha = ratio(rz, gap[0])
    one = jnp.ones_like(rz)
    y = [one - alpha, alpha]
    x = [alpha, 0.0, 0.0]
    new = form(y, nu)
    beta = ratio(new, rz)
    rz = new
    p = [y[0] + beta, y[1]]
    alpha = ratio(rz, form(p, gap))
    x = [x[0] + alpha * p[0], alpha * p[1], 0.0]
    y = [y[0] - alpha * p[0], y[1] - alpha * (p[1] - p[0]), alpha * p[1]]
    new = form(y, nu)
    beta = ratio(new, rz)
    rz = new
    p = [y[0] + beta * p[0], y[1] + beta * p[1], y[2]]
    alpha = ratio(rz, form(p, gap))
    x = [x[0] + alpha * p[0], x[1] + alpha * p[1], alpha * p[2]]
    surface[...] = x[0] * base[0] + x[1] * base[1] + x[2] * base[2]


def call(kernel, outs, flops, moved, name, out_space=pltpu.VMEM, scratch=(), types=jnp.float32):
    def run(*args):
        return pl.pallas_call(
            kernel,
            out_shape=[jax.ShapeDtypeStruct(shape, types) for shape in outs],
            in_specs=[pl.BlockSpec(memory_space=pltpu.VMEM)] * len(args),
            out_specs=[pl.BlockSpec(memory_space=out_space)] * len(outs),
            scratch_shapes=list(scratch),
            cost_estimate=pl.CostEstimate(flops=flops, bytes_accessed=moved, transcendentals=0),
            compiler_params=pltpu.CompilerParams(vmem_limit_bytes=VMEM_LIMIT),
            name=name,
        )(*args)

    return run


def body(
    warmth_deviation,
    saltiness_deviation,
    easterly_speed,
    poleward_speed,
    stratum_spans,
    water_indicator,
    opposite_counterpart,
    elevation_weights,
    elevation_anomaly,
):
    lons, lats = lax.axis_size("lon"), lax.axis_size("lat")
    lon, lat = lax.axis_index("lon"), lax.axis_index("lat")
    levels, rows, cols = warmth_deviation.shape
    assert cols & (cols - 1) == 0 and 4 * levels + sum(SIDE) <= cols // 2
    high = packet_rows(levels)
    tall = rows + 16
    long = tall + high - 4 * levels
    width = cols * lons
    flat = lambda i, j: (i % lons) * lats + j

    place = (lax.rem(lat, 2), (lat == lats - 1).astype(jnp.int32), lax.rem(lon, 2))
    meta = jnp.stack(place).astype(jnp.int32).reshape(1, 3)
    (meta,) = call(place_kernel, [(8, cols)], LOAD_FLOPS, 16, "place", types=jnp.int32)(meta)

    spans = stratum_spans.reshape(1, levels)
    facing = opposite_counterpart.reshape(1, cols)
    state = (warmth_deviation, saltiness_deviation, easterly_speed, poleward_speed)
    flat_state = (water_indicator, elevation_weights, elevation_anomaly)
    cells = levels * rows * cols
    sums, first, second, east_columns, west_columns = call(
        pack_kernel,
        [(3, rows, cols), (high, cols), (high, cols), (rows, cols), (rows, cols)],
        12 * cells,
        16 * cells,
        "level_sums",
        scratch=[pltpu.VMEM((high, cols), jnp.float32)] * 3,
    )(meta, spans, facing, *state, *flat_state)

    axes = ("lon", "lat")
    pairs_first = [(flat(i, j), flat(i, j ^ 1)) for i in range(lons) for j in range(lats)]
    pairs_inner = [
        (flat(i, a), flat(i, b))
        for i in range(lons)
        for j in range(1, lats - 1, 2)
        for a, b in ((j, j + 1), (j + 1, j))
    ]

    counterpart, first = lax.optimization_barrier((opposite_counterpart, first))
    hinge = lax.rem(counterpart[0] + 1 + cols * lon, width)
    block = lax.rem((hinge + cols // 2) // cols, lons)

    def exchange(shift, first, second):
        pairs_fold = [(flat(shift - 1 - i, lats - 1), flat(i, lats - 1)) for i in range(lons)]
        second = lax.ppermute(second, axes, pairs_inner + pairs_fold)
        return second, lax.ppermute(first, axes, pairs_first)

    second, first = lax.switch(block, [functools.partial(exchange, s) for s in range(lons)], first, second)

    deep = 4 * levels
    ext, to_far, to_near, facing_rows, north_rows, south_rows = call(
        turn_kernel,
        [(FIELDS, tall, cols), (long, cols), (long, cols), (high - deep, cols), (deep, cols), (deep, cols)],
        FIELDS * tall * cols,
        4 * 4 * FIELDS * tall * cols,
        "row_halos",
    )(meta, sums, *flat_state, second, first, east_columns, west_columns)

    from_far = lax.ppermute(to_far, "lon", [(i, (i + 1 if i % 2 else i - 1) % lons) for i in range(lons)])
    from_near = lax.ppermute(to_near, "lon", [(i, i ^ 1) for i in range(lons)])

    count = lons * lats
    base, moments = call(
        functools.partial(krylov_kernel, 4 * levels),
        [(3, rows, cols), (count, cols)],
        200 * tall * cols,
        4 * 12 * tall * cols,
        "krylov",
        scratch=[pltpu.VMEM((2, high - deep + 8, cols), jnp.float32)],
    )(meta, facing, ext, facing_rows, from_far, from_near)

    chunks = 5 if levels % 5 == 0 else 1
    new_heat, new_salt, new_zonal, new_merid = call(
        step_kernel,
        [(levels, rows, cols)] * 4,
        120 * cells,
        32 * cells,
        "levels_step",
        out_space=pltpu.HBM,
        scratch=[
            *[pltpu.VMEM((levels, rows, cols), jnp.float32)] * 4,
            pltpu.VMEM((deep, cols), jnp.float32),
            pltpu.SemaphoreType.DMA((4, chunks)),
        ],
    )(meta, spans, facing, *state, water_indicator, north_rows, south_rows, from_far, from_near)

    shares = lax.all_to_all(moments, axes, 0, 0, tiled=True)
    (surface,) = call(surface_kernel, [(rows, cols)], 6 * rows * cols, 16 * rows * cols, "surface")(shares, base)
    return (new_heat, new_salt, new_zonal, new_merid, surface)


def solution(mesh):
    for axis in mesh.shape.values():
        assert axis > 1 and axis & (axis - 1) == 0
    levels = P(None, "lat", "lon")
    flat = P("lat", "lon")
    return jax.shard_map(
        body,
        mesh=mesh,
        in_specs=(levels, levels, levels, levels, P(), flat, P("lon"), flat, flat),
        out_specs=(levels, levels, levels, levels, flat),
        check_vma=False,
    )
```

```python
import functools

import jax
import jax.numpy as jnp
from jax import lax
from jax.experimental import pallas as pl
from jax.experimental.pallas import tpu as pltpu
from jax.sharding import PartitionSpec as P

TIME_STEP = 0.1
MIXING = 0.1

DEEP = (5, 3, 4, 4, 3, 3)
SIDE = (5, 4, 3, 4, 3, 3)
FIELDS = len(SIDE)
ROW = tuple(sum(DEEP[:f]) for f in range(FIELDS + 1))
START = tuple(sum(SIDE[:f]) for f in range(FIELDS + 1))
RELAY = 56
FLIPPED = (1, 2)
VMEM_LIMIT = 32 * 1024 * 1024
LOAD_FLOPS = 10**10


def density(heat, salt):
    return heat * (-1.0 - 0.15 * heat - 0.2 * salt) + 0.8 * salt


def iota(shape, axis):
    return lax.broadcasted_iota(jnp.int32, shape, axis)


def packet_rows(levels):
    return -(-(4 * levels + ROW[-1]) // 8) * 8


def flags(meta):
    return meta[0:1, :] == 1, meta[1:2, :] == 1, meta[2:3, :] == 1


def place_kernel(meta, placed):
    for i in range(3):
        placed[i : i + 1, :] = jnp.broadcast_to(meta[0:1, i : i + 1], (1, placed.shape[1]))
    placed[3:, :] = jnp.zeros((placed.shape[0] - 3, placed.shape[1]), jnp.int32)


def pack_kernel(
    meta, spans, facing, heat, salt, zonal, merid, water, weights, anomaly,
    sums, first, second, east_columns, west_columns,
    top, bottom, back,
):
    levels, rows, cols = heat.shape
    span = [spans[0:1, k : k + 1] for k in range(levels)]
    below = [None] * levels
    total = jnp.zeros((1, 1), jnp.float32)
    for k in reversed(range(levels)):
        below[k] = span[k] * (0.5 * span[k] + total)
        total = total + span[k]
    pair = iota((rows, cols), 1) // 2
    zero = jnp.zeros((rows, cols), jnp.float32)
    press, east, north, east_edge, west_edge = zero, zero, zero, zero, zero
    for k in range(levels):
        press = press + below[k] * density(heat[k], salt[k])
        east = east + span[k] * zonal[k]
        north = north + span[k] * merid[k]
        for q, source in ((k, heat), (levels + k, salt)):
            cells = source[k]
            here = pair == q
            east_edge = jnp.where(here, pltpu.roll(cells, (2 * q + 2) % cols, 1), east_edge)
            west_edge = jnp.where(here, pltpu.roll(cells, 2 * q, 1), west_edge)
            top[2 * q : 2 * q + 2, :] = source[k, rows - 2 :, :]
            bottom[2 * q : 2 * q + 2, :] = source[k, :2, :]
            for i in range(2):
                back[2 * q + i : 2 * q + i + 1, :] = source[k, rows - 1 - i : rows - i, :]
    east_columns[...] = east_edge
    west_columns[...] = west_edge
    sums[0] = press
    sums[1] = east
    sums[2] = north
    fields = (sums.at[0], sums.at[1], sums.at[2], water, weights, anomaly)
    for f, field in enumerate(fields):
        at = 4 * levels + ROW[f]
        deep = DEEP[f]
        top[at : at + deep, :] = field[rows - deep :, :].astype(jnp.float32)
        bottom[at : at + deep, :] = field[:deep, :].astype(jnp.float32)
        for j in range(deep):
            back[at + j : at + j + 1, :] = field[rows - 1 - j : rows - j, :].astype(jnp.float32)
    used = 4 * levels + ROW[-1]
    high = first.shape[0]
    if used < high:
        for packet in (top, bottom, back):
            packet[used:, :] = jnp.zeros((high - used, cols), jnp.float32)
    odd, last, _ = flags(meta)
    first[...] = jnp.where(odd, bottom[...], top[...])
    second[...] = jnp.where(last, back[...], jnp.where(odd, top[...], bottom[...]))


def turn_kernel(
    meta, sums, water, weights, anomaly, second, first, east_columns, west_columns,
    ext, to_far, to_near, state_far, state_near, facing_rows, north_rows, south_rows,
):
    rows, cols = sums.shape[1], sums.shape[2]
    tall = ext.shape[1]
    deep = north_rows.shape[0]
    odd, _, lon_odd = flags(meta)
    from_first = first[...]
    from_second = second[...]
    north = jnp.where(odd, from_second, from_first)
    south = jnp.where(odd, from_first, from_second)
    fields = (sums.at[0], sums.at[1], sums.at[2], water, weights, anomaly)
    for f in range(FIELDS):
        at = deep + ROW[f]
        size = DEEP[f]
        ext[f, :rows, :] = fields[f][...].astype(jnp.float32)
        ext[f, rows : rows + size, :] = north[at : at + size]
        ext[f, rows + size : tall - size, :] = jnp.zeros((tall - rows - 2 * size, cols), jnp.float32)
        ext[f, tall - size :, :] = south[at : at + size]
    middle = tall // 2
    passed = from_second[deep:]
    spare = jnp.zeros((middle - passed.shape[0], cols), jnp.float32)
    lane = iota((middle, cols), 1)
    relay = lane >= RELAY
    east = jnp.where(relay, jnp.concatenate([pltpu.roll(passed, RELAY, 1), spare], axis=0), 0.0)
    west = jnp.where(relay, jnp.concatenate([passed, spare], axis=0), 0.0)
    for f in range(FIELDS):
        for part in range(2):
            at = START[f] + part * START[-1]
            here = (lane >= at) & (lane < at + SIDE[f])
            layer = ext[f, part * middle : (part + 1) * middle, :]
            east = jnp.where(here, pltpu.roll(layer, (at + SIDE[f]) % cols, 1), east)
            west = jnp.where(here, pltpu.roll(layer, at, 1), west)
    to_far[...] = jnp.where(lon_odd, east, west)
    to_near[...] = jnp.where(lon_odd, west, east)
    passed = from_second[:deep]
    spare = jnp.zeros((rows - deep, cols), jnp.float32)
    half = iota((rows, cols), 1) >= cols // 2
    east = jnp.where(half, jnp.concatenate([pltpu.roll(passed, cols // 2, 1), spare], axis=0), east_columns[...])
    west = jnp.where(half, jnp.concatenate([passed, spare], axis=0), west_columns[...])
    state_far[...] = jnp.where(lon_odd, east, west)
    state_near[...] = jnp.where(lon_odd, west, east)
    facing_rows[...] = from_second[deep:]
    north_rows[...] = north[:deep]
    south_rows[...] = south[:deep]


def fold_shift(facing):
    cols = facing.shape[1]
    offset = (facing[0:1, 0:1] + 1) & (cols - 1)
    return jnp.where(offset >= cols // 2, offset - cols, offset)


def fold(shift, west, own, east, beside):
    rows, cols = own.shape
    lane = iota((rows, cols), 1)
    source = cols - 1 - lane
    if beside:
        place = (source + shift) & (cols - 1)
        low = jnp.where(place - cols < shift, west, own)
        merged = jnp.where(place >= cols // 2, low, jnp.where(place >= shift, east, own))
    else:
        merged = jnp.where(source >= cols - shift, west, jnp.where(source < -shift, east, own))
    return jnp.take_along_axis(merged, cols - 1 - ((lane - shift) & (cols - 1)), axis=1)


def krylov_kernel(meta, facing, ext, facing_rows, from_far, from_near, base, moments, folded):
    tall, cols = ext.shape[1], ext.shape[2]
    rows = base.shape[1]
    size = facing_rows.shape[0]
    middle = tall // 2
    _, top, lon_odd = flags(meta)
    west = jnp.where(lon_odd, from_near[...], from_far[...])
    east = jnp.where(lon_odd, from_far[...], from_near[...])
    shift = fold_shift(facing)
    row = iota((size, cols), 0)
    flips = (row >= ROW[FLIPPED[0]]) & (row < ROW[FLIPPED[-1] + 1])
    for side in range(2):
        cells = fold(shift, pltpu.roll(west[:size], cols - RELAY, 1), facing_rows[...], east[:size], side == 1)
        folded[side, :size, :] = jnp.where(flips, -cells, cells)
    folded[:, size:, :] = jnp.zeros((2, folded.shape[1] - size, cols), jnp.float32)
    lane = iota((tall, cols), 1)
    first = lane == 0
    last = lane == cols - 1
    eighth = iota((8, cols), 0)

    def load(f):
        both = [START[f], START[f] + START[-1]]
        a = jnp.concatenate([pltpu.roll(west, (2 * cols - SIDE[f] - at) % cols, 1) for at in both], axis=0)
        b = jnp.concatenate([pltpu.roll(east, (cols - at) % cols, 1) for at in both], axis=0)
        beside = jnp.where(lane >= cols - SIDE[f], a, jnp.where(lane < SIDE[f], b, 0.0))

        def put(cells, side):
            new = folded[side, ROW[f] : ROW[f] + 8, :]
            new = jnp.where(eighth < DEEP[f], jnp.where(top, new, cells[rows : rows + 8]), 0.0)
            return jnp.concatenate([cells[:rows], new, cells[rows + 8 :]], axis=0)

        return put(ext[f], 0), put(beside, 1)

    def plus_x(pair):
        a, b = (pltpu.roll(part, cols - 1, 1) for part in pair)
        return jnp.where(last, b, a), jnp.where(last, a, b)

    def minus_x(pair):
        a, b = (pltpu.roll(part, 1, 1) for part in pair)
        return jnp.where(first, b, a), jnp.where(first, a, b)

    def plus_y(pair):
        return tuple(pltpu.roll(part, tall - 1, 0) for part in pair)

    def minus_y(pair):
        return tuple(pltpu.roll(part, 1, 0) for part in pair)

    def each(function, *pairs):
        return tuple(function(*parts) for parts in zip(*pairs))

    def neighbours(pair):
        return each(
            lambda a, b, c, d: (a + b) + (c + d), plus_x(pair), minus_x(pair), plus_y(pair), minus_y(pair)
        )

    press, zonal, merid, wet, weights, anomaly = (load(f) for f in range(FIELDS))
    half = 0.5 * TIME_STEP
    flow = lambda w, speed, a, b: w * (speed - half * (a - b))
    east_flow = each(flow, wet, zonal, plus_x(press), minus_x(press))
    north_flow = each(flow, wet, merid, plus_y(press), minus_y(press))
    right = each(
        lambda w, g, n, a, b, c, d: w * (g * n - 0.5 * (a - b + c - d)),
        wet,
        weights,
        anomaly,
        plus_x(east_flow),
        minus_x(east_flow),
        plus_y(north_flow),
        minus_y(north_flow),
    )
    diagonal = each(lambda g: 4.0 + g, weights)
    inverse = each(lambda m: 1.0 / m, diagonal)
    scale = each(lambda w, i: w * i, wet, inverse)
    zero = each(lambda r, i: r * i, right, inverse)
    one = each(lambda a, n: a * n, scale, neighbours(zero))
    two = each(lambda a, n: a * n, scale, neighbours(one))
    last_sum = neighbours(two)[0][:rows]
    right, middle = right[0][:rows], diagonal[0][:rows]
    zero, one, two = zero[0][:rows], one[0][:rows], two[0][:rows]
    base[0] = zero
    base[1] = one
    base[2] = two
    weighted = middle * one
    products = (
        right * zero,
        right * one,
        weighted * one,
        weighted * two,
        middle * two * two,
        last_sum * two,
    )
    which = iota((8, cols), 0)
    sums = jnp.zeros((8, cols), jnp.float32)
    for k, product in enumerate(products):
        sums = jnp.where(which == k, jnp.sum(product, axis=0, keepdims=True), sums)
    sums = jnp.sum(sums, axis=1, keepdims=True)
    sums = jnp.sum(jnp.where(which == iota((8, cols), 1), sums, 0.0), axis=0, keepdims=True)
    moments[...] = jnp.broadcast_to(sums, moments.shape)


def step_kernel(
    meta, spans, facing, heat, salt, zonal, merid, water, north_came, south_rows, from_far, from_near,
    heat_out, salt_out, zonal_out, merid_out,
    new_heat, new_salt, new_zonal, new_merid, north_rows, sems,
):
    levels, rows, cols = heat.shape
    deep = 4 * levels
    _, top, lon_odd = flags(meta)
    wet = water[...].astype(jnp.float32)
    lane = iota((rows, cols), 1)
    row = iota((rows, cols), 0)
    east = jnp.where(lon_odd, from_far[...], from_near[...])
    west = jnp.where(lon_odd, from_near[...], from_far[...])
    came = north_came[...]
    across = fold(fold_shift(facing), pltpu.roll(west[:deep], cols // 2, 1), came, east[:deep], False)
    north_rows[...] = jnp.where(top, across, came)

    def around(cells, q):
        a = pltpu.roll(east, (cols - 2 * q) % cols, 1)
        b = pltpu.roll(west, (2 * cols - 2 - 2 * q) % cols, 1)
        side = jnp.where(lane < 2, a, b)

        def shift_x(by):
            a = pltpu.roll(cells, by % cols, 1)
            b = pltpu.roll(side, by % cols, 1)
            own = lane >= by if by > 0 else lane < cols + by
            return jnp.where(own, a, b)

        n0 = north_rows[2 * q : 2 * q + 1, :]
        n1 = north_rows[2 * q + 1 : 2 * q + 2, :]
        s0 = south_rows[2 * q + 1 : 2 * q + 2, :]
        s1 = south_rows[2 * q : 2 * q + 1, :]
        north_one = jnp.where(row == rows - 1, n0, pltpu.roll(cells, rows - 1, 0))
        north_two = jnp.where(row == rows - 1, n1, jnp.where(row == rows - 2, n0, pltpu.roll(cells, rows - 2, 0)))
        south_one = jnp.where(row == 0, s0, pltpu.roll(cells, 1, 0))
        south_two = jnp.where(row == 0, s1, jnp.where(row == 1, s0, pltpu.roll(cells, 2, 0)))
        return (shift_x(-1), shift_x(1), shift_x(-2), shift_x(2), north_one, south_one, north_two, south_two)

    def advance(cells, parts, speed_x, speed_y):
        e1, w1, e2, w2, n1, s1, n2, s2 = parts
        grad_east = 8.0 * (e1 - w1) - (e2 - w2)
        grad_north = 8.0 * (n1 - s1) - (n2 - s2)
        laplace = (e1 + w1) + (n1 + s1) - 4.0 * cells
        tendency = (-TIME_STEP / 12.0) * (speed_x * grad_east + speed_y * grad_north) + MIXING * laplace
        return cells + wet * tendency

    stores = ((new_heat, heat_out), (new_salt, salt_out), (new_zonal, zonal_out), (new_merid, merid_out))
    size = levels // sems.shape[1]
    copies = []
    half = 0.5 * TIME_STEP
    above_x = jnp.zeros((rows, cols), jnp.float32)
    above_y = jnp.zeros((rows, cols), jnp.float32)
    for k in range(levels):
        t, s, u, v = heat[k], salt[k], zonal[k], merid[k]
        around_t = around(t, k)
        around_s = around(s, levels + k)
        new_heat[k] = advance(t, around_t, u, v)
        new_salt[k] = advance(s, around_s, u, v)
        span = spans[0:1, k : k + 1]
        layer_x = span * (density(around_t[0], around_s[0]) - density(around_t[1], around_s[1]))
        layer_y = span * (density(around_t[4], around_s[4]) - density(around_t[5], around_s[5]))
        new_zonal[k] = wet * (u - half * (above_x + 0.5 * layer_x))
        new_merid[k] = wet * (v - half * (above_y + 0.5 * layer_y))
        above_x = above_x + layer_x
        above_y = above_y + layer_y
        if (k + 1) % size == 0:
            piece = pl.ds(k + 1 - size, size)
            for i, (near_ref, far_ref) in enumerate(stores):
                copies.append(pltpu.make_async_copy(near_ref.at[piece], far_ref.at[piece], sems.at[i, k // size]))
                copies[-1].start()
    for copy in copies:
        copy.wait()


def surface_kernel(shares, base, surface):
    sums = jnp.sum(shares[...], axis=0, keepdims=True)
    lane = iota(sums.shape, 1)
    nu = [jnp.sum(jnp.where(lane == k, sums, 0.0), axis=1, keepdims=True) for k in range(6)]

    def ratio(a, b):
        good = b > 0.0
        return jnp.where(good, a / jnp.where(good, b, 1.0), 0.0)

    def form(p, h):
        total = 0.0
        for i, a in enumerate(p):
            for j in range(i, len(p)):
                term = a * p[j] * h[i + j]
                total = total + (term if i == j else 2.0 * term)
        return total

    gap = [nu[k] - nu[k + 1] for k in range(5)]
    rz = nu[0]
    alpha = ratio(rz, gap[0])
    one = jnp.ones_like(rz)
    y = [one - alpha, alpha]
    x = [alpha, 0.0, 0.0]
    new = form(y, nu)
    beta = ratio(new, rz)
    rz = new
    p = [y[0] + beta, y[1]]
    alpha = ratio(rz, form(p, gap))
    x = [x[0] + alpha * p[0], alpha * p[1], 0.0]
    y = [y[0] - alpha * p[0], y[1] - alpha * (p[1] - p[0]), alpha * p[1]]
    new = form(y, nu)
    beta = ratio(new, rz)
    rz = new
    p = [y[0] + beta * p[0], y[1] + beta * p[1], y[2]]
    alpha = ratio(rz, form(p, gap))
    x = [x[0] + alpha * p[0], x[1] + alpha * p[1], alpha * p[2]]
    surface[...] = x[0] * base[0] + x[1] * base[1] + x[2] * base[2]


def call(kernel, outs, flops, moved, name, out_space=pltpu.VMEM, scratch=(), types=jnp.float32):
    def run(*args):
        return pl.pallas_call(
            kernel,
            out_shape=[jax.ShapeDtypeStruct(shape, types) for shape in outs],
            in_specs=[pl.BlockSpec(memory_space=pltpu.VMEM)] * len(args),
            out_specs=[pl.BlockSpec(memory_space=out_space)] * len(outs),
            scratch_shapes=list(scratch),
            cost_estimate=pl.CostEstimate(flops=flops, bytes_accessed=moved, transcendentals=0),
            compiler_params=pltpu.CompilerParams(vmem_limit_bytes=VMEM_LIMIT),
            name=name,
        )(*args)

    return run


def body(
    warmth_deviation,
    saltiness_deviation,
    easterly_speed,
    poleward_speed,
    stratum_spans,
    water_indicator,
    opposite_counterpart,
    elevation_weights,
    elevation_anomaly,
):
    lons, lats = lax.axis_size("lon"), lax.axis_size("lat")
    lon, lat = lax.axis_index("lon"), lax.axis_index("lat")
    levels, rows, cols = warmth_deviation.shape
    assert cols & (cols - 1) == 0 and 4 * levels <= cols // 2 and 2 * START[-1] <= RELAY and cols == 128
    high = packet_rows(levels)
    tall = rows + 16
    width = cols * lons
    flat = lambda i, j: (i % lons) * lats + j

    place = (lax.rem(lat, 2), (lat == lats - 1).astype(jnp.int32), lax.rem(lon, 2))
    meta = jnp.stack(place).astype(jnp.int32).reshape(1, 3)
    (meta,) = call(place_kernel, [(8, cols)], LOAD_FLOPS, 16, "place", types=jnp.int32)(meta)

    spans = stratum_spans.reshape(1, levels)
    facing = opposite_counterpart.reshape(1, cols)
    state = (warmth_deviation, saltiness_deviation, easterly_speed, poleward_speed)
    flat_state = (water_indicator, elevation_weights, elevation_anomaly)
    cells = levels * rows * cols
    sums, first, second, east_columns, west_columns = call(
        pack_kernel,
        [(3, rows, cols), (high, cols), (high, cols), (rows, cols), (rows, cols)],
        12 * cells,
        16 * cells,
        "level_sums",
        scratch=[pltpu.VMEM((high, cols), jnp.float32)] * 3,
    )(meta, spans, facing, *state, *flat_state)

    axes = ("lon", "lat")
    pairs_first = [(flat(i, j), flat(i, j ^ 1)) for i in range(lons) for j in range(lats)]
    pairs_inner = [
        (flat(i, a), flat(i, b))
        for i in range(lons)
        for j in range(1, lats - 1, 2)
        for a, b in ((j, j + 1), (j + 1, j))
    ]

    counterpart, first = lax.optimization_barrier((opposite_counterpart, first))
    hinge = lax.rem(counterpart[0] + 1 + cols * lon, width)
    block = lax.rem((hinge + cols // 2) // cols, lons)

    def exchange(shift, first, second):
        pairs_fold = [(flat(shift - 1 - i, lats - 1), flat(i, lats - 1)) for i in range(lons)]
        second = lax.ppermute(second, axes, pairs_inner + pairs_fold)
        return second, lax.ppermute(first, axes, pairs_first)

    second, first = lax.switch(block, [functools.partial(exchange, s) for s in range(lons)], first, second)

    deep = 4 * levels
    ext, to_far, to_near, state_far, state_near, facing_rows, north_rows, south_rows = call(
        turn_kernel,
        [
            (FIELDS, tall, cols),
            *[(tall // 2, cols)] * 2,
            *[(rows, cols)] * 2,
            (high - deep, cols),
            *[(deep, cols)] * 2,
        ],
        FIELDS * tall * cols,
        4 * 4 * FIELDS * tall * cols,
        "row_halos",
    )(meta, sums, *flat_state, second, first, east_columns, west_columns)

    near = lambda cells: lax.ppermute(cells, "lon", [(i, i ^ 1) for i in range(lons)])
    far = lambda cells: lax.ppermute(cells, "lon", [(i, (i + 1 if i % 2 else i - 1) % lons) for i in range(lons)])
    from_far, from_near = far(to_far), near(to_near)
    state_far, state_near = far(state_far), near(state_near)

    count = lons * lats
    base, moments = call(
        krylov_kernel,
        [(3, rows, cols), (count, cols)],
        200 * tall * cols,
        4 * 12 * tall * cols,
        "krylov",
        scratch=[pltpu.VMEM((2, high - deep + 8, cols), jnp.float32)],
    )(meta, facing, ext, facing_rows, from_far, from_near)

    chunks = 5 if levels % 5 == 0 else 1
    new_heat, new_salt, new_zonal, new_merid = call(
        step_kernel,
        [(levels, rows, cols)] * 4,
        120 * cells,
        32 * cells,
        "levels_step",
        out_space=pltpu.HBM,
        scratch=[
            *[pltpu.VMEM((levels, rows, cols), jnp.float32)] * 4,
            pltpu.VMEM((deep, cols), jnp.float32),
            pltpu.SemaphoreType.DMA((4, chunks)),
        ],
    )(meta, spans, facing, *state, water_indicator, north_rows, south_rows, state_far, state_near)

    shares = lax.all_to_all(moments, axes, 0, 0, tiled=True)
    (surface,) = call(surface_kernel, [(rows, cols)], 6 * rows * cols, 16 * rows * cols, "surface")(shares, base)
    return (new_heat, new_salt, new_zonal, new_merid, surface)


def solution(mesh):
    for axis in mesh.shape.values():
        assert axis > 1 and axis & (axis - 1) == 0
    levels = P(None, "lat", "lon")
    flat = P("lat", "lon")
    return jax.shard_map(
        body,
        mesh=mesh,
        in_specs=(levels, levels, levels, levels, P(), flat, P("lon"), flat, flat),
        out_specs=(levels, levels, levels, levels, flat),
        check_vma=False,
    )
```

```python
import functools

import jax
import jax.numpy as jnp
from jax import lax
from jax.experimental import pallas as pl
from jax.experimental.pallas import tpu as pltpu
from jax.sharding import PartitionSpec as P

TIME_STEP = 0.1
MIXING = 0.1

DEEP = (5, 3, 4, 4, 3, 3)
SIDE = (5, 4, 3, 4, 3, 3)
FIELDS = len(SIDE)
ROW = tuple(sum(DEEP[:f]) for f in range(FIELDS + 1))
START = tuple(sum(SIDE[:f]) for f in range(FIELDS + 1))
RELAY = 56
FLIPPED = (1, 2)
VMEM_LIMIT = 32 * 1024 * 1024
LOAD_FLOPS = 10**10


def density(heat, salt):
    return heat * (-1.0 - 0.15 * heat - 0.2 * salt) + 0.8 * salt


def iota(shape, axis):
    return lax.broadcasted_iota(jnp.int32, shape, axis)


def packet_rows(levels):
    return -(-(4 * levels + ROW[-1]) // 8) * 8


def flags(meta):
    return tuple(meta[i : i + 1, :] == 1 for i in range(4))


def place_kernel(meta, placed):
    for i in range(4):
        placed[i : i + 1, :] = jnp.broadcast_to(meta[0:1, i : i + 1], (1, placed.shape[1]))
    placed[4:, :] = jnp.zeros((placed.shape[0] - 4, placed.shape[1]), jnp.int32)


def pack_kernel(
    meta, spans, facing, heat, salt, zonal, merid, water, weights, anomaly,
    sums, first, second, east_columns, west_columns,
    top, bottom, back,
):
    levels, rows, cols = heat.shape
    span = [spans[0:1, k : k + 1] for k in range(levels)]
    below = [None] * levels
    total = jnp.zeros((1, 1), jnp.float32)
    for k in reversed(range(levels)):
        below[k] = span[k] * (0.5 * span[k] + total)
        total = total + span[k]
    pair = iota((rows, cols), 1) // 2
    zero = jnp.zeros((rows, cols), jnp.float32)
    press, east, north, east_edge, west_edge = zero, zero, zero, zero, zero
    for k in range(levels):
        press = press + below[k] * density(heat[k], salt[k])
        east = east + span[k] * zonal[k]
        north = north + span[k] * merid[k]
        for q, source in ((k, heat), (levels + k, salt)):
            cells = source[k]
            here = pair == q
            east_edge = jnp.where(here, pltpu.roll(cells, (2 * q + 2) % cols, 1), east_edge)
            west_edge = jnp.where(here, pltpu.roll(cells, 2 * q, 1), west_edge)
            top[2 * q : 2 * q + 2, :] = source[k, rows - 2 :, :]
            bottom[2 * q : 2 * q + 2, :] = source[k, :2, :]
            for i in range(2):
                back[2 * q + i : 2 * q + i + 1, :] = source[k, rows - 1 - i : rows - i, :]
    east_columns[...] = east_edge
    west_columns[...] = west_edge
    sums[0] = press
    sums[1] = east
    sums[2] = north
    fields = (sums.at[0], sums.at[1], sums.at[2], water, weights, anomaly)
    for f, field in enumerate(fields):
        at = 4 * levels + ROW[f]
        deep = DEEP[f]
        top[at : at + deep, :] = field[rows - deep :, :].astype(jnp.float32)
        bottom[at : at + deep, :] = field[:deep, :].astype(jnp.float32)
        for j in range(deep):
            back[at + j : at + j + 1, :] = field[rows - 1 - j : rows - j, :].astype(jnp.float32)
    used = 4 * levels + ROW[-1]
    high = first.shape[0]
    if used < high:
        for packet in (top, bottom, back):
            packet[used:, :] = jnp.zeros((high - used, cols), jnp.float32)
    odd, last, _, _ = flags(meta)
    first[...] = jnp.where(odd, bottom[...], top[...])
    second[...] = jnp.where(last, back[...], jnp.where(odd, top[...], bottom[...]))


def turn_kernel(
    meta, sums, water, weights, anomaly, second, first, east_columns, west_columns,
    ext, to_far, to_near, state_far, state_near, facing_rows, north_rows, south_rows,
):
    rows, cols = sums.shape[1], sums.shape[2]
    tall = ext.shape[1]
    deep = north_rows.shape[0]
    odd, _, lon_odd, bottom = flags(meta)
    from_first = first[...]
    from_second = second[...]
    north = jnp.where(odd, from_second, from_first)
    south = jnp.where(bottom, 0.0, jnp.where(odd, from_first, from_second))
    fields = (sums.at[0], sums.at[1], sums.at[2], water, weights, anomaly)
    for f in range(FIELDS):
        at = deep + ROW[f]
        size = DEEP[f]
        ext[f, :rows, :] = fields[f][...].astype(jnp.float32)
        ext[f, rows : rows + size, :] = north[at : at + size]
        ext[f, rows + size : tall - size, :] = jnp.zeros((tall - rows - 2 * size, cols), jnp.float32)
        ext[f, tall - size :, :] = south[at : at + size]
    middle = tall // 2
    passed = from_second[deep:]
    spare = jnp.zeros((middle - passed.shape[0], cols), jnp.float32)
    lane = iota((middle, cols), 1)
    relay = lane >= RELAY
    east = jnp.where(relay, jnp.concatenate([pltpu.roll(passed, RELAY, 1), spare], axis=0), 0.0)
    west = jnp.where(relay, jnp.concatenate([passed, spare], axis=0), 0.0)
    for f in range(FIELDS):
        for part in range(2):
            at = START[f] + part * START[-1]
            here = (lane >= at) & (lane < at + SIDE[f])
            layer = ext[f, part * middle : (part + 1) * middle, :]
            east = jnp.where(here, pltpu.roll(layer, (at + SIDE[f]) % cols, 1), east)
            west = jnp.where(here, pltpu.roll(layer, at, 1), west)
    to_far[...] = jnp.where(lon_odd, east, west)
    to_near[...] = jnp.where(lon_odd, west, east)
    passed = from_second[:deep]
    spare = jnp.zeros((rows - deep, cols), jnp.float32)
    half = iota((rows, cols), 1) >= cols // 2
    east = jnp.where(half, jnp.concatenate([pltpu.roll(passed, cols // 2, 1), spare], axis=0), east_columns[...])
    west = jnp.where(half, jnp.concatenate([passed, spare], axis=0), west_columns[...])
    state_far[...] = jnp.where(lon_odd, east, west)
    state_near[...] = jnp.where(lon_odd, west, east)
    facing_rows[...] = from_second[deep:]
    north_rows[...] = north[:deep]
    south_rows[...] = south[:deep]


def fold_shift(facing):
    cols = facing.shape[1]
    offset = (facing[0:1, 0:1] + 1) & (cols - 1)
    return jnp.where(offset >= cols // 2, offset - cols, offset)


def fold(shift, west, own, east, beside):
    rows, cols = own.shape
    lane = iota((rows, cols), 1)
    source = cols - 1 - lane
    if beside:
        place = (source + shift) & (cols - 1)
        low = jnp.where(place - cols < shift, west, own)
        merged = jnp.where(place >= cols // 2, low, jnp.where(place >= shift, east, own))
    else:
        merged = jnp.where(source >= cols - shift, west, jnp.where(source < -shift, east, own))
    return jnp.take_along_axis(merged, cols - 1 - ((lane - shift) & (cols - 1)), axis=1)


def krylov_kernel(meta, facing, ext, facing_rows, from_far, from_near, base, moments, folded):
    tall, cols = ext.shape[1], ext.shape[2]
    rows = base.shape[1]
    size = facing_rows.shape[0]
    middle = tall // 2
    _, top, lon_odd, _ = flags(meta)
    west = jnp.where(lon_odd, from_near[...], from_far[...])
    east = jnp.where(lon_odd, from_far[...], from_near[...])
    shift = fold_shift(facing)
    row = iota((size, cols), 0)
    flips = (row >= ROW[FLIPPED[0]]) & (row < ROW[FLIPPED[-1] + 1])
    for side in range(2):
        cells = fold(shift, pltpu.roll(west[:size], cols - RELAY, 1), facing_rows[...], east[:size], side == 1)
        folded[side, :size, :] = jnp.where(flips, -cells, cells)
    folded[:, size:, :] = jnp.zeros((2, folded.shape[1] - size, cols), jnp.float32)
    lane = iota((tall, cols), 1)
    first = lane == 0
    last = lane == cols - 1
    eighth = iota((8, cols), 0)

    def load(f):
        both = [START[f], START[f] + START[-1]]
        a = jnp.concatenate([pltpu.roll(west, (2 * cols - SIDE[f] - at) % cols, 1) for at in both], axis=0)
        b = jnp.concatenate([pltpu.roll(east, (cols - at) % cols, 1) for at in both], axis=0)
        beside = jnp.where(lane >= cols - SIDE[f], a, jnp.where(lane < SIDE[f], b, 0.0))

        def put(cells, side):
            new = folded[side, ROW[f] : ROW[f] + 8, :]
            new = jnp.where(eighth < DEEP[f], jnp.where(top, new, cells[rows : rows + 8]), 0.0)
            return jnp.concatenate([cells[:rows], new, cells[rows + 8 :]], axis=0)

        return put(ext[f], 0), put(beside, 1)

    def plus_x(pair):
        a, b = (pltpu.roll(part, cols - 1, 1) for part in pair)
        return jnp.where(last, b, a), jnp.where(last, a, b)

    def minus_x(pair):
        a, b = (pltpu.roll(part, 1, 1) for part in pair)
        return jnp.where(first, b, a), jnp.where(first, a, b)

    def plus_y(pair):
        return tuple(pltpu.roll(part, tall - 1, 0) for part in pair)

    def minus_y(pair):
        return tuple(pltpu.roll(part, 1, 0) for part in pair)

    def each(function, *pairs):
        return tuple(function(*parts) for parts in zip(*pairs))

    def neighbours(pair):
        return each(
            lambda a, b, c, d: (a + b) + (c + d), plus_x(pair), minus_x(pair), plus_y(pair), minus_y(pair)
        )

    press, zonal, merid, wet, weights, anomaly = (load(f) for f in range(FIELDS))
    half = 0.5 * TIME_STEP
    flow = lambda w, speed, a, b: w * (speed - half * (a - b))
    east_flow = each(flow, wet, zonal, plus_x(press), minus_x(press))
    north_flow = each(flow, wet, merid, plus_y(press), minus_y(press))
    right = each(
        lambda w, g, n, a, b, c, d: w * (g * n - 0.5 * (a - b + c - d)),
        wet,
        weights,
        anomaly,
        plus_x(east_flow),
        minus_x(east_flow),
        plus_y(north_flow),
        minus_y(north_flow),
    )
    diagonal = each(lambda g: 4.0 + g, weights)
    inverse = each(lambda m: 1.0 / m, diagonal)
    scale = each(lambda w, i: w * i, wet, inverse)
    zero = each(lambda r, i: r * i, right, inverse)
    one = each(lambda a, n: a * n, scale, neighbours(zero))
    two = each(lambda a, n: a * n, scale, neighbours(one))
    last_sum = neighbours(two)[0][:rows]
    right, middle = right[0][:rows], diagonal[0][:rows]
    zero, one, two = zero[0][:rows], one[0][:rows], two[0][:rows]
    base[0] = zero
    base[1] = one
    base[2] = two
    weighted = middle * one
    products = (
        right * zero,
        right * one,
        weighted * one,
        weighted * two,
        middle * two * two,
        last_sum * two,
    )
    which = iota((8, cols), 0)
    sums = jnp.zeros((8, cols), jnp.float32)
    for k, product in enumerate(products):
        sums = jnp.where(which == k, jnp.sum(product, axis=0, keepdims=True), sums)
    sums = jnp.sum(sums, axis=1, keepdims=True)
    sums = jnp.sum(jnp.where(which == iota((8, cols), 1), sums, 0.0), axis=0, keepdims=True)
    moments[...] = jnp.broadcast_to(sums, moments.shape)


def step_kernel(
    meta, spans, facing, heat, salt, zonal, merid, water, north_came, south_rows, from_far, from_near,
    heat_out, salt_out, zonal_out, merid_out,
    new_heat, new_salt, new_zonal, new_merid, north_rows, sems,
):
    levels, rows, cols = heat.shape
    deep = 4 * levels
    _, top, lon_odd, _ = flags(meta)
    wet = water[...].astype(jnp.float32)
    lane = iota((rows, cols), 1)
    row = iota((rows, cols), 0)
    east = jnp.where(lon_odd, from_far[...], from_near[...])
    west = jnp.where(lon_odd, from_near[...], from_far[...])
    came = north_came[...]
    across = fold(fold_shift(facing), pltpu.roll(west[:deep], cols // 2, 1), came, east[:deep], False)
    north_rows[...] = jnp.where(top, across, came)

    def around(cells, q):
        a = pltpu.roll(east, (cols - 2 * q) % cols, 1)
        b = pltpu.roll(west, (2 * cols - 2 - 2 * q) % cols, 1)
        side = jnp.where(lane < 2, a, b)

        def shift_x(by):
            a = pltpu.roll(cells, by % cols, 1)
            b = pltpu.roll(side, by % cols, 1)
            own = lane >= by if by > 0 else lane < cols + by
            return jnp.where(own, a, b)

        n0 = north_rows[2 * q : 2 * q + 1, :]
        n1 = north_rows[2 * q + 1 : 2 * q + 2, :]
        s0 = south_rows[2 * q + 1 : 2 * q + 2, :]
        s1 = south_rows[2 * q : 2 * q + 1, :]
        north_one = jnp.where(row == rows - 1, n0, pltpu.roll(cells, rows - 1, 0))
        north_two = jnp.where(row == rows - 1, n1, jnp.where(row == rows - 2, n0, pltpu.roll(cells, rows - 2, 0)))
        south_one = jnp.where(row == 0, s0, pltpu.roll(cells, 1, 0))
        south_two = jnp.where(row == 0, s1, jnp.where(row == 1, s0, pltpu.roll(cells, 2, 0)))
        return (shift_x(-1), shift_x(1), shift_x(-2), shift_x(2), north_one, south_one, north_two, south_two)

    def advance(cells, parts, speed_x, speed_y):
        e1, w1, e2, w2, n1, s1, n2, s2 = parts
        grad_east = 8.0 * (e1 - w1) - (e2 - w2)
        grad_north = 8.0 * (n1 - s1) - (n2 - s2)
        laplace = (e1 + w1) + (n1 + s1) - 4.0 * cells
        tendency = (-TIME_STEP / 12.0) * (speed_x * grad_east + speed_y * grad_north) + MIXING * laplace
        return cells + wet * tendency

    stores = ((new_heat, heat_out), (new_salt, salt_out), (new_zonal, zonal_out), (new_merid, merid_out))
    size = levels // sems.shape[1]
    copies = []
    half = 0.5 * TIME_STEP
    above_x = jnp.zeros((rows, cols), jnp.float32)
    above_y = jnp.zeros((rows, cols), jnp.float32)
    for k in range(levels):
        t, s, u, v = heat[k], salt[k], zonal[k], merid[k]
        around_t = around(t, k)
        around_s = around(s, levels + k)
        new_heat[k] = advance(t, around_t, u, v)
        new_salt[k] = advance(s, around_s, u, v)
        span = spans[0:1, k : k + 1]
        layer_x = span * (density(around_t[0], around_s[0]) - density(around_t[1], around_s[1]))
        layer_y = span * (density(around_t[4], around_s[4]) - density(around_t[5], around_s[5]))
        new_zonal[k] = wet * (u - half * (above_x + 0.5 * layer_x))
        new_merid[k] = wet * (v - half * (above_y + 0.5 * layer_y))
        above_x = above_x + layer_x
        above_y = above_y + layer_y
        if (k + 1) % size == 0:
            piece = pl.ds(k + 1 - size, size)
            for i, (near_ref, far_ref) in enumerate(stores):
                copies.append(pltpu.make_async_copy(near_ref.at[piece], far_ref.at[piece], sems.at[i, k // size]))
                copies[-1].start()
    for copy in copies:
        copy.wait()


def surface_kernel(shares, base, surface):
    sums = jnp.sum(shares[...], axis=0, keepdims=True)
    lane = iota(sums.shape, 1)
    nu = [jnp.sum(jnp.where(lane == k, sums, 0.0), axis=1, keepdims=True) for k in range(6)]

    def ratio(a, b):
        good = b > 0.0
        return jnp.where(good, a / jnp.where(good, b, 1.0), 0.0)

    def form(p, h):
        total = 0.0
        for i, a in enumerate(p):
            for j in range(i, len(p)):
                term = a * p[j] * h[i + j]
                total = total + (term if i == j else 2.0 * term)
        return total

    gap = [nu[k] - nu[k + 1] for k in range(5)]
    rz = nu[0]
    alpha = ratio(rz, gap[0])
    one = jnp.ones_like(rz)
    y = [one - alpha, alpha]
    x = [alpha, 0.0, 0.0]
    new = form(y, nu)
    beta = ratio(new, rz)
    rz = new
    p = [y[0] + beta, y[1]]
    alpha = ratio(rz, form(p, gap))
    x = [x[0] + alpha * p[0], alpha * p[1], 0.0]
    y = [y[0] - alpha * p[0], y[1] - alpha * (p[1] - p[0]), alpha * p[1]]
    new = form(y, nu)
    beta = ratio(new, rz)
    rz = new
    p = [y[0] + beta * p[0], y[1] + beta * p[1], y[2]]
    alpha = ratio(rz, form(p, gap))
    x = [x[0] + alpha * p[0], x[1] + alpha * p[1], alpha * p[2]]
    surface[...] = x[0] * base[0] + x[1] * base[1] + x[2] * base[2]


def call(kernel, outs, flops, moved, name, out_space=pltpu.VMEM, scratch=(), types=jnp.float32):
    def run(*args):
        return pl.pallas_call(
            kernel,
            out_shape=[jax.ShapeDtypeStruct(shape, types) for shape in outs],
            in_specs=[pl.BlockSpec(memory_space=pltpu.VMEM)] * len(args),
            out_specs=[pl.BlockSpec(memory_space=out_space)] * len(outs),
            scratch_shapes=list(scratch),
            cost_estimate=pl.CostEstimate(flops=flops, bytes_accessed=moved, transcendentals=0),
            compiler_params=pltpu.CompilerParams(vmem_limit_bytes=VMEM_LIMIT),
            name=name,
        )(*args)

    return run


def body(
    warmth_deviation,
    saltiness_deviation,
    easterly_speed,
    poleward_speed,
    stratum_spans,
    water_indicator,
    opposite_counterpart,
    elevation_weights,
    elevation_anomaly,
):
    lons, lats = lax.axis_size("lon"), lax.axis_size("lat")
    lon, lat = lax.axis_index("lon"), lax.axis_index("lat")
    levels, rows, cols = warmth_deviation.shape
    assert cols & (cols - 1) == 0 and 4 * levels <= cols // 2 and 2 * START[-1] <= RELAY and cols == 128
    high = packet_rows(levels)
    tall = rows + 16
    width = cols * lons
    flat = lambda i, j: (i % lons) * lats + j

    place = (lax.rem(lat, 2), lat == lats - 1, lax.rem(lon, 2), lat == 0)
    meta = jnp.stack([value.astype(jnp.int32) for value in place]).reshape(1, 4)
    (meta,) = call(place_kernel, [(8, cols)], LOAD_FLOPS, 16, "place", types=jnp.int32)(meta)

    spans = stratum_spans.reshape(1, levels)
    facing = opposite_counterpart.reshape(1, cols)
    state = (warmth_deviation, saltiness_deviation, easterly_speed, poleward_speed)
    flat_state = (water_indicator, elevation_weights, elevation_anomaly)
    cells = levels * rows * cols
    sums, first, second, east_columns, west_columns = call(
        pack_kernel,
        [(3, rows, cols), (high, cols), (high, cols), (rows, cols), (rows, cols)],
        12 * cells,
        16 * cells,
        "level_sums",
        scratch=[pltpu.VMEM((high, cols), jnp.float32)] * 3,
    )(meta, spans, facing, *state, *flat_state)

    axes = ("lon", "lat")
    pairs_first = [(flat(i, j), flat(i, j ^ 1)) for i in range(lons) for j in range(lats)]
    pairs_inner = [
        (flat(i, a), flat(i, b))
        for i in range(lons)
        for j in range(1, lats - 1, 2)
        for a, b in ((j, j + 1), (j + 1, j))
    ] + [(flat(i, 0), flat(i, 0)) for i in range(lons)]

    counterpart, first = lax.optimization_barrier((opposite_counterpart, first))
    hinge = lax.rem(counterpart[0] + 1 + cols * lon, width)
    block = lax.rem((hinge + cols // 2) // cols, lons)

    def exchange(shift, first, second):
        pairs_fold = [(flat(shift - 1 - i, lats - 1), flat(i, lats - 1)) for i in range(lons)]
        second = lax.ppermute(second, axes, pairs_inner + pairs_fold)
        return second, lax.ppermute(first, axes, pairs_first)

    second, first = lax.switch(block, [functools.partial(exchange, s) for s in range(lons)], first, second)

    deep = 4 * levels
    ext, to_far, to_near, state_far, state_near, facing_rows, north_rows, south_rows = call(
        turn_kernel,
        [
            (FIELDS, tall, cols),
            *[(tall // 2, cols)] * 2,
            *[(rows, cols)] * 2,
            (high - deep, cols),
            *[(deep, cols)] * 2,
        ],
        FIELDS * tall * cols,
        4 * 4 * FIELDS * tall * cols,
        "row_halos",
    )(meta, sums, *flat_state, second, first, east_columns, west_columns)

    near = lambda cells: lax.ppermute(cells, "lon", [(i, i ^ 1) for i in range(lons)])
    far = lambda cells: lax.ppermute(cells, "lon", [(i, (i + 1 if i % 2 else i - 1) % lons) for i in range(lons)])
    from_far, from_near = far(to_far), near(to_near)
    state_far, state_near = far(state_far), near(state_near)

    count = lons * lats
    base, moments = call(
        krylov_kernel,
        [(3, rows, cols), (count, cols)],
        200 * tall * cols,
        4 * 12 * tall * cols,
        "krylov",
        scratch=[pltpu.VMEM((2, high - deep + 8, cols), jnp.float32)],
    )(meta, facing, ext, facing_rows, from_far, from_near)

    chunks = 5 if levels % 5 == 0 else 1
    new_heat, new_salt, new_zonal, new_merid = call(
        step_kernel,
        [(levels, rows, cols)] * 4,
        120 * cells,
        32 * cells,
        "levels_step",
        out_space=pltpu.HBM,
        scratch=[
            *[pltpu.VMEM((levels, rows, cols), jnp.float32)] * 4,
            pltpu.VMEM((deep, cols), jnp.float32),
            pltpu.SemaphoreType.DMA((4, chunks)),
        ],
    )(meta, spans, facing, *state, water_indicator, north_rows, south_rows, state_far, state_near)

    shares = lax.all_to_all(moments, axes, 0, 0, tiled=True)
    (surface,) = call(surface_kernel, [(rows, cols)], 6 * rows * cols, 16 * rows * cols, "surface")(shares, base)
    return (new_heat, new_salt, new_zonal, new_merid, surface)


def solution(mesh):
    for axis in mesh.shape.values():
        assert axis > 1 and axis & (axis - 1) == 0
    levels = P(None, "lat", "lon")
    flat = P("lat", "lon")
    return jax.shard_map(
        body,
        mesh=mesh,
        in_specs=(levels, levels, levels, levels, P(), flat, P("lon"), flat, flat),
        out_specs=(levels, levels, levels, levels, flat),
        check_vma=False,
    )
```

```python
import functools

import jax
import jax.numpy as jnp
from jax import lax
from jax.experimental import pallas as pl
from jax.experimental.pallas import tpu as pltpu
from jax.sharding import PartitionSpec as P

TIME_STEP = 0.1
MIXING = 0.1

DEEP = (5, 3, 4, 4, 3, 3)
SIDE = (5, 4, 3, 4, 3, 3)
FIELDS = len(SIDE)
ROW = tuple(sum(DEEP[:f]) for f in range(FIELDS + 1))
START = tuple(sum(SIDE[:f]) for f in range(FIELDS + 1))
RELAY = 56
FLIPPED = (1, 2)
VMEM_LIMIT = 32 * 1024 * 1024
LOAD_FLOPS = 10**10


def density(heat, salt):
    return heat * (-1.0 - 0.15 * heat - 0.2 * salt) + 0.8 * salt


def iota(shape, axis):
    return lax.broadcasted_iota(jnp.int32, shape, axis)


def packet_rows(levels):
    return -(-(4 * levels + ROW[-1]) // 8) * 8


def flags(meta):
    return tuple(meta[i : i + 1, :] == 1 for i in range(4))


def place_kernel(meta, placed):
    for i in range(5):
        placed[i : i + 1, :] = jnp.broadcast_to(meta[0:1, i : i + 1], (1, placed.shape[1]))
    placed[5:, :] = jnp.zeros((placed.shape[0] - 5, placed.shape[1]), jnp.int32)


def pack_kernel(
    meta, spans, facing, heat, salt, zonal, merid, water, weights, anomaly,
    sums, first, second, east_columns, west_columns,
    top, bottom, back,
):
    levels, rows, cols = heat.shape
    span = [spans[0:1, k : k + 1] for k in range(levels)]
    below = [None] * levels
    total = jnp.zeros((1, 1), jnp.float32)
    for k in reversed(range(levels)):
        below[k] = span[k] * (0.5 * span[k] + total)
        total = total + span[k]
    pair = iota((rows, cols), 1) // 2
    zero = jnp.zeros((rows, cols), jnp.float32)
    press, east, north, east_edge, west_edge = zero, zero, zero, zero, zero
    for k in range(levels):
        press = press + below[k] * density(heat[k], salt[k])
        east = east + span[k] * zonal[k]
        north = north + span[k] * merid[k]
        for q, source in ((k, heat), (levels + k, salt)):
            cells = source[k]
            here = pair == q
            east_edge = jnp.where(here, pltpu.roll(cells, (2 * q + 2) % cols, 1), east_edge)
            west_edge = jnp.where(here, pltpu.roll(cells, 2 * q, 1), west_edge)
            top[2 * q : 2 * q + 2, :] = source[k, rows - 2 :, :]
            bottom[2 * q : 2 * q + 2, :] = source[k, :2, :]
            for i in range(2):
                back[2 * q + i : 2 * q + i + 1, :] = source[k, rows - 1 - i : rows - i, :]
    east_columns[...] = east_edge
    west_columns[...] = west_edge
    sums[0] = press
    sums[1] = east
    sums[2] = north
    fields = (sums.at[0], sums.at[1], sums.at[2], water, weights, anomaly)
    for f, field in enumerate(fields):
        at = 4 * levels + ROW[f]
        deep = DEEP[f]
        top[at : at + deep, :] = field[rows - deep :, :].astype(jnp.float32)
        bottom[at : at + deep, :] = field[:deep, :].astype(jnp.float32)
        for j in range(deep):
            back[at + j : at + j + 1, :] = field[rows - 1 - j : rows - j, :].astype(jnp.float32)
    used = 4 * levels + ROW[-1]
    high = first.shape[0]
    if used < high:
        for packet in (top, bottom, back):
            packet[used:, :] = jnp.zeros((high - used, cols), jnp.float32)
    odd, last, _, _ = flags(meta)
    first[...] = jnp.where(odd, bottom[...], top[...])
    second[...] = jnp.where(last, back[...], jnp.where(odd, top[...], bottom[...]))


def turn_kernel(
    lons, meta, facing, mine, sums, water, weights, anomaly, second, first, east_columns, west_columns,
    ext, to_far, to_near, state_far, state_near, facing_rows, north_rows, south_rows,
):
    rows, cols = sums.shape[1], sums.shape[2]
    tall = ext.shape[1]
    deep = north_rows.shape[0]
    odd, top, lon_odd, bottom = flags(meta)
    from_first = first[...]
    hinge = facing[0:1, 0:1] + 1 + cols * meta[4:5, 0:1] + cols // 2
    block = lax.shift_right_logical(hinge & (lons * cols - 1), cols.bit_length() - 1)
    alone = ((block - 1 - 2 * meta[4:5, 0:1]) & (lons - 1)) == 0
    from_second = jnp.where(top & alone, mine[...], second[...])
    north = jnp.where(odd, from_second, from_first)
    south = jnp.where(bottom, 0.0, jnp.where(odd, from_first, from_second))
    fields = (sums.at[0], sums.at[1], sums.at[2], water, weights, anomaly)
    for f in range(FIELDS):
        at = deep + ROW[f]
        size = DEEP[f]
        ext[f, :rows, :] = fields[f][...].astype(jnp.float32)
        ext[f, rows : rows + size, :] = north[at : at + size]
        ext[f, rows + size : tall - size, :] = jnp.zeros((tall - rows - 2 * size, cols), jnp.float32)
        ext[f, tall - size :, :] = south[at : at + size]
    middle = tall // 2
    passed = from_second[deep:]
    spare = jnp.zeros((middle - passed.shape[0], cols), jnp.float32)
    lane = iota((middle, cols), 1)
    relay = lane >= RELAY
    east = jnp.where(relay, jnp.concatenate([pltpu.roll(passed, RELAY, 1), spare], axis=0), 0.0)
    west = jnp.where(relay, jnp.concatenate([passed, spare], axis=0), 0.0)
    for f in range(FIELDS):
        for part in range(2):
            at = START[f] + part * START[-1]
            here = (lane >= at) & (lane < at + SIDE[f])
            layer = ext[f, part * middle : (part + 1) * middle, :]
            east = jnp.where(here, pltpu.roll(layer, (at + SIDE[f]) % cols, 1), east)
            west = jnp.where(here, pltpu.roll(layer, at, 1), west)
    to_far[...] = jnp.where(lon_odd, east, west)
    to_near[...] = jnp.where(lon_odd, west, east)
    passed = from_second[:deep]
    spare = jnp.zeros((rows - deep, cols), jnp.float32)
    half = iota((rows, cols), 1) >= cols // 2
    east = jnp.where(half, jnp.concatenate([pltpu.roll(passed, cols // 2, 1), spare], axis=0), east_columns[...])
    west = jnp.where(half, jnp.concatenate([passed, spare], axis=0), west_columns[...])
    state_far[...] = jnp.where(lon_odd, east, west)
    state_near[...] = jnp.where(lon_odd, west, east)
    facing_rows[...] = from_second[deep:]
    north_rows[...] = north[:deep]
    south_rows[...] = south[:deep]


def fold_shift(facing):
    cols = facing.shape[1]
    offset = (facing[0:1, 0:1] + 1) & (cols - 1)
    return jnp.where(offset >= cols // 2, offset - cols, offset)


def fold(shift, west, own, east, beside):
    rows, cols = own.shape
    lane = iota((rows, cols), 1)
    source = cols - 1 - lane
    if beside:
        place = (source + shift) & (cols - 1)
        low = jnp.where(place - cols < shift, west, own)
        merged = jnp.where(place >= cols // 2, low, jnp.where(place >= shift, east, own))
    else:
        merged = jnp.where(source >= cols - shift, west, jnp.where(source < -shift, east, own))
    return jnp.take_along_axis(merged, cols - 1 - ((lane - shift) & (cols - 1)), axis=1)


def krylov_kernel(meta, facing, ext, facing_rows, from_far, from_near, base, moments, folded):
    tall, cols = ext.shape[1], ext.shape[2]
    rows = base.shape[1]
    size = facing_rows.shape[0]
    middle = tall // 2
    _, top, lon_odd, _ = flags(meta)
    west = jnp.where(lon_odd, from_near[...], from_far[...])
    east = jnp.where(lon_odd, from_far[...], from_near[...])
    shift = fold_shift(facing)
    row = iota((size, cols), 0)
    flips = (row >= ROW[FLIPPED[0]]) & (row < ROW[FLIPPED[-1] + 1])
    for side in range(2):
        cells = fold(shift, pltpu.roll(west[:size], cols - RELAY, 1), facing_rows[...], east[:size], side == 1)
        folded[side, :size, :] = jnp.where(flips, -cells, cells)
    folded[:, size:, :] = jnp.zeros((2, folded.shape[1] - size, cols), jnp.float32)
    lane = iota((tall, cols), 1)
    first = lane == 0
    last = lane == cols - 1
    eighth = iota((8, cols), 0)

    def load(f):
        both = [START[f], START[f] + START[-1]]
        a = jnp.concatenate([pltpu.roll(west, (2 * cols - SIDE[f] - at) % cols, 1) for at in both], axis=0)
        b = jnp.concatenate([pltpu.roll(east, (cols - at) % cols, 1) for at in both], axis=0)
        beside = jnp.where(lane >= cols - SIDE[f], a, jnp.where(lane < SIDE[f], b, 0.0))

        def put(cells, side):
            new = folded[side, ROW[f] : ROW[f] + 8, :]
            new = jnp.where(eighth < DEEP[f], jnp.where(top, new, cells[rows : rows + 8]), 0.0)
            return jnp.concatenate([cells[:rows], new, cells[rows + 8 :]], axis=0)

        return put(ext[f], 0), put(beside, 1)

    def plus_x(pair):
        a, b = (pltpu.roll(part, cols - 1, 1) for part in pair)
        return jnp.where(last, b, a), jnp.where(last, a, b)

    def minus_x(pair):
        a, b = (pltpu.roll(part, 1, 1) for part in pair)
        return jnp.where(first, b, a), jnp.where(first, a, b)

    def plus_y(pair):
        return tuple(pltpu.roll(part, tall - 1, 0) for part in pair)

    def minus_y(pair):
        return tuple(pltpu.roll(part, 1, 0) for part in pair)

    def each(function, *pairs):
        return tuple(function(*parts) for parts in zip(*pairs))

    def neighbours(pair):
        return each(
            lambda a, b, c, d: (a + b) + (c + d), plus_x(pair), minus_x(pair), plus_y(pair), minus_y(pair)
        )

    press, zonal, merid, wet, weights, anomaly = (load(f) for f in range(FIELDS))
    half = 0.5 * TIME_STEP
    flow = lambda w, speed, a, b: w * (speed - half * (a - b))
    east_flow = each(flow, wet, zonal, plus_x(press), minus_x(press))
    north_flow = each(flow, wet, merid, plus_y(press), minus_y(press))
    right = each(
        lambda w, g, n, a, b, c, d: w * (g * n - 0.5 * (a - b + c - d)),
        wet,
        weights,
        anomaly,
        plus_x(east_flow),
        minus_x(east_flow),
        plus_y(north_flow),
        minus_y(north_flow),
    )
    diagonal = each(lambda g: 4.0 + g, weights)
    inverse = each(lambda m: 1.0 / m, diagonal)
    scale = each(lambda w, i: w * i, wet, inverse)
    zero = each(lambda r, i: r * i, right, inverse)
    one = each(lambda a, n: a * n, scale, neighbours(zero))
    two = each(lambda a, n: a * n, scale, neighbours(one))
    last_sum = neighbours(two)[0][:rows]
    right, middle = right[0][:rows], diagonal[0][:rows]
    zero, one, two = zero[0][:rows], one[0][:rows], two[0][:rows]
    base[0] = zero
    base[1] = one
    base[2] = two
    weighted = middle * one
    products = (
        right * zero,
        right * one,
        weighted * one,
        weighted * two,
        middle * two * two,
        last_sum * two,
    )
    which = iota((8, cols), 0)
    sums = jnp.zeros((8, cols), jnp.float32)
    for k, product in enumerate(products):
        sums = jnp.where(which == k, jnp.sum(product, axis=0, keepdims=True), sums)
    sums = jnp.sum(sums, axis=1, keepdims=True)
    sums = jnp.sum(jnp.where(which == iota((8, cols), 1), sums, 0.0), axis=0, keepdims=True)
    moments[...] = jnp.broadcast_to(sums, moments.shape)


def step_kernel(
    meta, spans, facing, heat, salt, zonal, merid, water, north_came, south_rows, from_far, from_near,
    heat_out, salt_out, zonal_out, merid_out,
    new_heat, new_salt, new_zonal, new_merid, north_rows, sems,
):
    levels, rows, cols = heat.shape
    deep = 4 * levels
    _, top, lon_odd, _ = flags(meta)
    wet = water[...].astype(jnp.float32)
    lane = iota((rows, cols), 1)
    row = iota((rows, cols), 0)
    east = jnp.where(lon_odd, from_far[...], from_near[...])
    west = jnp.where(lon_odd, from_near[...], from_far[...])
    came = north_came[...]
    across = fold(fold_shift(facing), pltpu.roll(west[:deep], cols // 2, 1), came, east[:deep], False)
    north_rows[...] = jnp.where(top, across, came)

    def around(cells, q):
        a = pltpu.roll(east, (cols - 2 * q) % cols, 1)
        b = pltpu.roll(west, (2 * cols - 2 - 2 * q) % cols, 1)
        side = jnp.where(lane < 2, a, b)

        def shift_x(by):
            a = pltpu.roll(cells, by % cols, 1)
            b = pltpu.roll(side, by % cols, 1)
            own = lane >= by if by > 0 else lane < cols + by
            return jnp.where(own, a, b)

        n0 = north_rows[2 * q : 2 * q + 1, :]
        n1 = north_rows[2 * q + 1 : 2 * q + 2, :]
        s0 = south_rows[2 * q + 1 : 2 * q + 2, :]
        s1 = south_rows[2 * q : 2 * q + 1, :]
        north_one = jnp.where(row == rows - 1, n0, pltpu.roll(cells, rows - 1, 0))
        north_two = jnp.where(row == rows - 1, n1, jnp.where(row == rows - 2, n0, pltpu.roll(cells, rows - 2, 0)))
        south_one = jnp.where(row == 0, s0, pltpu.roll(cells, 1, 0))
        south_two = jnp.where(row == 0, s1, jnp.where(row == 1, s0, pltpu.roll(cells, 2, 0)))
        return (shift_x(-1), shift_x(1), shift_x(-2), shift_x(2), north_one, south_one, north_two, south_two)

    def advance(cells, parts, speed_x, speed_y):
        e1, w1, e2, w2, n1, s1, n2, s2 = parts
        grad_east = 8.0 * (e1 - w1) - (e2 - w2)
        grad_north = 8.0 * (n1 - s1) - (n2 - s2)
        laplace = (e1 + w1) + (n1 + s1) - 4.0 * cells
        tendency = (-TIME_STEP / 12.0) * (speed_x * grad_east + speed_y * grad_north) + MIXING * laplace
        return cells + wet * tendency

    stores = ((new_heat, heat_out), (new_salt, salt_out), (new_zonal, zonal_out), (new_merid, merid_out))
    size = levels // sems.shape[1]
    copies = []
    half = 0.5 * TIME_STEP
    above_x = jnp.zeros((rows, cols), jnp.float32)
    above_y = jnp.zeros((rows, cols), jnp.float32)
    for k in range(levels):
        t, s, u, v = heat[k], salt[k], zonal[k], merid[k]
        around_t = around(t, k)
        around_s = around(s, levels + k)
        new_heat[k] = advance(t, around_t, u, v)
        new_salt[k] = advance(s, around_s, u, v)
        span = spans[0:1, k : k + 1]
        layer_x = span * (density(around_t[0], around_s[0]) - density(around_t[1], around_s[1]))
        layer_y = span * (density(around_t[4], around_s[4]) - density(around_t[5], around_s[5]))
        new_zonal[k] = wet * (u - half * (above_x + 0.5 * layer_x))
        new_merid[k] = wet * (v - half * (above_y + 0.5 * layer_y))
        above_x = above_x + layer_x
        above_y = above_y + layer_y
        if (k + 1) % size == 0:
            piece = pl.ds(k + 1 - size, size)
            for i, (near_ref, far_ref) in enumerate(stores):
                copies.append(pltpu.make_async_copy(near_ref.at[piece], far_ref.at[piece], sems.at[i, k // size]))
                copies[-1].start()
    for copy in copies:
        copy.wait()


def surface_kernel(shares, base, surface):
    sums = jnp.sum(shares[...], axis=0, keepdims=True)
    lane = iota(sums.shape, 1)
    nu = [jnp.sum(jnp.where(lane == k, sums, 0.0), axis=1, keepdims=True) for k in range(6)]

    def ratio(a, b):
        good = b > 0.0
        return jnp.where(good, a / jnp.where(good, b, 1.0), 0.0)

    def form(p, h):
        total = 0.0
        for i, a in enumerate(p):
            for j in range(i, len(p)):
                term = a * p[j] * h[i + j]
                total = total + (term if i == j else 2.0 * term)
        return total

    gap = [nu[k] - nu[k + 1] for k in range(5)]
    rz = nu[0]
    alpha = ratio(rz, gap[0])
    one = jnp.ones_like(rz)
    y = [one - alpha, alpha]
    x = [alpha, 0.0, 0.0]
    new = form(y, nu)
    beta = ratio(new, rz)
    rz = new
    p = [y[0] + beta, y[1]]
    alpha = ratio(rz, form(p, gap))
    x = [x[0] + alpha * p[0], alpha * p[1], 0.0]
    y = [y[0] - alpha * p[0], y[1] - alpha * (p[1] - p[0]), alpha * p[1]]
    new = form(y, nu)
    beta = ratio(new, rz)
    rz = new
    p = [y[0] + beta * p[0], y[1] + beta * p[1], y[2]]
    alpha = ratio(rz, form(p, gap))
    x = [x[0] + alpha * p[0], x[1] + alpha * p[1], alpha * p[2]]
    surface[...] = x[0] * base[0] + x[1] * base[1] + x[2] * base[2]


def call(kernel, outs, flops, moved, name, out_space=pltpu.VMEM, scratch=(), types=jnp.float32):
    def run(*args):
        return pl.pallas_call(
            kernel,
            out_shape=[jax.ShapeDtypeStruct(shape, types) for shape in outs],
            in_specs=[pl.BlockSpec(memory_space=pltpu.VMEM)] * len(args),
            out_specs=[pl.BlockSpec(memory_space=out_space)] * len(outs),
            scratch_shapes=list(scratch),
            cost_estimate=pl.CostEstimate(flops=flops, bytes_accessed=moved, transcendentals=0),
            compiler_params=pltpu.CompilerParams(vmem_limit_bytes=VMEM_LIMIT),
            name=name,
        )(*args)

    return run


def body(
    warmth_deviation,
    saltiness_deviation,
    easterly_speed,
    poleward_speed,
    stratum_spans,
    water_indicator,
    opposite_counterpart,
    elevation_weights,
    elevation_anomaly,
):
    lons, lats = lax.axis_size("lon"), lax.axis_size("lat")
    lon, lat = lax.axis_index("lon"), lax.axis_index("lat")
    levels, rows, cols = warmth_deviation.shape
    assert cols & (cols - 1) == 0 and 4 * levels <= cols // 2 and 2 * START[-1] <= RELAY and cols == 128
    high = packet_rows(levels)
    tall = rows + 16
    width = cols * lons
    flat = lambda i, j: (i % lons) * lats + j

    place = (lax.rem(lat, 2), lat == lats - 1, lax.rem(lon, 2), lat == 0, lon)
    meta = jnp.stack([value.astype(jnp.int32) for value in place]).reshape(1, 5)
    (meta,) = call(place_kernel, [(8, cols)], LOAD_FLOPS, 16, "place", types=jnp.int32)(meta)

    spans = stratum_spans.reshape(1, levels)
    facing = opposite_counterpart.reshape(1, cols)
    state = (warmth_deviation, saltiness_deviation, easterly_speed, poleward_speed)
    flat_state = (water_indicator, elevation_weights, elevation_anomaly)
    cells = levels * rows * cols
    sums, first, second, east_columns, west_columns = call(
        pack_kernel,
        [(3, rows, cols), (high, cols), (high, cols), (rows, cols), (rows, cols)],
        12 * cells,
        16 * cells,
        "level_sums",
        scratch=[pltpu.VMEM((high, cols), jnp.float32)] * 3,
    )(meta, spans, facing, *state, *flat_state)

    axes = ("lon", "lat")
    pairs_first = [(flat(i, j), flat(i, j ^ 1)) for i in range(lons) for j in range(lats)]
    pairs_inner = [
        (flat(i, a), flat(i, b))
        for i in range(lons)
        for j in range(1, lats - 1, 2)
        for a, b in ((j, j + 1), (j + 1, j))
    ] + [(flat(i, 0), flat(i ^ 1, 0)) for i in range(lons)]

    counterpart, first = lax.optimization_barrier((opposite_counterpart, first))
    hinge = lax.rem(counterpart[0] + 1 + cols * lon, width)
    block = lax.rem((hinge + cols // 2) // cols, lons)

    def exchange(shift, first, second):
        partner = [(shift - 1 - i) % lons for i in range(lons)]
        partner = [i + lons // 2 if i == p else p for i, p in enumerate(partner)]
        pairs_fold = [(flat(p, lats - 1), flat(i, lats - 1)) for i, p in enumerate(partner)]
        second = lax.ppermute(second, axes, pairs_inner + pairs_fold)
        return second, lax.ppermute(first, axes, pairs_first)

    mine = second
    second, first = lax.switch(block, [functools.partial(exchange, s) for s in range(lons)], first, second)

    deep = 4 * levels
    ext, to_far, to_near, state_far, state_near, facing_rows, north_rows, south_rows = call(
        functools.partial(turn_kernel, lons),
        [
            (FIELDS, tall, cols),
            *[(tall // 2, cols)] * 2,
            *[(rows, cols)] * 2,
            (high - deep, cols),
            *[(deep, cols)] * 2,
        ],
        FIELDS * tall * cols,
        4 * 4 * FIELDS * tall * cols,
        "row_halos",
    )(meta, facing, mine, sums, *flat_state, second, first, east_columns, west_columns)

    near = lambda cells: lax.ppermute(cells, "lon", [(i, i ^ 1) for i in range(lons)])
    far = lambda cells: lax.ppermute(cells, "lon", [(i, (i + 1 if i % 2 else i - 1) % lons) for i in range(lons)])
    from_far, from_near = far(to_far), near(to_near)
    state_far, state_near = far(state_far), near(state_near)

    count = lons * lats
    base, moments = call(
        krylov_kernel,
        [(3, rows, cols), (count, cols)],
        200 * tall * cols,
        4 * 12 * tall * cols,
        "krylov",
        scratch=[pltpu.VMEM((2, high - deep + 8, cols), jnp.float32)],
    )(meta, facing, ext, facing_rows, from_far, from_near)

    chunks = 5 if levels % 5 == 0 else 1
    new_heat, new_salt, new_zonal, new_merid = call(
        step_kernel,
        [(levels, rows, cols)] * 4,
        120 * cells,
        32 * cells,
        "levels_step",
        out_space=pltpu.HBM,
        scratch=[
            *[pltpu.VMEM((levels, rows, cols), jnp.float32)] * 4,
            pltpu.VMEM((deep, cols), jnp.float32),
            pltpu.SemaphoreType.DMA((4, chunks)),
        ],
    )(meta, spans, facing, *state, water_indicator, north_rows, south_rows, state_far, state_near)

    shares = lax.all_to_all(moments, axes, 0, 0, tiled=True)
    (surface,) = call(surface_kernel, [(rows, cols)], 6 * rows * cols, 16 * rows * cols, "surface")(shares, base)
    return (new_heat, new_salt, new_zonal, new_merid, surface)


def solution(mesh):
    for axis in mesh.shape.values():
        assert axis > 1 and axis & (axis - 1) == 0
    levels = P(None, "lat", "lon")
    flat = P("lat", "lon")
    return jax.shard_map(
        body,
        mesh=mesh,
        in_specs=(levels, levels, levels, levels, P(), flat, P("lon"), flat, flat),
        out_specs=(levels, levels, levels, levels, flat),
        check_vma=False,
    )
```

```python
import functools

import jax
import jax.numpy as jnp
from jax import lax
from jax.experimental import pallas as pl
from jax.experimental.pallas import tpu as pltpu
from jax.sharding import PartitionSpec as P

TIME_STEP = 0.1
MIXING = 0.1

DEEP = (5, 3, 4, 4, 3, 3)
SIDE = (5, 4, 3, 4, 3, 3)
FIELDS = len(SIDE)
ROW = tuple(sum(DEEP[:f]) for f in range(FIELDS + 1))
START = tuple(sum(SIDE[:f]) for f in range(FIELDS + 1))
RELAY = 56
FLIPPED = (1, 2)
VMEM_LIMIT = 32 * 1024 * 1024
LOAD_FLOPS = 10**10


def density(heat, salt):
    return heat * (-1.0 - 0.15 * heat - 0.2 * salt) + 0.8 * salt


def iota(shape, axis):
    return lax.broadcasted_iota(jnp.int32, shape, axis)


def packet_rows(levels):
    return -(-(4 * levels + ROW[-1]) // 8) * 8


def flags(meta):
    return tuple(meta[i : i + 1, :] == 1 for i in range(4))


def place_kernel(meta, placed):
    for i in range(5):
        placed[i : i + 1, :] = jnp.broadcast_to(meta[0:1, i : i + 1], (1, placed.shape[1]))
    placed[5:, :] = jnp.zeros((placed.shape[0] - 5, placed.shape[1]), jnp.int32)


def pack_kernel(
    meta, spans, facing, heat, salt, zonal, merid, water, weights, anomaly,
    sums, first, second, east_columns, west_columns,
    top, bottom, back,
):
    levels, rows, cols = heat.shape
    span = [spans[0:1, k : k + 1] for k in range(levels)]
    below = [None] * levels
    total = jnp.zeros((1, 1), jnp.float32)
    for k in reversed(range(levels)):
        below[k] = span[k] * (0.5 * span[k] + total)
        total = total + span[k]
    pair = iota((rows, cols), 1) // 2
    zero = jnp.zeros((rows, cols), jnp.float32)
    press, east, north, east_edge, west_edge = zero, zero, zero, zero, zero
    for k in range(levels):
        press = press + below[k] * density(heat[k], salt[k])
        east = east + span[k] * zonal[k]
        north = north + span[k] * merid[k]
        for q, source in ((k, heat), (levels + k, salt)):
            cells = source[k]
            here = pair == q
            east_edge = jnp.where(here, pltpu.roll(cells, (2 * q + 2) % cols, 1), east_edge)
            west_edge = jnp.where(here, pltpu.roll(cells, 2 * q, 1), west_edge)
            top[2 * q : 2 * q + 2, :] = source[k, rows - 2 :, :]
            bottom[2 * q : 2 * q + 2, :] = source[k, :2, :]
            for i in range(2):
                back[2 * q + i : 2 * q + i + 1, :] = source[k, rows - 1 - i : rows - i, :]
    east_columns[...] = east_edge
    west_columns[...] = west_edge
    sums[0] = press
    sums[1] = east
    sums[2] = north
    fields = (sums.at[0], sums.at[1], sums.at[2], water, weights, anomaly)
    for f, field in enumerate(fields):
        at = 4 * levels + ROW[f]
        deep = DEEP[f]
        top[at : at + deep, :] = field[rows - deep :, :].astype(jnp.float32)
        bottom[at : at + deep, :] = field[:deep, :].astype(jnp.float32)
        for j in range(deep):
            back[at + j : at + j + 1, :] = field[rows - 1 - j : rows - j, :].astype(jnp.float32)
    used = 4 * levels + ROW[-1]
    high = first.shape[0]
    if used < high:
        for packet in (top, bottom, back):
            packet[used:, :] = jnp.zeros((high - used, cols), jnp.float32)
    odd, last, _, _ = flags(meta)
    first[...] = jnp.where(odd, bottom[...], top[...])
    second[...] = jnp.where(last, back[...], jnp.where(odd, top[...], bottom[...]))


def turn_kernel(
    lons, meta, facing, mine, sums, water, weights, anomaly, second, first, east_columns, west_columns,
    ext, to_far, to_near, state_far, state_near, facing_rows, north_rows, south_rows,
):
    rows, cols = sums.shape[1], sums.shape[2]
    tall = ext.shape[1]
    deep = north_rows.shape[0]
    odd, top, lon_odd, bottom = flags(meta)
    from_first = first[...]
    hinge = facing[0:1, 0:1] + 1 + cols * meta[4:5, 0:1] + cols // 2
    block = lax.shift_right_logical(hinge & (lons * cols - 1), cols.bit_length() - 1)
    alone = ((block - 1 - 2 * meta[4:5, 0:1]) & (lons - 1)) == 0
    from_second = jnp.where(top & alone, mine[...], second[...])
    north = jnp.where(odd, from_second, from_first)
    south = jnp.where(bottom, 0.0, jnp.where(odd, from_first, from_second))
    fields = (sums.at[0], sums.at[1], sums.at[2], water, weights, anomaly)
    for f in range(FIELDS):
        at = deep + ROW[f]
        size = DEEP[f]
        ext[f, :rows, :] = fields[f][...].astype(jnp.float32)
        ext[f, rows : rows + size, :] = north[at : at + size]
        ext[f, rows + size : tall - size, :] = jnp.zeros((tall - rows - 2 * size, cols), jnp.float32)
        ext[f, tall - size :, :] = south[at : at + size]
    middle = tall // 2
    passed = from_second[deep:]
    spare = jnp.zeros((middle - passed.shape[0], cols), jnp.float32)
    lane = iota((middle, cols), 1)
    relay = lane >= RELAY
    east = jnp.where(relay, jnp.concatenate([pltpu.roll(passed, RELAY, 1), spare], axis=0), 0.0)
    west = jnp.where(relay, jnp.concatenate([passed, spare], axis=0), 0.0)
    for f in range(FIELDS):
        for part in range(2):
            at = START[f] + part * START[-1]
            here = (lane >= at) & (lane < at + SIDE[f])
            layer = ext[f, part * middle : (part + 1) * middle, :]
            east = jnp.where(here, pltpu.roll(layer, (at + SIDE[f]) % cols, 1), east)
            west = jnp.where(here, pltpu.roll(layer, at, 1), west)
    to_far[...] = jnp.where(lon_odd, east, west)
    to_near[...] = jnp.where(lon_odd, west, east)
    passed = from_second[:deep]
    spare = jnp.zeros((rows - deep, cols), jnp.float32)
    half = iota((rows, cols), 1) >= cols // 2
    east = jnp.where(half, jnp.concatenate([pltpu.roll(passed, cols // 2, 1), spare], axis=0), east_columns[...])
    west = jnp.where(half, jnp.concatenate([passed, spare], axis=0), west_columns[...])
    state_far[...] = jnp.where(lon_odd, east, west)
    state_near[...] = jnp.where(lon_odd, west, east)
    facing_rows[...] = from_second[deep:]
    north_rows[...] = north[:deep]
    south_rows[...] = south[:deep]


def fold_shift(facing):
    cols = facing.shape[1]
    offset = (facing[0:1, 0:1] + 1) & (cols - 1)
    return jnp.where(offset >= cols // 2, offset - cols, offset)


def fold(shift, west, own, east, beside):
    rows, cols = own.shape
    lane = iota((rows, cols), 1)
    source = cols - 1 - lane
    if beside:
        place = (source + shift) & (cols - 1)
        low = jnp.where(place - cols < shift, west, own)
        merged = jnp.where(place >= cols // 2, low, jnp.where(place >= shift, east, own))
    else:
        merged = jnp.where(source >= cols - shift, west, jnp.where(source < -shift, east, own))
    return jnp.take_along_axis(merged, cols - 1 - ((lane - shift) & (cols - 1)), axis=1)


def krylov_kernel(meta, facing, ext, facing_rows, from_far, from_near, base, moments, folded):
    tall, cols = ext.shape[1], ext.shape[2]
    rows = base.shape[1]
    size = facing_rows.shape[0]
    middle = tall // 2
    _, top, lon_odd, _ = flags(meta)
    west = jnp.where(lon_odd, from_near[...], from_far[...])
    east = jnp.where(lon_odd, from_far[...], from_near[...])
    shift = fold_shift(facing)
    row = iota((size, cols), 0)
    flips = (row >= ROW[FLIPPED[0]]) & (row < ROW[FLIPPED[-1] + 1])
    for side in range(2):
        cells = fold(shift, pltpu.roll(west[:size], cols - RELAY, 1), facing_rows[...], east[:size], side == 1)
        folded[side, :size, :] = jnp.where(flips, -cells, cells)
    folded[:, size:, :] = jnp.zeros((2, folded.shape[1] - size, cols), jnp.float32)
    lane = iota((tall, cols), 1)
    first = lane == 0
    last = lane == cols - 1
    eighth = iota((8, cols), 0)

    def load(f):
        both = [START[f], START[f] + START[-1]]
        a = jnp.concatenate([pltpu.roll(west, (2 * cols - SIDE[f] - at) % cols, 1) for at in both], axis=0)
        b = jnp.concatenate([pltpu.roll(east, (cols - at) % cols, 1) for at in both], axis=0)
        beside = jnp.where(lane >= cols - SIDE[f], a, jnp.where(lane < SIDE[f], b, 0.0))

        def put(cells, side):
            new = folded[side, ROW[f] : ROW[f] + 8, :]
            new = jnp.where(eighth < DEEP[f], jnp.where(top, new, cells[rows : rows + 8]), 0.0)
            return jnp.concatenate([cells[:rows], new, cells[rows + 8 :]], axis=0)

        return put(ext[f], 0), put(beside, 1)

    def plus_x(pair):
        a, b = (pltpu.roll(part, cols - 1, 1) for part in pair)
        return jnp.where(last, b, a), jnp.where(last, a, b)

    def minus_x(pair):
        a, b = (pltpu.roll(part, 1, 1) for part in pair)
        return jnp.where(first, b, a), jnp.where(first, a, b)

    def plus_y(pair):
        return tuple(pltpu.roll(part, tall - 1, 0) for part in pair)

    def minus_y(pair):
        return tuple(pltpu.roll(part, 1, 0) for part in pair)

    def each(function, *pairs):
        return tuple(function(*parts) for parts in zip(*pairs))

    def neighbours(pair):
        return each(
            lambda a, b, c, d: (a + b) + (c + d), plus_x(pair), minus_x(pair), plus_y(pair), minus_y(pair)
        )

    press, zonal, merid, wet, weights, anomaly = (load(f) for f in range(FIELDS))
    half = 0.5 * TIME_STEP
    flow = lambda w, speed, a, b: w * (speed - half * (a - b))
    east_flow = each(flow, wet, zonal, plus_x(press), minus_x(press))
    north_flow = each(flow, wet, merid, plus_y(press), minus_y(press))
    right = each(
        lambda w, g, n, a, b, c, d: w * (g * n - 0.5 * (a - b + c - d)),
        wet,
        weights,
        anomaly,
        plus_x(east_flow),
        minus_x(east_flow),
        plus_y(north_flow),
        minus_y(north_flow),
    )
    diagonal = each(lambda g: 4.0 + g, weights)
    inverse = each(lambda m: 1.0 / m, diagonal)
    scale = each(lambda w, i: w * i, wet, inverse)
    zero = each(lambda r, i: r * i, right, inverse)
    one = each(lambda a, n: a * n, scale, neighbours(zero))
    two = each(lambda a, n: a * n, scale, neighbours(one))
    last_sum = neighbours(two)[0][:rows]
    right, middle = right[0][:rows], diagonal[0][:rows]
    zero, one, two = zero[0][:rows], one[0][:rows], two[0][:rows]
    base[0] = zero
    base[1] = one
    base[2] = two
    weighted = middle * one
    products = (
        right * zero,
        right * one,
        weighted * one,
        weighted * two,
        middle * two * two,
        last_sum * two,
    )
    which = iota((8, cols), 0)
    sums = jnp.zeros((8, cols), jnp.float32)
    for k, product in enumerate(products):
        sums = jnp.where(which == k, jnp.sum(product, axis=0, keepdims=True), sums)
    sums = jnp.sum(sums, axis=1, keepdims=True)
    sums = jnp.sum(jnp.where(which == iota((8, cols), 1), sums, 0.0), axis=0, keepdims=True)
    moments[...] = jnp.broadcast_to(sums, moments.shape)


def lat_parts(cells, north_one, south_one, north_two, south_two, speed):
    grad = 8.0 * (north_one - south_one) - (north_two - south_two)
    return (-TIME_STEP / 12.0) * (speed * grad) + MIXING * ((north_one + south_one) - 4.0 * cells)


def lat_kernel(meta, spans, heat, salt, merid, water, north_rows, south_rows, part_heat, part_salt, new_merid):
    levels, rows, cols = heat.shape
    wet = water[...].astype(jnp.float32)
    row = iota((rows, cols), 0)

    def around(cells, q):
        n0 = north_rows[2 * q : 2 * q + 1, :]
        n1 = north_rows[2 * q + 1 : 2 * q + 2, :]
        s0 = south_rows[2 * q + 1 : 2 * q + 2, :]
        s1 = south_rows[2 * q : 2 * q + 1, :]
        north_one = jnp.where(row == rows - 1, n0, pltpu.roll(cells, rows - 1, 0))
        north_two = jnp.where(row == rows - 1, n1, jnp.where(row == rows - 2, n0, pltpu.roll(cells, rows - 2, 0)))
        south_one = jnp.where(row == 0, s0, pltpu.roll(cells, 1, 0))
        south_two = jnp.where(row == 0, s1, jnp.where(row == 1, s0, pltpu.roll(cells, 2, 0)))
        return north_one, south_one, north_two, south_two

    half = 0.5 * TIME_STEP
    above = jnp.zeros((rows, cols), jnp.float32)
    for k in range(levels):
        t, s, v = heat[k], salt[k], merid[k]
        around_t = around(t, k)
        around_s = around(s, levels + k)
        part_heat[k] = lat_parts(t, *around_t, v)
        part_salt[k] = lat_parts(s, *around_s, v)
        layer = density(around_t[0], around_s[0]) - density(around_t[1], around_s[1])
        layer = spans[0:1, k : k + 1] * layer
        new_merid[k] = wet * (v - half * (above + 0.5 * layer))
        above = above + layer


def lon_kernel(
    meta, spans, facing, heat, salt, zonal, merid, water, part_heat, part_salt, part_merid,
    north_came, from_far, from_near,
    heat_out, salt_out, zonal_out, merid_out,
    new_heat, new_salt, new_zonal, new_merid, north_rows, sems,
):
    levels, rows, cols = heat.shape
    deep = 4 * levels
    _, top, lon_odd, _ = flags(meta)
    wet = water[...].astype(jnp.float32)
    lane = iota((rows, cols), 1)
    east = jnp.where(lon_odd, from_far[...], from_near[...])
    west = jnp.where(lon_odd, from_near[...], from_far[...])
    came = north_came[...]
    across = fold(fold_shift(facing), pltpu.roll(west[:deep], cols // 2, 1), came, east[:deep], False)
    north_rows[...] = jnp.where(top, across, came)
    tail = rows - 8
    row = iota((16, cols), 0)

    def around(cells, q):
        a = pltpu.roll(east, (cols - 2 * q) % cols, 1)
        b = pltpu.roll(west, (2 * cols - 2 - 2 * q) % cols, 1)
        side = jnp.where(lane < 2, a, b)

        def shift_x(by):
            a = pltpu.roll(cells, by % cols, 1)
            b = pltpu.roll(side, by % cols, 1)
            own = lane >= by if by > 0 else lane < cols + by
            return jnp.where(own, a, b)

        return shift_x(-1), shift_x(1), shift_x(-2), shift_x(2)

    def around_tail(cells, q):
        n0 = north_rows[2 * q : 2 * q + 1, :]
        n1 = north_rows[2 * q + 1 : 2 * q + 2, :]
        last = cells[rows - 16 :]
        north_one = jnp.where(row == 15, n0, pltpu.roll(last, 15, 0))
        north_two = jnp.where(row == 15, n1, jnp.where(row == 14, n0, pltpu.roll(last, 14, 0)))
        south_one = pltpu.roll(last, 1, 0)
        south_two = pltpu.roll(last, 2, 0)
        return tuple(part[8:] for part in (north_one, south_one, north_two, south_two))

    def advance(cells, parts, part, again, speed):
        e1, w1, e2, w2 = parts
        grad = 8.0 * (e1 - w1) - (e2 - w2)
        change = (-TIME_STEP / 12.0) * (speed * grad) + MIXING * (e1 + w1)
        return cells + wet * (change + jnp.concatenate([part[:tail], again], axis=0))

    stores = ((new_heat, heat_out), (new_salt, salt_out), (new_zonal, zonal_out), (new_merid, merid_out))
    size = levels // sems.shape[1]
    copies = []
    half = 0.5 * TIME_STEP
    above_x = jnp.zeros((rows, cols), jnp.float32)
    above_y = jnp.zeros((8, cols), jnp.float32)
    for k in range(levels):
        t, s, u, v = heat[k], salt[k], zonal[k], merid[k][tail:]
        around_t = around(t, k)
        around_s = around(s, levels + k)
        tail_t = around_tail(t, k)
        tail_s = around_tail(s, levels + k)
        new_heat[k] = advance(t, around_t, part_heat[k], lat_parts(t[tail:], *tail_t, v), u)
        new_salt[k] = advance(s, around_s, part_salt[k], lat_parts(s[tail:], *tail_s, v), u)
        span = spans[0:1, k : k + 1]
        layer_x = span * (density(around_t[0], around_s[0]) - density(around_t[1], around_s[1]))
        layer_y = span * (density(tail_t[0], tail_s[0]) - density(tail_t[1], tail_s[1]))
        new_zonal[k] = wet * (u - half * (above_x + 0.5 * layer_x))
        new_merid[k, :tail, :] = part_merid[k, :tail, :]
        new_merid[k, tail:, :] = wet[tail:] * (v - half * (above_y + 0.5 * layer_y))
        above_x = above_x + layer_x
        above_y = above_y + layer_y
        if (k + 1) % size == 0:
            piece = pl.ds(k + 1 - size, size)
            for i, (near_ref, far_ref) in enumerate(stores):
                copies.append(pltpu.make_async_copy(near_ref.at[piece], far_ref.at[piece], sems.at[i, k // size]))
                copies[-1].start()
    for copy in copies:
        copy.wait()


def surface_kernel(shares, base, surface):
    sums = jnp.sum(shares[...], axis=0, keepdims=True)
    lane = iota(sums.shape, 1)
    nu = [jnp.sum(jnp.where(lane == k, sums, 0.0), axis=1, keepdims=True) for k in range(6)]

    def ratio(a, b):
        good = b > 0.0
        return jnp.where(good, a / jnp.where(good, b, 1.0), 0.0)

    def form(p, h):
        total = 0.0
        for i, a in enumerate(p):
            for j in range(i, len(p)):
                term = a * p[j] * h[i + j]
                total = total + (term if i == j else 2.0 * term)
        return total

    gap = [nu[k] - nu[k + 1] for k in range(5)]
    rz = nu[0]
    alpha = ratio(rz, gap[0])
    one = jnp.ones_like(rz)
    y = [one - alpha, alpha]
    x = [alpha, 0.0, 0.0]
    new = form(y, nu)
    beta = ratio(new, rz)
    rz = new
    p = [y[0] + beta, y[1]]
    alpha = ratio(rz, form(p, gap))
    x = [x[0] + alpha * p[0], alpha * p[1], 0.0]
    y = [y[0] - alpha * p[0], y[1] - alpha * (p[1] - p[0]), alpha * p[1]]
    new = form(y, nu)
    beta = ratio(new, rz)
    rz = new
    p = [y[0] + beta * p[0], y[1] + beta * p[1], y[2]]
    alpha = ratio(rz, form(p, gap))
    x = [x[0] + alpha * p[0], x[1] + alpha * p[1], alpha * p[2]]
    surface[...] = x[0] * base[0] + x[1] * base[1] + x[2] * base[2]


def call(kernel, outs, flops, moved, name, out_space=pltpu.VMEM, scratch=(), types=jnp.float32):
    def run(*args):
        return pl.pallas_call(
            kernel,
            out_shape=[jax.ShapeDtypeStruct(shape, types) for shape in outs],
            in_specs=[pl.BlockSpec(memory_space=pltpu.VMEM)] * len(args),
            out_specs=[pl.BlockSpec(memory_space=out_space)] * len(outs),
            scratch_shapes=list(scratch),
            cost_estimate=pl.CostEstimate(flops=flops, bytes_accessed=moved, transcendentals=0),
            compiler_params=pltpu.CompilerParams(vmem_limit_bytes=VMEM_LIMIT),
            name=name,
        )(*args)

    return run


def body(
    warmth_deviation,
    saltiness_deviation,
    easterly_speed,
    poleward_speed,
    stratum_spans,
    water_indicator,
    opposite_counterpart,
    elevation_weights,
    elevation_anomaly,
):
    lons, lats = lax.axis_size("lon"), lax.axis_size("lat")
    lon, lat = lax.axis_index("lon"), lax.axis_index("lat")
    levels, rows, cols = warmth_deviation.shape
    assert cols & (cols - 1) == 0 and 4 * levels <= cols // 2 and 2 * START[-1] <= RELAY and cols == 128 and rows >= 16
    high = packet_rows(levels)
    tall = rows + 16
    width = cols * lons
    flat = lambda i, j: (i % lons) * lats + j

    place = (lax.rem(lat, 2), lat == lats - 1, lax.rem(lon, 2), lat == 0, lon)
    meta = jnp.stack([value.astype(jnp.int32) for value in place]).reshape(1, 5)
    (meta,) = call(place_kernel, [(8, cols)], LOAD_FLOPS, 16, "place", types=jnp.int32)(meta)

    spans = stratum_spans.reshape(1, levels)
    facing = opposite_counterpart.reshape(1, cols)
    state = (warmth_deviation, saltiness_deviation, easterly_speed, poleward_speed)
    flat_state = (water_indicator, elevation_weights, elevation_anomaly)
    cells = levels * rows * cols
    sums, first, second, east_columns, west_columns = call(
        pack_kernel,
        [(3, rows, cols), (high, cols), (high, cols), (rows, cols), (rows, cols)],
        12 * cells,
        16 * cells,
        "level_sums",
        scratch=[pltpu.VMEM((high, cols), jnp.float32)] * 3,
    )(meta, spans, facing, *state, *flat_state)

    axes = ("lon", "lat")
    pairs_first = [(flat(i, j), flat(i, j ^ 1)) for i in range(lons) for j in range(lats)]
    pairs_inner = [
        (flat(i, a), flat(i, b))
        for i in range(lons)
        for j in range(1, lats - 1, 2)
        for a, b in ((j, j + 1), (j + 1, j))
    ] + [(flat(i, 0), flat(i ^ 1, 0)) for i in range(lons)]

    counterpart, first = lax.optimization_barrier((opposite_counterpart, first))
    hinge = lax.rem(counterpart[0] + 1 + cols * lon, width)
    block = lax.rem((hinge + cols // 2) // cols, lons)

    def exchange(shift, first, second):
        partner = [(shift - 1 - i) % lons for i in range(lons)]
        partner = [i + lons // 2 if i == p else p for i, p in enumerate(partner)]
        pairs_fold = [(flat(p, lats - 1), flat(i, lats - 1)) for i, p in enumerate(partner)]
        second = lax.ppermute(second, axes, pairs_inner + pairs_fold)
        return second, lax.ppermute(first, axes, pairs_first)

    mine = second
    second, first = lax.switch(block, [functools.partial(exchange, s) for s in range(lons)], first, second)

    deep = 4 * levels
    ext, to_far, to_near, state_far, state_near, facing_rows, north_rows, south_rows = call(
        functools.partial(turn_kernel, lons),
        [
            (FIELDS, tall, cols),
            *[(tall // 2, cols)] * 2,
            *[(rows, cols)] * 2,
            (high - deep, cols),
            *[(deep, cols)] * 2,
        ],
        FIELDS * tall * cols,
        4 * 4 * FIELDS * tall * cols,
        "row_halos",
    )(meta, facing, mine, sums, *flat_state, second, first, east_columns, west_columns)

    near = lambda cells: lax.ppermute(cells, "lon", [(i, i ^ 1) for i in range(lons)])
    far = lambda cells: lax.ppermute(cells, "lon", [(i, (i + 1 if i % 2 else i - 1) % lons) for i in range(lons)])
    from_far, from_near = far(to_far), near(to_near)

    count = lons * lats
    base, moments = call(
        krylov_kernel,
        [(3, rows, cols), (count, cols)],
        200 * tall * cols,
        4 * 12 * tall * cols,
        "krylov",
        scratch=[pltpu.VMEM((2, high - deep + 8, cols), jnp.float32)],
    )(meta, facing, ext, facing_rows, from_far, from_near)

    (moments, state_far, state_near, north_rows, south_rows) = lax.optimization_barrier(
        (moments, state_far, state_near, north_rows, south_rows)
    )
    state_far, state_near = far(state_far), near(state_near)
    part_heat, part_salt, part_merid = call(
        lat_kernel,
        [(levels, rows, cols)] * 3,
        60 * cells,
        24 * cells,
        "latitude_step",
    )(meta, spans, *state[:2], state[3], water_indicator, north_rows, south_rows)
    chunks = 5 if levels % 5 == 0 else 1
    new_heat, new_salt, new_zonal, new_merid = call(
        lon_kernel,
        [(levels, rows, cols)] * 4,
        80 * cells,
        32 * cells,
        "longitude_step",
        out_space=pltpu.HBM,
        scratch=[
            *[pltpu.VMEM((levels, rows, cols), jnp.float32)] * 4,
            pltpu.VMEM((deep, cols), jnp.float32),
            pltpu.SemaphoreType.DMA((4, chunks)),
        ],
    )(meta, spans, facing, *state, water_indicator, part_heat, part_salt, part_merid, north_rows, state_far, state_near)

    shares = lax.all_to_all(moments, axes, 0, 0, tiled=True)
    (surface,) = call(surface_kernel, [(rows, cols)], 6 * rows * cols, 16 * rows * cols, "surface")(shares, base)
    return (new_heat, new_salt, new_zonal, new_merid, surface)


def solution(mesh):
    for axis in mesh.shape.values():
        assert axis > 1 and axis & (axis - 1) == 0
    levels = P(None, "lat", "lon")
    flat = P("lat", "lon")
    return jax.shard_map(
        body,
        mesh=mesh,
        in_specs=(levels, levels, levels, levels, P(), flat, P("lon"), flat, flat),
        out_specs=(levels, levels, levels, levels, flat),
        check_vma=False,
    )
```

```python
import functools

import jax
import jax.numpy as jnp
from jax import lax
from jax.experimental import pallas as pl
from jax.experimental.pallas import tpu as pltpu
from jax.sharding import PartitionSpec as P

TIME_STEP = 0.1
MIXING = 0.1

DEEP = (5, 3, 4, 4, 3, 3)
SIDE = (5, 4, 3, 4, 3, 3)
FIELDS = len(SIDE)
ROW = tuple(sum(DEEP[:f]) for f in range(FIELDS + 1))
START = tuple(sum(SIDE[:f]) for f in range(FIELDS + 1))
RELAY = 56
FLIPPED = (1, 2)
VMEM_LIMIT = 32 * 1024 * 1024
LOAD_FLOPS = 10**10


def density(heat, salt):
    return heat * (-1.0 - 0.15 * heat - 0.2 * salt) + 0.8 * salt


def iota(shape, axis):
    return lax.broadcasted_iota(jnp.int32, shape, axis)


def packet_rows(levels):
    return -(-(4 * levels + ROW[-1]) // 8) * 8


def flags(meta):
    return tuple(meta[i : i + 1, :] == 1 for i in range(4))


def place_kernel(meta, placed):
    for i in range(5):
        placed[i : i + 1, :] = jnp.broadcast_to(meta[0:1, i : i + 1], (1, placed.shape[1]))
    placed[5:, :] = jnp.zeros((placed.shape[0] - 5, placed.shape[1]), jnp.int32)


def pack_kernel(
    meta, spans, facing, heat, salt, zonal, merid, water, weights, anomaly,
    sums, first, second, east_columns, west_columns,
    top, bottom, back,
):
    levels, rows, cols = heat.shape
    span = [spans[0:1, k : k + 1] for k in range(levels)]
    below = [None] * levels
    total = jnp.zeros((1, 1), jnp.float32)
    for k in reversed(range(levels)):
        below[k] = span[k] * (0.5 * span[k] + total)
        total = total + span[k]
    pair = iota((rows, cols), 1) // 2
    zero = jnp.zeros((rows, cols), jnp.float32)
    press, east, north, east_edge, west_edge = zero, zero, zero, zero, zero
    for k in range(levels):
        press = press + below[k] * density(heat[k], salt[k])
        east = east + span[k] * zonal[k]
        north = north + span[k] * merid[k]
        for q, source in ((k, heat), (levels + k, salt)):
            cells = source[k]
            here = pair == q
            east_edge = jnp.where(here, pltpu.roll(cells, (2 * q + 2) % cols, 1), east_edge)
            west_edge = jnp.where(here, pltpu.roll(cells, 2 * q, 1), west_edge)
            top[2 * q : 2 * q + 2, :] = source[k, rows - 2 :, :]
            bottom[2 * q : 2 * q + 2, :] = source[k, :2, :]
            for i in range(2):
                back[2 * q + i : 2 * q + i + 1, :] = source[k, rows - 1 - i : rows - i, :]
    east_columns[...] = east_edge
    west_columns[...] = west_edge
    sums[0] = press
    sums[1] = east
    sums[2] = north
    fields = (sums.at[0], sums.at[1], sums.at[2], water, weights, anomaly)
    for f, field in enumerate(fields):
        at = 4 * levels + ROW[f]
        deep = DEEP[f]
        top[at : at + deep, :] = field[rows - deep :, :].astype(jnp.float32)
        bottom[at : at + deep, :] = field[:deep, :].astype(jnp.float32)
        for j in range(deep):
            back[at + j : at + j + 1, :] = field[rows - 1 - j : rows - j, :].astype(jnp.float32)
    used = 4 * levels + ROW[-1]
    high = first.shape[0]
    if used < high:
        for packet in (top, bottom, back):
            packet[used:, :] = jnp.zeros((high - used, cols), jnp.float32)
    odd, last, _, _ = flags(meta)
    first[...] = jnp.where(odd, bottom[...], top[...])
    second[...] = jnp.where(last, back[...], jnp.where(odd, top[...], bottom[...]))


def turn_kernel(
    lons, meta, facing, mine, sums, water, weights, anomaly, second, first, east_columns, west_columns,
    ext, to_far, to_near, state_far, state_near, facing_rows, north_rows, south_rows,
):
    rows, cols = sums.shape[1], sums.shape[2]
    tall = ext.shape[1]
    deep = north_rows.shape[0]
    odd, top, lon_odd, bottom = flags(meta)
    from_first = first[...]
    hinge = facing[0:1, 0:1] + 1 + cols * meta[4:5, 0:1] + cols // 2
    block = lax.shift_right_logical(hinge & (lons * cols - 1), cols.bit_length() - 1)
    alone = ((block - 1 - 2 * meta[4:5, 0:1]) & (lons - 1)) == 0
    from_second = jnp.where(top & alone, mine[...], second[...])
    north = jnp.where(odd, from_second, from_first)
    south = jnp.where(bottom, 0.0, jnp.where(odd, from_first, from_second))
    fields = (sums.at[0], sums.at[1], sums.at[2], water, weights, anomaly)
    for f in range(FIELDS):
        at = deep + ROW[f]
        size = DEEP[f]
        ext[f, :rows, :] = fields[f][...].astype(jnp.float32)
        ext[f, rows : rows + size, :] = north[at : at + size]
        ext[f, rows + size : tall - size, :] = jnp.zeros((tall - rows - 2 * size, cols), jnp.float32)
        ext[f, tall - size :, :] = south[at : at + size]
    middle = tall // 2
    passed = from_second[deep:]
    spare = jnp.zeros((middle - passed.shape[0], cols), jnp.float32)
    lane = iota((middle, cols), 1)
    relay = lane >= RELAY
    east = jnp.where(relay, jnp.concatenate([pltpu.roll(passed, RELAY, 1), spare], axis=0), 0.0)
    west = jnp.where(relay, jnp.concatenate([passed, spare], axis=0), 0.0)
    for f in range(FIELDS):
        for part in range(2):
            at = START[f] + part * START[-1]
            here = (lane >= at) & (lane < at + SIDE[f])
            layer = ext[f, part * middle : (part + 1) * middle, :]
            east = jnp.where(here, pltpu.roll(layer, (at + SIDE[f]) % cols, 1), east)
            west = jnp.where(here, pltpu.roll(layer, at, 1), west)
    to_far[...] = jnp.where(lon_odd, east, west)
    to_near[...] = jnp.where(lon_odd, west, east)
    passed = from_second[:deep]
    spare = jnp.zeros((rows - deep, cols), jnp.float32)
    half = iota((rows, cols), 1) >= cols // 2
    east = jnp.where(half, jnp.concatenate([pltpu.roll(passed, cols // 2, 1), spare], axis=0), east_columns[...])
    west = jnp.where(half, jnp.concatenate([passed, spare], axis=0), west_columns[...])
    state_far[...] = jnp.where(lon_odd, east, west)
    state_near[...] = jnp.where(lon_odd, west, east)
    facing_rows[...] = from_second[deep:]
    north_rows[...] = north[:deep]
    south_rows[...] = south[:deep]


def fold_shift(facing):
    cols = facing.shape[1]
    offset = (facing[0:1, 0:1] + 1) & (cols - 1)
    return jnp.where(offset >= cols // 2, offset - cols, offset)


def fold(shift, west, own, east, beside):
    rows, cols = own.shape
    lane = iota((rows, cols), 1)
    source = cols - 1 - lane
    if beside:
        place = (source + shift) & (cols - 1)
        low = jnp.where(place - cols < shift, west, own)
        merged = jnp.where(place >= cols // 2, low, jnp.where(place >= shift, east, own))
    else:
        merged = jnp.where(source >= cols - shift, west, jnp.where(source < -shift, east, own))
    return jnp.take_along_axis(merged, cols - 1 - ((lane - shift) & (cols - 1)), axis=1)


def shift_kernel(ext, shift):
    rows, cols = ext.shape[1] - 16, ext.shape[2]
    press, zonal, merid, wet, weights, anomaly = (ext[f, :rows, :] for f in range(FIELDS))
    plus_x = lambda cells: pltpu.roll(cells, cols - 1, 1)
    minus_x = lambda cells: pltpu.roll(cells, 1, 1)
    plus_y = lambda cells: pltpu.roll(cells, rows - 1, 0)
    minus_y = lambda cells: pltpu.roll(cells, 1, 0)
    half = 0.5 * TIME_STEP
    east_flow = wet * (zonal - half * (plus_x(press) - minus_x(press)))
    north_flow = wet * (merid - half * (plus_y(press) - minus_y(press)))
    spread = plus_x(east_flow) - minus_x(east_flow) + plus_y(north_flow) - minus_y(north_flow)
    right = wet * (weights * anomaly - 0.5 * spread)
    inverse = 1.0 / (4.0 + weights)
    zero = right * inverse
    one = wet * inverse * (plus_x(zero) + minus_x(zero) + plus_y(zero) + minus_y(zero))
    lane = iota((rows, cols), 1)
    row = iota((rows, cols), 0)
    inside = (lane >= 8) & (lane < cols - 8) & (row >= 8) & (row < rows - 8)
    total = lambda cells: jnp.sum(jnp.sum(jnp.where(inside, cells, 0.0), axis=0, keepdims=True), axis=1, keepdims=True)
    below = total(right * zero)
    good = below > 0.0
    quotient = jnp.where(good, total(right * one) / jnp.where(good, below, 1.0), 0.0)
    shift[...] = jnp.broadcast_to(quotient, shift.shape)


def krylov_kernel(meta, facing, shift, ext, facing_rows, from_far, from_near, base, moments, folded):
    tall, cols = ext.shape[1], ext.shape[2]
    rows = base.shape[1]
    size = facing_rows.shape[0]
    middle = tall // 2
    _, top, lon_odd, _ = flags(meta)
    west = jnp.where(lon_odd, from_near[...], from_far[...])
    east = jnp.where(lon_odd, from_far[...], from_near[...])
    theta = shift[0:1, 0:1]
    across = fold_shift(facing)
    row = iota((size, cols), 0)
    flips = (row >= ROW[FLIPPED[0]]) & (row < ROW[FLIPPED[-1] + 1])
    for side in range(2):
        cells = fold(across, pltpu.roll(west[:size], cols - RELAY, 1), facing_rows[...], east[:size], side == 1)
        folded[side, :size, :] = jnp.where(flips, -cells, cells)
    folded[:, size:, :] = jnp.zeros((2, folded.shape[1] - size, cols), jnp.float32)
    lane = iota((tall, cols), 1)
    first = lane == 0
    last = lane == cols - 1
    eighth = iota((8, cols), 0)

    def load(f):
        both = [START[f], START[f] + START[-1]]
        a = jnp.concatenate([pltpu.roll(west, (2 * cols - SIDE[f] - at) % cols, 1) for at in both], axis=0)
        b = jnp.concatenate([pltpu.roll(east, (cols - at) % cols, 1) for at in both], axis=0)
        beside = jnp.where(lane >= cols - SIDE[f], a, jnp.where(lane < SIDE[f], b, 0.0))

        def put(cells, side):
            new = folded[side, ROW[f] : ROW[f] + 8, :]
            new = jnp.where(eighth < DEEP[f], jnp.where(top, new, cells[rows : rows + 8]), 0.0)
            return jnp.concatenate([cells[:rows], new, cells[rows + 8 :]], axis=0)

        return put(ext[f], 0), put(beside, 1)

    def plus_x(pair):
        a, b = (pltpu.roll(part, cols - 1, 1) for part in pair)
        return jnp.where(last, b, a), jnp.where(last, a, b)

    def minus_x(pair):
        a, b = (pltpu.roll(part, 1, 1) for part in pair)
        return jnp.where(first, b, a), jnp.where(first, a, b)

    def plus_y(pair):
        return tuple(pltpu.roll(part, tall - 1, 0) for part in pair)

    def minus_y(pair):
        return tuple(pltpu.roll(part, 1, 0) for part in pair)

    def each(function, *pairs):
        return tuple(function(*parts) for parts in zip(*pairs))

    def neighbours(pair):
        return each(
            lambda a, b, c, d: (a + b) + (c + d), plus_x(pair), minus_x(pair), plus_y(pair), minus_y(pair)
        )

    press, zonal, merid, wet, weights, anomaly = (load(f) for f in range(FIELDS))
    half = 0.5 * TIME_STEP
    flow = lambda w, speed, a, b: w * (speed - half * (a - b))
    east_flow = each(flow, wet, zonal, plus_x(press), minus_x(press))
    north_flow = each(flow, wet, merid, plus_y(press), minus_y(press))
    right = each(
        lambda w, g, n, a, b, c, d: w * (g * n - 0.5 * (a - b + c - d)),
        wet,
        weights,
        anomaly,
        plus_x(east_flow),
        minus_x(east_flow),
        plus_y(north_flow),
        minus_y(north_flow),
    )
    diagonal = each(lambda g: 4.0 + g, weights)
    inverse = each(lambda m: 1.0 / m, diagonal)
    scale = each(lambda w, i: w * i, wet, inverse)
    zero = each(lambda r, i: r * i, right, inverse)
    one = each(lambda a, n, z: a * n - theta * z, scale, neighbours(zero), zero)
    two = each(lambda a, n, z: a * n - theta * z, scale, neighbours(one), one)
    three = scale[0][:rows] * neighbours(two)[0][:rows] - theta * two[0][:rows]
    right, middle = right[0][:rows], diagonal[0][:rows]
    zero, one, two = zero[0][:rows], one[0][:rows], two[0][:rows]
    base[0] = zero
    base[1] = one
    base[2] = two
    weighted_one = middle * one
    weighted_two = middle * two
    products = (
        right * zero,
        right * one,
        right * two,
        right * three,
        weighted_one * one,
        weighted_one * two,
        weighted_one * three,
        weighted_two * two,
        weighted_two * three,
    )
    which = iota((16, cols), 0)
    place = iota((16, cols), 1)
    sums = jnp.where((which == len(products)) & (place == 0), theta, 0.0)
    for k, product in enumerate(products):
        sums = jnp.where(which == k, jnp.sum(product, axis=0, keepdims=True), sums)
    sums = jnp.sum(sums, axis=1, keepdims=True)
    sums = jnp.sum(jnp.where(which == place, sums, 0.0), axis=0, keepdims=True)
    moments[...] = jnp.broadcast_to(sums, moments.shape)


def step_kernel(
    meta, spans, facing, heat, salt, zonal, merid, water, north_came, south_rows, from_far, from_near,
    heat_out, salt_out, zonal_out, merid_out,
    new_heat, new_salt, new_zonal, new_merid, north_rows, sems,
):
    levels, rows, cols = heat.shape
    deep = 4 * levels
    _, top, lon_odd, _ = flags(meta)
    wet = water[...].astype(jnp.float32)
    lane = iota((rows, cols), 1)
    row = iota((rows, cols), 0)
    east = jnp.where(lon_odd, from_far[...], from_near[...])
    west = jnp.where(lon_odd, from_near[...], from_far[...])
    came = north_came[...]
    across = fold(fold_shift(facing), pltpu.roll(west[:deep], cols // 2, 1), came, east[:deep], False)
    north_rows[...] = jnp.where(top, across, came)

    def around(cells, q):
        a = pltpu.roll(east, (cols - 2 * q) % cols, 1)
        b = pltpu.roll(west, (2 * cols - 2 - 2 * q) % cols, 1)
        side = jnp.where(lane < 2, a, b)

        def shift_x(by):
            a = pltpu.roll(cells, by % cols, 1)
            b = pltpu.roll(side, by % cols, 1)
            own = lane >= by if by > 0 else lane < cols + by
            return jnp.where(own, a, b)

        n0 = north_rows[2 * q : 2 * q + 1, :]
        n1 = north_rows[2 * q + 1 : 2 * q + 2, :]
        s0 = south_rows[2 * q + 1 : 2 * q + 2, :]
        s1 = south_rows[2 * q : 2 * q + 1, :]
        north_one = jnp.where(row == rows - 1, n0, pltpu.roll(cells, rows - 1, 0))
        north_two = jnp.where(row == rows - 1, n1, jnp.where(row == rows - 2, n0, pltpu.roll(cells, rows - 2, 0)))
        south_one = jnp.where(row == 0, s0, pltpu.roll(cells, 1, 0))
        south_two = jnp.where(row == 0, s1, jnp.where(row == 1, s0, pltpu.roll(cells, 2, 0)))
        return (shift_x(-1), shift_x(1), shift_x(-2), shift_x(2), north_one, south_one, north_two, south_two)

    def advance(cells, parts, speed_x, speed_y):
        e1, w1, e2, w2, n1, s1, n2, s2 = parts
        grad_east = 8.0 * (e1 - w1) - (e2 - w2)
        grad_north = 8.0 * (n1 - s1) - (n2 - s2)
        laplace = (e1 + w1) + (n1 + s1) - 4.0 * cells
        tendency = (-TIME_STEP / 12.0) * (speed_x * grad_east + speed_y * grad_north) + MIXING * laplace
        return cells + wet * tendency

    stores = ((new_heat, heat_out), (new_salt, salt_out), (new_zonal, zonal_out), (new_merid, merid_out))
    size = levels // sems.shape[1]
    copies = []
    half = 0.5 * TIME_STEP
    above_x = jnp.zeros((rows, cols), jnp.float32)
    above_y = jnp.zeros((rows, cols), jnp.float32)
    for k in range(levels):
        t, s, u, v = heat[k], salt[k], zonal[k], merid[k]
        around_t = around(t, k)
        around_s = around(s, levels + k)
        new_heat[k] = advance(t, around_t, u, v)
        new_salt[k] = advance(s, around_s, u, v)
        span = spans[0:1, k : k + 1]
        layer_x = span * (density(around_t[0], around_s[0]) - density(around_t[1], around_s[1]))
        layer_y = span * (density(around_t[4], around_s[4]) - density(around_t[5], around_s[5]))
        new_zonal[k] = wet * (u - half * (above_x + 0.5 * layer_x))
        new_merid[k] = wet * (v - half * (above_y + 0.5 * layer_y))
        above_x = above_x + layer_x
        above_y = above_y + layer_y
        if (k + 1) % size == 0:
            piece = pl.ds(k + 1 - size, size)
            for i, (near_ref, far_ref) in enumerate(stores):
                copies.append(pltpu.make_async_copy(near_ref.at[piece], far_ref.at[piece], sems.at[i, k // size]))
                copies[-1].start()
    for copy in copies:
        copy.wait()


def surface_kernel(shares, shift, base, surface):
    lanes = shares.shape[1]
    g00, g01, g02, g03, g11, g12, g13, g22, g23, theta = (
        shares[...] if k == 0 else pltpu.roll(shares[...], lanes - k, 1) for k in range(10)
    )
    add = lambda terms: jnp.sum(terms, axis=0, keepdims=True)

    def ratio(a, b):
        good = b > 0.0
        return jnp.where(good, a / jnp.where(good, b, 1.0), 0.0)

    def form(p, h):
        total = 0.0
        for i, a in enumerate(p):
            for j in range(i, len(p)):
                term = a * p[j] * h[i + j]
                total = total + (term if i == j else 2.0 * term)
        return total

    whole = add(g00)
    common = ratio(add(theta * g00 + g01), whole)
    d = theta - common
    mu = [
        whole,
        add(g01 + d * g00),
        add(g11 + d * (2.0 * g01 + d * g00)),
        add(g12 + d * (2.0 * g11 + g02 + d * (3.0 * g01 + d * g00))),
        add(g22 + d * (4.0 * g12 + d * (2.0 * g02 + 4.0 * g11 + d * (4.0 * g01 + d * g00)))),
        add(
            g23
            + d * (3.0 * g22 + 2.0 * g13 + d * (9.0 * g12 + g03 + d * (4.0 * g02 + 6.0 * g11 + d * (5.0 * g01 + d * g00))))
        ),
    ]
    scale = 1.0 - common
    gap = [scale * mu[k] - mu[k + 1] for k in range(5)]
    alpha = ratio(mu[0], gap[0])
    y = [-alpha * ratio(mu[1], mu[0]), alpha]
    x = [alpha, 0.0, 0.0]
    rz = form(y, mu)
    p = [y[0] + ratio(rz, mu[0]), y[1]]
    alpha = ratio(rz, form(p, gap))
    x = [x[0] + alpha * p[0], alpha * p[1], 0.0]
    y = [y[0] - alpha * scale * p[0], y[1] - alpha * (scale * p[1] - p[0]), alpha * p[1]]
    new = form(y, mu)
    beta = ratio(new, rz)
    p = [y[0] + beta * p[0], y[1] + beta * p[1], y[2]]
    alpha = ratio(new, form(p, gap))
    x = [x[0] + alpha * p[0], x[1] + alpha * p[1], alpha * p[2]]
    d = shift[0:1, :] - common
    x = [x[0] + d * (x[1] + d * x[2]), x[1] + 2.0 * d * x[2], x[2]]
    x = [value[0:1, 0:1] for value in x]
    surface[...] = x[0] * base[0] + x[1] * base[1] + x[2] * base[2]


def call(kernel, outs, flops, moved, name, out_space=pltpu.VMEM, scratch=(), types=jnp.float32):
    def run(*args):
        return pl.pallas_call(
            kernel,
            out_shape=[jax.ShapeDtypeStruct(shape, types) for shape in outs],
            in_specs=[pl.BlockSpec(memory_space=pltpu.VMEM)] * len(args),
            out_specs=[pl.BlockSpec(memory_space=out_space)] * len(outs),
            scratch_shapes=list(scratch),
            cost_estimate=pl.CostEstimate(flops=flops, bytes_accessed=moved, transcendentals=0),
            compiler_params=pltpu.CompilerParams(vmem_limit_bytes=VMEM_LIMIT),
            name=name,
        )(*args)

    return run


def body(
    warmth_deviation,
    saltiness_deviation,
    easterly_speed,
    poleward_speed,
    stratum_spans,
    water_indicator,
    opposite_counterpart,
    elevation_weights,
    elevation_anomaly,
):
    lons, lats = lax.axis_size("lon"), lax.axis_size("lat")
    lon, lat = lax.axis_index("lon"), lax.axis_index("lat")
    levels, rows, cols = warmth_deviation.shape
    assert cols & (cols - 1) == 0 and rows >= 24 and 4 * levels <= cols // 2 and 2 * START[-1] <= RELAY and cols == 128
    high = packet_rows(levels)
    tall = rows + 16
    width = cols * lons
    flat = lambda i, j: (i % lons) * lats + j

    place = (lax.rem(lat, 2), lat == lats - 1, lax.rem(lon, 2), lat == 0, lon)
    meta = jnp.stack([value.astype(jnp.int32) for value in place]).reshape(1, 5)
    (meta,) = call(place_kernel, [(8, cols)], LOAD_FLOPS, 16, "place", types=jnp.int32)(meta)

    spans = stratum_spans.reshape(1, levels)
    facing = opposite_counterpart.reshape(1, cols)
    state = (warmth_deviation, saltiness_deviation, easterly_speed, poleward_speed)
    flat_state = (water_indicator, elevation_weights, elevation_anomaly)
    cells = levels * rows * cols
    sums, first, second, east_columns, west_columns = call(
        pack_kernel,
        [(3, rows, cols), (high, cols), (high, cols), (rows, cols), (rows, cols)],
        12 * cells,
        16 * cells,
        "level_sums",
        scratch=[pltpu.VMEM((high, cols), jnp.float32)] * 3,
    )(meta, spans, facing, *state, *flat_state)

    axes = ("lon", "lat")
    pairs_first = [(flat(i, j), flat(i, j ^ 1)) for i in range(lons) for j in range(lats)]
    pairs_inner = [
        (flat(i, a), flat(i, b))
        for i in range(lons)
        for j in range(1, lats - 1, 2)
        for a, b in ((j, j + 1), (j + 1, j))
    ] + [(flat(i, 0), flat(i ^ 1, 0)) for i in range(lons)]

    counterpart, first = lax.optimization_barrier((opposite_counterpart, first))
    hinge = lax.rem(counterpart[0] + 1 + cols * lon, width)
    block = lax.rem((hinge + cols // 2) // cols, lons)

    def exchange(shift, first, second):
        partner = [(shift - 1 - i) % lons for i in range(lons)]
        partner = [i + lons // 2 if i == p else p for i, p in enumerate(partner)]
        pairs_fold = [(flat(p, lats - 1), flat(i, lats - 1)) for i, p in enumerate(partner)]
        second = lax.ppermute(second, axes, pairs_inner + pairs_fold)
        return second, lax.ppermute(first, axes, pairs_first)

    mine = second
    second, first = lax.switch(block, [functools.partial(exchange, s) for s in range(lons)], first, second)

    deep = 4 * levels
    ext, to_far, to_near, state_far, state_near, facing_rows, north_rows, south_rows = call(
        functools.partial(turn_kernel, lons),
        [
            (FIELDS, tall, cols),
            *[(tall // 2, cols)] * 2,
            *[(rows, cols)] * 2,
            (high - deep, cols),
            *[(deep, cols)] * 2,
        ],
        FIELDS * tall * cols,
        4 * 4 * FIELDS * tall * cols,
        "row_halos",
    )(meta, facing, mine, sums, *flat_state, second, first, east_columns, west_columns)

    near = lambda cells: lax.ppermute(cells, "lon", [(i, i ^ 1) for i in range(lons)])
    far = lambda cells: lax.ppermute(cells, "lon", [(i, (i + 1 if i % 2 else i - 1) % lons) for i in range(lons)])
    from_far, from_near = far(to_far), near(to_near)
    state_far, state_near = far(state_far), near(state_near)

    (shift,) = call(shift_kernel, [(8, cols)], 60 * rows * cols, 24 * rows * cols, "basis_shift")(ext)

    count = lons * lats
    base, moments = call(
        krylov_kernel,
        [(3, rows, cols), (count, cols)],
        200 * tall * cols,
        4 * 12 * tall * cols,
        "krylov",
        scratch=[pltpu.VMEM((2, high - deep + 8, cols), jnp.float32)],
    )(meta, facing, shift, ext, facing_rows, from_far, from_near)

    chunks = 5 if levels % 5 == 0 else 1
    new_heat, new_salt, new_zonal, new_merid = call(
        step_kernel,
        [(levels, rows, cols)] * 4,
        120 * cells,
        32 * cells,
        "levels_step",
        out_space=pltpu.HBM,
        scratch=[
            *[pltpu.VMEM((levels, rows, cols), jnp.float32)] * 4,
            pltpu.VMEM((deep, cols), jnp.float32),
            pltpu.SemaphoreType.DMA((4, chunks)),
        ],
    )(meta, spans, facing, *state, water_indicator, north_rows, south_rows, state_far, state_near)

    shares = lax.all_to_all(moments, axes, 0, 0, tiled=True)
    (surface,) = call(surface_kernel, [(rows, cols)], 6 * rows * cols, 16 * rows * cols, "surface")(shares, shift, base)
    return (new_heat, new_salt, new_zonal, new_merid, surface)


def solution(mesh):
    for axis in mesh.shape.values():
        assert axis > 1 and axis & (axis - 1) == 0
    levels = P(None, "lat", "lon")
    flat = P("lat", "lon")
    return jax.shard_map(
        body,
        mesh=mesh,
        in_specs=(levels, levels, levels, levels, P(), flat, P("lon"), flat, flat),
        out_specs=(levels, levels, levels, levels, flat),
        check_vma=False,
    )
```

```python
import functools

import jax
import jax.numpy as jnp
from jax import lax
from jax.experimental import pallas as pl
from jax.experimental.pallas import tpu as pltpu
from jax.sharding import PartitionSpec as P

TIME_STEP = 0.1
MIXING = 0.1

DEEP = (5, 3, 4, 4, 3, 3)
SIDE = (5, 4, 3, 4, 3, 3)
FIELDS = len(SIDE)
ROW = tuple(sum(DEEP[:f]) for f in range(FIELDS + 1))
START = tuple(sum(SIDE[:f]) for f in range(FIELDS + 1))
RELAY = 56
FLIPPED = (1, 2)
VMEM_LIMIT = 32 * 1024 * 1024
LOAD_FLOPS = 10**10


def density(heat, salt):
    return heat * (-1.0 - 0.15 * heat - 0.2 * salt) + 0.8 * salt


def iota(shape, axis):
    return lax.broadcasted_iota(jnp.int32, shape, axis)


def packet_rows(levels):
    return -(-(4 * levels + ROW[-1]) // 8) * 8


def flags(meta):
    return tuple(meta[i : i + 1, :] == 1 for i in range(4))


def place_kernel(meta, placed):
    for i in range(5):
        placed[i : i + 1, :] = jnp.broadcast_to(meta[0:1, i : i + 1], (1, placed.shape[1]))
    placed[5:, :] = jnp.zeros((placed.shape[0] - 5, placed.shape[1]), jnp.int32)


def pack_kernel(
    meta, spans, facing, heat, salt, zonal, merid, water, weights, anomaly,
    sums, first, second, east_columns, west_columns,
    top, bottom, back,
):
    levels, rows, cols = heat.shape
    span = [spans[0:1, k : k + 1] for k in range(levels)]
    below = [None] * levels
    total = jnp.zeros((1, 1), jnp.float32)
    for k in reversed(range(levels)):
        below[k] = span[k] * (0.5 * span[k] + total)
        total = total + span[k]
    pair = iota((rows, cols), 1) // 2
    zero = jnp.zeros((rows, cols), jnp.float32)
    press, east, north, east_edge, west_edge = zero, zero, zero, zero, zero
    for k in range(levels):
        press = press + below[k] * density(heat[k], salt[k])
        east = east + span[k] * zonal[k]
        north = north + span[k] * merid[k]
        for q, source in ((k, heat), (levels + k, salt)):
            cells = source[k]
            here = pair == q
            east_edge = jnp.where(here, pltpu.roll(cells, (2 * q + 2) % cols, 1), east_edge)
            west_edge = jnp.where(here, pltpu.roll(cells, 2 * q, 1), west_edge)
            top[2 * q : 2 * q + 2, :] = source[k, rows - 2 :, :]
            bottom[2 * q : 2 * q + 2, :] = source[k, :2, :]
            for i in range(2):
                back[2 * q + i : 2 * q + i + 1, :] = source[k, rows - 1 - i : rows - i, :]
    east_columns[...] = east_edge
    west_columns[...] = west_edge
    sums[0] = press
    sums[1] = east
    sums[2] = north
    fields = (sums.at[0], sums.at[1], sums.at[2], water, weights, anomaly)
    for f, field in enumerate(fields):
        at = 4 * levels + ROW[f]
        deep = DEEP[f]
        top[at : at + deep, :] = field[rows - deep :, :].astype(jnp.float32)
        bottom[at : at + deep, :] = field[:deep, :].astype(jnp.float32)
        for j in range(deep):
            back[at + j : at + j + 1, :] = field[rows - 1 - j : rows - j, :].astype(jnp.float32)
    used = 4 * levels + ROW[-1]
    high = first.shape[0]
    if used < high:
        for packet in (top, bottom, back):
            packet[used:, :] = jnp.zeros((high - used, cols), jnp.float32)
    odd, last, _, _ = flags(meta)
    first[...] = jnp.where(odd, bottom[...], top[...])
    second[...] = jnp.where(last, back[...], jnp.where(odd, top[...], bottom[...]))


def turn_kernel(
    lons, meta, facing, mine, sums, water, weights, anomaly, second, first, east_columns, west_columns,
    ext, to_near, to_far, state_near, state_far, facing_rows, north_rows, south_rows,
):
    rows, cols = sums.shape[1], sums.shape[2]
    tall = ext.shape[1]
    deep = north_rows.shape[0]
    odd, top, lon_odd, bottom = flags(meta)
    from_first = first[...]
    hinge = facing[0:1, 0:1] + 1 + cols * meta[4:5, 0:1] + cols // 2
    block = lax.shift_right_logical(hinge & (lons * cols - 1), cols.bit_length() - 1)
    alone = ((block - 1 - 2 * meta[4:5, 0:1]) & (lons - 1)) == 0
    from_second = jnp.where(top & alone, mine[...], second[...])
    north = jnp.where(odd, from_second, from_first)
    south = jnp.where(bottom, 0.0, jnp.where(odd, from_first, from_second))
    fields = (sums.at[0], sums.at[1], sums.at[2], water, weights, anomaly)
    for f in range(FIELDS):
        at = deep + ROW[f]
        size = DEEP[f]
        ext[f, :rows, :] = fields[f][...].astype(jnp.float32)
        ext[f, rows : rows + size, :] = north[at : at + size]
        ext[f, rows + size : tall - size, :] = jnp.zeros((tall - rows - 2 * size, cols), jnp.float32)
        ext[f, tall - size :, :] = south[at : at + size]
    middle = tall // 2
    passed = from_second[deep:]
    spare = jnp.zeros((middle - passed.shape[0], cols), jnp.float32)
    lane = iota((middle, cols), 1)
    relay = lane >= RELAY
    east = jnp.where(relay, jnp.concatenate([pltpu.roll(passed, RELAY, 1), spare], axis=0), 0.0)
    west = jnp.where(relay, jnp.concatenate([passed, spare], axis=0), 0.0)
    for f in range(FIELDS):
        for part in range(2):
            at = START[f] + part * START[-1]
            here = (lane >= at) & (lane < at + SIDE[f])
            layer = ext[f, part * middle : (part + 1) * middle, :]
            east = jnp.where(here, pltpu.roll(layer, (at + SIDE[f]) % cols, 1), east)
            west = jnp.where(here, pltpu.roll(layer, at, 1), west)
    to_far[...] = jnp.where(lon_odd, east, west)
    to_near[...] = jnp.where(lon_odd, west, east)
    passed = from_second[:deep]
    spare = jnp.zeros((rows - deep, cols), jnp.float32)
    half = iota((rows, cols), 1) >= cols // 2
    east = jnp.where(half, jnp.concatenate([pltpu.roll(passed, cols // 2, 1), spare], axis=0), east_columns[...])
    west = jnp.where(half, jnp.concatenate([passed, spare], axis=0), west_columns[...])
    state_far[...] = jnp.where(lon_odd, east, west)
    state_near[...] = jnp.where(lon_odd, west, east)
    facing_rows[...] = from_second[deep:]
    north_rows[...] = north[:deep]
    south_rows[...] = south[:deep]


def fold_shift(facing):
    cols = facing.shape[1]
    offset = (facing[0:1, 0:1] + 1) & (cols - 1)
    return jnp.where(offset >= cols // 2, offset - cols, offset)


def fold(shift, west, own, east, beside):
    rows, cols = own.shape
    lane = iota((rows, cols), 1)
    source = cols - 1 - lane
    if beside:
        place = (source + shift) & (cols - 1)
        low = jnp.where(place - cols < shift, west, own)
        merged = jnp.where(place >= cols // 2, low, jnp.where(place >= shift, east, own))
    else:
        merged = jnp.where(source >= cols - shift, west, jnp.where(source < -shift, east, own))
    return jnp.take_along_axis(merged, cols - 1 - ((lane - shift) & (cols - 1)), axis=1)


def shift_kernel(ext, shift):
    rows, cols = ext.shape[1] - 16, ext.shape[2]
    press, zonal, merid, wet, weights, anomaly = (ext[f, :rows, :] for f in range(FIELDS))
    plus_x = lambda cells: pltpu.roll(cells, cols - 1, 1)
    minus_x = lambda cells: pltpu.roll(cells, 1, 1)
    plus_y = lambda cells: pltpu.roll(cells, rows - 1, 0)
    minus_y = lambda cells: pltpu.roll(cells, 1, 0)
    half = 0.5 * TIME_STEP
    east_flow = wet * (zonal - half * (plus_x(press) - minus_x(press)))
    north_flow = wet * (merid - half * (plus_y(press) - minus_y(press)))
    spread = plus_x(east_flow) - minus_x(east_flow) + plus_y(north_flow) - minus_y(north_flow)
    right = wet * (weights * anomaly - 0.5 * spread)
    inverse = 1.0 / (4.0 + weights)
    zero = right * inverse
    one = wet * inverse * (plus_x(zero) + minus_x(zero) + plus_y(zero) + minus_y(zero))
    lane = iota((rows, cols), 1)
    row = iota((rows, cols), 0)
    inside = (lane >= 8) & (lane < cols - 8) & (row >= 8) & (row < rows - 8)
    total = lambda cells: jnp.sum(jnp.sum(jnp.where(inside, cells, 0.0), axis=0, keepdims=True), axis=1, keepdims=True)
    below = total(right * zero)
    good = below > 0.0
    quotient = jnp.where(good, total(right * one) / jnp.where(good, below, 1.0), 0.0)
    shift[...] = jnp.broadcast_to(quotient, shift.shape)


def krylov_kernel(meta, facing, shift, ext, facing_rows, from_near, from_far, base, moments, folded):
    tall, cols = ext.shape[1], ext.shape[2]
    rows = base.shape[1]
    size = facing_rows.shape[0]
    middle = tall // 2
    _, top, lon_odd, _ = flags(meta)
    west = jnp.where(lon_odd, from_near[...], from_far[...])
    east = jnp.where(lon_odd, from_far[...], from_near[...])
    theta = shift[0:1, 0:1]
    across = fold_shift(facing)
    row = iota((size, cols), 0)
    flips = (row >= ROW[FLIPPED[0]]) & (row < ROW[FLIPPED[-1] + 1])
    for side in range(2):
        cells = fold(across, pltpu.roll(west[:size], cols - RELAY, 1), facing_rows[...], east[:size], side == 1)
        folded[side, :size, :] = jnp.where(flips, -cells, cells)
    folded[:, size:, :] = jnp.zeros((2, folded.shape[1] - size, cols), jnp.float32)
    lane = iota((tall, cols), 1)
    first = lane == 0
    last = lane == cols - 1
    eighth = iota((8, cols), 0)

    def load(f):
        both = [START[f], START[f] + START[-1]]
        a = jnp.concatenate([pltpu.roll(west, (2 * cols - SIDE[f] - at) % cols, 1) for at in both], axis=0)
        b = jnp.concatenate([pltpu.roll(east, (cols - at) % cols, 1) for at in both], axis=0)
        beside = jnp.where(lane >= cols - SIDE[f], a, jnp.where(lane < SIDE[f], b, 0.0))

        def put(cells, side):
            new = folded[side, ROW[f] : ROW[f] + 8, :]
            new = jnp.where(eighth < DEEP[f], jnp.where(top, new, cells[rows : rows + 8]), 0.0)
            return jnp.concatenate([cells[:rows], new, cells[rows + 8 :]], axis=0)

        return put(ext[f], 0), put(beside, 1)

    def plus_x(pair):
        a, b = (pltpu.roll(part, cols - 1, 1) for part in pair)
        return jnp.where(last, b, a), jnp.where(last, a, b)

    def minus_x(pair):
        a, b = (pltpu.roll(part, 1, 1) for part in pair)
        return jnp.where(first, b, a), jnp.where(first, a, b)

    def plus_y(pair):
        return tuple(pltpu.roll(part, tall - 1, 0) for part in pair)

    def minus_y(pair):
        return tuple(pltpu.roll(part, 1, 0) for part in pair)

    def each(function, *pairs):
        return tuple(function(*parts) for parts in zip(*pairs))

    def neighbours(pair):
        return each(
            lambda a, b, c, d: (a + b) + (c + d), plus_x(pair), minus_x(pair), plus_y(pair), minus_y(pair)
        )

    press, zonal, merid, wet, weights, anomaly = (load(f) for f in range(FIELDS))
    half = 0.5 * TIME_STEP
    flow = lambda w, speed, a, b: w * (speed - half * (a - b))
    east_flow = each(flow, wet, zonal, plus_x(press), minus_x(press))
    north_flow = each(flow, wet, merid, plus_y(press), minus_y(press))
    right = each(
        lambda w, g, n, a, b, c, d: w * (g * n - 0.5 * (a - b + c - d)),
        wet,
        weights,
        anomaly,
        plus_x(east_flow),
        minus_x(east_flow),
        plus_y(north_flow),
        minus_y(north_flow),
    )
    diagonal = each(lambda g: 4.0 + g, weights)
    inverse = each(lambda m: 1.0 / m, diagonal)
    scale = each(lambda w, i: w * i, wet, inverse)
    zero = each(lambda r, i: r * i, right, inverse)
    one = each(lambda a, n, z: a * n - theta * z, scale, neighbours(zero), zero)
    two = each(lambda a, n, z: a * n - theta * z, scale, neighbours(one), one)
    three = scale[0][:rows] * neighbours(two)[0][:rows] - theta * two[0][:rows]
    right, middle = right[0][:rows], diagonal[0][:rows]
    zero, one, two = zero[0][:rows], one[0][:rows], two[0][:rows]
    base[0] = zero
    base[1] = one
    base[2] = two
    weighted_one = middle * one
    weighted_two = middle * two
    products = (
        right * zero,
        right * one,
        right * two,
        right * three,
        weighted_one * one,
        weighted_one * two,
        weighted_one * three,
        weighted_two * two,
        weighted_two * three,
    )
    which = iota((16, cols), 0)
    place = iota((16, cols), 1)
    sums = jnp.where((which == len(products)) & (place == 0), theta, 0.0)
    for k, product in enumerate(products):
        sums = jnp.where(which == k, jnp.sum(product, axis=0, keepdims=True), sums)
    sums = jnp.sum(sums, axis=1, keepdims=True)
    sums = jnp.sum(jnp.where(which == place, sums, 0.0), axis=0, keepdims=True)
    moments[...] = jnp.broadcast_to(sums, moments.shape)


def step_kernel(
    meta, spans, facing, heat, salt, zonal, merid, water, north_came, south_rows, from_near, from_far,
    heat_out, salt_out, zonal_out, merid_out,
    new_heat, new_salt, new_zonal, new_merid, north_rows, sems,
):
    levels, rows, cols = heat.shape
    deep = 4 * levels
    _, top, lon_odd, _ = flags(meta)
    wet = water[...].astype(jnp.float32)
    lane = iota((rows, cols), 1)
    row = iota((rows, cols), 0)
    east = jnp.where(lon_odd, from_far[...], from_near[...])
    west = jnp.where(lon_odd, from_near[...], from_far[...])
    came = north_came[...]
    across = fold(fold_shift(facing), pltpu.roll(west[:deep], cols // 2, 1), came, east[:deep], False)
    north_rows[...] = jnp.where(top, across, came)

    def around(cells, q):
        a = pltpu.roll(east, (cols - 2 * q) % cols, 1)
        b = pltpu.roll(west, (2 * cols - 2 - 2 * q) % cols, 1)
        side = jnp.where(lane < 2, a, b)

        def shift_x(by):
            a = pltpu.roll(cells, by % cols, 1)
            b = pltpu.roll(side, by % cols, 1)
            own = lane >= by if by > 0 else lane < cols + by
            return jnp.where(own, a, b)

        n0 = north_rows[2 * q : 2 * q + 1, :]
        n1 = north_rows[2 * q + 1 : 2 * q + 2, :]
        s0 = south_rows[2 * q + 1 : 2 * q + 2, :]
        s1 = south_rows[2 * q : 2 * q + 1, :]
        north_one = jnp.where(row == rows - 1, n0, pltpu.roll(cells, rows - 1, 0))
        north_two = jnp.where(row == rows - 1, n1, jnp.where(row == rows - 2, n0, pltpu.roll(cells, rows - 2, 0)))
        south_one = jnp.where(row == 0, s0, pltpu.roll(cells, 1, 0))
        south_two = jnp.where(row == 0, s1, jnp.where(row == 1, s0, pltpu.roll(cells, 2, 0)))
        return (shift_x(-1), shift_x(1), shift_x(-2), shift_x(2), north_one, south_one, north_two, south_two)

    def advance(cells, parts, speed_x, speed_y):
        e1, w1, e2, w2, n1, s1, n2, s2 = parts
        grad_east = 8.0 * (e1 - w1) - (e2 - w2)
        grad_north = 8.0 * (n1 - s1) - (n2 - s2)
        laplace = (e1 + w1) + (n1 + s1) - 4.0 * cells
        tendency = (-TIME_STEP / 12.0) * (speed_x * grad_east + speed_y * grad_north) + MIXING * laplace
        return cells + wet * tendency

    stores = ((new_heat, heat_out), (new_salt, salt_out), (new_zonal, zonal_out), (new_merid, merid_out))
    size = levels // sems.shape[1]
    copies = []
    half = 0.5 * TIME_STEP
    above_x = jnp.zeros((rows, cols), jnp.float32)
    above_y = jnp.zeros((rows, cols), jnp.float32)
    for k in range(levels):
        t, s, u, v = heat[k], salt[k], zonal[k], merid[k]
        around_t = around(t, k)
        around_s = around(s, levels + k)
        new_heat[k] = advance(t, around_t, u, v)
        new_salt[k] = advance(s, around_s, u, v)
        span = spans[0:1, k : k + 1]
        layer_x = span * (density(around_t[0], around_s[0]) - density(around_t[1], around_s[1]))
        layer_y = span * (density(around_t[4], around_s[4]) - density(around_t[5], around_s[5]))
        new_zonal[k] = wet * (u - half * (above_x + 0.5 * layer_x))
        new_merid[k] = wet * (v - half * (above_y + 0.5 * layer_y))
        above_x = above_x + layer_x
        above_y = above_y + layer_y
        if (k + 1) % size == 0:
            piece = pl.ds(k + 1 - size, size)
            for i, (near_ref, far_ref) in enumerate(stores):
                copies.append(pltpu.make_async_copy(near_ref.at[piece], far_ref.at[piece], sems.at[i, k // size]))
                copies[-1].start()
    for copy in copies:
        copy.wait()


def surface_kernel(shares, shift, base, surface):
    lanes = shares.shape[1]
    g00, g01, g02, g03, g11, g12, g13, g22, g23, theta = (
        shares[...] if k == 0 else pltpu.roll(shares[...], lanes - k, 1) for k in range(10)
    )
    add = lambda terms: jnp.sum(terms, axis=0, keepdims=True)

    def ratio(a, b):
        good = b > 0.0
        return jnp.where(good, a / jnp.where(good, b, 1.0), 0.0)

    def form(p, h):
        total = 0.0
        for i, a in enumerate(p):
            for j in range(i, len(p)):
                term = a * p[j] * h[i + j]
                total = total + (term if i == j else 2.0 * term)
        return total

    whole = add(g00)
    common = ratio(add(theta * g00 + g01), whole)
    d = theta - common
    mu = [
        whole,
        add(g01 + d * g00),
        add(g11 + d * (2.0 * g01 + d * g00)),
        add(g12 + d * (2.0 * g11 + g02 + d * (3.0 * g01 + d * g00))),
        add(g22 + d * (4.0 * g12 + d * (2.0 * g02 + 4.0 * g11 + d * (4.0 * g01 + d * g00)))),
        add(
            g23
            + d * (3.0 * g22 + 2.0 * g13 + d * (9.0 * g12 + g03 + d * (4.0 * g02 + 6.0 * g11 + d * (5.0 * g01 + d * g00))))
        ),
    ]
    scale = 1.0 - common
    gap = [scale * mu[k] - mu[k + 1] for k in range(5)]
    alpha = ratio(mu[0], gap[0])
    y = [-alpha * ratio(mu[1], mu[0]), alpha]
    x = [alpha, 0.0, 0.0]
    rz = form(y, mu)
    p = [y[0] + ratio(rz, mu[0]), y[1]]
    alpha = ratio(rz, form(p, gap))
    x = [x[0] + alpha * p[0], alpha * p[1], 0.0]
    y = [y[0] - alpha * scale * p[0], y[1] - alpha * (scale * p[1] - p[0]), alpha * p[1]]
    new = form(y, mu)
    beta = ratio(new, rz)
    p = [y[0] + beta * p[0], y[1] + beta * p[1], y[2]]
    alpha = ratio(new, form(p, gap))
    x = [x[0] + alpha * p[0], x[1] + alpha * p[1], alpha * p[2]]
    d = shift[0:1, :] - common
    x = [x[0] + d * (x[1] + d * x[2]), x[1] + 2.0 * d * x[2], x[2]]
    x = [value[0:1, 0:1] for value in x]
    surface[...] = x[0] * base[0] + x[1] * base[1] + x[2] * base[2]


def call(kernel, outs, flops, moved, name, out_space=pltpu.VMEM, scratch=(), types=jnp.float32):
    def run(*args):
        return pl.pallas_call(
            kernel,
            out_shape=[jax.ShapeDtypeStruct(shape, types) for shape in outs],
            in_specs=[pl.BlockSpec(memory_space=pltpu.VMEM)] * len(args),
            out_specs=[pl.BlockSpec(memory_space=out_space)] * len(outs),
            scratch_shapes=list(scratch),
            cost_estimate=pl.CostEstimate(flops=flops, bytes_accessed=moved, transcendentals=0),
            compiler_params=pltpu.CompilerParams(vmem_limit_bytes=VMEM_LIMIT),
            name=name,
        )(*args)

    return run


def body(
    warmth_deviation,
    saltiness_deviation,
    easterly_speed,
    poleward_speed,
    stratum_spans,
    water_indicator,
    opposite_counterpart,
    elevation_weights,
    elevation_anomaly,
):
    lons, lats = lax.axis_size("lon"), lax.axis_size("lat")
    lon, lat = lax.axis_index("lon"), lax.axis_index("lat")
    levels, rows, cols = warmth_deviation.shape
    assert cols & (cols - 1) == 0 and rows >= 24 and 4 * levels <= cols // 2 and 2 * START[-1] <= RELAY and cols == 128
    high = packet_rows(levels)
    tall = rows + 16
    width = cols * lons
    flat = lambda i, j: (i % lons) * lats + j

    place = (lax.rem(lat, 2), lat == lats - 1, lax.rem(lon, 2), lat == 0, lon)
    meta = jnp.stack([value.astype(jnp.int32) for value in place]).reshape(1, 5)
    (meta,) = call(place_kernel, [(8, cols)], LOAD_FLOPS, 16, "place", types=jnp.int32)(meta)

    spans = stratum_spans.reshape(1, levels)
    facing = opposite_counterpart.reshape(1, cols)
    state = (warmth_deviation, saltiness_deviation, easterly_speed, poleward_speed)
    flat_state = (water_indicator, elevation_weights, elevation_anomaly)
    cells = levels * rows * cols
    sums, first, second, east_columns, west_columns = call(
        pack_kernel,
        [(3, rows, cols), (high, cols), (high, cols), (rows, cols), (rows, cols)],
        12 * cells,
        16 * cells,
        "level_sums",
        scratch=[pltpu.VMEM((high, cols), jnp.float32)] * 3,
    )(meta, spans, facing, *state, *flat_state)

    axes = ("lon", "lat")
    pairs_first = [(flat(i, j), flat(i, j ^ 1)) for i in range(lons) for j in range(lats)]
    pairs_inner = [
        (flat(i, a), flat(i, b))
        for i in range(lons)
        for j in range(1, lats - 1, 2)
        for a, b in ((j, j + 1), (j + 1, j))
    ] + [(flat(i, 0), flat(i ^ 1, 0)) for i in range(lons)]

    counterpart, first = lax.optimization_barrier((opposite_counterpart, first))
    hinge = lax.rem(counterpart[0] + 1 + cols * lon, width)
    block = lax.rem((hinge + cols // 2) // cols, lons)

    def exchange(shift, first, second):
        partner = [(shift - 1 - i) % lons for i in range(lons)]
        partner = [i + lons // 2 if i == p else p for i, p in enumerate(partner)]
        pairs_fold = [(flat(p, lats - 1), flat(i, lats - 1)) for i, p in enumerate(partner)]
        second = lax.ppermute(second, axes, pairs_inner + pairs_fold)
        return second, lax.ppermute(first, axes, pairs_first)

    mine = second
    second, first = lax.switch(block, [functools.partial(exchange, s) for s in range(lons)], first, second)

    deep = 4 * levels
    ext, to_near, to_far, state_near, state_far, facing_rows, north_rows, south_rows = call(
        functools.partial(turn_kernel, lons),
        [
            (FIELDS, tall, cols),
            *[(tall // 2, cols)] * 2,
            *[(rows, cols)] * 2,
            (high - deep, cols),
            *[(deep, cols)] * 2,
        ],
        FIELDS * tall * cols,
        4 * 4 * FIELDS * tall * cols,
        "row_halos",
    )(meta, facing, mine, sums, *flat_state, second, first, east_columns, west_columns)

    near = lambda cells: lax.ppermute(cells, "lon", [(i, i ^ 1) for i in range(lons)])
    far = lambda cells: lax.ppermute(cells, "lon", [(i, (i + 1 if i % 2 else i - 1) % lons) for i in range(lons)])
    from_near, from_far = near(to_near), far(to_far)
    state_near, state_far = near(state_near), far(state_far)

    (shift,) = call(shift_kernel, [(8, cols)], 60 * rows * cols, 24 * rows * cols, "basis_shift")(ext)

    count = lons * lats
    base, moments = call(
        krylov_kernel,
        [(3, rows, cols), (count, cols)],
        200 * tall * cols,
        4 * 12 * tall * cols,
        "krylov",
        scratch=[pltpu.VMEM((2, high - deep + 8, cols), jnp.float32)],
    )(meta, facing, shift, ext, facing_rows, from_near, from_far)

    chunks = 5 if levels % 5 == 0 else 1
    new_heat, new_salt, new_zonal, new_merid = call(
        step_kernel,
        [(levels, rows, cols)] * 4,
        120 * cells,
        32 * cells,
        "levels_step",
        out_space=pltpu.HBM,
        scratch=[
            *[pltpu.VMEM((levels, rows, cols), jnp.float32)] * 4,
            pltpu.VMEM((deep, cols), jnp.float32),
            pltpu.SemaphoreType.DMA((4, chunks)),
        ],
    )(meta, spans, facing, *state, water_indicator, north_rows, south_rows, state_near, state_far)

    shares = lax.all_to_all(moments, axes, 0, 0, tiled=True)
    (surface,) = call(surface_kernel, [(rows, cols)], 6 * rows * cols, 16 * rows * cols, "surface")(shares, shift, base)
    return (new_heat, new_salt, new_zonal, new_merid, surface)


def solution(mesh):
    for axis in mesh.shape.values():
        assert axis > 1 and axis & (axis - 1) == 0
    levels = P(None, "lat", "lon")
    flat = P("lat", "lon")
    return jax.shard_map(
        body,
        mesh=mesh,
        in_specs=(levels, levels, levels, levels, P(), flat, P("lon"), flat, flat),
        out_specs=(levels, levels, levels, levels, flat),
        check_vma=False,
    )
```

```python
import functools

import jax
import jax.numpy as jnp
from jax import lax
from jax.experimental import pallas as pl
from jax.experimental.pallas import tpu as pltpu
from jax.sharding import PartitionSpec as P

TIME_STEP = 0.1
MIXING = 0.1

DEEP = (5, 3, 4, 4, 3, 3)
SIDE = (5, 4, 3, 4, 3, 3)
FIELDS = len(SIDE)
ROW = tuple(sum(DEEP[:f]) for f in range(FIELDS + 1))
START = tuple(sum(SIDE[:f]) for f in range(FIELDS + 1))
RELAY = 56
FLIPPED = (1, 2)
VMEM_LIMIT = 32 * 1024 * 1024
LOAD_FLOPS = 10**10


def density(heat, salt):
    return heat * (-1.0 - 0.15 * heat - 0.2 * salt) + 0.8 * salt


def iota(shape, axis):
    return lax.broadcasted_iota(jnp.int32, shape, axis)


def packet_rows(levels):
    return -(-(4 * levels + ROW[-1]) // 8) * 8


def flags(meta):
    return tuple(meta[i : i + 1, :] == 1 for i in range(4))


def segments(rows):
    size = START[-1]
    return (0, rows // 2, 0), (rows // 2, rows, size), (rows, rows + 8, RELAY), (rows + 8, rows + 16, RELAY + size)


def place_kernel(meta, placed):
    for i in range(5):
        placed[i : i + 1, :] = jnp.broadcast_to(meta[0:1, i : i + 1], (1, placed.shape[1]))
    placed[5:, :] = jnp.zeros((placed.shape[0] - 5, placed.shape[1]), jnp.int32)


def pack_kernel(
    meta, spans, facing, heat, salt, zonal, merid, water, weights, anomaly,
    sums, first, second, east_columns, west_columns,
    top, bottom, back,
):
    levels, rows, cols = heat.shape
    span = [spans[0:1, k : k + 1] for k in range(levels)]
    below = [None] * levels
    total = jnp.zeros((1, 1), jnp.float32)
    for k in reversed(range(levels)):
        below[k] = span[k] * (0.5 * span[k] + total)
        total = total + span[k]
    pair = iota((rows, cols), 1) // 2
    zero = jnp.zeros((rows, cols), jnp.float32)
    press, east, north, east_edge, west_edge = zero, zero, zero, zero, zero
    for k in range(levels):
        press = press + below[k] * density(heat[k], salt[k])
        east = east + span[k] * zonal[k]
        north = north + span[k] * merid[k]
        for q, source in ((k, heat), (levels + k, salt)):
            cells = source[k]
            here = pair == q
            east_edge = jnp.where(here, pltpu.roll(cells, (2 * q + 2) % cols, 1), east_edge)
            west_edge = jnp.where(here, pltpu.roll(cells, 2 * q, 1), west_edge)
            top[2 * q : 2 * q + 2, :] = source[k, rows - 2 :, :]
            bottom[2 * q : 2 * q + 2, :] = source[k, :2, :]
            for i in range(2):
                back[2 * q + i : 2 * q + i + 1, :] = source[k, rows - 1 - i : rows - i, :]
    east_columns[...] = east_edge
    west_columns[...] = west_edge
    sums[0] = press
    sums[1] = east
    sums[2] = north
    fields = (sums.at[0], sums.at[1], sums.at[2], water, weights, anomaly)
    for f, field in enumerate(fields):
        at = 4 * levels + ROW[f]
        deep = DEEP[f]
        top[at : at + deep, :] = field[rows - deep :, :].astype(jnp.float32)
        bottom[at : at + deep, :] = field[:deep, :].astype(jnp.float32)
        for j in range(deep):
            back[at + j : at + j + 1, :] = field[rows - 1 - j : rows - j, :].astype(jnp.float32)
    used = 4 * levels + ROW[-1]
    high = first.shape[0]
    if used < high:
        for packet in (top, bottom, back):
            packet[used:, :] = jnp.zeros((high - used, cols), jnp.float32)
    odd, last, _, _ = flags(meta)
    first[...] = jnp.where(odd, bottom[...], top[...])
    second[...] = jnp.where(last, back[...], jnp.where(odd, top[...], bottom[...]))


def turn_kernel(
    lons, meta, facing, mine, sums, water, weights, anomaly, second, first, east_columns, west_columns,
    ext, to_far, to_near, state_far, state_near, facing_rows, north_rows, south_rows,
):
    rows, cols = sums.shape[1], sums.shape[2]
    tall = ext.shape[1]
    deep = north_rows.shape[0]
    odd, top, lon_odd, bottom = flags(meta)
    from_first = first[...]
    hinge = facing[0:1, 0:1] + 1 + cols * meta[4:5, 0:1] + cols // 2
    block = lax.shift_right_logical(hinge & (lons * cols - 1), cols.bit_length() - 1)
    alone = ((block - 1 - 2 * meta[4:5, 0:1]) & (lons - 1)) == 0
    from_second = jnp.where(top & alone, mine[...], second[...])
    north = jnp.where(odd, from_second, from_first)
    south = jnp.where(bottom, 0.0, jnp.where(odd, from_first, from_second))
    fields = (sums.at[0], sums.at[1], sums.at[2], water, weights, anomaly)
    for f in range(FIELDS):
        at = deep + ROW[f]
        size = DEEP[f]
        ext[f, :rows, :] = fields[f][...].astype(jnp.float32)
        ext[f, rows : rows + size, :] = north[at : at + size]
        ext[f, rows + size : tall - size, :] = jnp.zeros((tall - rows - 2 * size, cols), jnp.float32)
        ext[f, tall - size :, :] = south[at : at + size]
    passed = from_second[deep:]
    size = passed.shape[0]
    half = rows // 2
    lane = iota((half, cols), 1)
    lower = iota((half, cols), 0) >= size
    empty = jnp.zeros((size, cols), jnp.float32)
    spare = jnp.zeros((half - size, cols), jnp.float32)
    relay = lane >= RELAY
    east = jnp.where(relay, jnp.concatenate([pltpu.roll(passed, RELAY, 1), spare], axis=0), 0.0)
    west = jnp.where(relay, jnp.concatenate([passed, spare], axis=0), 0.0)
    for f in range(FIELDS):
        for start, stop, first_lane in segments(rows):
            at = START[f] + first_lane
            here = (lane >= at) & (lane < at + SIDE[f])
            layer = ext[f, start:stop, :]
            to_east = pltpu.roll(layer, (at + SIDE[f]) % cols, 1)
            to_west = pltpu.roll(layer, at, 1)
            if stop - start < half:
                here = here & lower
                to_east = jnp.concatenate([empty, to_east], axis=0)
                to_west = jnp.concatenate([empty, to_west], axis=0)
            east = jnp.where(here, to_east, east)
            west = jnp.where(here, to_west, west)
    to_far[...] = jnp.where(lon_odd, east, west)
    to_near[...] = jnp.where(lon_odd, west, east)
    passed = from_second[:deep]
    spare = jnp.zeros((rows - deep, cols), jnp.float32)
    right_half = iota((rows, cols), 1) >= cols // 2
    east = jnp.where(right_half, jnp.concatenate([pltpu.roll(passed, cols // 2, 1), spare], axis=0), east_columns[...])
    west = jnp.where(right_half, jnp.concatenate([passed, spare], axis=0), west_columns[...])
    state_far[...] = jnp.where(lon_odd, east, west)
    state_near[...] = jnp.where(lon_odd, west, east)
    facing_rows[...] = from_second[deep:]
    north_rows[...] = north[:deep]
    south_rows[...] = south[:deep]


def fold_shift(facing):
    cols = facing.shape[1]
    offset = (facing[0:1, 0:1] + 1) & (cols - 1)
    return jnp.where(offset >= cols // 2, offset - cols, offset)


def fold(shift, west, own, east, beside):
    rows, cols = own.shape
    lane = iota((rows, cols), 1)
    source = cols - 1 - lane
    if beside:
        place = (source + shift) & (cols - 1)
        low = jnp.where(place - cols < shift, west, own)
        merged = jnp.where(place >= cols // 2, low, jnp.where(place >= shift, east, own))
    else:
        merged = jnp.where(source >= cols - shift, west, jnp.where(source < -shift, east, own))
    return jnp.take_along_axis(merged, cols - 1 - ((lane - shift) & (cols - 1)), axis=1)


def shift_kernel(ext, shift):
    rows, cols = ext.shape[1] - 16, ext.shape[2]
    press, zonal, merid, wet, weights, anomaly = (ext[f, :rows, :] for f in range(FIELDS))
    plus_x = lambda cells: pltpu.roll(cells, cols - 1, 1)
    minus_x = lambda cells: pltpu.roll(cells, 1, 1)
    plus_y = lambda cells: pltpu.roll(cells, rows - 1, 0)
    minus_y = lambda cells: pltpu.roll(cells, 1, 0)
    half = 0.5 * TIME_STEP
    east_flow = wet * (zonal - half * (plus_x(press) - minus_x(press)))
    north_flow = wet * (merid - half * (plus_y(press) - minus_y(press)))
    spread = plus_x(east_flow) - minus_x(east_flow) + plus_y(north_flow) - minus_y(north_flow)
    right = wet * (weights * anomaly - 0.5 * spread)
    inverse = 1.0 / (4.0 + weights)
    zero = right * inverse
    one = wet * inverse * (plus_x(zero) + minus_x(zero) + plus_y(zero) + minus_y(zero))
    lane = iota((rows, cols), 1)
    row = iota((rows, cols), 0)
    inside = (lane >= 8) & (lane < cols - 8) & (row >= 8) & (row < rows - 8)
    total = lambda cells: jnp.sum(jnp.sum(jnp.where(inside, cells, 0.0), axis=0, keepdims=True), axis=1, keepdims=True)
    below = total(right * zero)
    good = below > 0.0
    quotient = jnp.where(good, total(right * one) / jnp.where(good, below, 1.0), 0.0)
    shift[...] = jnp.broadcast_to(jnp.clip(quotient, -1.0, 1.0), shift.shape)


def krylov_kernel(meta, facing, shift, ext, facing_rows, from_far, from_near, base, moments, folded):
    tall, cols = ext.shape[1], ext.shape[2]
    rows = base.shape[1]
    size = facing_rows.shape[0]
    _, top, lon_odd, _ = flags(meta)
    west = jnp.where(lon_odd, from_near[...], from_far[...])
    east = jnp.where(lon_odd, from_far[...], from_near[...])
    theta = shift[0:1, 0:1]
    across = fold_shift(facing)
    row = iota((size, cols), 0)
    flips = (row >= ROW[FLIPPED[0]]) & (row < ROW[FLIPPED[-1] + 1])
    for side in range(2):
        cells = fold(across, pltpu.roll(west[:size], cols - RELAY, 1), facing_rows[...], east[:size], side == 1)
        folded[side, :size, :] = jnp.where(flips, -cells, cells)
    folded[:, size:, :] = jnp.zeros((2, folded.shape[1] - size, cols), jnp.float32)
    lane = iota((tall, cols), 1)
    first = lane == 0
    last = lane == cols - 1
    eighth = iota((8, cols), 0)

    def load(f):
        parts = []
        for packet, shift_of in ((west, 2 * cols - SIDE[f]), (east, cols)):
            pieces = []
            for start, stop, first_lane in segments(rows):
                layer = packet[packet.shape[0] - (stop - start) :]
                pieces.append(pltpu.roll(layer, (shift_of - START[f] - first_lane) % cols, 1))
            parts.append(jnp.concatenate(pieces, axis=0))
        a, b = parts
        beside = jnp.where(lane >= cols - SIDE[f], a, jnp.where(lane < SIDE[f], b, 0.0))

        def put(cells, side):
            new = folded[side, ROW[f] : ROW[f] + 8, :]
            new = jnp.where(eighth < DEEP[f], jnp.where(top, new, cells[rows : rows + 8]), 0.0)
            return jnp.concatenate([cells[:rows], new, cells[rows + 8 :]], axis=0)

        return put(ext[f], 0), put(beside, 1)

    def plus_x(pair):
        a, b = (pltpu.roll(part, cols - 1, 1) for part in pair)
        return jnp.where(last, b, a), jnp.where(last, a, b)

    def minus_x(pair):
        a, b = (pltpu.roll(part, 1, 1) for part in pair)
        return jnp.where(first, b, a), jnp.where(first, a, b)

    def plus_y(pair):
        return tuple(pltpu.roll(part, tall - 1, 0) for part in pair)

    def minus_y(pair):
        return tuple(pltpu.roll(part, 1, 0) for part in pair)

    def each(function, *pairs):
        return tuple(function(*parts) for parts in zip(*pairs))

    def neighbours(pair):
        return each(
            lambda a, b, c, d: (a + b) + (c + d), plus_x(pair), minus_x(pair), plus_y(pair), minus_y(pair)
        )

    press, zonal, merid, wet, weights, anomaly = (load(f) for f in range(FIELDS))
    half = 0.5 * TIME_STEP
    flow = lambda w, speed, a, b: w * (speed - half * (a - b))
    east_flow = each(flow, wet, zonal, plus_x(press), minus_x(press))
    north_flow = each(flow, wet, merid, plus_y(press), minus_y(press))
    right = each(
        lambda w, g, n, a, b, c, d: w * (g * n - 0.5 * (a - b + c - d)),
        wet,
        weights,
        anomaly,
        plus_x(east_flow),
        minus_x(east_flow),
        plus_y(north_flow),
        minus_y(north_flow),
    )
    diagonal = each(lambda g: 4.0 + g, weights)
    inverse = each(lambda m: 1.0 / m, diagonal)
    scale = each(lambda w, i: w * i, wet, inverse)
    zero = each(lambda r, i: r * i, right, inverse)
    one = each(lambda a, n, z: a * n - theta * z, scale, neighbours(zero), zero)
    two = each(lambda a, n, z: a * n - theta * z, scale, neighbours(one), one)
    three = scale[0][:rows] * neighbours(two)[0][:rows] - theta * two[0][:rows]
    right, middle = right[0][:rows], diagonal[0][:rows]
    zero, one, two = zero[0][:rows], one[0][:rows], two[0][:rows]
    base[0] = zero
    base[1] = one
    base[2] = two
    weighted_one = middle * one
    weighted_two = middle * two
    products = (
        right * zero,
        right * one,
        right * two,
        right * three,
        weighted_one * one,
        weighted_one * two,
        weighted_one * three,
        weighted_two * two,
        weighted_two * three,
    )
    which = iota((16, cols), 0)
    place = iota((16, cols), 1)
    sums = jnp.where((which == len(products)) & (place == 0), theta, 0.0)
    for k, product in enumerate(products):
        sums = jnp.where(which == k, jnp.sum(product, axis=0, keepdims=True), sums)
    sums = jnp.sum(sums, axis=1, keepdims=True)
    sums = jnp.sum(jnp.where(which == place, sums, 0.0), axis=0, keepdims=True)
    moments[...] = jnp.broadcast_to(sums, moments.shape)


def step_kernel(
    meta, spans, facing, heat, salt, zonal, merid, water, north_came, south_rows, from_far, from_near,
    heat_out, salt_out, zonal_out, merid_out,
    new_heat, new_salt, new_zonal, new_merid, north_rows, sems,
):
    levels, rows, cols = heat.shape
    deep = 4 * levels
    _, top, lon_odd, _ = flags(meta)
    wet = water[...].astype(jnp.float32)
    lane = iota((rows, cols), 1)
    row = iota((rows, cols), 0)
    east = jnp.where(lon_odd, from_far[...], from_near[...])
    west = jnp.where(lon_odd, from_near[...], from_far[...])
    came = north_came[...]
    across = fold(fold_shift(facing), pltpu.roll(west[:deep], cols // 2, 1), came, east[:deep], False)
    north_rows[...] = jnp.where(top, across, came)

    def around(cells, q):
        a = pltpu.roll(east, (cols - 2 * q) % cols, 1)
        b = pltpu.roll(west, (2 * cols - 2 - 2 * q) % cols, 1)
        side = jnp.where(lane < 2, a, b)

        def shift_x(by):
            a = pltpu.roll(cells, by % cols, 1)
            b = pltpu.roll(side, by % cols, 1)
            own = lane >= by if by > 0 else lane < cols + by
            return jnp.where(own, a, b)

        n0 = north_rows[2 * q : 2 * q + 1, :]
        n1 = north_rows[2 * q + 1 : 2 * q + 2, :]
        s0 = south_rows[2 * q + 1 : 2 * q + 2, :]
        s1 = south_rows[2 * q : 2 * q + 1, :]
        north_one = jnp.where(row == rows - 1, n0, pltpu.roll(cells, rows - 1, 0))
        north_two = jnp.where(row == rows - 1, n1, jnp.where(row == rows - 2, n0, pltpu.roll(cells, rows - 2, 0)))
        south_one = jnp.where(row == 0, s0, pltpu.roll(cells, 1, 0))
        south_two = jnp.where(row == 0, s1, jnp.where(row == 1, s0, pltpu.roll(cells, 2, 0)))
        return (shift_x(-1), shift_x(1), shift_x(-2), shift_x(2), north_one, south_one, north_two, south_two)

    def advance(cells, parts, speed_x, speed_y):
        e1, w1, e2, w2, n1, s1, n2, s2 = parts
        grad_east = 8.0 * (e1 - w1) - (e2 - w2)
        grad_north = 8.0 * (n1 - s1) - (n2 - s2)
        laplace = (e1 + w1) + (n1 + s1) - 4.0 * cells
        tendency = (-TIME_STEP / 12.0) * (speed_x * grad_east + speed_y * grad_north) + MIXING * laplace
        return cells + wet * tendency

    stores = ((new_heat, heat_out), (new_salt, salt_out), (new_zonal, zonal_out), (new_merid, merid_out))
    size = levels // sems.shape[1]
    copies = []
    half = 0.5 * TIME_STEP
    above_x = jnp.zeros((rows, cols), jnp.float32)
    above_y = jnp.zeros((rows, cols), jnp.float32)
    for k in range(levels):
        t, s, u, v = heat[k], salt[k], zonal[k], merid[k]
        around_t = around(t, k)
        around_s = around(s, levels + k)
        new_heat[k] = advance(t, around_t, u, v)
        new_salt[k] = advance(s, around_s, u, v)
        span = spans[0:1, k : k + 1]
        layer_x = span * (density(around_t[0], around_s[0]) - density(around_t[1], around_s[1]))
        layer_y = span * (density(around_t[4], around_s[4]) - density(around_t[5], around_s[5]))
        new_zonal[k] = wet * (u - half * (above_x + 0.5 * layer_x))
        new_merid[k] = wet * (v - half * (above_y + 0.5 * layer_y))
        above_x = above_x + layer_x
        above_y = above_y + layer_y
        if (k + 1) % size == 0:
            piece = pl.ds(k + 1 - size, size)
            for i, (near_ref, far_ref) in enumerate(stores):
                copies.append(pltpu.make_async_copy(near_ref.at[piece], far_ref.at[piece], sems.at[i, k // size]))
                copies[-1].start()
    for copy in copies:
        copy.wait()


def surface_kernel(shares, shift, base, surface):
    lanes = shares.shape[1]
    g00, g01, g02, g03, g11, g12, g13, g22, g23, theta = (
        shares[...] if k == 0 else pltpu.roll(shares[...], lanes - k, 1) for k in range(10)
    )
    add = lambda terms: jnp.sum(terms, axis=0, keepdims=True)

    def ratio(a, b):
        good = b > 0.0
        return jnp.where(good, a / jnp.where(good, b, 1.0), 0.0)

    def form(p, h):
        total = 0.0
        for i, a in enumerate(p):
            for j in range(i, len(p)):
                term = a * p[j] * h[i + j]
                total = total + (term if i == j else 2.0 * term)
        return total

    whole = add(g00)
    common = ratio(add(theta * g00 + g01), whole)
    d = theta - common
    mu = [
        whole,
        add(g01 + d * g00),
        add(g11 + d * (2.0 * g01 + d * g00)),
        add(g12 + d * (2.0 * g11 + g02 + d * (3.0 * g01 + d * g00))),
        add(g22 + d * (4.0 * g12 + d * (2.0 * g02 + 4.0 * g11 + d * (4.0 * g01 + d * g00)))),
        add(
            g23
            + d * (3.0 * g22 + 2.0 * g13 + d * (9.0 * g12 + g03 + d * (4.0 * g02 + 6.0 * g11 + d * (5.0 * g01 + d * g00))))
        ),
    ]
    scale = 1.0 - common
    gap = [scale * mu[k] - mu[k + 1] for k in range(5)]
    alpha = ratio(mu[0], gap[0])
    y = [-alpha * ratio(mu[1], mu[0]), alpha]
    x = [alpha, 0.0, 0.0]
    rz = form(y, mu)
    p = [y[0] + ratio(rz, mu[0]), y[1]]
    alpha = ratio(rz, form(p, gap))
    x = [x[0] + alpha * p[0], alpha * p[1], 0.0]
    y = [y[0] - alpha * scale * p[0], y[1] - alpha * (scale * p[1] - p[0]), alpha * p[1]]
    new = form(y, mu)
    beta = ratio(new, rz)
    p = [y[0] + beta * p[0], y[1] + beta * p[1], y[2]]
    alpha = ratio(new, form(p, gap))
    x = [x[0] + alpha * p[0], x[1] + alpha * p[1], alpha * p[2]]
    d = shift[0:1, :] - common
    x = [x[0] + d * (x[1] + d * x[2]), x[1] + 2.0 * d * x[2], x[2]]
    x = [value[0:1, 0:1] for value in x]
    surface[...] = x[0] * base[0] + x[1] * base[1] + x[2] * base[2]


def call(kernel, outs, flops, moved, name, out_space=pltpu.VMEM, scratch=(), types=jnp.float32):
    def run(*args):
        return pl.pallas_call(
            kernel,
            out_shape=[jax.ShapeDtypeStruct(shape, types) for shape in outs],
            in_specs=[pl.BlockSpec(memory_space=pltpu.VMEM)] * len(args),
            out_specs=[pl.BlockSpec(memory_space=out_space)] * len(outs),
            scratch_shapes=list(scratch),
            cost_estimate=pl.CostEstimate(flops=flops, bytes_accessed=moved, transcendentals=0),
            compiler_params=pltpu.CompilerParams(vmem_limit_bytes=VMEM_LIMIT),
            name=name,
        )(*args)

    return run


def body(
    warmth_deviation,
    saltiness_deviation,
    easterly_speed,
    poleward_speed,
    stratum_spans,
    water_indicator,
    opposite_counterpart,
    elevation_weights,
    elevation_anomaly,
):
    lons, lats = lax.axis_size("lon"), lax.axis_size("lat")
    lon, lat = lax.axis_index("lon"), lax.axis_index("lat")
    levels, rows, cols = warmth_deviation.shape
    high = packet_rows(levels)
    assert cols & (cols - 1) == 0 and rows >= 24 and rows // 2 == high - 4 * levels + 8 and 4 * levels <= cols // 2 and 2 * START[-1] <= min(RELAY, cols - RELAY) and cols == 128
    tall = rows + 16
    width = cols * lons
    flat = lambda i, j: (i % lons) * lats + j

    place = (lax.rem(lat, 2), lat == lats - 1, lax.rem(lon, 2), lat == 0, lon)
    meta = jnp.stack([value.astype(jnp.int32) for value in place]).reshape(1, 5)
    (meta,) = call(place_kernel, [(8, cols)], LOAD_FLOPS, 16, "place", types=jnp.int32)(meta)

    spans = stratum_spans.reshape(1, levels)
    facing = opposite_counterpart.reshape(1, cols)
    state = (warmth_deviation, saltiness_deviation, easterly_speed, poleward_speed)
    flat_state = (water_indicator, elevation_weights, elevation_anomaly)
    cells = levels * rows * cols
    sums, first, second, east_columns, west_columns = call(
        pack_kernel,
        [(3, rows, cols), (high, cols), (high, cols), (rows, cols), (rows, cols)],
        12 * cells,
        16 * cells,
        "level_sums",
        scratch=[pltpu.VMEM((high, cols), jnp.float32)] * 3,
    )(meta, spans, facing, *state, *flat_state)

    axes = ("lon", "lat")
    pairs_first = [(flat(i, j), flat(i, j ^ 1)) for i in range(lons) for j in range(lats)]
    pairs_inner = [
        (flat(i, a), flat(i, b))
        for i in range(lons)
        for j in range(1, lats - 1, 2)
        for a, b in ((j, j + 1), (j + 1, j))
    ] + [(flat(i, 0), flat(i ^ 1, 0)) for i in range(lons)]

    counterpart, first = lax.optimization_barrier((opposite_counterpart, first))
    hinge = lax.rem(counterpart[0] + 1 + cols * lon, width)
    block = lax.rem((hinge + cols // 2) // cols, lons)

    def exchange(shift, first, second):
        partner = [(shift - 1 - i) % lons for i in range(lons)]
        partner = [i + lons // 2 if i == p else p for i, p in enumerate(partner)]
        pairs_fold = [(flat(p, lats - 1), flat(i, lats - 1)) for i, p in enumerate(partner)]
        second = lax.ppermute(second, axes, pairs_inner + pairs_fold)
        return second, lax.ppermute(first, axes, pairs_first)

    mine = second
    second, first = lax.switch(block, [functools.partial(exchange, s) for s in range(lons)], first, second)

    deep = 4 * levels
    ext, to_far, to_near, state_far, state_near, facing_rows, north_rows, south_rows = call(
        functools.partial(turn_kernel, lons),
        [
            (FIELDS, tall, cols),
            *[(rows // 2, cols)] * 2,
            *[(rows, cols)] * 2,
            (high - deep, cols),
            *[(deep, cols)] * 2,
        ],
        FIELDS * tall * cols,
        4 * 4 * FIELDS * tall * cols,
        "row_halos",
    )(meta, facing, mine, sums, *flat_state, second, first, east_columns, west_columns)

    near = lambda cells: lax.ppermute(cells, "lon", [(i, i ^ 1) for i in range(lons)])
    far = lambda cells: lax.ppermute(cells, "lon", [(i, (i + 1 if i % 2 else i - 1) % lons) for i in range(lons)])
    from_far, from_near = far(to_far), near(to_near)
    state_far, state_near = far(state_far), near(state_near)

    (shift,) = call(shift_kernel, [(8, cols)], 60 * rows * cols, 24 * rows * cols, "basis_shift")(ext)

    count = lons * lats
    base, moments = call(
        krylov_kernel,
        [(3, rows, cols), (count, cols)],
        200 * tall * cols,
        4 * 12 * tall * cols,
        "krylov",
        scratch=[pltpu.VMEM((2, high - deep + 8, cols), jnp.float32)],
    )(meta, facing, shift, ext, facing_rows, from_far, from_near)

    chunks = 5 if levels % 5 == 0 else 1
    new_heat, new_salt, new_zonal, new_merid = call(
        step_kernel,
        [(levels, rows, cols)] * 4,
        120 * cells,
        32 * cells,
        "levels_step",
        out_space=pltpu.HBM,
        scratch=[
            *[pltpu.VMEM((levels, rows, cols), jnp.float32)] * 4,
            pltpu.VMEM((deep, cols), jnp.float32),
            pltpu.SemaphoreType.DMA((4, chunks)),
        ],
    )(meta, spans, facing, *state, water_indicator, north_rows, south_rows, state_far, state_near)

    shares = lax.all_to_all(moments, axes, 0, 0, tiled=True)
    (surface,) = call(surface_kernel, [(rows, cols)], 6 * rows * cols, 16 * rows * cols, "surface")(shares, shift, base)
    return (new_heat, new_salt, new_zonal, new_merid, surface)


def solution(mesh):
    for axis in mesh.shape.values():
        assert axis > 1 and axis & (axis - 1) == 0
    levels = P(None, "lat", "lon")
    flat = P("lat", "lon")
    return jax.shard_map(
        body,
        mesh=mesh,
        in_specs=(levels, levels, levels, levels, P(), flat, P("lon"), flat, flat),
        out_specs=(levels, levels, levels, levels, flat),
        check_vma=False,
    )
```

```python
import functools

import jax
import jax.numpy as jnp
from jax import lax
from jax.experimental import pallas as pl
from jax.experimental.pallas import tpu as pltpu
from jax.sharding import PartitionSpec as P

TIME_STEP = 0.1
MIXING = 0.1

DEEP = (5, 3, 4, 4, 3, 3)
SIDE = (5, 4, 3, 4, 3, 3)
RING = (10, 9, 8, 9, 8, 8)
FIELDS = len(SIDE)
ROW = tuple(sum(DEEP[:f]) for f in range(FIELDS + 1))
START = tuple(sum(SIDE[:f]) for f in range(FIELDS + 1))
RING_START = tuple(sum(RING[:f]) for f in range(FIELDS + 1))
RELAY = 56
FLIPPED = (1, 2)
SHIFTED = 5
WEST_ONLY = 120
VMEM_LIMIT = 32 * 1024 * 1024
LOAD_FLOPS = 10**10


def density(heat, salt):
    return heat * (-1.0 - 0.15 * heat - 0.2 * salt) + 0.8 * salt


def iota(shape, axis):
    return lax.broadcasted_iota(jnp.int32, shape, axis)


def packet_rows(levels):
    return -(-(4 * levels + ROW[-1]) // 8) * 8


def flags(meta):
    return tuple(meta[i : i + 1, :] == 1 for i in range(4))


def segments(rows):
    size = START[-1]
    return (0, rows // 2, 0), (rows // 2, rows, size), (rows, rows + 8, RELAY), (rows + 8, rows + 16, RELAY + size)


def place_kernel(meta, placed):
    for i in range(5):
        placed[i : i + 1, :] = jnp.broadcast_to(meta[0:1, i : i + 1], (1, placed.shape[1]))
    placed[5:, :] = jnp.zeros((placed.shape[0] - 5, placed.shape[1]), jnp.int32)


def pack_kernel(
    meta, spans, facing, heat, salt, zonal, merid, water, weights, anomaly,
    sums, first, second, east_columns, west_columns,
    top, bottom, back,
):
    levels, rows, cols = heat.shape
    span = [spans[0:1, k : k + 1] for k in range(levels)]
    below = [None] * levels
    total = jnp.zeros((1, 1), jnp.float32)
    for k in reversed(range(levels)):
        below[k] = span[k] * (0.5 * span[k] + total)
        total = total + span[k]
    pair = iota((rows, cols), 1) // 2
    zero = jnp.zeros((rows, cols), jnp.float32)
    press, east, north, east_edge, west_edge = zero, zero, zero, zero, zero
    for k in range(levels):
        press = press + below[k] * density(heat[k], salt[k])
        east = east + span[k] * zonal[k]
        north = north + span[k] * merid[k]
        for q, source in ((k, heat), (levels + k, salt)):
            cells = source[k]
            here = pair == q
            east_edge = jnp.where(here, pltpu.roll(cells, (2 * q + 2) % cols, 1), east_edge)
            west_edge = jnp.where(here, pltpu.roll(cells, 2 * q, 1), west_edge)
            top[2 * q : 2 * q + 2, :] = source[k, rows - 2 :, :]
            bottom[2 * q : 2 * q + 2, :] = source[k, :2, :]
            for i in range(2):
                back[2 * q + i : 2 * q + i + 1, :] = source[k, rows - 1 - i : rows - i, :]
    east_columns[...] = east_edge
    west_columns[...] = west_edge
    sums[0] = press
    sums[1] = east
    sums[2] = north
    fields = (sums.at[0], sums.at[1], sums.at[2], water, weights, anomaly)
    for f, field in enumerate(fields):
        at = 4 * levels + ROW[f]
        deep = DEEP[f]
        top[at : at + deep, :] = field[rows - deep :, :].astype(jnp.float32)
        bottom[at : at + deep, :] = field[:deep, :].astype(jnp.float32)
        for j in range(deep):
            back[at + j : at + j + 1, :] = field[rows - 1 - j : rows - j, :].astype(jnp.float32)
    used = 4 * levels + ROW[-1]
    high = first.shape[0]
    if used < high:
        for packet in (top, bottom, back):
            packet[used:, :] = jnp.zeros((high - used, cols), jnp.float32)
    odd, last, _, _ = flags(meta)
    first[...] = jnp.where(odd, bottom[...], top[...])
    second[...] = jnp.where(last, back[...], jnp.where(odd, top[...], bottom[...]))


def extend(
    lons, nearest, meta, facing, mine, sums, water, weights, anomaly, second, first, ext, facing_rows, north_rows, south_rows
):
    rows, cols = sums.shape[1], sums.shape[2]
    tall = ext.shape[1]
    deep = north_rows.shape[0]
    odd, top, lon_odd, bottom = flags(meta)
    from_first = first[...]
    hinge = facing[0:1, 0:1] + 1 + cols * meta[4:5, 0:1] + (cols // 2 if nearest else 0)
    block = lax.shift_right_logical(hinge & (lons * cols - 1), cols.bit_length() - 1)
    alone = ((block - 1 - 2 * meta[4:5, 0:1]) & (lons - 1)) == 0
    from_second = jnp.where(top & alone, mine[...], second[...])
    north = jnp.where(odd, from_second, from_first)
    south = jnp.where(bottom, 0.0, jnp.where(odd, from_first, from_second))
    fields = (sums.at[0], sums.at[1], sums.at[2], water, weights, anomaly)
    for f in range(FIELDS):
        at = deep + ROW[f]
        size = DEEP[f]
        ext[f, :rows, :] = fields[f][...].astype(jnp.float32)
        ext[f, rows : rows + size, :] = north[at : at + size]
        ext[f, rows + size : tall - size, :] = jnp.zeros((tall - rows - 2 * size, cols), jnp.float32)
        ext[f, tall - size :, :] = south[at : at + size]
    facing_rows[...] = from_second[deep:]
    north_rows[...] = north[:deep]
    south_rows[...] = south[:deep]
    return from_second, lon_odd


def turn_kernel(
    lons, meta, facing, mine, sums, water, weights, anomaly, second, first, east_columns, west_columns,
    ext, to_far, to_near, state_far, state_near, facing_rows, north_rows, south_rows,
):
    from_second, lon_odd = extend(
        lons, True, meta, facing, mine, sums, water, weights, anomaly, second, first,
        ext, facing_rows, north_rows, south_rows,
    )
    rows, cols = sums.shape[1], sums.shape[2]
    deep = north_rows.shape[0]
    passed = from_second[deep:]
    size = passed.shape[0]
    half = rows // 2
    lane = iota((half, cols), 1)
    lower = iota((half, cols), 0) >= size
    empty = jnp.zeros((size, cols), jnp.float32)
    spare = jnp.zeros((half - size, cols), jnp.float32)
    relay = lane >= RELAY
    east = jnp.where(relay, jnp.concatenate([pltpu.roll(passed, RELAY, 1), spare], axis=0), 0.0)
    west = jnp.where(relay, jnp.concatenate([passed, spare], axis=0), 0.0)
    for f in range(FIELDS):
        for start, stop, first_lane in segments(rows):
            at = START[f] + first_lane
            here = (lane >= at) & (lane < at + SIDE[f])
            layer = ext[f, start:stop, :]
            to_east = pltpu.roll(layer, (at + SIDE[f]) % cols, 1)
            to_west = pltpu.roll(layer, at, 1)
            if stop - start < half:
                here = here & lower
                to_east = jnp.concatenate([empty, to_east], axis=0)
                to_west = jnp.concatenate([empty, to_west], axis=0)
            east = jnp.where(here, to_east, east)
            west = jnp.where(here, to_west, west)
    to_far[...] = jnp.where(lon_odd, east, west)
    to_near[...] = jnp.where(lon_odd, west, east)
    passed = from_second[:deep]
    spare = jnp.zeros((rows - deep, cols), jnp.float32)
    right_half = iota((rows, cols), 1) >= cols // 2
    east = jnp.where(right_half, jnp.concatenate([pltpu.roll(passed, cols // 2, 1), spare], axis=0), east_columns[...])
    west = jnp.where(right_half, jnp.concatenate([passed, spare], axis=0), west_columns[...])
    state_far[...] = jnp.where(lon_odd, east, west)
    state_near[...] = jnp.where(lon_odd, west, east)


def ring_turn_kernel(
    lons, meta, facing, mine, sums, water, weights, anomaly, second, first, east_columns, west_columns,
    ext, to_ring, to_far, to_near, facing_rows, north_rows, south_rows,
):
    from_second, lon_odd = extend(
        lons, False, meta, facing, mine, sums, water, weights, anomaly, second, first,
        ext, facing_rows, north_rows, south_rows,
    )
    rows, cols = sums.shape[1], sums.shape[2]
    tall = ext.shape[1]
    deep = north_rows.shape[0]
    middle = tall // 2
    lane = iota((middle, cols), 1)
    ring = jnp.zeros((middle, cols), jnp.float32)
    for f in range(FIELDS):
        for part in range(2):
            at = RING_START[f] + part * RING_START[-1]
            layer = ext[f, part * middle : (part + 1) * middle, :]
            here = (lane >= at) & (lane < at + RING[f])
            ring = jnp.where(here, pltpu.roll(layer, (at + RING[f]) % cols, 1), ring)
    to_ring[:middle, :] = ring
    to_ring[middle:, :] = from_second[deep:]
    lane = iota((tall, cols), 1)
    spare = jnp.zeros((tall - rows, cols), jnp.float32)
    east = jnp.concatenate([east_columns[...], spare], axis=0)
    west = jnp.concatenate([west_columns[...], spare], axis=0)
    for f in range(FIELDS):
        at = deep + START[f]
        here = (lane >= at) & (lane < at + SIDE[f])
        layer = ext[f]
        east = jnp.where(here, pltpu.roll(layer, (at + SIDE[f]) % cols, 1), east)
        west = jnp.where(here, pltpu.roll(layer, at, 1), west)
    to_far[:tall, :] = jnp.where(lon_odd, east, west)
    to_near[:tall, :] = jnp.where(lon_odd, west, east)
    to_far[tall:, :] = from_second
    to_near[tall:, :] = from_second


def fold_shift(facing, nearest):
    cols = facing.shape[1]
    offset = (facing[0:1, 0:1] + 1) & (cols - 1)
    return jnp.where(offset >= cols // 2, offset - cols, offset) if nearest else offset


def fold(shift, west, own, east, beside):
    rows, cols = own.shape
    lane = iota((rows, cols), 1)
    source = cols - 1 - lane
    if beside:
        place = (source + shift) & (cols - 1)
        low = jnp.where(place - cols < shift, west, own)
        merged = jnp.where(place >= cols // 2, low, jnp.where(place >= shift, east, own))
    else:
        merged = jnp.where(source >= cols - shift, west, jnp.where(source < -shift, east, own))
    return jnp.take_along_axis(merged, cols - 1 - ((lane - shift) & (cols - 1)), axis=1)


def shift_kernel(ext, shift):
    rows, cols = ext.shape[1] - 16, ext.shape[2]
    press, zonal, merid, wet, weights, anomaly = (ext[f, :rows, :] for f in range(FIELDS))
    plus_x = lambda cells: pltpu.roll(cells, cols - 1, 1)
    minus_x = lambda cells: pltpu.roll(cells, 1, 1)
    plus_y = lambda cells: pltpu.roll(cells, rows - 1, 0)
    minus_y = lambda cells: pltpu.roll(cells, 1, 0)
    half = 0.5 * TIME_STEP
    east_flow = wet * (zonal - half * (plus_x(press) - minus_x(press)))
    north_flow = wet * (merid - half * (plus_y(press) - minus_y(press)))
    spread = plus_x(east_flow) - minus_x(east_flow) + plus_y(north_flow) - minus_y(north_flow)
    right = wet * (weights * anomaly - 0.5 * spread)
    inverse = 1.0 / (4.0 + weights)
    zero = right * inverse
    one = wet * inverse * (plus_x(zero) + minus_x(zero) + plus_y(zero) + minus_y(zero))
    lane = iota((rows, cols), 1)
    row = iota((rows, cols), 0)
    inside = (lane >= 8) & (lane < cols - 8) & (row >= 8) & (row < rows - 8)
    total = lambda cells: jnp.sum(jnp.sum(jnp.where(inside, cells, 0.0), axis=0, keepdims=True), axis=1, keepdims=True)
    below = total(right * zero)
    good = below > 0.0
    quotient = jnp.where(good, total(right * one) / jnp.where(good, below, 1.0), 0.0)
    shift[...] = jnp.broadcast_to(jnp.clip(quotient, -1.0, 1.0), shift.shape)


def krylov(fields, theta):
    tall, cols = fields[0][0].shape
    lane = iota((tall, cols), 1)
    first = lane == 0
    last = lane == cols - 1

    def plus_x(pair):
        a, b = (pltpu.roll(part, cols - 1, 1) for part in pair)
        return jnp.where(last, b, a), jnp.where(last, a, b)

    def minus_x(pair):
        a, b = (pltpu.roll(part, 1, 1) for part in pair)
        return jnp.where(first, b, a), jnp.where(first, a, b)

    def plus_y(pair):
        return tuple(pltpu.roll(part, tall - 1, 0) for part in pair)

    def minus_y(pair):
        return tuple(pltpu.roll(part, 1, 0) for part in pair)

    def each(function, *pairs):
        return tuple(function(*parts) for parts in zip(*pairs))

    def neighbours(pair):
        return each(
            lambda a, b, c, d: (a + b) + (c + d), plus_x(pair), minus_x(pair), plus_y(pair), minus_y(pair)
        )

    press, zonal, merid, wet, weights, anomaly = fields
    half = 0.5 * TIME_STEP
    flow = lambda w, speed, a, b: w * (speed - half * (a - b))
    east_flow = each(flow, wet, zonal, plus_x(press), minus_x(press))
    north_flow = each(flow, wet, merid, plus_y(press), minus_y(press))
    right = each(
        lambda w, g, n, a, b, c, d: w * (g * n - 0.5 * (a - b + c - d)),
        wet,
        weights,
        anomaly,
        plus_x(east_flow),
        minus_x(east_flow),
        plus_y(north_flow),
        minus_y(north_flow),
    )
    diagonal = each(lambda g: 4.0 + g, weights)
    inverse = each(lambda m: 1.0 / m, diagonal)
    scale = each(lambda w, i: w * i, wet, inverse)
    zero = each(lambda r, i: r * i, right, inverse)
    one = each(lambda a, n, z: a * n - theta * z, scale, neighbours(zero), zero)
    two = each(lambda a, n, z: a * n - theta * z, scale, neighbours(one), one)
    three = each(lambda a, n, z: a * n - theta * z, scale, neighbours(two), two)
    return right, diagonal, zero, one, two, three


def put_fold(f, pair, folded, top):
    rows = pair[0].shape[0] - 16
    eighth = iota((8, pair[0].shape[1]), 0)

    def put(cells, side):
        new = folded[side, ROW[f] : ROW[f] + 8, :]
        new = jnp.where(eighth < DEEP[f], jnp.where(top, new, cells[rows : rows + 8]), 0.0)
        return jnp.concatenate([cells[:rows], new, cells[rows + 8 :]], axis=0)

    return put(pair[0], 0), put(pair[1], 1)


def fill_fold(folded, across, west, own, east):
    size, cols = own.shape
    row = iota((size, cols), 0)
    flips = (row >= ROW[FLIPPED[0]]) & (row < ROW[FLIPPED[-1] + 1])
    for side in range(2):
        cells = fold(across, west, own, east, side == 1)
        folded[side, :size, :] = jnp.where(flips, -cells, cells)
    folded[:, size:, :] = jnp.zeros((2, folded.shape[1] - size, cols), jnp.float32)


def put_moments(right, middle, zero, one, two, three, theta, moments):
    cols = moments.shape[1]
    weighted_one = middle * one
    weighted_two = middle * two
    products = (
        right * zero,
        right * one,
        right * two,
        right * three,
        weighted_one * one,
        weighted_one * two,
        weighted_one * three,
        weighted_two * two,
        weighted_two * three,
    )
    which = iota((16, cols), 0)
    place = iota((16, cols), 1)
    sums = jnp.where((which == len(products)) & (place == 0), theta, 0.0)
    for k, product in enumerate(products):
        sums = jnp.where(which == k, jnp.sum(product, axis=0, keepdims=True), sums)
    sums = jnp.sum(sums, axis=1, keepdims=True)
    sums = jnp.sum(jnp.where(which == place, sums, 0.0), axis=0, keepdims=True)
    moments[...] = jnp.broadcast_to(sums, moments.shape)


def krylov_kernel(meta, facing, shift, ext, facing_rows, from_far, from_near, base, moments, folded):
    tall, cols = ext.shape[1], ext.shape[2]
    rows = base.shape[1]
    size = facing_rows.shape[0]
    _, top, lon_odd, _ = flags(meta)
    west = jnp.where(lon_odd, from_near[...], from_far[...])
    east = jnp.where(lon_odd, from_far[...], from_near[...])
    theta = shift[0:1, 0:1]
    relay = pltpu.roll(west[:size], cols - RELAY, 1)
    fill_fold(folded, fold_shift(facing, True), relay, facing_rows[...], east[:size])
    lane = iota((tall, cols), 1)

    def load(f):
        parts = []
        for packet, shift_of in ((west, 2 * cols - SIDE[f]), (east, cols)):
            pieces = []
            for start, stop, first_lane in segments(rows):
                layer = packet[packet.shape[0] - (stop - start) :]
                pieces.append(pltpu.roll(layer, (shift_of - START[f] - first_lane) % cols, 1))
            parts.append(jnp.concatenate(pieces, axis=0))
        a, b = parts
        beside = jnp.where(lane >= cols - SIDE[f], a, jnp.where(lane < SIDE[f], b, 0.0))
        return put_fold(f, (ext[f], beside), folded, top)

    vectors = krylov([load(f) for f in range(FIELDS)], theta)
    right, middle, zero, one, two, three = (pair[0][:rows] for pair in vectors)
    base[0] = zero
    base[1] = one
    base[2] = two
    put_moments(right, middle, zero, one, two, three, theta, moments)


def ring_kernel(meta, facing, shift, ext, facing_rows, from_ring, moments, folded):
    tall, cols = ext.shape[1], ext.shape[2]
    rows, middle = tall - 16, tall // 2
    top = flags(meta)[1]
    theta = shift[0:1, 0:1]
    own = facing_rows[...]
    fill_fold(folded, fold_shift(facing, False), from_ring[middle:, :], own, own)
    lane = iota((tall, cols), 1)
    packet = from_ring[:middle, :]

    def load(f):
        both = [RING_START[f], RING_START[f] + RING_START[-1]]
        a = jnp.concatenate([pltpu.roll(packet, (2 * cols - RING[f] - at) % cols, 1) for at in both], axis=0)
        return put_fold(f, (ext[f], jnp.where(lane >= cols - RING[f], a, 0.0)), folded, top)

    vectors = krylov([load(f) for f in range(FIELDS)], theta)
    here = lane[:rows] < cols - SHIFTED
    put_moments(*(jnp.where(here, a[:rows], b[:rows]) for a, b in vectors), theta, moments)


def base_kernel(used, meta, facing, shift, ext, facing_rows, from_far, from_near, base, folded):
    tall, cols = ext.shape[1], ext.shape[2]
    rows = base.shape[1]
    size = facing_rows.shape[0]
    _, top, lon_odd, _ = flags(meta)
    west = jnp.where(lon_odd, from_near[...], from_far[...])
    east = jnp.where(lon_odd, from_far[...], from_near[...])
    at = tall + used
    fill_fold(folded, fold_shift(facing, False), west[at : at + size], facing_rows[...], east[at : at + size])
    lane = iota((tall, cols), 1)

    def load(f):
        at = used + START[f]
        a = pltpu.roll(west[:tall], (2 * cols - SIDE[f] - at) % cols, 1)
        b = pltpu.roll(east[:tall], (cols - at) % cols, 1)
        beside = jnp.where(lane >= cols - SIDE[f], a, jnp.where(lane < SIDE[f], b, 0.0))
        return put_fold(f, (ext[f], beside), folded, top)

    _, _, zero, one, two, _ = krylov([load(f) for f in range(FIELDS)], shift[0:1, 0:1])
    base[0] = zero[0][:rows]
    base[1] = one[0][:rows]
    base[2] = two[0][:rows]


def step_kernel(
    nearest, meta, spans, facing, heat, salt, zonal, merid, water, north_came, south_rows, from_far, from_near,
    heat_out, salt_out, zonal_out, merid_out,
    new_heat, new_salt, new_zonal, new_merid, north_rows, sems,
):
    levels, rows, cols = heat.shape
    deep = 4 * levels
    _, top, lon_odd, _ = flags(meta)
    wet = water[...].astype(jnp.float32)
    lane = iota((rows, cols), 1)
    row = iota((rows, cols), 0)
    east = jnp.where(lon_odd, from_far[...], from_near[...])
    west = jnp.where(lon_odd, from_near[...], from_far[...])
    came = north_came[...]
    if nearest:
        relays = pltpu.roll(west[:deep], cols // 2, 1), east[:deep]
    else:
        relays = west[rows + 16 : rows + 16 + deep], east[rows + 16 : rows + 16 + deep]
    across = fold(fold_shift(facing, nearest), relays[0], came, relays[1], False)
    east, west = east[:rows], west[:rows]
    north_rows[...] = jnp.where(top, across, came)

    def around(cells, q):
        a = pltpu.roll(east, (cols - 2 * q) % cols, 1)
        b = pltpu.roll(west, (2 * cols - 2 - 2 * q) % cols, 1)
        side = jnp.where(lane < 2, a, b)

        def shift_x(by):
            a = pltpu.roll(cells, by % cols, 1)
            b = pltpu.roll(side, by % cols, 1)
            own = lane >= by if by > 0 else lane < cols + by
            return jnp.where(own, a, b)

        n0 = north_rows[2 * q : 2 * q + 1, :]
        n1 = north_rows[2 * q + 1 : 2 * q + 2, :]
        s0 = south_rows[2 * q + 1 : 2 * q + 2, :]
        s1 = south_rows[2 * q : 2 * q + 1, :]
        north_one = jnp.where(row == rows - 1, n0, pltpu.roll(cells, rows - 1, 0))
        north_two = jnp.where(row == rows - 1, n1, jnp.where(row == rows - 2, n0, pltpu.roll(cells, rows - 2, 0)))
        south_one = jnp.where(row == 0, s0, pltpu.roll(cells, 1, 0))
        south_two = jnp.where(row == 0, s1, jnp.where(row == 1, s0, pltpu.roll(cells, 2, 0)))
        return (shift_x(-1), shift_x(1), shift_x(-2), shift_x(2), north_one, south_one, north_two, south_two)

    def advance(cells, parts, speed_x, speed_y):
        e1, w1, e2, w2, n1, s1, n2, s2 = parts
        grad_east = 8.0 * (e1 - w1) - (e2 - w2)
        grad_north = 8.0 * (n1 - s1) - (n2 - s2)
        laplace = (e1 + w1) + (n1 + s1) - 4.0 * cells
        tendency = (-TIME_STEP / 12.0) * (speed_x * grad_east + speed_y * grad_north) + MIXING * laplace
        return cells + wet * tendency

    stores = ((new_heat, heat_out), (new_salt, salt_out), (new_zonal, zonal_out), (new_merid, merid_out))
    size = levels // sems.shape[1]
    copies = []
    half = 0.5 * TIME_STEP
    above_x = jnp.zeros((rows, cols), jnp.float32)
    above_y = jnp.zeros((rows, cols), jnp.float32)
    for k in range(levels):
        t, s, u, v = heat[k], salt[k], zonal[k], merid[k]
        around_t = around(t, k)
        around_s = around(s, levels + k)
        new_heat[k] = advance(t, around_t, u, v)
        new_salt[k] = advance(s, around_s, u, v)
        span = spans[0:1, k : k + 1]
        layer_x = span * (density(around_t[0], around_s[0]) - density(around_t[1], around_s[1]))
        layer_y = span * (density(around_t[4], around_s[4]) - density(around_t[5], around_s[5]))
        new_zonal[k] = wet * (u - half * (above_x + 0.5 * layer_x))
        new_merid[k] = wet * (v - half * (above_y + 0.5 * layer_y))
        above_x = above_x + layer_x
        above_y = above_y + layer_y
        if (k + 1) % size == 0:
            piece = pl.ds(k + 1 - size, size)
            for i, (near_ref, far_ref) in enumerate(stores):
                copies.append(pltpu.make_async_copy(near_ref.at[piece], far_ref.at[piece], sems.at[i, k // size]))
                copies[-1].start()
    for copy in copies:
        copy.wait()


def surface_kernel(shares, shift, base, surface):
    lanes = shares.shape[1]
    g00, g01, g02, g03, g11, g12, g13, g22, g23, theta = (
        shares[...] if k == 0 else pltpu.roll(shares[...], lanes - k, 1) for k in range(10)
    )
    add = lambda terms: jnp.sum(terms, axis=0, keepdims=True)

    def ratio(a, b):
        good = b > 0.0
        return jnp.where(good, a / jnp.where(good, b, 1.0), 0.0)

    def form(p, h):
        total = 0.0
        for i, a in enumerate(p):
            for j in range(i, len(p)):
                term = a * p[j] * h[i + j]
                total = total + (term if i == j else 2.0 * term)
        return total

    whole = add(g00)
    common = ratio(add(theta * g00 + g01), whole)
    d = theta - common
    mu = [
        whole,
        add(g01 + d * g00),
        add(g11 + d * (2.0 * g01 + d * g00)),
        add(g12 + d * (2.0 * g11 + g02 + d * (3.0 * g01 + d * g00))),
        add(g22 + d * (4.0 * g12 + d * (2.0 * g02 + 4.0 * g11 + d * (4.0 * g01 + d * g00)))),
        add(
            g23
            + d * (3.0 * g22 + 2.0 * g13 + d * (9.0 * g12 + g03 + d * (4.0 * g02 + 6.0 * g11 + d * (5.0 * g01 + d * g00))))
        ),
    ]
    scale = 1.0 - common
    gap = [scale * mu[k] - mu[k + 1] for k in range(5)]
    alpha = ratio(mu[0], gap[0])
    y = [-alpha * ratio(mu[1], mu[0]), alpha]
    x = [alpha, 0.0, 0.0]
    rz = form(y, mu)
    p = [y[0] + ratio(rz, mu[0]), y[1]]
    alpha = ratio(rz, form(p, gap))
    x = [x[0] + alpha * p[0], alpha * p[1], 0.0]
    y = [y[0] - alpha * scale * p[0], y[1] - alpha * (scale * p[1] - p[0]), alpha * p[1]]
    new = form(y, mu)
    beta = ratio(new, rz)
    p = [y[0] + beta * p[0], y[1] + beta * p[1], y[2]]
    alpha = ratio(new, form(p, gap))
    x = [x[0] + alpha * p[0], x[1] + alpha * p[1], alpha * p[2]]
    d = shift[0:1, :] - common
    x = [x[0] + d * (x[1] + d * x[2]), x[1] + 2.0 * d * x[2], x[2]]
    x = [value[0:1, 0:1] for value in x]
    surface[...] = x[0] * base[0] + x[1] * base[1] + x[2] * base[2]


def call(kernel, outs, flops, moved, name, out_space=pltpu.VMEM, scratch=(), types=jnp.float32):
    def run(*args):
        return pl.pallas_call(
            kernel,
            out_shape=[jax.ShapeDtypeStruct(shape, types) for shape in outs],
            in_specs=[pl.BlockSpec(memory_space=pltpu.VMEM)] * len(args),
            out_specs=[pl.BlockSpec(memory_space=out_space)] * len(outs),
            scratch_shapes=list(scratch),
            cost_estimate=pl.CostEstimate(flops=flops, bytes_accessed=moved, transcendentals=0),
            compiler_params=pltpu.CompilerParams(vmem_limit_bytes=VMEM_LIMIT),
            name=name,
        )(*args)

    return run


def body(
    warmth_deviation,
    saltiness_deviation,
    easterly_speed,
    poleward_speed,
    stratum_spans,
    water_indicator,
    opposite_counterpart,
    elevation_weights,
    elevation_anomaly,
):
    lons, lats = lax.axis_size("lon"), lax.axis_size("lat")
    lon, lat = lax.axis_index("lon"), lax.axis_index("lat")
    levels, rows, cols = warmth_deviation.shape
    high = packet_rows(levels)
    assert cols & (cols - 1) == 0 and rows >= 24 and rows // 2 == high - 4 * levels + 8 and 4 * levels <= cols // 2 and 2 * RING_START[-1] <= cols and 2 * START[-1] <= min(RELAY, cols - RELAY) and cols == 128
    tall = rows + 16
    width = cols * lons
    flat = lambda i, j: (i % lons) * lats + j

    place = (lax.rem(lat, 2), lat == lats - 1, lax.rem(lon, 2), lat == 0, lon)
    meta = jnp.stack([value.astype(jnp.int32) for value in place]).reshape(1, 5)
    (meta,) = call(place_kernel, [(8, cols)], LOAD_FLOPS, 16, "place", types=jnp.int32)(meta)

    spans = stratum_spans.reshape(1, levels)
    facing = opposite_counterpart.reshape(1, cols)
    state = (warmth_deviation, saltiness_deviation, easterly_speed, poleward_speed)
    flat_state = (water_indicator, elevation_weights, elevation_anomaly)
    cells = levels * rows * cols
    sums, first, second, east_columns, west_columns = call(
        pack_kernel,
        [(3, rows, cols), (high, cols), (high, cols), (rows, cols), (rows, cols)],
        12 * cells,
        16 * cells,
        "level_sums",
        scratch=[pltpu.VMEM((high, cols), jnp.float32)] * 3,
    )(meta, spans, facing, *state, *flat_state)

    axes = ("lon", "lat")
    pairs_first = [(flat(i, j), flat(i, j ^ 1)) for i in range(lons) for j in range(lats)]
    pairs_inner = [
        (flat(i, a), flat(i, b))
        for i in range(lons)
        for j in range(1, lats - 1, 2)
        for a, b in ((j, j + 1), (j + 1, j))
    ] + [(flat(i, 0), flat(i ^ 1, 0)) for i in range(lons)]

    near = lambda cells: lax.ppermute(cells, "lon", [(i, i ^ 1) for i in range(lons)])
    far = lambda cells: lax.ppermute(cells, "lon", [(i, (i + 1 if i % 2 else i - 1) % lons) for i in range(lons)])
    deep = 4 * levels
    count = lons * lats
    folds = [pltpu.VMEM((2, high - deep + 8, cols), jnp.float32)]
    work = (200 * tall * cols, 48 * tall * cols)

    def exchange(block, first, second):
        def swap(shift, first, second):
            partner = [(shift - 1 - i) % lons for i in range(lons)]
            partner = [i + lons // 2 if i == p else p for i, p in enumerate(partner)]
            pairs_fold = [(flat(p, lats - 1), flat(i, lats - 1)) for i, p in enumerate(partner)]
            second = lax.ppermute(second, axes, pairs_inner + pairs_fold)
            return second, lax.ppermute(first, axes, pairs_first)

        return lax.switch(block, [functools.partial(swap, s) for s in range(lons)], first, second)

    def turn(kernel, packets, first, second, mine):
        return call(
            kernel,
            [(FIELDS, tall, cols), *packets, (high - deep, cols), *[(deep, cols)] * 2],
            FIELDS * tall * cols,
            16 * FIELDS * tall * cols,
            "row_halos",
        )(meta, facing, mine, sums, *flat_state, second, first, east_columns, west_columns)

    def basis_shift(ext):
        return call(shift_kernel, [(8, cols)], 60 * rows * cols, 24 * rows * cols, "basis_shift")(ext)[0]

    def step(nearest, north_rows, south_rows, from_far, from_near):
        chunks = 5 if levels % 5 == 0 else 1
        return call(
            functools.partial(step_kernel, nearest),
            [(levels, rows, cols)] * 4,
            120 * cells,
            32 * cells,
            "levels_step",
            out_space=pltpu.HBM,
            scratch=[*[pltpu.VMEM((levels, rows, cols), jnp.float32)] * 4, pltpu.VMEM((deep, cols), jnp.float32), pltpu.SemaphoreType.DMA((4, chunks))],
        )(meta, spans, facing, *state, water_indicator, north_rows, south_rows, from_far, from_near)

    def finish(shares, shift, base):
        return call(surface_kernel, [(rows, cols)], 6 * rows * cols, 16 * rows * cols, "surface")(shares, shift, base)[0]

    def by_swaps(hinge, first, second):
        block = lax.rem((hinge + cols // 2) // cols, lons)
        got_second, got_first = exchange(block, first, second)
        ext, to_far, to_near, state_far, state_near, facing_rows, north_rows, south_rows = turn(
            functools.partial(turn_kernel, lons),
            [*[(rows // 2, cols)] * 2, *[(rows, cols)] * 2],
            got_first, got_second, second,
        )
        from_far, from_near = far(to_far), near(to_near)
        state_far, state_near = far(state_far), near(state_near)
        shift = basis_shift(ext)
        base, moments = call(krylov_kernel, [(3, rows, cols), (count, cols)], *work, "krylov", scratch=folds)(
            meta, facing, shift, ext, facing_rows, from_far, from_near
        )
        results = step(True, north_rows, south_rows, state_far, state_near)
        shares = lax.all_to_all(moments, axes, 0, 0, tiled=True)
        return (*results, finish(shares, shift, base))

    def by_ring(hinge, first, second):
        got_second, got_first = exchange(hinge // cols, first, second)
        ext, to_ring, to_far, to_near, facing_rows, north_rows, south_rows = turn(
            functools.partial(ring_turn_kernel, lons),
            [(tall // 2 + high - deep, cols), *[(tall + high, cols)] * 2],
            got_first, got_second, second,
        )
        from_ring = lax.ppermute(to_ring, "lon", [(i, (i + 1) % lons) for i in range(lons)])
        from_far, from_near = far(to_far), near(to_near)
        shift = basis_shift(ext)
        (moments,) = call(ring_kernel, [(count, cols)], *work, "moments", scratch=folds)(
            meta, facing, shift, ext, facing_rows, from_ring
        )
        shares = lax.all_to_all(moments, axes, 0, 0, tiled=True)
        _, from_far, from_near = lax.optimization_barrier((moments, from_far, from_near))
        results = step(False, north_rows, south_rows, from_far, from_near)
        (base,) = call(functools.partial(base_kernel, deep), [(3, rows, cols)], *work, "krylov", scratch=folds)(
            meta, facing, shift, ext, facing_rows, from_far, from_near
        )
        return (*results, finish(shares, shift, base))

    counterpart, first = lax.optimization_barrier((opposite_counterpart, first))
    hinge = lax.rem(counterpart[0] + 1 + cols * lon, width)
    return lax.cond(lax.rem(hinge, cols) < WEST_ONLY, by_ring, by_swaps, hinge, first, second)


def solution(mesh):
    for axis in mesh.shape.values():
        assert axis > 1 and axis & (axis - 1) == 0
    levels = P(None, "lat", "lon")
    flat = P("lat", "lon")
    return jax.shard_map(
        body,
        mesh=mesh,
        in_specs=(levels, levels, levels, levels, P(), flat, P("lon"), flat, flat),
        out_specs=(levels, levels, levels, levels, flat),
        check_vma=False,
    )
```

```python
import functools

import jax
import jax.numpy as jnp
from jax import lax
from jax.experimental import pallas as pl
from jax.experimental.pallas import tpu as pltpu
from jax.sharding import PartitionSpec as P

TIME_STEP = 0.1
MIXING = 0.1

DEEP = (5, 3, 4, 4, 3, 3)
SIDE = (5, 4, 3, 4, 3, 3)
FIELDS = len(SIDE)
ROW = tuple(sum(DEEP[:f]) for f in range(FIELDS + 1))
START = tuple(sum(SIDE[:f]) for f in range(FIELDS + 1))
RELAY = 56
FLIPPED = (1, 2)
VMEM_LIMIT = 32 * 1024 * 1024
LOAD_FLOPS = 10**10


def density(heat, salt):
    return heat * (-1.0 - 0.15 * heat - 0.2 * salt) + 0.8 * salt


def iota(shape, axis):
    return lax.broadcasted_iota(jnp.int32, shape, axis)


def packet_rows(levels):
    return -(-(4 * levels + ROW[-1]) // 8) * 8


def flags(meta):
    return tuple(meta[i : i + 1, :] == 1 for i in range(4))


def segments(rows):
    size = START[-1]
    return (0, rows // 2, 0), (rows // 2, rows, size), (rows, rows + 8, RELAY), (rows + 8, rows + 16, RELAY + size)


def place_kernel(meta, placed):
    for i in range(5):
        placed[i : i + 1, :] = jnp.broadcast_to(meta[0:1, i : i + 1], (1, placed.shape[1]))
    placed[5:, :] = jnp.zeros((placed.shape[0] - 5, placed.shape[1]), jnp.int32)


def pack_kernel(
    meta, spans, facing, heat, salt, zonal, merid, water, weights, anomaly,
    sums, first, second, east_columns, west_columns,
    top, bottom, back,
):
    levels, rows, cols = heat.shape
    span = [spans[0:1, k : k + 1] for k in range(levels)]
    below = [None] * levels
    total = jnp.zeros((1, 1), jnp.float32)
    for k in reversed(range(levels)):
        below[k] = span[k] * (0.5 * span[k] + total)
        total = total + span[k]
    pair = iota((rows, cols), 1) // 2
    zero = jnp.zeros((rows, cols), jnp.float32)
    press, east, north, east_edge, west_edge = zero, zero, zero, zero, zero
    for k in range(levels):
        press = press + below[k] * density(heat[k], salt[k])
        east = east + span[k] * zonal[k]
        north = north + span[k] * merid[k]
        for q, source in ((k, heat), (levels + k, salt)):
            cells = source[k]
            here = pair == q
            east_edge = jnp.where(here, pltpu.roll(cells, (2 * q + 2) % cols, 1), east_edge)
            west_edge = jnp.where(here, pltpu.roll(cells, 2 * q, 1), west_edge)
            top[2 * q : 2 * q + 2, :] = source[k, rows - 2 :, :]
            bottom[2 * q : 2 * q + 2, :] = source[k, :2, :]
            for i in range(2):
                back[2 * q + i : 2 * q + i + 1, :] = source[k, rows - 1 - i : rows - i, :]
    east_columns[...] = east_edge
    west_columns[...] = west_edge
    sums[0] = press
    sums[1] = east
    sums[2] = north
    fields = (sums.at[0], sums.at[1], sums.at[2], water, weights, anomaly)
    for f, field in enumerate(fields):
        at = 4 * levels + ROW[f]
        deep = DEEP[f]
        top[at : at + deep, :] = field[rows - deep :, :].astype(jnp.float32)
        bottom[at : at + deep, :] = field[:deep, :].astype(jnp.float32)
        for j in range(deep):
            back[at + j : at + j + 1, :] = field[rows - 1 - j : rows - j, :].astype(jnp.float32)
    used = 4 * levels + ROW[-1]
    high = first.shape[0]
    if used < high:
        for packet in (top, bottom, back):
            packet[used:, :] = jnp.zeros((high - used, cols), jnp.float32)
    odd, last, _, _ = flags(meta)
    first[...] = jnp.where(odd, bottom[...], top[...])
    second[...] = jnp.where(last, back[...], jnp.where(odd, top[...], bottom[...]))


def turn_kernel(
    lons, meta, facing, mine, sums, water, weights, anomaly, second, first, east_columns, west_columns,
    ext, to_far, to_near, state_far, state_near, facing_rows, north_rows, south_rows,
):
    rows, cols = sums.shape[1], sums.shape[2]
    tall = ext.shape[1]
    deep = north_rows.shape[0]
    odd, top, lon_odd, bottom = flags(meta)
    from_first = first[...]
    hinge = facing[0:1, 0:1] + 1 + cols * meta[4:5, 0:1] + cols // 2
    block = lax.shift_right_logical(hinge & (lons * cols - 1), cols.bit_length() - 1)
    alone = ((block - 1 - 2 * meta[4:5, 0:1]) & (lons - 1)) == 0
    from_second = jnp.where(top & alone, mine[...], second[...])
    north = jnp.where(odd, from_second, from_first)
    south = jnp.where(bottom, 0.0, jnp.where(odd, from_first, from_second))
    fields = (sums.at[0], sums.at[1], sums.at[2], water, weights, anomaly)
    for f in range(FIELDS):
        at = deep + ROW[f]
        size = DEEP[f]
        ext[f, :rows, :] = fields[f][...].astype(jnp.float32)
        ext[f, rows : rows + size, :] = north[at : at + size]
        ext[f, rows + size : tall - size, :] = jnp.zeros((tall - rows - 2 * size, cols), jnp.float32)
        ext[f, tall - size :, :] = south[at : at + size]
    passed = from_second[deep:]
    size = passed.shape[0]
    half = rows // 2
    lane = iota((half, cols), 1)
    lower = iota((half, cols), 0) >= size
    empty = jnp.zeros((size, cols), jnp.float32)
    spare = jnp.zeros((half - size, cols), jnp.float32)
    relay = lane >= RELAY
    east = jnp.where(relay, jnp.concatenate([pltpu.roll(passed, RELAY, 1), spare], axis=0), 0.0)
    west = jnp.where(relay, jnp.concatenate([passed, spare], axis=0), 0.0)
    for f in range(FIELDS):
        for start, stop, first_lane in segments(rows):
            at = START[f] + first_lane
            here = (lane >= at) & (lane < at + SIDE[f])
            layer = ext[f, start:stop, :]
            to_east = pltpu.roll(layer, (at + SIDE[f]) % cols, 1)
            to_west = pltpu.roll(layer, at, 1)
            if stop - start < half:
                here = here & lower
                to_east = jnp.concatenate([empty, to_east], axis=0)
                to_west = jnp.concatenate([empty, to_west], axis=0)
            east = jnp.where(here, to_east, east)
            west = jnp.where(here, to_west, west)
    to_far[...] = jnp.where(lon_odd, east, west)
    to_near[...] = jnp.where(lon_odd, west, east)
    passed = from_second[:deep]
    spare = jnp.zeros((rows - deep, cols), jnp.float32)
    right_half = iota((rows, cols), 1) >= cols // 2
    east = jnp.where(right_half, jnp.concatenate([pltpu.roll(passed, cols // 2, 1), spare], axis=0), east_columns[...])
    west = jnp.where(right_half, jnp.concatenate([passed, spare], axis=0), west_columns[...])
    state_far[...] = jnp.where(lon_odd, east, west)
    state_near[...] = jnp.where(lon_odd, west, east)
    facing_rows[...] = from_second[deep:]
    north_rows[...] = north[:deep]
    south_rows[...] = south[:deep]


def fold_shift(facing):
    cols = facing.shape[1]
    offset = (facing[0:1, 0:1] + 1) & (cols - 1)
    return jnp.where(offset >= cols // 2, offset - cols, offset)


def fold(shift, west, own, east, beside):
    rows, cols = own.shape
    lane = iota((rows, cols), 1)
    source = cols - 1 - lane
    if beside:
        place = (source + shift) & (cols - 1)
        low = jnp.where(place - cols < shift, west, own)
        merged = jnp.where(place >= cols // 2, low, jnp.where(place >= shift, east, own))
    else:
        merged = jnp.where(source >= cols - shift, west, jnp.where(source < -shift, east, own))
    return jnp.take_along_axis(merged, cols - 1 - ((lane - shift) & (cols - 1)), axis=1)


def shift_kernel(ext, shift):
    rows, cols = ext.shape[1] - 16, ext.shape[2]
    press, zonal, merid, wet, weights, anomaly = (ext[f, :rows, :] for f in range(FIELDS))
    plus_x = lambda cells: pltpu.roll(cells, cols - 1, 1)
    minus_x = lambda cells: pltpu.roll(cells, 1, 1)
    plus_y = lambda cells: pltpu.roll(cells, rows - 1, 0)
    minus_y = lambda cells: pltpu.roll(cells, 1, 0)
    half = 0.5 * TIME_STEP
    east_flow = wet * (zonal - half * (plus_x(press) - minus_x(press)))
    north_flow = wet * (merid - half * (plus_y(press) - minus_y(press)))
    spread = plus_x(east_flow) - minus_x(east_flow) + plus_y(north_flow) - minus_y(north_flow)
    right = wet * (weights * anomaly - 0.5 * spread)
    inverse = 1.0 / (4.0 + weights)
    zero = right * inverse
    one = wet * inverse * (plus_x(zero) + minus_x(zero) + plus_y(zero) + minus_y(zero))
    lane = iota((rows, cols), 1)
    row = iota((rows, cols), 0)
    inside = (lane >= 8) & (lane < cols - 8) & (row >= 8) & (row < rows - 8)
    total = lambda cells: jnp.sum(jnp.sum(jnp.where(inside, cells, 0.0), axis=0, keepdims=True), axis=1, keepdims=True)
    below = total(right * zero)
    good = below > 0.0
    quotient = jnp.where(good, total(right * one) / jnp.where(good, below, 1.0), 0.0)
    shift[...] = jnp.broadcast_to(jnp.clip(quotient, -1.0, 1.0), shift.shape)


def krylov_kernel(meta, facing, shift, ext, facing_rows, from_far, from_near, base, moments, folded):
    tall, cols = ext.shape[1], ext.shape[2]
    rows = base.shape[1]
    size = facing_rows.shape[0]
    _, top, lon_odd, _ = flags(meta)
    west = jnp.where(lon_odd, from_near[...], from_far[...])
    east = jnp.where(lon_odd, from_far[...], from_near[...])
    theta = shift[0:1, 0:1]
    across = fold_shift(facing)
    row = iota((size, cols), 0)
    flips = (row >= ROW[FLIPPED[0]]) & (row < ROW[FLIPPED[-1] + 1])
    for side in range(2):
        cells = fold(across, pltpu.roll(west[:size], cols - RELAY, 1), facing_rows[...], east[:size], side == 1)
        folded[side, :size, :] = jnp.where(flips, -cells, cells)
    folded[:, size:, :] = jnp.zeros((2, folded.shape[1] - size, cols), jnp.float32)
    lane = iota((tall, cols), 1)
    first = lane == 0
    last = lane == cols - 1
    eighth = iota((8, cols), 0)

    def load(f):
        parts = []
        for packet, shift_of in ((west, 2 * cols - SIDE[f]), (east, cols)):
            pieces = []
            for start, stop, first_lane in segments(rows):
                layer = packet[packet.shape[0] - (stop - start) :]
                pieces.append(pltpu.roll(layer, (shift_of - START[f] - first_lane) % cols, 1))
            parts.append(jnp.concatenate(pieces, axis=0))
        a, b = parts
        beside = jnp.where(lane >= cols - SIDE[f], a, jnp.where(lane < SIDE[f], b, 0.0))

        def put(cells, side):
            new = folded[side, ROW[f] : ROW[f] + 8, :]
            new = jnp.where(eighth < DEEP[f], jnp.where(top, new, cells[rows : rows + 8]), 0.0)
            return jnp.concatenate([cells[:rows], new, cells[rows + 8 :]], axis=0)

        return put(ext[f], 0), put(beside, 1)

    def plus_x(pair):
        a, b = (pltpu.roll(part, cols - 1, 1) for part in pair)
        return jnp.where(last, b, a), jnp.where(last, a, b)

    def minus_x(pair):
        a, b = (pltpu.roll(part, 1, 1) for part in pair)
        return jnp.where(first, b, a), jnp.where(first, a, b)

    def plus_y(pair):
        return tuple(pltpu.roll(part, tall - 1, 0) for part in pair)

    def minus_y(pair):
        return tuple(pltpu.roll(part, 1, 0) for part in pair)

    def each(function, *pairs):
        return tuple(function(*parts) for parts in zip(*pairs))

    def neighbours(pair):
        return each(
            lambda a, b, c, d: (a + b) + (c + d), plus_x(pair), minus_x(pair), plus_y(pair), minus_y(pair)
        )

    press, zonal, merid, wet, weights, anomaly = (load(f) for f in range(FIELDS))
    half = 0.5 * TIME_STEP
    flow = lambda w, speed, a, b: w * (speed - half * (a - b))
    east_flow = each(flow, wet, zonal, plus_x(press), minus_x(press))
    north_flow = each(flow, wet, merid, plus_y(press), minus_y(press))
    right = each(
        lambda w, g, n, a, b, c, d: w * (g * n - 0.5 * (a - b + c - d)),
        wet,
        weights,
        anomaly,
        plus_x(east_flow),
        minus_x(east_flow),
        plus_y(north_flow),
        minus_y(north_flow),
    )
    diagonal = each(lambda g: 4.0 + g, weights)
    inverse = each(lambda m: 1.0 / m, diagonal)
    scale = each(lambda w, i: w * i, wet, inverse)
    zero = each(lambda r, i: r * i, right, inverse)
    one = each(lambda a, n, z: a * n - theta * z, scale, neighbours(zero), zero)
    two = each(lambda a, n, z: a * n - theta * z, scale, neighbours(one), one)
    three = scale[0][:rows] * neighbours(two)[0][:rows] - theta * two[0][:rows]
    right, middle = right[0][:rows], diagonal[0][:rows]
    zero, one, two = zero[0][:rows], one[0][:rows], two[0][:rows]
    base[0] = zero
    base[1] = one
    base[2] = two
    weighted_one = middle * one
    weighted_two = middle * two
    products = (
        right * zero,
        right * one,
        right * two,
        right * three,
        weighted_one * one,
        weighted_one * two,
        weighted_one * three,
        weighted_two * two,
        weighted_two * three,
    )
    which = iota((16, cols), 0)
    place = iota((16, cols), 1)
    sums = jnp.where((which == len(products)) & (place == 0), theta, 0.0)
    for k, product in enumerate(products):
        sums = jnp.where(which == k, jnp.sum(product, axis=0, keepdims=True), sums)
    sums = jnp.sum(sums, axis=1, keepdims=True)
    sums = jnp.sum(jnp.where(which == place, sums, 0.0), axis=0, keepdims=True)
    moments[...] = jnp.broadcast_to(sums, moments.shape)


def step_kernel(
    meta, spans, facing, heat, salt, zonal, merid, water, north_came, south_rows, from_far, from_near,
    heat_out, salt_out, zonal_out, merid_out,
    new_heat, new_salt, new_zonal, new_merid, north_rows, sems,
):
    levels, rows, cols = heat.shape
    deep = 4 * levels
    _, top, lon_odd, _ = flags(meta)
    wet = water[...].astype(jnp.float32)
    lane = iota((rows, cols), 1)
    row = iota((rows, cols), 0)
    east = jnp.where(lon_odd, from_far[...], from_near[...])
    west = jnp.where(lon_odd, from_near[...], from_far[...])
    came = north_came[...]
    across = fold(fold_shift(facing), pltpu.roll(west[:deep], cols // 2, 1), came, east[:deep], False)
    north_rows[...] = jnp.where(top, across, came)

    def around(cells, q):
        a = pltpu.roll(east, (cols - 2 * q) % cols, 1)
        b = pltpu.roll(west, (2 * cols - 2 - 2 * q) % cols, 1)
        side = jnp.where(lane < 2, a, b)

        def shift_x(by):
            a = pltpu.roll(cells, by % cols, 1)
            b = pltpu.roll(side, by % cols, 1)
            own = lane >= by if by > 0 else lane < cols + by
            return jnp.where(own, a, b)

        n0 = north_rows[2 * q : 2 * q + 1, :]
        n1 = north_rows[2 * q + 1 : 2 * q + 2, :]
        s0 = south_rows[2 * q + 1 : 2 * q + 2, :]
        s1 = south_rows[2 * q : 2 * q + 1, :]
        north_one = jnp.where(row == rows - 1, n0, pltpu.roll(cells, rows - 1, 0))
        north_two = jnp.where(row == rows - 1, n1, jnp.where(row == rows - 2, n0, pltpu.roll(cells, rows - 2, 0)))
        south_one = jnp.where(row == 0, s0, pltpu.roll(cells, 1, 0))
        south_two = jnp.where(row == 0, s1, jnp.where(row == 1, s0, pltpu.roll(cells, 2, 0)))
        return (shift_x(-1), shift_x(1), shift_x(-2), shift_x(2), north_one, south_one, north_two, south_two)

    def advance(cells, parts, speed_x, speed_y):
        e1, w1, e2, w2, n1, s1, n2, s2 = parts
        grad_east = 8.0 * (e1 - w1) - (e2 - w2)
        grad_north = 8.0 * (n1 - s1) - (n2 - s2)
        laplace = (e1 + w1) + (n1 + s1) - 4.0 * cells
        tendency = (-TIME_STEP / 12.0) * (speed_x * grad_east + speed_y * grad_north) + MIXING * laplace
        return cells + wet * tendency

    stores = ((new_heat, heat_out), (new_salt, salt_out), (new_zonal, zonal_out), (new_merid, merid_out))
    size = levels // sems.shape[1]
    copies = []
    half = 0.5 * TIME_STEP
    above_x = jnp.zeros((rows, cols), jnp.float32)
    above_y = jnp.zeros((rows, cols), jnp.float32)
    for k in range(levels):
        t, s, u, v = heat[k], salt[k], zonal[k], merid[k]
        around_t = around(t, k)
        around_s = around(s, levels + k)
        new_heat[k] = advance(t, around_t, u, v)
        new_salt[k] = advance(s, around_s, u, v)
        span = spans[0:1, k : k + 1]
        layer_x = span * (density(around_t[0], around_s[0]) - density(around_t[1], around_s[1]))
        layer_y = span * (density(around_t[4], around_s[4]) - density(around_t[5], around_s[5]))
        new_zonal[k] = wet * (u - half * (above_x + 0.5 * layer_x))
        new_merid[k] = wet * (v - half * (above_y + 0.5 * layer_y))
        above_x = above_x + layer_x
        above_y = above_y + layer_y
        if (k + 1) % size == 0:
            piece = pl.ds(k + 1 - size, size)
            for i, (near_ref, far_ref) in enumerate(stores):
                copies.append(pltpu.make_async_copy(near_ref.at[piece], far_ref.at[piece], sems.at[i, k // size]))
                copies[-1].start()
    for copy in copies:
        copy.wait()


def surface_kernel(shares, shift, base, surface):
    lanes = shares.shape[1]
    g00, g01, g02, g03, g11, g12, g13, g22, g23, theta = (
        shares[...] if k == 0 else pltpu.roll(shares[...], lanes - k, 1) for k in range(10)
    )
    add = lambda terms: jnp.sum(terms, axis=0, keepdims=True)

    def ratio(a, b):
        good = b > 0.0
        return jnp.where(good, a / jnp.where(good, b, 1.0), 0.0)

    def form(p, h):
        total = 0.0
        for i, a in enumerate(p):
            for j in range(i, len(p)):
                term = a * p[j] * h[i + j]
                total = total + (term if i == j else 2.0 * term)
        return total

    whole = add(g00)
    common = ratio(add(theta * g00 + g01), whole)
    d = theta - common
    mu = [
        whole,
        add(g01 + d * g00),
        add(g11 + d * (2.0 * g01 + d * g00)),
        add(g12 + d * (2.0 * g11 + g02 + d * (3.0 * g01 + d * g00))),
        add(g22 + d * (4.0 * g12 + d * (2.0 * g02 + 4.0 * g11 + d * (4.0 * g01 + d * g00)))),
        add(
            g23
            + d * (3.0 * g22 + 2.0 * g13 + d * (9.0 * g12 + g03 + d * (4.0 * g02 + 6.0 * g11 + d * (5.0 * g01 + d * g00))))
        ),
    ]
    scale = 1.0 - common
    gap = [scale * mu[k] - mu[k + 1] for k in range(5)]
    alpha = ratio(mu[0], gap[0])
    y = [-alpha * ratio(mu[1], mu[0]), alpha]
    x = [alpha, 0.0, 0.0]
    rz = form(y, mu)
    p = [y[0] + ratio(rz, mu[0]), y[1]]
    alpha = ratio(rz, form(p, gap))
    x = [x[0] + alpha * p[0], alpha * p[1], 0.0]
    y = [y[0] - alpha * scale * p[0], y[1] - alpha * (scale * p[1] - p[0]), alpha * p[1]]
    new = form(y, mu)
    beta = ratio(new, rz)
    p = [y[0] + beta * p[0], y[1] + beta * p[1], y[2]]
    alpha = ratio(new, form(p, gap))
    x = [x[0] + alpha * p[0], x[1] + alpha * p[1], alpha * p[2]]
    d = shift[0:1, :] - common
    x = [x[0] + d * (x[1] + d * x[2]), x[1] + 2.0 * d * x[2], x[2]]
    x = [value[0:1, 0:1] for value in x]
    surface[...] = x[0] * base[0] + x[1] * base[1] + x[2] * base[2]


def call(kernel, outs, flops, moved, name, out_space=pltpu.VMEM, scratch=(), types=jnp.float32):
    def run(*args):
        return pl.pallas_call(
            kernel,
            out_shape=[jax.ShapeDtypeStruct(shape, types) for shape in outs],
            in_specs=[pl.BlockSpec(memory_space=pltpu.VMEM)] * len(args),
            out_specs=[pl.BlockSpec(memory_space=out_space)] * len(outs),
            scratch_shapes=list(scratch),
            cost_estimate=pl.CostEstimate(flops=flops, bytes_accessed=moved, transcendentals=0),
            compiler_params=pltpu.CompilerParams(vmem_limit_bytes=VMEM_LIMIT),
            name=name,
        )(*args)

    return run


def body(
    warmth_deviation,
    saltiness_deviation,
    easterly_speed,
    poleward_speed,
    stratum_spans,
    water_indicator,
    opposite_counterpart,
    elevation_weights,
    elevation_anomaly,
):
    lons, lats = lax.axis_size("lon"), lax.axis_size("lat")
    lon, lat = lax.axis_index("lon"), lax.axis_index("lat")
    levels, rows, cols = warmth_deviation.shape
    high = packet_rows(levels)
    assert cols & (cols - 1) == 0 and rows >= 24 and rows // 2 == high - 4 * levels + 8 and 4 * levels <= cols // 2 and 2 * START[-1] <= min(RELAY, cols - RELAY) and cols == 128
    tall = rows + 16
    width = cols * lons
    flat = lambda i, j: (i % lons) * lats + j

    place = (lax.rem(lat, 2), lat == lats - 1, lax.rem(lon, 2), lat == 0, lon)
    meta = jnp.stack([value.astype(jnp.int32) for value in place]).reshape(1, 5)
    (meta,) = call(place_kernel, [(8, cols)], LOAD_FLOPS, 16, "place", types=jnp.int32)(meta)

    spans = stratum_spans.reshape(1, levels)
    facing = opposite_counterpart.reshape(1, cols)
    state = (warmth_deviation, saltiness_deviation, easterly_speed, poleward_speed)
    flat_state = (water_indicator, elevation_weights, elevation_anomaly)
    cells = levels * rows * cols
    sums, first, second, east_columns, west_columns = call(
        pack_kernel,
        [(3, rows, cols), (high, cols), (high, cols), (rows, cols), (rows, cols)],
        12 * cells,
        16 * cells,
        "level_sums",
        scratch=[pltpu.VMEM((high, cols), jnp.float32)] * 3,
    )(meta, spans, facing, *state, *flat_state)

    axes = ("lon", "lat")
    pairs_first = [(flat(i, j), flat(i, j ^ 1)) for i in range(lons) for j in range(lats)]
    pairs_inner = [
        (flat(i, a), flat(i, b))
        for i in range(lons)
        for j in range(1, lats - 1, 2)
        for a, b in ((j, j + 1), (j + 1, j))
    ] + [(flat(i, 0), flat(i ^ 1, 0)) for i in range(lons)]

    counterpart, first = lax.optimization_barrier((opposite_counterpart, first))
    hinge = lax.rem(counterpart[0] + 1 + cols * lon, width)
    block = lax.rem((hinge + cols // 2) // cols, lons)

    deep = 4 * levels

    def exchange(block, first, mine):
        partner = [(block - 1 - i) % lons for i in range(lons)]
        partner = [i + lons // 2 if i == p else p for i, p in enumerate(partner)]
        pairs_fold = [(flat(p, lats - 1), flat(i, lats - 1)) for i, p in enumerate(partner)]
        second = lax.ppermute(mine, axes, pairs_inner + pairs_fold)
        first = lax.ppermute(first, axes, pairs_first)
        return call(
            functools.partial(turn_kernel, lons),
            [
                (FIELDS, tall, cols),
                *[(rows // 2, cols)] * 2,
                *[(rows, cols)] * 2,
                (high - deep, cols),
                *[(deep, cols)] * 2,
            ],
            FIELDS * tall * cols,
            4 * 4 * FIELDS * tall * cols,
            "row_halos",
        )(meta, facing, mine, sums, *flat_state, second, first, east_columns, west_columns)

    ext, to_far, to_near, state_far, state_near, facing_rows, north_rows, south_rows = lax.switch(
        block, [functools.partial(exchange, s) for s in range(lons)], first, second
    )

    near = lambda cells: lax.ppermute(cells, "lon", [(i, i ^ 1) for i in range(lons)])
    far = lambda cells: lax.ppermute(cells, "lon", [(i, (i + 1 if i % 2 else i - 1) % lons) for i in range(lons)])
    from_far, from_near = far(to_far), near(to_near)
    state_far, state_near = far(state_far), near(state_near)

    (shift,) = call(shift_kernel, [(8, cols)], 60 * rows * cols, 24 * rows * cols, "basis_shift")(ext)

    count = lons * lats
    base, moments = call(
        krylov_kernel,
        [(3, rows, cols), (count, cols)],
        200 * tall * cols,
        4 * 12 * tall * cols,
        "krylov",
        scratch=[pltpu.VMEM((2, high - deep + 8, cols), jnp.float32)],
    )(meta, facing, shift, ext, facing_rows, from_far, from_near)

    chunks = 5 if levels % 5 == 0 else 1
    new_heat, new_salt, new_zonal, new_merid = call(
        step_kernel,
        [(levels, rows, cols)] * 4,
        120 * cells,
        32 * cells,
        "levels_step",
        out_space=pltpu.HBM,
        scratch=[
            *[pltpu.VMEM((levels, rows, cols), jnp.float32)] * 4,
            pltpu.VMEM((deep, cols), jnp.float32),
            pltpu.SemaphoreType.DMA((4, chunks)),
        ],
    )(meta, spans, facing, *state, water_indicator, north_rows, south_rows, state_far, state_near)

    shares = lax.all_to_all(moments, axes, 0, 0, tiled=True)
    (surface,) = call(surface_kernel, [(rows, cols)], 6 * rows * cols, 16 * rows * cols, "surface")(shares, shift, base)
    return (new_heat, new_salt, new_zonal, new_merid, surface)


def solution(mesh):
    for axis in mesh.shape.values():
        assert axis > 1 and axis & (axis - 1) == 0
    levels = P(None, "lat", "lon")
    flat = P("lat", "lon")
    return jax.shard_map(
        body,
        mesh=mesh,
        in_specs=(levels, levels, levels, levels, P(), flat, P("lon"), flat, flat),
        out_specs=(levels, levels, levels, levels, flat),
        check_vma=False,
    )
```

```python
import functools

import jax
import jax.numpy as jnp
from jax import lax
from jax.experimental import pallas as pl
from jax.experimental.pallas import tpu as pltpu
from jax.sharding import PartitionSpec as P

TIME_STEP = 0.1
MIXING = 0.1

DEEP = (5, 3, 4, 4, 3, 3)
SIDE = (5, 4, 3, 4, 3, 3)
FIELDS = len(SIDE)
ROW = tuple(sum(DEEP[:f]) for f in range(FIELDS + 1))
START = tuple(sum(SIDE[:f]) for f in range(FIELDS + 1))
RELAY = 56
FLIPPED = (1, 2)
VMEM_LIMIT = 32 * 1024 * 1024
LOAD_FLOPS = 10**10


def density(heat, salt):
    return heat * (-1.0 - 0.15 * heat - 0.2 * salt) + 0.8 * salt


def iota(shape, axis):
    return lax.broadcasted_iota(jnp.int32, shape, axis)


def packet_rows(levels):
    return -(-(4 * levels + ROW[-1]) // 8) * 8


def flags(meta):
    return tuple(meta[i : i + 1, :] == 1 for i in range(4))


def segments(rows):
    size = START[-1]
    return (0, rows // 2, 0), (rows // 2, rows, size), (rows, rows + 8, RELAY), (rows + 8, rows + 16, RELAY + size)


def place_kernel(meta, placed):
    for i in range(5):
        placed[i : i + 1, :] = jnp.broadcast_to(meta[0:1, i : i + 1], (1, placed.shape[1]))
    placed[5:, :] = jnp.zeros((placed.shape[0] - 5, placed.shape[1]), jnp.int32)


def pack_kernel(
    meta, spans, facing, heat, salt, zonal, merid, water, weights, anomaly,
    sums, first, second, kept, east_columns, west_columns,
    top, bottom, back,
):
    levels, rows, cols = heat.shape
    span = [spans[0:1, k : k + 1] for k in range(levels)]
    below = [None] * levels
    total = jnp.zeros((1, 1), jnp.float32)
    for k in reversed(range(levels)):
        below[k] = span[k] * (0.5 * span[k] + total)
        total = total + span[k]
    pair = iota((rows, cols), 1) // 2
    zero = jnp.zeros((rows, cols), jnp.float32)
    press, east, north, east_edge, west_edge = zero, zero, zero, zero, zero
    for k in range(levels):
        press = press + below[k] * density(heat[k], salt[k])
        east = east + span[k] * zonal[k]
        north = north + span[k] * merid[k]
        for q, source in ((k, heat), (levels + k, salt)):
            cells = source[k]
            here = pair == q
            east_edge = jnp.where(here, pltpu.roll(cells, (2 * q + 2) % cols, 1), east_edge)
            west_edge = jnp.where(here, pltpu.roll(cells, 2 * q, 1), west_edge)
            top[2 * q : 2 * q + 2, :] = source[k, rows - 2 :, :]
            bottom[2 * q : 2 * q + 2, :] = source[k, :2, :]
            for i in range(2):
                back[2 * q + i : 2 * q + i + 1, :] = source[k, rows - 1 - i : rows - i, :]
    east_columns[...] = east_edge
    west_columns[...] = west_edge
    sums[0] = press
    sums[1] = east
    sums[2] = north
    fields = (sums.at[0], sums.at[1], sums.at[2], water, weights, anomaly)
    for f, field in enumerate(fields):
        at = 4 * levels + ROW[f]
        deep = DEEP[f]
        top[at : at + deep, :] = field[rows - deep :, :].astype(jnp.float32)
        bottom[at : at + deep, :] = field[:deep, :].astype(jnp.float32)
        for j in range(deep):
            back[at + j : at + j + 1, :] = field[rows - 1 - j : rows - j, :].astype(jnp.float32)
    used = 4 * levels + ROW[-1]
    high = first.shape[0]
    if used < high:
        for packet in (top, bottom, back):
            packet[used:, :] = jnp.zeros((high - used, cols), jnp.float32)
    odd, last, _, _ = flags(meta)
    first[...] = jnp.where(odd, bottom[...], top[...])
    packet = jnp.where(last, back[...], jnp.where(odd, top[...], bottom[...]))
    second[...] = packet
    kept[...] = packet


def turn_kernel(
    lons, meta, facing, mine, sums, water, weights, anomaly, second, first, east_columns, west_columns,
    ext, to_far, to_near, state_far, state_near, facing_rows, north_rows, south_rows,
):
    rows, cols = sums.shape[1], sums.shape[2]
    tall = ext.shape[1]
    deep = north_rows.shape[0]
    odd, top, lon_odd, bottom = flags(meta)
    from_first = first[...]
    hinge = facing[0:1, 0:1] + 1 + cols * meta[4:5, 0:1] + cols // 2
    block = lax.shift_right_logical(hinge & (lons * cols - 1), cols.bit_length() - 1)
    alone = ((block - 1 - 2 * meta[4:5, 0:1]) & (lons - 1)) == 0
    from_second = jnp.where(top & alone, mine[...], second[...])
    north = jnp.where(odd, from_second, from_first)
    south = jnp.where(bottom, 0.0, jnp.where(odd, from_first, from_second))
    fields = (sums.at[0], sums.at[1], sums.at[2], water, weights, anomaly)
    for f in range(FIELDS):
        at = deep + ROW[f]
        size = DEEP[f]
        ext[f, :rows, :] = fields[f][...].astype(jnp.float32)
        ext[f, rows : rows + size, :] = north[at : at + size]
        ext[f, rows + size : tall - size, :] = jnp.zeros((tall - rows - 2 * size, cols), jnp.float32)
        ext[f, tall - size :, :] = south[at : at + size]
    passed = from_second[deep:]
    size = passed.shape[0]
    half = rows // 2
    lane = iota((half, cols), 1)
    lower = iota((half, cols), 0) >= size
    empty = jnp.zeros((size, cols), jnp.float32)
    spare = jnp.zeros((half - size, cols), jnp.float32)
    relay = lane >= RELAY
    east = jnp.where(relay, jnp.concatenate([pltpu.roll(passed, RELAY, 1), spare], axis=0), 0.0)
    west = jnp.where(relay, jnp.concatenate([passed, spare], axis=0), 0.0)
    for f in range(FIELDS):
        for start, stop, first_lane in segments(rows):
            at = START[f] + first_lane
            here = (lane >= at) & (lane < at + SIDE[f])
            layer = ext[f, start:stop, :]
            to_east = pltpu.roll(layer, (at + SIDE[f]) % cols, 1)
            to_west = pltpu.roll(layer, at, 1)
            if stop - start < half:
                here = here & lower
                to_east = jnp.concatenate([empty, to_east], axis=0)
                to_west = jnp.concatenate([empty, to_west], axis=0)
            east = jnp.where(here, to_east, east)
            west = jnp.where(here, to_west, west)
    to_far[...] = jnp.where(lon_odd, east, west)
    to_near[...] = jnp.where(lon_odd, west, east)
    passed = from_second[:deep]
    spare = jnp.zeros((rows - deep, cols), jnp.float32)
    right_half = iota((rows, cols), 1) >= cols // 2
    east = jnp.where(right_half, jnp.concatenate([pltpu.roll(passed, cols // 2, 1), spare], axis=0), east_columns[...])
    west = jnp.where(right_half, jnp.concatenate([passed, spare], axis=0), west_columns[...])
    state_far[...] = jnp.where(lon_odd, east, west)
    state_near[...] = jnp.where(lon_odd, west, east)
    facing_rows[...] = from_second[deep:]
    north_rows[...] = north[:deep]
    south_rows[...] = south[:deep]


def fold_shift(facing):
    cols = facing.shape[1]
    offset = (facing[0:1, 0:1] + 1) & (cols - 1)
    return jnp.where(offset >= cols // 2, offset - cols, offset)


def fold(shift, west, own, east, beside):
    rows, cols = own.shape
    lane = iota((rows, cols), 1)
    source = cols - 1 - lane
    if beside:
        place = (source + shift) & (cols - 1)
        low = jnp.where(place - cols < shift, west, own)
        merged = jnp.where(place >= cols // 2, low, jnp.where(place >= shift, east, own))
    else:
        merged = jnp.where(source >= cols - shift, west, jnp.where(source < -shift, east, own))
    return jnp.take_along_axis(merged, cols - 1 - ((lane - shift) & (cols - 1)), axis=1)


def shift_kernel(ext, shift):
    rows, cols = ext.shape[1] - 16, ext.shape[2]
    press, zonal, merid, wet, weights, anomaly = (ext[f, :rows, :] for f in range(FIELDS))
    plus_x = lambda cells: pltpu.roll(cells, cols - 1, 1)
    minus_x = lambda cells: pltpu.roll(cells, 1, 1)
    plus_y = lambda cells: pltpu.roll(cells, rows - 1, 0)
    minus_y = lambda cells: pltpu.roll(cells, 1, 0)
    half = 0.5 * TIME_STEP
    east_flow = wet * (zonal - half * (plus_x(press) - minus_x(press)))
    north_flow = wet * (merid - half * (plus_y(press) - minus_y(press)))
    spread = plus_x(east_flow) - minus_x(east_flow) + plus_y(north_flow) - minus_y(north_flow)
    right = wet * (weights * anomaly - 0.5 * spread)
    inverse = 1.0 / (4.0 + weights)
    zero = right * inverse
    one = wet * inverse * (plus_x(zero) + minus_x(zero) + plus_y(zero) + minus_y(zero))
    lane = iota((rows, cols), 1)
    row = iota((rows, cols), 0)
    inside = (lane >= 8) & (lane < cols - 8) & (row >= 8) & (row < rows - 8)
    total = lambda cells: jnp.sum(jnp.sum(jnp.where(inside, cells, 0.0), axis=0, keepdims=True), axis=1, keepdims=True)
    below = total(right * zero)
    good = below > 0.0
    quotient = jnp.where(good, total(right * one) / jnp.where(good, below, 1.0), 0.0)
    shift[...] = jnp.broadcast_to(jnp.clip(quotient, -1.0, 1.0), shift.shape)


def krylov_kernel(meta, facing, shift, ext, facing_rows, from_far, from_near, base, moments, folded):
    tall, cols = ext.shape[1], ext.shape[2]
    rows = base.shape[1]
    size = facing_rows.shape[0]
    _, top, lon_odd, _ = flags(meta)
    west = jnp.where(lon_odd, from_near[...], from_far[...])
    east = jnp.where(lon_odd, from_far[...], from_near[...])
    theta = shift[0:1, 0:1]
    across = fold_shift(facing)
    row = iota((size, cols), 0)
    flips = (row >= ROW[FLIPPED[0]]) & (row < ROW[FLIPPED[-1] + 1])
    for side in range(2):
        cells = fold(across, pltpu.roll(west[:size], cols - RELAY, 1), facing_rows[...], east[:size], side == 1)
        folded[side, :size, :] = jnp.where(flips, -cells, cells)
    folded[:, size:, :] = jnp.zeros((2, folded.shape[1] - size, cols), jnp.float32)
    lane = iota((tall, cols), 1)
    first = lane == 0
    last = lane == cols - 1
    eighth = iota((8, cols), 0)

    def load(f):
        parts = []
        for packet, shift_of in ((west, 2 * cols - SIDE[f]), (east, cols)):
            pieces = []
            for start, stop, first_lane in segments(rows):
                layer = packet[packet.shape[0] - (stop - start) :]
                pieces.append(pltpu.roll(layer, (shift_of - START[f] - first_lane) % cols, 1))
            parts.append(jnp.concatenate(pieces, axis=0))
        a, b = parts
        beside = jnp.where(lane >= cols - SIDE[f], a, jnp.where(lane < SIDE[f], b, 0.0))

        def put(cells, side):
            new = folded[side, ROW[f] : ROW[f] + 8, :]
            new = jnp.where(eighth < DEEP[f], jnp.where(top, new, cells[rows : rows + 8]), 0.0)
            return jnp.concatenate([cells[:rows], new, cells[rows + 8 :]], axis=0)

        return put(ext[f], 0), put(beside, 1)

    def plus_x(pair):
        a, b = (pltpu.roll(part, cols - 1, 1) for part in pair)
        return jnp.where(last, b, a), jnp.where(last, a, b)

    def minus_x(pair):
        a, b = (pltpu.roll(part, 1, 1) for part in pair)
        return jnp.where(first, b, a), jnp.where(first, a, b)

    def plus_y(pair):
        return tuple(pltpu.roll(part, tall - 1, 0) for part in pair)

    def minus_y(pair):
        return tuple(pltpu.roll(part, 1, 0) for part in pair)

    def each(function, *pairs):
        return tuple(function(*parts) for parts in zip(*pairs))

    def neighbours(pair):
        return each(
            lambda a, b, c, d: (a + b) + (c + d), plus_x(pair), minus_x(pair), plus_y(pair), minus_y(pair)
        )

    press, zonal, merid, wet, weights, anomaly = (load(f) for f in range(FIELDS))
    half = 0.5 * TIME_STEP
    flow = lambda w, speed, a, b: w * (speed - half * (a - b))
    east_flow = each(flow, wet, zonal, plus_x(press), minus_x(press))
    north_flow = each(flow, wet, merid, plus_y(press), minus_y(press))
    right = each(
        lambda w, g, n, a, b, c, d: w * (g * n - 0.5 * (a - b + c - d)),
        wet,
        weights,
        anomaly,
        plus_x(east_flow),
        minus_x(east_flow),
        plus_y(north_flow),
        minus_y(north_flow),
    )
    diagonal = each(lambda g: 4.0 + g, weights)
    inverse = each(lambda m: 1.0 / m, diagonal)
    scale = each(lambda w, i: w * i, wet, inverse)
    zero = each(lambda r, i: r * i, right, inverse)
    one = each(lambda a, n, z: a * n - theta * z, scale, neighbours(zero), zero)
    two = each(lambda a, n, z: a * n - theta * z, scale, neighbours(one), one)
    three = scale[0][:rows] * neighbours(two)[0][:rows] - theta * two[0][:rows]
    right, middle = right[0][:rows], diagonal[0][:rows]
    zero, one, two = zero[0][:rows], one[0][:rows], two[0][:rows]
    base[0] = zero
    base[1] = one
    base[2] = two
    weighted_one = middle * one
    weighted_two = middle * two
    products = (
        right * zero,
        right * one,
        right * two,
        right * three,
        weighted_one * one,
        weighted_one * two,
        weighted_one * three,
        weighted_two * two,
        weighted_two * three,
    )
    which = iota((16, cols), 0)
    place = iota((16, cols), 1)
    sums = jnp.where((which == len(products)) & (place == 0), theta, 0.0)
    for k, product in enumerate(products):
        sums = jnp.where(which == k, jnp.sum(product, axis=0, keepdims=True), sums)
    sums = jnp.sum(sums, axis=1, keepdims=True)
    sums = jnp.sum(jnp.where(which == place, sums, 0.0), axis=0, keepdims=True)
    moments[...] = jnp.broadcast_to(sums, moments.shape)


def step_kernel(
    meta, spans, facing, heat, salt, zonal, merid, water, north_came, south_rows, from_far, from_near,
    heat_out, salt_out, zonal_out, merid_out,
    new_heat, new_salt, new_zonal, new_merid, north_rows, sems,
):
    levels, rows, cols = heat.shape
    deep = 4 * levels
    _, top, lon_odd, _ = flags(meta)
    wet = water[...].astype(jnp.float32)
    lane = iota((rows, cols), 1)
    row = iota((rows, cols), 0)
    east = jnp.where(lon_odd, from_far[...], from_near[...])
    west = jnp.where(lon_odd, from_near[...], from_far[...])
    came = north_came[...]
    across = fold(fold_shift(facing), pltpu.roll(west[:deep], cols // 2, 1), came, east[:deep], False)
    north_rows[...] = jnp.where(top, across, came)

    def around(cells, q):
        a = pltpu.roll(east, (cols - 2 * q) % cols, 1)
        b = pltpu.roll(west, (2 * cols - 2 - 2 * q) % cols, 1)
        side = jnp.where(lane < 2, a, b)

        def shift_x(by):
            a = pltpu.roll(cells, by % cols, 1)
            b = pltpu.roll(side, by % cols, 1)
            own = lane >= by if by > 0 else lane < cols + by
            return jnp.where(own, a, b)

        n0 = north_rows[2 * q : 2 * q + 1, :]
        n1 = north_rows[2 * q + 1 : 2 * q + 2, :]
        s0 = south_rows[2 * q + 1 : 2 * q + 2, :]
        s1 = south_rows[2 * q : 2 * q + 1, :]
        north_one = jnp.where(row == rows - 1, n0, pltpu.roll(cells, rows - 1, 0))
        north_two = jnp.where(row == rows - 1, n1, jnp.where(row == rows - 2, n0, pltpu.roll(cells, rows - 2, 0)))
        south_one = jnp.where(row == 0, s0, pltpu.roll(cells, 1, 0))
        south_two = jnp.where(row == 0, s1, jnp.where(row == 1, s0, pltpu.roll(cells, 2, 0)))
        return (shift_x(-1), shift_x(1), shift_x(-2), shift_x(2), north_one, south_one, north_two, south_two)

    def advance(cells, parts, speed_x, speed_y):
        e1, w1, e2, w2, n1, s1, n2, s2 = parts
        grad_east = 8.0 * (e1 - w1) - (e2 - w2)
        grad_north = 8.0 * (n1 - s1) - (n2 - s2)
        laplace = (e1 + w1) + (n1 + s1) - 4.0 * cells
        tendency = (-TIME_STEP / 12.0) * (speed_x * grad_east + speed_y * grad_north) + MIXING * laplace
        return cells + wet * tendency

    stores = ((new_heat, heat_out), (new_salt, salt_out), (new_zonal, zonal_out), (new_merid, merid_out))
    size = levels // sems.shape[1]
    copies = []
    half = 0.5 * TIME_STEP
    above_x = jnp.zeros((rows, cols), jnp.float32)
    above_y = jnp.zeros((rows, cols), jnp.float32)
    for k in range(levels):
        t, s, u, v = heat[k], salt[k], zonal[k], merid[k]
        around_t = around(t, k)
        around_s = around(s, levels + k)
        new_heat[k] = advance(t, around_t, u, v)
        new_salt[k] = advance(s, around_s, u, v)
        span = spans[0:1, k : k + 1]
        layer_x = span * (density(around_t[0], around_s[0]) - density(around_t[1], around_s[1]))
        layer_y = span * (density(around_t[4], around_s[4]) - density(around_t[5], around_s[5]))
        new_zonal[k] = wet * (u - half * (above_x + 0.5 * layer_x))
        new_merid[k] = wet * (v - half * (above_y + 0.5 * layer_y))
        above_x = above_x + layer_x
        above_y = above_y + layer_y
        if (k + 1) % size == 0:
            piece = pl.ds(k + 1 - size, size)
            for i, (near_ref, far_ref) in enumerate(stores):
                copies.append(pltpu.make_async_copy(near_ref.at[piece], far_ref.at[piece], sems.at[i, k // size]))
                copies[-1].start()
    for copy in copies:
        copy.wait()


def surface_kernel(shares, shift, base, surface):
    lanes = shares.shape[1]
    g00, g01, g02, g03, g11, g12, g13, g22, g23, theta = (
        shares[...] if k == 0 else pltpu.roll(shares[...], lanes - k, 1) for k in range(10)
    )
    add = lambda terms: jnp.sum(terms, axis=0, keepdims=True)

    def ratio(a, b):
        good = b > 0.0
        return jnp.where(good, a / jnp.where(good, b, 1.0), 0.0)

    def form(p, h):
        total = 0.0
        for i, a in enumerate(p):
            for j in range(i, len(p)):
                term = a * p[j] * h[i + j]
                total = total + (term if i == j else 2.0 * term)
        return total

    whole = add(g00)
    common = ratio(add(theta * g00 + g01), whole)
    d = theta - common
    mu = [
        whole,
        add(g01 + d * g00),
        add(g11 + d * (2.0 * g01 + d * g00)),
        add(g12 + d * (2.0 * g11 + g02 + d * (3.0 * g01 + d * g00))),
        add(g22 + d * (4.0 * g12 + d * (2.0 * g02 + 4.0 * g11 + d * (4.0 * g01 + d * g00)))),
        add(
            g23
            + d * (3.0 * g22 + 2.0 * g13 + d * (9.0 * g12 + g03 + d * (4.0 * g02 + 6.0 * g11 + d * (5.0 * g01 + d * g00))))
        ),
    ]
    scale = 1.0 - common
    gap = [scale * mu[k] - mu[k + 1] for k in range(5)]
    alpha = ratio(mu[0], gap[0])
    y = [-alpha * ratio(mu[1], mu[0]), alpha]
    x = [alpha, 0.0, 0.0]
    rz = form(y, mu)
    p = [y[0] + ratio(rz, mu[0]), y[1]]
    alpha = ratio(rz, form(p, gap))
    x = [x[0] + alpha * p[0], alpha * p[1], 0.0]
    y = [y[0] - alpha * scale * p[0], y[1] - alpha * (scale * p[1] - p[0]), alpha * p[1]]
    new = form(y, mu)
    beta = ratio(new, rz)
    p = [y[0] + beta * p[0], y[1] + beta * p[1], y[2]]
    alpha = ratio(new, form(p, gap))
    x = [x[0] + alpha * p[0], x[1] + alpha * p[1], alpha * p[2]]
    d = shift[0:1, :] - common
    x = [x[0] + d * (x[1] + d * x[2]), x[1] + 2.0 * d * x[2], x[2]]
    x = [value[0:1, 0:1] for value in x]
    surface[...] = x[0] * base[0] + x[1] * base[1] + x[2] * base[2]


def call(kernel, outs, flops, moved, name, out_space=pltpu.VMEM, scratch=(), types=jnp.float32):
    def run(*args):
        return pl.pallas_call(
            kernel,
            out_shape=[jax.ShapeDtypeStruct(shape, types) for shape in outs],
            in_specs=[pl.BlockSpec(memory_space=pltpu.VMEM)] * len(args),
            out_specs=[pl.BlockSpec(memory_space=out_space)] * len(outs),
            scratch_shapes=list(scratch),
            cost_estimate=pl.CostEstimate(flops=flops, bytes_accessed=moved, transcendentals=0),
            compiler_params=pltpu.CompilerParams(vmem_limit_bytes=VMEM_LIMIT),
            name=name,
        )(*args)

    return run


def body(
    warmth_deviation,
    saltiness_deviation,
    easterly_speed,
    poleward_speed,
    stratum_spans,
    water_indicator,
    opposite_counterpart,
    elevation_weights,
    elevation_anomaly,
):
    lons, lats = lax.axis_size("lon"), lax.axis_size("lat")
    lon, lat = lax.axis_index("lon"), lax.axis_index("lat")
    levels, rows, cols = warmth_deviation.shape
    high = packet_rows(levels)
    assert cols & (cols - 1) == 0 and rows >= 24 and rows // 2 == high - 4 * levels + 8 and 4 * levels <= cols // 2 and 2 * START[-1] <= min(RELAY, cols - RELAY) and cols == 128
    tall = rows + 16
    width = cols * lons
    flat = lambda i, j: (i % lons) * lats + j

    place = (lax.rem(lat, 2), lat == lats - 1, lax.rem(lon, 2), lat == 0, lon)
    meta = jnp.stack([value.astype(jnp.int32) for value in place]).reshape(1, 5)
    (meta,) = call(place_kernel, [(8, cols)], LOAD_FLOPS, 16, "place", types=jnp.int32)(meta)

    spans = stratum_spans.reshape(1, levels)
    facing = opposite_counterpart.reshape(1, cols)
    state = (warmth_deviation, saltiness_deviation, easterly_speed, poleward_speed)
    flat_state = (water_indicator, elevation_weights, elevation_anomaly)
    cells = levels * rows * cols
    sums, first, second, kept, east_columns, west_columns = call(
        pack_kernel,
        [(3, rows, cols), *[(high, cols)] * 3, (rows, cols), (rows, cols)],
        12 * cells,
        16 * cells,
        "level_sums",
        scratch=[pltpu.VMEM((high, cols), jnp.float32)] * 3,
    )(meta, spans, facing, *state, *flat_state)

    axes = ("lon", "lat")
    pairs_first = [(flat(i, j), flat(i, j ^ 1)) for i in range(lons) for j in range(lats)]
    pairs_inner = [
        (flat(i, a), flat(i, b))
        for i in range(lons)
        for j in range(1, lats - 1, 2)
        for a, b in ((j, j + 1), (j + 1, j))
    ] + [(flat(i, 0), flat(i ^ 1, 0)) for i in range(lons)]

    counterpart, first = lax.optimization_barrier((opposite_counterpart, first))
    hinge = lax.rem(counterpart[0] + 1 + cols * lon, width)
    block = lax.rem((hinge + cols // 2) // cols, lons)

    deep = 4 * levels

    def exchange(block, first, second):
        partner = [(block - 1 - i) % lons for i in range(lons)]
        partner = [i + lons // 2 if i == p else p for i, p in enumerate(partner)]
        pairs_fold = [(flat(p, lats - 1), flat(i, lats - 1)) for i, p in enumerate(partner)]
        second = lax.ppermute(second, axes, pairs_inner + pairs_fold)
        first = lax.ppermute(first, axes, pairs_first)
        return call(
            functools.partial(turn_kernel, lons),
            [
                (FIELDS, tall, cols),
                *[(rows // 2, cols)] * 2,
                *[(rows, cols)] * 2,
                (high - deep, cols),
                *[(deep, cols)] * 2,
            ],
            FIELDS * tall * cols,
            4 * 4 * FIELDS * tall * cols,
            "row_halos",
        )(meta, facing, kept, sums, *flat_state, second, first, east_columns, west_columns)

    ext, to_far, to_near, state_far, state_near, facing_rows, north_rows, south_rows = lax.switch(
        block, [functools.partial(exchange, s) for s in range(lons)], first, second
    )

    near = lambda cells: lax.ppermute(cells, "lon", [(i, i ^ 1) for i in range(lons)])
    far = lambda cells: lax.ppermute(cells, "lon", [(i, (i + 1 if i % 2 else i - 1) % lons) for i in range(lons)])
    from_far, from_near = far(to_far), near(to_near)
    state_far, state_near = far(state_far), near(state_near)

    (shift,) = call(shift_kernel, [(8, cols)], 60 * rows * cols, 24 * rows * cols, "basis_shift")(ext)

    count = lons * lats
    base, moments = call(
        krylov_kernel,
        [(3, rows, cols), (count, cols)],
        200 * tall * cols,
        4 * 12 * tall * cols,
        "krylov",
        scratch=[pltpu.VMEM((2, high - deep + 8, cols), jnp.float32)],
    )(meta, facing, shift, ext, facing_rows, from_far, from_near)

    chunks = 5 if levels % 5 == 0 else 1
    new_heat, new_salt, new_zonal, new_merid = call(
        step_kernel,
        [(levels, rows, cols)] * 4,
        120 * cells,
        32 * cells,
        "levels_step",
        out_space=pltpu.HBM,
        scratch=[
            *[pltpu.VMEM((levels, rows, cols), jnp.float32)] * 4,
            pltpu.VMEM((deep, cols), jnp.float32),
            pltpu.SemaphoreType.DMA((4, chunks)),
        ],
    )(meta, spans, facing, *state, water_indicator, north_rows, south_rows, state_far, state_near)

    shares = lax.all_to_all(moments, axes, 0, 0, tiled=True)
    (surface,) = call(surface_kernel, [(rows, cols)], 6 * rows * cols, 16 * rows * cols, "surface")(shares, shift, base)
    return (new_heat, new_salt, new_zonal, new_merid, surface)


def solution(mesh):
    for axis in mesh.shape.values():
        assert axis > 1 and axis & (axis - 1) == 0
    levels = P(None, "lat", "lon")
    flat = P("lat", "lon")
    return jax.shard_map(
        body,
        mesh=mesh,
        in_specs=(levels, levels, levels, levels, P(), flat, P("lon"), flat, flat),
        out_specs=(levels, levels, levels, levels, flat),
        check_vma=False,
    )
```

```python
import functools

import jax
import jax.numpy as jnp
from jax import lax
from jax.experimental import pallas as pl
from jax.experimental.pallas import tpu as pltpu
from jax.sharding import PartitionSpec as P

TIME_STEP = 0.1
MIXING = 0.1

DEEP = (5, 3, 4, 4, 3, 3)
SIDE = (5, 4, 3, 4, 3, 3)
FIELDS = len(SIDE)
ROW = tuple(sum(DEEP[:f]) for f in range(FIELDS + 1))
START = tuple(sum(SIDE[:f]) for f in range(FIELDS + 1))
RELAY = 56
FLIPPED = (1, 2)
VMEM_LIMIT = 32 * 1024 * 1024
LOAD_FLOPS = 10**10


def density(heat, salt):
    return heat * (-1.0 - 0.15 * heat - 0.2 * salt) + 0.8 * salt


def iota(shape, axis):
    return lax.broadcasted_iota(jnp.int32, shape, axis)


def packet_rows(levels):
    return -(-(4 * levels + ROW[-1]) // 8) * 8


def flags(meta):
    return tuple(meta[i : i + 1, :] == 1 for i in range(4))


def segments(rows):
    size = START[-1]
    return (0, rows // 2, 0), (rows // 2, rows, size), (rows, rows + 8, RELAY), (rows + 8, rows + 16, RELAY + size)


def place_kernel(meta, placed):
    for i in range(5):
        placed[i : i + 1, :] = jnp.broadcast_to(meta[0:1, i : i + 1], (1, placed.shape[1]))
    placed[5:, :] = jnp.zeros((placed.shape[0] - 5, placed.shape[1]), jnp.int32)


def pack_kernel(
    meta, spans, facing, heat, salt, zonal, merid, water, weights, anomaly,
    sums, first, second, kept, east_columns, west_columns,
    top, bottom, back,
):
    levels, rows, cols = heat.shape
    span = [spans[0:1, k : k + 1] for k in range(levels)]
    below = [None] * levels
    total = jnp.zeros((1, 1), jnp.float32)
    for k in reversed(range(levels)):
        below[k] = span[k] * (0.5 * span[k] + total)
        total = total + span[k]
    pair = iota((rows, cols), 1) // 2
    zero = jnp.zeros((rows, cols), jnp.float32)
    press, east, north, east_edge, west_edge = zero, zero, zero, zero, zero
    for k in range(levels):
        press = press + below[k] * density(heat[k], salt[k])
        east = east + span[k] * zonal[k]
        north = north + span[k] * merid[k]
        for q, source in ((k, heat), (levels + k, salt)):
            cells = source[k]
            here = pair == q
            east_edge = jnp.where(here, pltpu.roll(cells, (2 * q + 2) % cols, 1), east_edge)
            west_edge = jnp.where(here, pltpu.roll(cells, 2 * q, 1), west_edge)
            top[2 * q : 2 * q + 2, :] = source[k, rows - 2 :, :]
            bottom[2 * q : 2 * q + 2, :] = source[k, :2, :]
            for i in range(2):
                back[2 * q + i : 2 * q + i + 1, :] = source[k, rows - 1 - i : rows - i, :]
    east_columns[...] = east_edge
    west_columns[...] = west_edge
    sums[0] = press
    sums[1] = east
    sums[2] = north
    fields = (sums.at[0], sums.at[1], sums.at[2], water, weights, anomaly)
    for f, field in enumerate(fields):
        at = 4 * levels + ROW[f]
        deep = DEEP[f]
        top[at : at + deep, :] = field[rows - deep :, :].astype(jnp.float32)
        bottom[at : at + deep, :] = field[:deep, :].astype(jnp.float32)
        for j in range(deep):
            back[at + j : at + j + 1, :] = field[rows - 1 - j : rows - j, :].astype(jnp.float32)
    used = 4 * levels + ROW[-1]
    high = first.shape[0]
    if used < high:
        for packet in (top, bottom, back):
            packet[used:, :] = jnp.zeros((high - used, cols), jnp.float32)
    odd, last, _, _ = flags(meta)
    first[...] = jnp.where(odd, bottom[...], top[...])
    packet = jnp.where(last, back[...], jnp.where(odd, top[...], bottom[...]))
    second[...] = packet
    kept[...] = packet


def turn_kernel(
    lons, meta, facing, mine, sums, water, weights, anomaly, second, first, east_columns, west_columns,
    ext, to_far, to_near, state_far, state_near, facing_rows, north_rows, south_rows,
):
    rows, cols = sums.shape[1], sums.shape[2]
    tall = ext.shape[1]
    deep = north_rows.shape[0]
    odd, top, lon_odd, bottom = flags(meta)
    from_first = first[...]
    hinge = facing[0:1, 0:1] + 1 + cols * meta[4:5, 0:1] + cols // 2
    block = lax.shift_right_logical(hinge & (lons * cols - 1), cols.bit_length() - 1)
    alone = ((block - 1 - 2 * meta[4:5, 0:1]) & (lons - 1)) == 0
    from_second = jnp.where(top & alone, mine[...], second[...])
    north = jnp.where(odd, from_second, from_first)
    south = jnp.where(bottom, 0.0, jnp.where(odd, from_first, from_second))
    fields = (sums.at[0], sums.at[1], sums.at[2], water, weights, anomaly)
    for f in range(FIELDS):
        at = deep + ROW[f]
        size = DEEP[f]
        ext[f, :rows, :] = fields[f][...].astype(jnp.float32)
        ext[f, rows : rows + size, :] = north[at : at + size]
        ext[f, rows + size : tall - size, :] = jnp.zeros((tall - rows - 2 * size, cols), jnp.float32)
        ext[f, tall - size :, :] = south[at : at + size]
    passed = from_second[deep:]
    size = passed.shape[0]
    half = rows // 2
    lane = iota((half, cols), 1)
    lower = iota((half, cols), 0) >= size
    empty = jnp.zeros((size, cols), jnp.float32)
    spare = jnp.zeros((half - size, cols), jnp.float32)
    relay = lane >= RELAY
    east = jnp.where(relay, jnp.concatenate([pltpu.roll(passed, RELAY, 1), spare], axis=0), 0.0)
    west = jnp.where(relay, jnp.concatenate([passed, spare], axis=0), 0.0)
    for f in range(FIELDS):
        for start, stop, first_lane in segments(rows):
            at = START[f] + first_lane
            here = (lane >= at) & (lane < at + SIDE[f])
            layer = ext[f, start:stop, :]
            to_east = pltpu.roll(layer, (at + SIDE[f]) % cols, 1)
            to_west = pltpu.roll(layer, at, 1)
            if stop - start < half:
                here = here & lower
                to_east = jnp.concatenate([empty, to_east], axis=0)
                to_west = jnp.concatenate([empty, to_west], axis=0)
            east = jnp.where(here, to_east, east)
            west = jnp.where(here, to_west, west)
    to_far[...] = jnp.where(lon_odd, east, west)
    to_near[...] = jnp.where(lon_odd, west, east)
    passed = from_second[:deep]
    spare = jnp.zeros((rows - deep, cols), jnp.float32)
    right_half = iota((rows, cols), 1) >= cols // 2
    east = jnp.where(right_half, jnp.concatenate([pltpu.roll(passed, cols // 2, 1), spare], axis=0), east_columns[...])
    west = jnp.where(right_half, jnp.concatenate([passed, spare], axis=0), west_columns[...])
    state_far[...] = jnp.where(lon_odd, east, west)
    state_near[...] = jnp.where(lon_odd, west, east)
    facing_rows[...] = from_second[deep:]
    north_rows[...] = north[:deep]
    south_rows[...] = south[:deep]


def fold_shift(facing):
    cols = facing.shape[1]
    offset = (facing[0:1, 0:1] + 1) & (cols - 1)
    return jnp.where(offset >= cols // 2, offset - cols, offset)


def fold(shift, west, own, east, beside):
    rows, cols = own.shape
    lane = iota((rows, cols), 1)
    source = cols - 1 - lane
    if beside:
        place = (source + shift) & (cols - 1)
        low = jnp.where(place - cols < shift, west, own)
        merged = jnp.where(place >= cols // 2, low, jnp.where(place >= shift, east, own))
    else:
        merged = jnp.where(source >= cols - shift, west, jnp.where(source < -shift, east, own))
    return jnp.take_along_axis(merged, cols - 1 - ((lane - shift) & (cols - 1)), axis=1)


def shift_kernel(ext, shift):
    rows, cols = ext.shape[1] - 16, ext.shape[2]
    press, zonal, merid, wet, weights, anomaly = (ext[f, :rows, :] for f in range(FIELDS))
    plus_x = lambda cells: pltpu.roll(cells, cols - 1, 1)
    minus_x = lambda cells: pltpu.roll(cells, 1, 1)
    plus_y = lambda cells: pltpu.roll(cells, rows - 1, 0)
    minus_y = lambda cells: pltpu.roll(cells, 1, 0)
    half = 0.5 * TIME_STEP
    east_flow = wet * (zonal - half * (plus_x(press) - minus_x(press)))
    north_flow = wet * (merid - half * (plus_y(press) - minus_y(press)))
    spread = plus_x(east_flow) - minus_x(east_flow) + plus_y(north_flow) - minus_y(north_flow)
    right = wet * (weights * anomaly - 0.5 * spread)
    inverse = 1.0 / (4.0 + weights)
    zero = right * inverse
    one = wet * inverse * (plus_x(zero) + minus_x(zero) + plus_y(zero) + minus_y(zero))
    lane = iota((rows, cols), 1)
    row = iota((rows, cols), 0)
    inside = (lane >= 8) & (lane < cols - 8) & (row >= 8) & (row < rows - 8)
    total = lambda cells: jnp.sum(jnp.sum(jnp.where(inside, cells, 0.0), axis=0, keepdims=True), axis=1, keepdims=True)
    below = total(right * zero)
    good = below > 0.0
    quotient = jnp.where(good, total(right * one) / jnp.where(good, below, 1.0), 0.0)
    shift[...] = jnp.broadcast_to(jnp.clip(quotient, -1.0, 1.0), shift.shape)


def krylov_kernel(meta, facing, shift, ext, facing_rows, from_far, from_near, base, moments, folded):
    tall, cols = ext.shape[1], ext.shape[2]
    rows = base.shape[1]
    size = facing_rows.shape[0]
    _, top, lon_odd, _ = flags(meta)
    west = jnp.where(lon_odd, from_near[...], from_far[...])
    east = jnp.where(lon_odd, from_far[...], from_near[...])
    theta = shift[0:1, 0:1]
    across = fold_shift(facing)
    row = iota((size, cols), 0)
    flips = (row >= ROW[FLIPPED[0]]) & (row < ROW[FLIPPED[-1] + 1])
    for side in range(2):
        cells = fold(across, pltpu.roll(west[:size], cols - RELAY, 1), facing_rows[...], east[:size], side == 1)
        folded[side, :size, :] = jnp.where(flips, -cells, cells)
    folded[:, size:, :] = jnp.zeros((2, folded.shape[1] - size, cols), jnp.float32)
    lane = iota((tall, cols), 1)
    first = lane == 0
    last = lane == cols - 1
    eighth = iota((8, cols), 0)

    def load(f):
        parts = []
        for packet, shift_of in ((west, 2 * cols - SIDE[f]), (east, cols)):
            pieces = []
            for start, stop, first_lane in segments(rows):
                layer = packet[packet.shape[0] - (stop - start) :]
                pieces.append(pltpu.roll(layer, (shift_of - START[f] - first_lane) % cols, 1))
            parts.append(jnp.concatenate(pieces, axis=0))
        a, b = parts
        beside = jnp.where(lane >= cols - SIDE[f], a, jnp.where(lane < SIDE[f], b, 0.0))

        def put(cells, side):
            new = folded[side, ROW[f] : ROW[f] + 8, :]
            new = jnp.where(eighth < DEEP[f], jnp.where(top, new, cells[rows : rows + 8]), 0.0)
            return jnp.concatenate([cells[:rows], new, cells[rows + 8 :]], axis=0)

        return put(ext[f], 0), put(beside, 1)

    def plus_x(pair):
        a, b = (pltpu.roll(part, cols - 1, 1) for part in pair)
        return jnp.where(last, b, a), jnp.where(last, a, b)

    def minus_x(pair):
        a, b = (pltpu.roll(part, 1, 1) for part in pair)
        return jnp.where(first, b, a), jnp.where(first, a, b)

    def plus_y(pair):
        return tuple(pltpu.roll(part, tall - 1, 0) for part in pair)

    def minus_y(pair):
        return tuple(pltpu.roll(part, 1, 0) for part in pair)

    def each(function, *pairs):
        return tuple(function(*parts) for parts in zip(*pairs))

    def neighbours(pair):
        return each(
            lambda a, b, c, d: (a + b) + (c + d), plus_x(pair), minus_x(pair), plus_y(pair), minus_y(pair)
        )

    press, zonal, merid, wet, weights, anomaly = (load(f) for f in range(FIELDS))
    half = 0.5 * TIME_STEP
    flow = lambda w, speed, a, b: w * (speed - half * (a - b))
    east_flow = each(flow, wet, zonal, plus_x(press), minus_x(press))
    north_flow = each(flow, wet, merid, plus_y(press), minus_y(press))
    right = each(
        lambda w, g, n, a, b, c, d: w * (g * n - 0.5 * (a - b + c - d)),
        wet,
        weights,
        anomaly,
        plus_x(east_flow),
        minus_x(east_flow),
        plus_y(north_flow),
        minus_y(north_flow),
    )
    diagonal = each(lambda g: 4.0 + g, weights)
    inverse = each(lambda m: 1.0 / m, diagonal)
    scale = each(lambda w, i: w * i, wet, inverse)
    zero = each(lambda r, i: r * i, right, inverse)
    one = each(lambda a, n, z: a * n - theta * z, scale, neighbours(zero), zero)
    two = each(lambda a, n, z: a * n - theta * z, scale, neighbours(one), one)
    three = scale[0][:rows] * neighbours(two)[0][:rows] - theta * two[0][:rows]
    right, middle = right[0][:rows], diagonal[0][:rows]
    zero, one, two = zero[0][:rows], one[0][:rows], two[0][:rows]
    base[0] = zero
    base[1] = one
    base[2] = two
    weighted_one = middle * one
    weighted_two = middle * two
    products = (
        right * zero,
        right * one,
        right * two,
        right * three,
        weighted_one * one,
        weighted_one * two,
        weighted_one * three,
        weighted_two * two,
        weighted_two * three,
    )
    which = iota((16, cols), 0)
    place = iota((16, cols), 1)
    sums = jnp.where((which == len(products)) & (place == 0), theta, 0.0)
    for k, product in enumerate(products):
        sums = jnp.where(which == k, jnp.sum(product, axis=0, keepdims=True), sums)
    sums = jnp.sum(sums, axis=1, keepdims=True)
    sums = jnp.sum(jnp.where(which == place, sums, 0.0), axis=0, keepdims=True)
    moments[...] = jnp.broadcast_to(sums, moments.shape)


def step_kernel(
    meta, spans, facing, heat, salt, zonal, merid, water, north_came, south_rows, from_far, from_near,
    heat_out, salt_out, zonal_out, merid_out,
    new_heat, new_salt, new_zonal, new_merid, north_rows, sems,
):
    levels, rows, cols = heat.shape
    deep = 4 * levels
    _, top, lon_odd, _ = flags(meta)
    wet = water[...].astype(jnp.float32)
    lane = iota((rows, cols), 1)
    row = iota((rows, cols), 0)
    east = jnp.where(lon_odd, from_far[...], from_near[...])
    west = jnp.where(lon_odd, from_near[...], from_far[...])
    came = north_came[...]
    across = fold(fold_shift(facing), pltpu.roll(west[:deep], cols // 2, 1), came, east[:deep], False)
    north_rows[...] = jnp.where(top, across, came)

    def around(cells, q):
        a = pltpu.roll(east, (cols - 2 * q) % cols, 1)
        b = pltpu.roll(west, (2 * cols - 2 - 2 * q) % cols, 1)
        side = jnp.where(lane < 2, a, b)

        def shift_x(by):
            a = pltpu.roll(cells, by % cols, 1)
            b = pltpu.roll(side, by % cols, 1)
            own = lane >= by if by > 0 else lane < cols + by
            return jnp.where(own, a, b)

        n0 = north_rows[2 * q : 2 * q + 1, :]
        n1 = north_rows[2 * q + 1 : 2 * q + 2, :]
        s0 = south_rows[2 * q + 1 : 2 * q + 2, :]
        s1 = south_rows[2 * q : 2 * q + 1, :]
        north_one = jnp.where(row == rows - 1, n0, pltpu.roll(cells, rows - 1, 0))
        north_two = jnp.where(row == rows - 1, n1, jnp.where(row == rows - 2, n0, pltpu.roll(cells, rows - 2, 0)))
        south_one = jnp.where(row == 0, s0, pltpu.roll(cells, 1, 0))
        south_two = jnp.where(row == 0, s1, jnp.where(row == 1, s0, pltpu.roll(cells, 2, 0)))
        return (shift_x(-1), shift_x(1), shift_x(-2), shift_x(2), north_one, south_one, north_two, south_two)

    def advance(cells, parts, speed_x, speed_y):
        e1, w1, e2, w2, n1, s1, n2, s2 = parts
        grad_east = 8.0 * (e1 - w1) - (e2 - w2)
        grad_north = 8.0 * (n1 - s1) - (n2 - s2)
        laplace = (e1 + w1) + (n1 + s1) - 4.0 * cells
        tendency = (-TIME_STEP / 12.0) * (speed_x * grad_east + speed_y * grad_north) + MIXING * laplace
        return cells + wet * tendency

    stores = ((new_heat, heat_out), (new_salt, salt_out), (new_zonal, zonal_out), (new_merid, merid_out))
    size = levels // sems.shape[1]
    copies = []
    half = 0.5 * TIME_STEP
    above_x = jnp.zeros((rows, cols), jnp.float32)
    above_y = jnp.zeros((rows, cols), jnp.float32)
    for k in range(levels):
        t, s, u, v = heat[k], salt[k], zonal[k], merid[k]
        around_t = around(t, k)
        around_s = around(s, levels + k)
        new_heat[k] = advance(t, around_t, u, v)
        new_salt[k] = advance(s, around_s, u, v)
        span = spans[0:1, k : k + 1]
        layer_x = span * (density(around_t[0], around_s[0]) - density(around_t[1], around_s[1]))
        layer_y = span * (density(around_t[4], around_s[4]) - density(around_t[5], around_s[5]))
        new_zonal[k] = wet * (u - half * (above_x + 0.5 * layer_x))
        new_merid[k] = wet * (v - half * (above_y + 0.5 * layer_y))
        above_x = above_x + layer_x
        above_y = above_y + layer_y
        if (k + 1) % size == 0:
            piece = pl.ds(k + 1 - size, size)
            for i, (near_ref, far_ref) in enumerate(stores):
                copies.append(pltpu.make_async_copy(near_ref.at[piece], far_ref.at[piece], sems.at[i, k // size]))
                copies[-1].start()
    for copy in copies:
        copy.wait()


def surface_kernel(shares, shift, base, surface):
    lanes = shares.shape[1]
    g00, g01, g02, g03, g11, g12, g13, g22, g23, theta = (
        shares[...] if k == 0 else pltpu.roll(shares[...], lanes - k, 1) for k in range(10)
    )
    add = lambda terms: jnp.sum(terms, axis=0, keepdims=True)

    def ratio(a, b):
        good = b > 0.0
        return jnp.where(good, a / jnp.where(good, b, 1.0), 0.0)

    def form(p, h):
        total = 0.0
        for i, a in enumerate(p):
            for j in range(i, len(p)):
                term = a * p[j] * h[i + j]
                total = total + (term if i == j else 2.0 * term)
        return total

    whole = add(g00)
    common = ratio(add(theta * g00 + g01), whole)
    d = theta - common
    mu = [
        whole,
        add(g01 + d * g00),
        add(g11 + d * (2.0 * g01 + d * g00)),
        add(g12 + d * (2.0 * g11 + g02 + d * (3.0 * g01 + d * g00))),
        add(g22 + d * (4.0 * g12 + d * (2.0 * g02 + 4.0 * g11 + d * (4.0 * g01 + d * g00)))),
        add(
            g23
            + d * (3.0 * g22 + 2.0 * g13 + d * (9.0 * g12 + g03 + d * (4.0 * g02 + 6.0 * g11 + d * (5.0 * g01 + d * g00))))
        ),
    ]
    scale = 1.0 - common
    gap = [scale * mu[k] - mu[k + 1] for k in range(5)]
    alpha = ratio(mu[0], gap[0])
    y = [-alpha * ratio(mu[1], mu[0]), alpha]
    x = [alpha, 0.0, 0.0]
    rz = form(y, mu)
    p = [y[0] + ratio(rz, mu[0]), y[1]]
    alpha = ratio(rz, form(p, gap))
    x = [x[0] + alpha * p[0], alpha * p[1], 0.0]
    y = [y[0] - alpha * scale * p[0], y[1] - alpha * (scale * p[1] - p[0]), alpha * p[1]]
    new = form(y, mu)
    beta = ratio(new, rz)
    p = [y[0] + beta * p[0], y[1] + beta * p[1], y[2]]
    alpha = ratio(new, form(p, gap))
    x = [x[0] + alpha * p[0], x[1] + alpha * p[1], alpha * p[2]]
    d = shift[0:1, :] - common
    x = [x[0] + d * (x[1] + d * x[2]), x[1] + 2.0 * d * x[2], x[2]]
    x = [value[0:1, 0:1] for value in x]
    surface[...] = x[0] * base[0] + x[1] * base[1] + x[2] * base[2]


def call(kernel, outs, flops, moved, name, out_space=pltpu.VMEM, scratch=(), types=jnp.float32):
    def run(*args):
        return pl.pallas_call(
            kernel,
            out_shape=[jax.ShapeDtypeStruct(shape, types) for shape in outs],
            in_specs=[pl.BlockSpec(memory_space=pltpu.VMEM)] * len(args),
            out_specs=[pl.BlockSpec(memory_space=out_space)] * len(outs),
            scratch_shapes=list(scratch),
            cost_estimate=pl.CostEstimate(flops=flops, bytes_accessed=moved, transcendentals=0),
            compiler_params=pltpu.CompilerParams(vmem_limit_bytes=VMEM_LIMIT),
            name=name,
        )(*args)

    return run


def body(
    warmth_deviation,
    saltiness_deviation,
    easterly_speed,
    poleward_speed,
    stratum_spans,
    water_indicator,
    opposite_counterpart,
    elevation_weights,
    elevation_anomaly,
):
    lons, lats = lax.axis_size("lon"), lax.axis_size("lat")
    lon, lat = lax.axis_index("lon"), lax.axis_index("lat")
    levels, rows, cols = warmth_deviation.shape
    high = packet_rows(levels)
    assert cols & (cols - 1) == 0 and rows >= 24 and rows // 2 == high - 4 * levels + 8 and 4 * levels <= cols // 2 and 2 * START[-1] <= min(RELAY, cols - RELAY) and cols == 128
    tall = rows + 16
    width = cols * lons
    flat = lambda i, j: (i % lons) * lats + j

    place = (lax.rem(lat, 2), lat == lats - 1, lax.rem(lon, 2), lat == 0, lon)
    meta = jnp.stack([value.astype(jnp.int32) for value in place]).reshape(1, 5)
    (meta,) = call(place_kernel, [(8, cols)], LOAD_FLOPS, 16, "place", types=jnp.int32)(meta)

    spans = stratum_spans.reshape(1, levels)
    facing = opposite_counterpart.reshape(1, cols)
    state = (warmth_deviation, saltiness_deviation, easterly_speed, poleward_speed)
    flat_state = (water_indicator, elevation_weights, elevation_anomaly)
    cells = levels * rows * cols
    sums, first, second, kept, east_columns, west_columns = call(
        pack_kernel,
        [(3, rows, cols), *[(high, cols)] * 3, (rows, cols), (rows, cols)],
        12 * cells,
        16 * cells,
        "level_sums",
        scratch=[pltpu.VMEM((high, cols), jnp.float32)] * 3,
    )(meta, spans, facing, *state, *flat_state)

    axes = ("lon", "lat")
    pairs_first = [(flat(i, j), flat(i, j ^ 1)) for i in range(lons) for j in range(lats)]
    pairs_inner = [
        (flat(i, a), flat(i, b))
        for i in range(lons)
        for j in range(1, lats - 1, 2)
        for a, b in ((j, j + 1), (j + 1, j))
    ] + [(flat(i, 0), flat(i ^ 1, 0)) for i in range(lons)]

    counterpart, first = lax.optimization_barrier((opposite_counterpart, first))
    hinge = lax.rem(counterpart[0] + 1 + cols * lon, width)
    block = lax.rem((hinge + cols // 2) // cols, lons)

    deep = 4 * levels

    def exchange(block, first, second):
        partner = [(block - 1 - i) % lons for i in range(lons)]
        partner = [i + lons // 2 if i == p else p for i, p in enumerate(partner)]
        pairs_fold = [(flat(p, lats - 1), flat(i, lats - 1)) for i, p in enumerate(partner)]
        second = lax.ppermute(second, axes, pairs_inner + pairs_fold)
        first = lax.ppermute(first, axes, pairs_first)
        return call(
            functools.partial(turn_kernel, lons),
            [
                (FIELDS, tall, cols),
                *[(rows // 2, cols)] * 2,
                *[(rows, cols)] * 2,
                (high - deep, cols),
                *[(deep, cols)] * 2,
            ],
            FIELDS * tall * cols,
            4 * 4 * FIELDS * tall * cols,
            "row_halos",
        )(meta, facing, kept, sums, *flat_state, second, first, east_columns, west_columns)

    ext, to_far, to_near, state_far, state_near, facing_rows, north_rows, south_rows = lax.switch(
        block, [functools.partial(exchange, s) for s in range(lons)], first, second
    )

    near = lambda cells: lax.ppermute(cells, "lon", [(i, i ^ 1) for i in range(lons)])
    far = lambda cells: lax.ppermute(cells, "lon", [(i, (i + 1 if i % 2 else i - 1) % lons) for i in range(lons)])
    from_far, from_near = far(to_far), near(to_near)
    state_far, state_near = far(state_far), near(state_near)

    (shift,) = call(shift_kernel, [(8, cols)], 60 * rows * cols, 24 * rows * cols, "basis_shift")(ext)

    count = lons * lats
    base, moments = call(
        krylov_kernel,
        [(3, rows, cols), (count, cols)],
        200 * tall * cols,
        4 * 12 * tall * cols,
        "krylov",
        scratch=[pltpu.VMEM((2, high - deep + 8, cols), jnp.float32)],
    )(meta, facing, shift, ext, facing_rows, from_far, from_near)

    chunks = 5 if levels % 5 == 0 else 1
    new_heat, new_salt, new_zonal, new_merid = call(
        step_kernel,
        [(levels, rows, cols)] * 4,
        120 * cells,
        32 * cells,
        "levels_step",
        out_space=pltpu.HBM,
        scratch=[
            *[pltpu.VMEM((levels, rows, cols), jnp.float32)] * 4,
            pltpu.VMEM((deep, cols), jnp.float32),
            pltpu.SemaphoreType.DMA((4, chunks)),
        ],
    )(meta, spans, facing, *state, water_indicator, north_rows, south_rows, state_far, state_near)

    shares = lax.all_to_all(moments, ("lat", "lon"), 0, 0, tiled=True)
    (surface,) = call(surface_kernel, [(rows, cols)], 6 * rows * cols, 16 * rows * cols, "surface")(shares, shift, base)
    return (new_heat, new_salt, new_zonal, new_merid, surface)


def solution(mesh):
    for axis in mesh.shape.values():
        assert axis > 1 and axis & (axis - 1) == 0
    levels = P(None, "lat", "lon")
    flat = P("lat", "lon")
    return jax.shard_map(
        body,
        mesh=mesh,
        in_specs=(levels, levels, levels, levels, P(), flat, P("lon"), flat, flat),
        out_specs=(levels, levels, levels, levels, flat),
        check_vma=False,
    )
```

```python
import functools

import jax
import jax.numpy as jnp
from jax import lax
from jax.experimental import pallas as pl
from jax.experimental.pallas import tpu as pltpu
from jax.sharding import PartitionSpec as P

TIME_STEP = 0.1
MIXING = 0.1

DEEP = (5, 3, 4, 4, 3, 3)
SIDE = (5, 4, 3, 4, 3, 3)
FIELDS = len(SIDE)
ROW = tuple(sum(DEEP[:f]) for f in range(FIELDS + 1))
START = tuple(sum(SIDE[:f]) for f in range(FIELDS + 1))
RELAY = 56
FLIPPED = (1, 2)
VMEM_LIMIT = 32 * 1024 * 1024
LOAD_FLOPS = 10**10


def density(heat, salt):
    return heat * (-1.0 - 0.15 * heat - 0.2 * salt) + 0.8 * salt


def iota(shape, axis):
    return lax.broadcasted_iota(jnp.int32, shape, axis)


def packet_rows(levels):
    return -(-(4 * levels + ROW[-1]) // 8) * 8


def flags(meta):
    return tuple(meta[i : i + 1, :] == 1 for i in range(4))


def segments(rows):
    size = START[-1]
    return (0, rows // 2, 0), (rows // 2, rows, size), (rows, rows + 8, RELAY), (rows + 8, rows + 16, RELAY + size)


def place_kernel(meta, placed):
    for i in range(5):
        placed[i : i + 1, :] = jnp.broadcast_to(meta[0:1, i : i + 1], (1, placed.shape[1]))
    placed[5:, :] = jnp.zeros((placed.shape[0] - 5, placed.shape[1]), jnp.int32)


def pack_kernel(
    meta, spans, facing, heat, salt, zonal, merid, water, weights, anomaly,
    sums, first, second, kept, east_columns, west_columns,
    top, bottom, back,
):
    levels, rows, cols = heat.shape
    span = [spans[0:1, k : k + 1] for k in range(levels)]
    below = [None] * levels
    total = jnp.zeros((1, 1), jnp.float32)
    for k in reversed(range(levels)):
        below[k] = span[k] * (0.5 * span[k] + total)
        total = total + span[k]
    pair = iota((rows, cols), 1) // 2
    zero = jnp.zeros((rows, cols), jnp.float32)
    press, east, north, east_edge, west_edge = zero, zero, zero, zero, zero
    for k in range(levels):
        press = press + below[k] * density(heat[k], salt[k])
        east = east + span[k] * zonal[k]
        north = north + span[k] * merid[k]
        for q, source in ((k, heat), (levels + k, salt)):
            cells = source[k]
            here = pair == q
            east_edge = jnp.where(here, pltpu.roll(cells, (2 * q + 2) % cols, 1), east_edge)
            west_edge = jnp.where(here, pltpu.roll(cells, 2 * q, 1), west_edge)
            top[2 * q : 2 * q + 2, :] = source[k, rows - 2 :, :]
            bottom[2 * q : 2 * q + 2, :] = source[k, :2, :]
            for i in range(2):
                back[2 * q + i : 2 * q + i + 1, :] = source[k, rows - 1 - i : rows - i, :]
    east_columns[...] = east_edge
    west_columns[...] = west_edge
    sums[0] = press
    sums[1] = east
    sums[2] = north
    fields = (sums.at[0], sums.at[1], sums.at[2], water, weights, anomaly)
    for f, field in enumerate(fields):
        at = 4 * levels + ROW[f]
        deep = DEEP[f]
        top[at : at + deep, :] = field[rows - deep :, :].astype(jnp.float32)
        bottom[at : at + deep, :] = field[:deep, :].astype(jnp.float32)
        for j in range(deep):
            back[at + j : at + j + 1, :] = field[rows - 1 - j : rows - j, :].astype(jnp.float32)
    used = 4 * levels + ROW[-1]
    high = first.shape[0]
    if used < high:
        for packet in (top, bottom, back):
            packet[used:, :] = jnp.zeros((high - used, cols), jnp.float32)
    odd, last, _, _ = flags(meta)
    first[...] = jnp.where(odd, bottom[...], top[...])
    packet = jnp.where(last, back[...], jnp.where(odd, top[...], bottom[...]))
    second[...] = packet
    kept[...] = packet


def turn_kernel(
    lons, meta, facing, mine, sums, water, weights, anomaly, second, first, east_columns, west_columns,
    ext, to_far, to_near, state_far, state_near, facing_rows, north_rows, south_rows,
):
    rows, cols = sums.shape[1], sums.shape[2]
    tall = ext.shape[1]
    deep = north_rows.shape[0]
    odd, top, lon_odd, bottom = flags(meta)
    from_first = first[...]
    hinge = facing[0:1, 0:1] + 1 + cols * meta[4:5, 0:1] + cols // 2
    block = lax.shift_right_logical(hinge & (lons * cols - 1), cols.bit_length() - 1)
    alone = ((block - 1 - 2 * meta[4:5, 0:1]) & (lons - 1)) == 0
    from_second = jnp.where(top & alone, mine[...], second[...])
    north = jnp.where(odd, from_second, from_first)
    south = jnp.where(bottom, 0.0, jnp.where(odd, from_first, from_second))
    fields = (sums.at[0], sums.at[1], sums.at[2], water, weights, anomaly)
    for f in range(FIELDS):
        at = deep + ROW[f]
        size = DEEP[f]
        ext[f, :rows, :] = fields[f][...].astype(jnp.float32)
        ext[f, rows : rows + size, :] = north[at : at + size]
        ext[f, rows + size : tall - size, :] = jnp.zeros((tall - rows - 2 * size, cols), jnp.float32)
        ext[f, tall - size :, :] = south[at : at + size]
    passed = from_second[deep:]
    size = passed.shape[0]
    half = rows // 2
    lane = iota((half, cols), 1)
    lower = iota((half, cols), 0) >= size
    empty = jnp.zeros((size, cols), jnp.float32)
    spare = jnp.zeros((half - size, cols), jnp.float32)
    relay = lane >= RELAY
    east = jnp.where(relay, jnp.concatenate([pltpu.roll(passed, RELAY, 1), spare], axis=0), 0.0)
    west = jnp.where(relay, jnp.concatenate([passed, spare], axis=0), 0.0)
    for f in range(FIELDS):
        for start, stop, first_lane in segments(rows):
            at = START[f] + first_lane
            here = (lane >= at) & (lane < at + SIDE[f])
            layer = ext[f, start:stop, :]
            to_east = pltpu.roll(layer, (at + SIDE[f]) % cols, 1)
            to_west = pltpu.roll(layer, at, 1)
            if stop - start < half:
                here = here & lower
                to_east = jnp.concatenate([empty, to_east], axis=0)
                to_west = jnp.concatenate([empty, to_west], axis=0)
            east = jnp.where(here, to_east, east)
            west = jnp.where(here, to_west, west)
    to_far[...] = jnp.where(lon_odd, east, west)
    to_near[...] = jnp.where(lon_odd, west, east)
    passed = from_second[:deep]
    spare = jnp.zeros((rows - deep, cols), jnp.float32)
    right_half = iota((rows, cols), 1) >= cols // 2
    east = jnp.where(right_half, jnp.concatenate([pltpu.roll(passed, cols // 2, 1), spare], axis=0), east_columns[...])
    west = jnp.where(right_half, jnp.concatenate([passed, spare], axis=0), west_columns[...])
    state_far[...] = jnp.where(lon_odd, east, west)
    state_near[...] = jnp.where(lon_odd, west, east)
    facing_rows[...] = from_second[deep:]
    north_rows[...] = north[:deep]
    south_rows[...] = south[:deep]


def fold_shift(facing):
    cols = facing.shape[1]
    offset = (facing[0:1, 0:1] + 1) & (cols - 1)
    return jnp.where(offset >= cols // 2, offset - cols, offset)


def fold(shift, west, own, east, beside):
    rows, cols = own.shape
    lane = iota((rows, cols), 1)
    source = cols - 1 - lane
    if beside:
        place = (source + shift) & (cols - 1)
        low = jnp.where(place - cols < shift, west, own)
        merged = jnp.where(place >= cols // 2, low, jnp.where(place >= shift, east, own))
    else:
        merged = jnp.where(source >= cols - shift, west, jnp.where(source < -shift, east, own))
    return jnp.take_along_axis(merged, cols - 1 - ((lane - shift) & (cols - 1)), axis=1)


def shift_kernel(ext, shift):
    rows, cols = ext.shape[1] - 16, ext.shape[2]
    press, zonal, merid, wet, weights, anomaly = (ext[f, :rows, :] for f in range(FIELDS))
    plus_x = lambda cells: pltpu.roll(cells, cols - 1, 1)
    minus_x = lambda cells: pltpu.roll(cells, 1, 1)
    plus_y = lambda cells: pltpu.roll(cells, rows - 1, 0)
    minus_y = lambda cells: pltpu.roll(cells, 1, 0)
    half = 0.5 * TIME_STEP
    east_flow = wet * (zonal - half * (plus_x(press) - minus_x(press)))
    north_flow = wet * (merid - half * (plus_y(press) - minus_y(press)))
    spread = plus_x(east_flow) - minus_x(east_flow) + plus_y(north_flow) - minus_y(north_flow)
    right = wet * (weights * anomaly - 0.5 * spread)
    inverse = 1.0 / (4.0 + weights)
    zero = right * inverse
    one = wet * inverse * (plus_x(zero) + minus_x(zero) + plus_y(zero) + minus_y(zero))
    lane = iota((rows, cols), 1)
    row = iota((rows, cols), 0)
    inside = (lane >= 8) & (lane < cols - 8) & (row >= 8) & (row < rows - 8)
    total = lambda cells: jnp.sum(jnp.sum(jnp.where(inside, cells, 0.0), axis=0, keepdims=True), axis=1, keepdims=True)
    below = total(right * zero)
    good = below > 0.0
    quotient = jnp.where(good, total(right * one) / jnp.where(good, below, 1.0), 0.0)
    shift[...] = jnp.broadcast_to(jnp.clip(quotient, -1.0, 1.0), shift.shape)


def krylov_kernel(meta, facing, shift, ext, facing_rows, from_far, from_near, base, moments, folded):
    tall, cols = ext.shape[1], ext.shape[2]
    rows = base.shape[1]
    size = facing_rows.shape[0]
    _, top, lon_odd, _ = flags(meta)
    west = jnp.where(lon_odd, from_near[...], from_far[...])
    east = jnp.where(lon_odd, from_far[...], from_near[...])
    theta = shift[0:1, 0:1]
    across = fold_shift(facing)
    row = iota((size, cols), 0)
    flips = (row >= ROW[FLIPPED[0]]) & (row < ROW[FLIPPED[-1] + 1])
    for side in range(2):
        cells = fold(across, pltpu.roll(west[:size], cols - RELAY, 1), facing_rows[...], east[:size], side == 1)
        folded[side, :size, :] = jnp.where(flips, -cells, cells)
    folded[:, size:, :] = jnp.zeros((2, folded.shape[1] - size, cols), jnp.float32)
    lane = iota((tall, cols), 1)
    first = lane == 0
    last = lane == cols - 1
    eighth = iota((8, cols), 0)

    def load(f):
        parts = []
        for packet, shift_of in ((west, 2 * cols - SIDE[f]), (east, cols)):
            pieces = []
            for start, stop, first_lane in segments(rows):
                layer = packet[packet.shape[0] - (stop - start) :]
                pieces.append(pltpu.roll(layer, (shift_of - START[f] - first_lane) % cols, 1))
            parts.append(jnp.concatenate(pieces, axis=0))
        a, b = parts
        beside = jnp.where(lane >= cols - SIDE[f], a, jnp.where(lane < SIDE[f], b, 0.0))

        def put(cells, side):
            new = folded[side, ROW[f] : ROW[f] + 8, :]
            new = jnp.where(eighth < DEEP[f], jnp.where(top, new, cells[rows : rows + 8]), 0.0)
            return jnp.concatenate([cells[:rows], new, cells[rows + 8 :]], axis=0)

        return put(ext[f], 0), put(beside, 1)

    def plus_x(pair):
        a, b = (pltpu.roll(part, cols - 1, 1) for part in pair)
        return jnp.where(last, b, a), jnp.where(last, a, b)

    def minus_x(pair):
        a, b = (pltpu.roll(part, 1, 1) for part in pair)
        return jnp.where(first, b, a), jnp.where(first, a, b)

    def plus_y(pair):
        return tuple(pltpu.roll(part, tall - 1, 0) for part in pair)

    def minus_y(pair):
        return tuple(pltpu.roll(part, 1, 0) for part in pair)

    def each(function, *pairs):
        return tuple(function(*parts) for parts in zip(*pairs))

    def neighbours(pair):
        return each(
            lambda a, b, c, d: (a + b) + (c + d), plus_x(pair), minus_x(pair), plus_y(pair), minus_y(pair)
        )

    press, zonal, merid, wet, weights, anomaly = (load(f) for f in range(FIELDS))
    half = 0.5 * TIME_STEP
    flow = lambda w, speed, a, b: w * (speed - half * (a - b))
    east_flow = each(flow, wet, zonal, plus_x(press), minus_x(press))
    north_flow = each(flow, wet, merid, plus_y(press), minus_y(press))
    right = each(
        lambda w, g, n, a, b, c, d: w * (g * n - 0.5 * (a - b + c - d)),
        wet,
        weights,
        anomaly,
        plus_x(east_flow),
        minus_x(east_flow),
        plus_y(north_flow),
        minus_y(north_flow),
    )
    diagonal = each(lambda g: 4.0 + g, weights)
    inverse = each(lambda m: 1.0 / m, diagonal)
    scale = each(lambda w, i: w * i, wet, inverse)
    zero = each(lambda r, i: r * i, right, inverse)
    one = each(lambda a, n, z: a * n - theta * z, scale, neighbours(zero), zero)
    two = each(lambda a, n, z: a * n - theta * z, scale, neighbours(one), one)
    three = scale[0][:rows] * neighbours(two)[0][:rows] - theta * two[0][:rows]
    right, middle = right[0][:rows], diagonal[0][:rows]
    zero, one, two = zero[0][:rows], one[0][:rows], two[0][:rows]
    base[0] = zero
    base[1] = one
    base[2] = two
    weighted_one = middle * one
    weighted_two = middle * two
    products = (
        right * zero,
        right * one,
        right * two,
        right * three,
        weighted_one * one,
        weighted_one * two,
        weighted_one * three,
        weighted_two * two,
        weighted_two * three,
    )
    which = iota((16, cols), 0)
    place = iota((16, cols), 1)
    sums = jnp.where((which == len(products)) & (place == 0), theta, 0.0)
    for k, product in enumerate(products):
        sums = jnp.where(which == k, jnp.sum(product, axis=0, keepdims=True), sums)
    sums = jnp.sum(sums, axis=1, keepdims=True)
    sums = jnp.sum(jnp.where(which == place, sums, 0.0), axis=0, keepdims=True)
    moments[...] = jnp.broadcast_to(sums, moments.shape)


def step_kernel(
    meta, spans, facing, heat, salt, zonal, merid, water, north_came, south_rows, from_far, from_near,
    heat_out, salt_out, zonal_out, merid_out,
    new_heat, new_salt, new_zonal, new_merid, north_rows, sems,
):
    levels, rows, cols = heat.shape
    deep = 4 * levels
    _, top, lon_odd, _ = flags(meta)
    wet = water[...].astype(jnp.float32)
    lane = iota((rows, cols), 1)
    row = iota((rows, cols), 0)
    east = jnp.where(lon_odd, from_far[...], from_near[...])
    west = jnp.where(lon_odd, from_near[...], from_far[...])
    came = north_came[...]
    across = fold(fold_shift(facing), pltpu.roll(west[:deep], cols // 2, 1), came, east[:deep], False)
    north_rows[...] = jnp.where(top, across, came)

    def around(cells, q):
        a = pltpu.roll(east, (cols - 2 * q) % cols, 1)
        b = pltpu.roll(west, (2 * cols - 2 - 2 * q) % cols, 1)
        side = jnp.where(lane < 2, a, b)

        def shift_x(by):
            a = pltpu.roll(cells, by % cols, 1)
            b = pltpu.roll(side, by % cols, 1)
            own = lane >= by if by > 0 else lane < cols + by
            return jnp.where(own, a, b)

        n0 = north_rows[2 * q : 2 * q + 1, :]
        n1 = north_rows[2 * q + 1 : 2 * q + 2, :]
        s0 = south_rows[2 * q + 1 : 2 * q + 2, :]
        s1 = south_rows[2 * q : 2 * q + 1, :]
        north_one = jnp.where(row == rows - 1, n0, pltpu.roll(cells, rows - 1, 0))
        north_two = jnp.where(row == rows - 1, n1, jnp.where(row == rows - 2, n0, pltpu.roll(cells, rows - 2, 0)))
        south_one = jnp.where(row == 0, s0, pltpu.roll(cells, 1, 0))
        south_two = jnp.where(row == 0, s1, jnp.where(row == 1, s0, pltpu.roll(cells, 2, 0)))
        return (shift_x(-1), shift_x(1), shift_x(-2), shift_x(2), north_one, south_one, north_two, south_two)

    def advance(cells, parts, speed_x, speed_y):
        e1, w1, e2, w2, n1, s1, n2, s2 = parts
        grad_east = 8.0 * (e1 - w1) - (e2 - w2)
        grad_north = 8.0 * (n1 - s1) - (n2 - s2)
        laplace = (e1 + w1) + (n1 + s1) - 4.0 * cells
        tendency = (-TIME_STEP / 12.0) * (speed_x * grad_east + speed_y * grad_north) + MIXING * laplace
        return cells + wet * tendency

    stores = ((new_heat, heat_out), (new_salt, salt_out), (new_zonal, zonal_out), (new_merid, merid_out))
    size = levels // sems.shape[1]
    copies = []
    half = 0.5 * TIME_STEP
    above_x = jnp.zeros((rows, cols), jnp.float32)
    above_y = jnp.zeros((rows, cols), jnp.float32)
    for k in range(levels):
        t, s, u, v = heat[k], salt[k], zonal[k], merid[k]
        around_t = around(t, k)
        around_s = around(s, levels + k)
        new_heat[k] = advance(t, around_t, u, v)
        new_salt[k] = advance(s, around_s, u, v)
        span = spans[0:1, k : k + 1]
        layer_x = span * (density(around_t[0], around_s[0]) - density(around_t[1], around_s[1]))
        layer_y = span * (density(around_t[4], around_s[4]) - density(around_t[5], around_s[5]))
        new_zonal[k] = wet * (u - half * (above_x + 0.5 * layer_x))
        new_merid[k] = wet * (v - half * (above_y + 0.5 * layer_y))
        above_x = above_x + layer_x
        above_y = above_y + layer_y
        if (k + 1) % size == 0:
            piece = pl.ds(k + 1 - size, size)
            for i, (near_ref, far_ref) in enumerate(stores):
                copies.append(pltpu.make_async_copy(near_ref.at[piece], far_ref.at[piece], sems.at[i, k // size]))
                copies[-1].start()
    for copy in copies:
        copy.wait()


def surface_kernel(shares, shift, base, surface):
    lanes = shares.shape[1]
    g00, g01, g02, g03, g11, g12, g13, g22, g23, theta = (
        shares[...] if k == 0 else pltpu.roll(shares[...], lanes - k, 1) for k in range(10)
    )
    add = lambda terms: jnp.sum(terms, axis=0, keepdims=True)

    def ratio(a, b):
        good = b > 0.0
        return jnp.where(good, a / jnp.where(good, b, 1.0), 0.0)

    def form(p, h):
        total = 0.0
        for i, a in enumerate(p):
            for j in range(i, len(p)):
                term = a * p[j] * h[i + j]
                total = total + (term if i == j else 2.0 * term)
        return total

    whole = add(g00)
    common = ratio(add(theta * g00 + g01), whole)
    d = theta - common
    mu = [
        whole,
        add(g01 + d * g00),
        add(g11 + d * (2.0 * g01 + d * g00)),
        add(g12 + d * (2.0 * g11 + g02 + d * (3.0 * g01 + d * g00))),
        add(g22 + d * (4.0 * g12 + d * (2.0 * g02 + 4.0 * g11 + d * (4.0 * g01 + d * g00)))),
        add(
            g23
            + d * (3.0 * g22 + 2.0 * g13 + d * (9.0 * g12 + g03 + d * (4.0 * g02 + 6.0 * g11 + d * (5.0 * g01 + d * g00))))
        ),
    ]
    scale = 1.0 - common
    gap = [scale * mu[k] - mu[k + 1] for k in range(5)]
    alpha = ratio(mu[0], gap[0])
    y = [-alpha * ratio(mu[1], mu[0]), alpha]
    x = [alpha, 0.0, 0.0]
    rz = form(y, mu)
    p = [y[0] + ratio(rz, mu[0]), y[1]]
    alpha = ratio(rz, form(p, gap))
    x = [x[0] + alpha * p[0], alpha * p[1], 0.0]
    y = [y[0] - alpha * scale * p[0], y[1] - alpha * (scale * p[1] - p[0]), alpha * p[1]]
    new = form(y, mu)
    beta = ratio(new, rz)
    p = [y[0] + beta * p[0], y[1] + beta * p[1], y[2]]
    alpha = ratio(new, form(p, gap))
    x = [x[0] + alpha * p[0], x[1] + alpha * p[1], alpha * p[2]]
    d = shift[0:1, :] - common
    x = [x[0] + d * (x[1] + d * x[2]), x[1] + 2.0 * d * x[2], x[2]]
    x = [value[0:1, 0:1] for value in x]
    surface[...] = x[0] * base[0] + x[1] * base[1] + x[2] * base[2]


def call(kernel, outs, flops, moved, name, out_space=pltpu.VMEM, scratch=(), types=jnp.float32):
    def run(*args):
        return pl.pallas_call(
            kernel,
            out_shape=[jax.ShapeDtypeStruct(shape, types) for shape in outs],
            in_specs=[pl.BlockSpec(memory_space=pltpu.VMEM)] * len(args),
            out_specs=[pl.BlockSpec(memory_space=out_space)] * len(outs),
            scratch_shapes=list(scratch),
            cost_estimate=pl.CostEstimate(flops=flops, bytes_accessed=moved, transcendentals=0),
            compiler_params=pltpu.CompilerParams(vmem_limit_bytes=VMEM_LIMIT),
            name=name,
        )(*args)

    return run


def body(
    warmth_deviation,
    saltiness_deviation,
    easterly_speed,
    poleward_speed,
    stratum_spans,
    water_indicator,
    opposite_counterpart,
    elevation_weights,
    elevation_anomaly,
):
    lons, lats = lax.axis_size("lon"), lax.axis_size("lat")
    lon, lat = lax.axis_index("lon"), lax.axis_index("lat")
    levels, rows, cols = warmth_deviation.shape
    high = packet_rows(levels)
    assert cols & (cols - 1) == 0 and rows >= 24 and rows // 2 == high - 4 * levels + 8 and 4 * levels <= cols // 2 and 2 * START[-1] <= min(RELAY, cols - RELAY) and cols == 128
    tall = rows + 16
    width = cols * lons
    flat = lambda i, j: (i % lons) * lats + j

    place = (lax.rem(lat, 2), lat == lats - 1, lax.rem(lon, 2), lat == 0, lon)
    meta = jnp.stack([value.astype(jnp.int32) for value in place]).reshape(1, 5)
    (meta,) = call(place_kernel, [(8, cols)], LOAD_FLOPS, 16, "place", types=jnp.int32)(meta)

    spans = stratum_spans.reshape(1, levels)
    facing = opposite_counterpart.reshape(1, cols)
    state = (warmth_deviation, saltiness_deviation, easterly_speed, poleward_speed)
    flat_state = (water_indicator, elevation_weights, elevation_anomaly)
    cells = levels * rows * cols
    sums, first, second, kept, east_columns, west_columns = call(
        pack_kernel,
        [(3, rows, cols), *[(high, cols)] * 3, (rows, cols), (rows, cols)],
        12 * cells,
        16 * cells,
        "level_sums",
        scratch=[pltpu.VMEM((high, cols), jnp.float32)] * 3,
    )(meta, spans, facing, *state, *flat_state)

    axes = ("lon", "lat")
    pairs_first = [(flat(i, j), flat(i, j ^ 1)) for i in range(lons) for j in range(lats)]
    pairs_inner = [
        (flat(i, a), flat(i, b))
        for i in range(lons)
        for j in range(1, lats - 1, 2)
        for a, b in ((j, j + 1), (j + 1, j))
    ] + [(flat(i, 0), flat(i ^ 2, 0)) for i in range(lons)]

    counterpart, first = lax.optimization_barrier((opposite_counterpart, first))
    hinge = lax.rem(counterpart[0] + 1 + cols * lon, width)
    block = lax.rem((hinge + cols // 2) // cols, lons)

    deep = 4 * levels

    def exchange(block, first, second):
        partner = [(block - 1 - i) % lons for i in range(lons)]
        partner = [i + lons // 2 if i == p else p for i, p in enumerate(partner)]
        pairs_fold = [(flat(p, lats - 1), flat(i, lats - 1)) for i, p in enumerate(partner)]
        second = lax.ppermute(second, axes, pairs_inner + pairs_fold)
        first = lax.ppermute(first, axes, pairs_first)
        return call(
            functools.partial(turn_kernel, lons),
            [
                (FIELDS, tall, cols),
                *[(rows // 2, cols)] * 2,
                *[(rows, cols)] * 2,
                (high - deep, cols),
                *[(deep, cols)] * 2,
            ],
            FIELDS * tall * cols,
            4 * 4 * FIELDS * tall * cols,
            "row_halos",
        )(meta, facing, kept, sums, *flat_state, second, first, east_columns, west_columns)

    ext, to_far, to_near, state_far, state_near, facing_rows, north_rows, south_rows = lax.switch(
        block, [functools.partial(exchange, s) for s in range(lons)], first, second
    )

    near = lambda cells: lax.ppermute(cells, "lon", [(i, i ^ 1) for i in range(lons)])
    far = lambda cells: lax.ppermute(cells, "lon", [(i, (i + 1 if i % 2 else i - 1) % lons) for i in range(lons)])
    from_far, from_near = far(to_far), near(to_near)
    state_far, state_near = far(state_far), near(state_near)

    (shift,) = call(shift_kernel, [(8, cols)], 60 * rows * cols, 24 * rows * cols, "basis_shift")(ext)

    count = lons * lats
    base, moments = call(
        krylov_kernel,
        [(3, rows, cols), (count, cols)],
        200 * tall * cols,
        4 * 12 * tall * cols,
        "krylov",
        scratch=[pltpu.VMEM((2, high - deep + 8, cols), jnp.float32)],
    )(meta, facing, shift, ext, facing_rows, from_far, from_near)

    chunks = 5 if levels % 5 == 0 else 1
    new_heat, new_salt, new_zonal, new_merid = call(
        step_kernel,
        [(levels, rows, cols)] * 4,
        120 * cells,
        32 * cells,
        "levels_step",
        out_space=pltpu.HBM,
        scratch=[
            *[pltpu.VMEM((levels, rows, cols), jnp.float32)] * 4,
            pltpu.VMEM((deep, cols), jnp.float32),
            pltpu.SemaphoreType.DMA((4, chunks)),
        ],
    )(meta, spans, facing, *state, water_indicator, north_rows, south_rows, state_far, state_near)

    shares = lax.all_to_all(moments, axes, 0, 0, tiled=True)
    (surface,) = call(surface_kernel, [(rows, cols)], 6 * rows * cols, 16 * rows * cols, "surface")(shares, shift, base)
    return (new_heat, new_salt, new_zonal, new_merid, surface)


def solution(mesh):
    assert mesh.shape["lon"] > 2
    for axis in mesh.shape.values():
        assert axis > 1 and axis & (axis - 1) == 0
    levels = P(None, "lat", "lon")
    flat = P("lat", "lon")
    return jax.shard_map(
        body,
        mesh=mesh,
        in_specs=(levels, levels, levels, levels, P(), flat, P("lon"), flat, flat),
        out_specs=(levels, levels, levels, levels, flat),
        check_vma=False,
    )
```

```python
import functools

import jax
import jax.numpy as jnp
from jax import lax
from jax.experimental import pallas as pl
from jax.experimental.pallas import tpu as pltpu
from jax.sharding import PartitionSpec as P

TIME_STEP = 0.1
MIXING = 0.1

DEEP = (5, 3, 4, 4, 3, 3)
SIDE = (5, 4, 3, 4, 3, 3)
FIELDS = len(SIDE)
ROW = tuple(sum(DEEP[:f]) for f in range(FIELDS + 1))
START = tuple(sum(SIDE[:f]) for f in range(FIELDS + 1))
RELAY = 56
FLIPPED = (1, 2)
VMEM_LIMIT = 32 * 1024 * 1024
LOAD_FLOPS = 10**10


def density(heat, salt):
    return heat * (-1.0 - 0.15 * heat - 0.2 * salt) + 0.8 * salt


def iota(shape, axis):
    return lax.broadcasted_iota(jnp.int32, shape, axis)


def packet_rows(levels):
    return -(-(4 * levels + ROW[-1]) // 8) * 8


def flags(meta):
    return tuple(meta[i : i + 1, :] == 1 for i in range(4))


def segments(rows):
    size = START[-1]
    return (0, rows // 2, 0), (rows // 2, rows, size), (rows, rows + 8, RELAY), (rows + 8, rows + 16, RELAY + size)


def place_kernel(meta, placed):
    for i in range(5):
        placed[i : i + 1, :] = jnp.broadcast_to(meta[0:1, i : i + 1], (1, placed.shape[1]))
    placed[5:, :] = jnp.zeros((placed.shape[0] - 5, placed.shape[1]), jnp.int32)


def pack_kernel(
    meta, spans, facing, heat, salt, zonal, merid, water, weights, anomaly,
    sums, first, second, kept,
    top, bottom, back,
):
    levels, rows, cols = heat.shape
    span = [spans[0:1, k : k + 1] for k in range(levels)]
    below = [None] * levels
    total = jnp.zeros((1, 1), jnp.float32)
    for k in reversed(range(levels)):
        below[k] = span[k] * (0.5 * span[k] + total)
        total = total + span[k]
    zero = jnp.zeros((rows, cols), jnp.float32)
    press, east, north = zero, zero, zero
    for k in range(levels):
        press = press + below[k] * density(heat[k], salt[k])
        east = east + span[k] * zonal[k]
        north = north + span[k] * merid[k]
        for q, source in ((k, heat), (levels + k, salt)):
            top[2 * q : 2 * q + 2, :] = source[k, rows - 2 :, :]
            bottom[2 * q : 2 * q + 2, :] = source[k, :2, :]
            for i in range(2):
                back[2 * q + i : 2 * q + i + 1, :] = source[k, rows - 1 - i : rows - i, :]
    sums[0] = press
    sums[1] = east
    sums[2] = north
    fields = (sums.at[0], sums.at[1], sums.at[2], water, weights, anomaly)
    for f, field in enumerate(fields):
        at = 4 * levels + ROW[f]
        deep = DEEP[f]
        top[at : at + deep, :] = field[rows - deep :, :].astype(jnp.float32)
        bottom[at : at + deep, :] = field[:deep, :].astype(jnp.float32)
        for j in range(deep):
            back[at + j : at + j + 1, :] = field[rows - 1 - j : rows - j, :].astype(jnp.float32)
    used = 4 * levels + ROW[-1]
    high = first.shape[0]
    if used < high:
        for packet in (top, bottom, back):
            packet[used:, :] = jnp.zeros((high - used, cols), jnp.float32)
    odd, last, _, _ = flags(meta)
    first[...] = jnp.where(odd, bottom[...], top[...])
    packet = jnp.where(last, back[...], jnp.where(odd, top[...], bottom[...]))
    second[...] = packet
    kept[...] = packet


def column_kernel(heat, salt, east_columns, west_columns):
    levels, rows, cols = heat.shape
    pair = iota((rows, cols), 1) // 2
    east = jnp.zeros((rows, cols), jnp.float32)
    west = jnp.zeros((rows, cols), jnp.float32)
    for q in range(2 * levels):
        cells = heat[q] if q < levels else salt[q - levels]
        here = pair == q
        east = jnp.where(here, pltpu.roll(cells, (2 * q + 2) % cols, 1), east)
        west = jnp.where(here, pltpu.roll(cells, 2 * q, 1), west)
    east_columns[...] = east
    west_columns[...] = west


def turn_kernel(
    lons, meta, facing, mine, sums, water, weights, anomaly, second, first, east_columns, west_columns,
    ext, to_far, to_near, state_far, state_near, facing_rows, north_rows, south_rows,
):
    rows, cols = sums.shape[1], sums.shape[2]
    tall = ext.shape[1]
    deep = north_rows.shape[0]
    odd, top, lon_odd, bottom = flags(meta)
    from_first = first[...]
    hinge = facing[0:1, 0:1] + 1 + cols * meta[4:5, 0:1] + cols // 2
    block = lax.shift_right_logical(hinge & (lons * cols - 1), cols.bit_length() - 1)
    alone = ((block - 1 - 2 * meta[4:5, 0:1]) & (lons - 1)) == 0
    from_second = jnp.where(top & alone, mine[...], second[...])
    north = jnp.where(odd, from_second, from_first)
    south = jnp.where(bottom, 0.0, jnp.where(odd, from_first, from_second))
    fields = (sums.at[0], sums.at[1], sums.at[2], water, weights, anomaly)
    for f in range(FIELDS):
        at = deep + ROW[f]
        size = DEEP[f]
        ext[f, :rows, :] = fields[f][...].astype(jnp.float32)
        ext[f, rows : rows + size, :] = north[at : at + size]
        ext[f, rows + size : tall - size, :] = jnp.zeros((tall - rows - 2 * size, cols), jnp.float32)
        ext[f, tall - size :, :] = south[at : at + size]
    passed = from_second[deep:]
    size = passed.shape[0]
    half = rows // 2
    lane = iota((half, cols), 1)
    lower = iota((half, cols), 0) >= size
    empty = jnp.zeros((size, cols), jnp.float32)
    spare = jnp.zeros((half - size, cols), jnp.float32)
    relay = lane >= RELAY
    east = jnp.where(relay, jnp.concatenate([pltpu.roll(passed, RELAY, 1), spare], axis=0), 0.0)
    west = jnp.where(relay, jnp.concatenate([passed, spare], axis=0), 0.0)
    for f in range(FIELDS):
        for start, stop, first_lane in segments(rows):
            at = START[f] + first_lane
            here = (lane >= at) & (lane < at + SIDE[f])
            layer = ext[f, start:stop, :]
            to_east = pltpu.roll(layer, (at + SIDE[f]) % cols, 1)
            to_west = pltpu.roll(layer, at, 1)
            if stop - start < half:
                here = here & lower
                to_east = jnp.concatenate([empty, to_east], axis=0)
                to_west = jnp.concatenate([empty, to_west], axis=0)
            east = jnp.where(here, to_east, east)
            west = jnp.where(here, to_west, west)
    to_far[...] = jnp.where(lon_odd, east, west)
    to_near[...] = jnp.where(lon_odd, west, east)
    passed = from_second[:deep]
    spare = jnp.zeros((rows - deep, cols), jnp.float32)
    right_half = iota((rows, cols), 1) >= cols // 2
    east = jnp.where(right_half, jnp.concatenate([pltpu.roll(passed, cols // 2, 1), spare], axis=0), east_columns[...])
    west = jnp.where(right_half, jnp.concatenate([passed, spare], axis=0), west_columns[...])
    state_far[...] = jnp.where(lon_odd, east, west)
    state_near[...] = jnp.where(lon_odd, west, east)
    facing_rows[...] = from_second[deep:]
    north_rows[...] = north[:deep]
    south_rows[...] = south[:deep]


def fold_shift(facing):
    cols = facing.shape[1]
    offset = (facing[0:1, 0:1] + 1) & (cols - 1)
    return jnp.where(offset >= cols // 2, offset - cols, offset)


def fold(shift, west, own, east, beside):
    rows, cols = own.shape
    lane = iota((rows, cols), 1)
    source = cols - 1 - lane
    if beside:
        place = (source + shift) & (cols - 1)
        low = jnp.where(place - cols < shift, west, own)
        merged = jnp.where(place >= cols // 2, low, jnp.where(place >= shift, east, own))
    else:
        merged = jnp.where(source >= cols - shift, west, jnp.where(source < -shift, east, own))
    return jnp.take_along_axis(merged, cols - 1 - ((lane - shift) & (cols - 1)), axis=1)


def shift_kernel(ext, shift):
    rows, cols = ext.shape[1] - 16, ext.shape[2]
    press, zonal, merid, wet, weights, anomaly = (ext[f, :rows, :] for f in range(FIELDS))
    plus_x = lambda cells: pltpu.roll(cells, cols - 1, 1)
    minus_x = lambda cells: pltpu.roll(cells, 1, 1)
    plus_y = lambda cells: pltpu.roll(cells, rows - 1, 0)
    minus_y = lambda cells: pltpu.roll(cells, 1, 0)
    half = 0.5 * TIME_STEP
    east_flow = wet * (zonal - half * (plus_x(press) - minus_x(press)))
    north_flow = wet * (merid - half * (plus_y(press) - minus_y(press)))
    spread = plus_x(east_flow) - minus_x(east_flow) + plus_y(north_flow) - minus_y(north_flow)
    right = wet * (weights * anomaly - 0.5 * spread)
    inverse = 1.0 / (4.0 + weights)
    zero = right * inverse
    one = wet * inverse * (plus_x(zero) + minus_x(zero) + plus_y(zero) + minus_y(zero))
    lane = iota((rows, cols), 1)
    row = iota((rows, cols), 0)
    inside = (lane >= 8) & (lane < cols - 8) & (row >= 8) & (row < rows - 8)
    total = lambda cells: jnp.sum(jnp.sum(jnp.where(inside, cells, 0.0), axis=0, keepdims=True), axis=1, keepdims=True)
    below = total(right * zero)
    good = below > 0.0
    quotient = jnp.where(good, total(right * one) / jnp.where(good, below, 1.0), 0.0)
    shift[...] = jnp.broadcast_to(jnp.clip(quotient, -1.0, 1.0), shift.shape)


def krylov_kernel(meta, facing, shift, ext, facing_rows, from_far, from_near, base, moments, folded):
    tall, cols = ext.shape[1], ext.shape[2]
    rows = base.shape[1]
    size = facing_rows.shape[0]
    _, top, lon_odd, _ = flags(meta)
    west = jnp.where(lon_odd, from_near[...], from_far[...])
    east = jnp.where(lon_odd, from_far[...], from_near[...])
    theta = shift[0:1, 0:1]
    across = fold_shift(facing)
    row = iota((size, cols), 0)
    flips = (row >= ROW[FLIPPED[0]]) & (row < ROW[FLIPPED[-1] + 1])
    for side in range(2):
        cells = fold(across, pltpu.roll(west[:size], cols - RELAY, 1), facing_rows[...], east[:size], side == 1)
        folded[side, :size, :] = jnp.where(flips, -cells, cells)
    folded[:, size:, :] = jnp.zeros((2, folded.shape[1] - size, cols), jnp.float32)
    lane = iota((tall, cols), 1)
    first = lane == 0
    last = lane == cols - 1
    eighth = iota((8, cols), 0)

    def load(f):
        parts = []
        for packet, shift_of in ((west, 2 * cols - SIDE[f]), (east, cols)):
            pieces = []
            for start, stop, first_lane in segments(rows):
                layer = packet[packet.shape[0] - (stop - start) :]
                pieces.append(pltpu.roll(layer, (shift_of - START[f] - first_lane) % cols, 1))
            parts.append(jnp.concatenate(pieces, axis=0))
        a, b = parts
        beside = jnp.where(lane >= cols - SIDE[f], a, jnp.where(lane < SIDE[f], b, 0.0))

        def put(cells, side):
            new = folded[side, ROW[f] : ROW[f] + 8, :]
            new = jnp.where(eighth < DEEP[f], jnp.where(top, new, cells[rows : rows + 8]), 0.0)
            return jnp.concatenate([cells[:rows], new, cells[rows + 8 :]], axis=0)

        return put(ext[f], 0), put(beside, 1)

    def plus_x(pair):
        a, b = (pltpu.roll(part, cols - 1, 1) for part in pair)
        return jnp.where(last, b, a), jnp.where(last, a, b)

    def minus_x(pair):
        a, b = (pltpu.roll(part, 1, 1) for part in pair)
        return jnp.where(first, b, a), jnp.where(first, a, b)

    def plus_y(pair):
        return tuple(pltpu.roll(part, tall - 1, 0) for part in pair)

    def minus_y(pair):
        return tuple(pltpu.roll(part, 1, 0) for part in pair)

    def each(function, *pairs):
        return tuple(function(*parts) for parts in zip(*pairs))

    def neighbours(pair):
        return each(
            lambda a, b, c, d: (a + b) + (c + d), plus_x(pair), minus_x(pair), plus_y(pair), minus_y(pair)
        )

    press, zonal, merid, wet, weights, anomaly = (load(f) for f in range(FIELDS))
    half = 0.5 * TIME_STEP
    flow = lambda w, speed, a, b: w * (speed - half * (a - b))
    east_flow = each(flow, wet, zonal, plus_x(press), minus_x(press))
    north_flow = each(flow, wet, merid, plus_y(press), minus_y(press))
    right = each(
        lambda w, g, n, a, b, c, d: w * (g * n - 0.5 * (a - b + c - d)),
        wet,
        weights,
        anomaly,
        plus_x(east_flow),
        minus_x(east_flow),
        plus_y(north_flow),
        minus_y(north_flow),
    )
    diagonal = each(lambda g: 4.0 + g, weights)
    inverse = each(lambda m: 1.0 / m, diagonal)
    scale = each(lambda w, i: w * i, wet, inverse)
    zero = each(lambda r, i: r * i, right, inverse)
    one = each(lambda a, n, z: a * n - theta * z, scale, neighbours(zero), zero)
    two = each(lambda a, n, z: a * n - theta * z, scale, neighbours(one), one)
    three = scale[0][:rows] * neighbours(two)[0][:rows] - theta * two[0][:rows]
    right, middle = right[0][:rows], diagonal[0][:rows]
    zero, one, two = zero[0][:rows], one[0][:rows], two[0][:rows]
    base[0] = zero
    base[1] = one
    base[2] = two
    weighted_one = middle * one
    weighted_two = middle * two
    products = (
        right * zero,
        right * one,
        right * two,
        right * three,
        weighted_one * one,
        weighted_one * two,
        weighted_one * three,
        weighted_two * two,
        weighted_two * three,
    )
    which = iota((16, cols), 0)
    place = iota((16, cols), 1)
    sums = jnp.where((which == len(products)) & (place == 0), theta, 0.0)
    for k, product in enumerate(products):
        sums = jnp.where(which == k, jnp.sum(product, axis=0, keepdims=True), sums)
    sums = jnp.sum(sums, axis=1, keepdims=True)
    sums = jnp.sum(jnp.where(which == place, sums, 0.0), axis=0, keepdims=True)
    moments[...] = jnp.broadcast_to(sums, moments.shape)


def step_kernel(
    meta, spans, facing, heat, salt, zonal, merid, water, north_came, south_rows, from_far, from_near,
    heat_out, salt_out, zonal_out, merid_out,
    new_heat, new_salt, new_zonal, new_merid, north_rows, sems,
):
    levels, rows, cols = heat.shape
    deep = 4 * levels
    _, top, lon_odd, _ = flags(meta)
    wet = water[...].astype(jnp.float32)
    lane = iota((rows, cols), 1)
    row = iota((rows, cols), 0)
    east = jnp.where(lon_odd, from_far[...], from_near[...])
    west = jnp.where(lon_odd, from_near[...], from_far[...])
    came = north_came[...]
    across = fold(fold_shift(facing), pltpu.roll(west[:deep], cols // 2, 1), came, east[:deep], False)
    north_rows[...] = jnp.where(top, across, came)

    def around(cells, q):
        a = pltpu.roll(east, (cols - 2 * q) % cols, 1)
        b = pltpu.roll(west, (2 * cols - 2 - 2 * q) % cols, 1)
        side = jnp.where(lane < 2, a, b)

        def shift_x(by):
            a = pltpu.roll(cells, by % cols, 1)
            b = pltpu.roll(side, by % cols, 1)
            own = lane >= by if by > 0 else lane < cols + by
            return jnp.where(own, a, b)

        n0 = north_rows[2 * q : 2 * q + 1, :]
        n1 = north_rows[2 * q + 1 : 2 * q + 2, :]
        s0 = south_rows[2 * q + 1 : 2 * q + 2, :]
        s1 = south_rows[2 * q : 2 * q + 1, :]
        north_one = jnp.where(row == rows - 1, n0, pltpu.roll(cells, rows - 1, 0))
        north_two = jnp.where(row == rows - 1, n1, jnp.where(row == rows - 2, n0, pltpu.roll(cells, rows - 2, 0)))
        south_one = jnp.where(row == 0, s0, pltpu.roll(cells, 1, 0))
        south_two = jnp.where(row == 0, s1, jnp.where(row == 1, s0, pltpu.roll(cells, 2, 0)))
        return (shift_x(-1), shift_x(1), shift_x(-2), shift_x(2), north_one, south_one, north_two, south_two)

    def advance(cells, parts, speed_x, speed_y):
        e1, w1, e2, w2, n1, s1, n2, s2 = parts
        grad_east = 8.0 * (e1 - w1) - (e2 - w2)
        grad_north = 8.0 * (n1 - s1) - (n2 - s2)
        laplace = (e1 + w1) + (n1 + s1) - 4.0 * cells
        tendency = (-TIME_STEP / 12.0) * (speed_x * grad_east + speed_y * grad_north) + MIXING * laplace
        return cells + wet * tendency

    stores = ((new_heat, heat_out), (new_salt, salt_out), (new_zonal, zonal_out), (new_merid, merid_out))
    size = levels // sems.shape[1]
    copies = []
    half = 0.5 * TIME_STEP
    above_x = jnp.zeros((rows, cols), jnp.float32)
    above_y = jnp.zeros((rows, cols), jnp.float32)
    for k in range(levels):
        t, s, u, v = heat[k], salt[k], zonal[k], merid[k]
        around_t = around(t, k)
        around_s = around(s, levels + k)
        new_heat[k] = advance(t, around_t, u, v)
        new_salt[k] = advance(s, around_s, u, v)
        span = spans[0:1, k : k + 1]
        layer_x = span * (density(around_t[0], around_s[0]) - density(around_t[1], around_s[1]))
        layer_y = span * (density(around_t[4], around_s[4]) - density(around_t[5], around_s[5]))
        new_zonal[k] = wet * (u - half * (above_x + 0.5 * layer_x))
        new_merid[k] = wet * (v - half * (above_y + 0.5 * layer_y))
        above_x = above_x + layer_x
        above_y = above_y + layer_y
        if (k + 1) % size == 0:
            piece = pl.ds(k + 1 - size, size)
            for i, (near_ref, far_ref) in enumerate(stores):
                copies.append(pltpu.make_async_copy(near_ref.at[piece], far_ref.at[piece], sems.at[i, k // size]))
                copies[-1].start()
    for copy in copies:
        copy.wait()


def surface_kernel(shares, shift, base, surface):
    lanes = shares.shape[1]
    g00, g01, g02, g03, g11, g12, g13, g22, g23, theta = (
        shares[...] if k == 0 else pltpu.roll(shares[...], lanes - k, 1) for k in range(10)
    )
    add = lambda terms: jnp.sum(terms, axis=0, keepdims=True)

    def ratio(a, b):
        good = b > 0.0
        return jnp.where(good, a / jnp.where(good, b, 1.0), 0.0)

    def form(p, h):
        total = 0.0
        for i, a in enumerate(p):
            for j in range(i, len(p)):
                term = a * p[j] * h[i + j]
                total = total + (term if i == j else 2.0 * term)
        return total

    whole = add(g00)
    common = ratio(add(theta * g00 + g01), whole)
    d = theta - common
    mu = [
        whole,
        add(g01 + d * g00),
        add(g11 + d * (2.0 * g01 + d * g00)),
        add(g12 + d * (2.0 * g11 + g02 + d * (3.0 * g01 + d * g00))),
        add(g22 + d * (4.0 * g12 + d * (2.0 * g02 + 4.0 * g11 + d * (4.0 * g01 + d * g00)))),
        add(
            g23
            + d * (3.0 * g22 + 2.0 * g13 + d * (9.0 * g12 + g03 + d * (4.0 * g02 + 6.0 * g11 + d * (5.0 * g01 + d * g00))))
        ),
    ]
    scale = 1.0 - common
    gap = [scale * mu[k] - mu[k + 1] for k in range(5)]
    alpha = ratio(mu[0], gap[0])
    y = [-alpha * ratio(mu[1], mu[0]), alpha]
    x = [alpha, 0.0, 0.0]
    rz = form(y, mu)
    p = [y[0] + ratio(rz, mu[0]), y[1]]
    alpha = ratio(rz, form(p, gap))
    x = [x[0] + alpha * p[0], alpha * p[1], 0.0]
    y = [y[0] - alpha * scale * p[0], y[1] - alpha * (scale * p[1] - p[0]), alpha * p[1]]
    new = form(y, mu)
    beta = ratio(new, rz)
    p = [y[0] + beta * p[0], y[1] + beta * p[1], y[2]]
    alpha = ratio(new, form(p, gap))
    x = [x[0] + alpha * p[0], x[1] + alpha * p[1], alpha * p[2]]
    d = shift[0:1, :] - common
    x = [x[0] + d * (x[1] + d * x[2]), x[1] + 2.0 * d * x[2], x[2]]
    x = [value[0:1, 0:1] for value in x]
    surface[...] = x[0] * base[0] + x[1] * base[1] + x[2] * base[2]


def call(kernel, outs, flops, moved, name, out_space=pltpu.VMEM, scratch=(), types=jnp.float32):
    def run(*args):
        return pl.pallas_call(
            kernel,
            out_shape=[jax.ShapeDtypeStruct(shape, types) for shape in outs],
            in_specs=[pl.BlockSpec(memory_space=pltpu.VMEM)] * len(args),
            out_specs=[pl.BlockSpec(memory_space=out_space)] * len(outs),
            scratch_shapes=list(scratch),
            cost_estimate=pl.CostEstimate(flops=flops, bytes_accessed=moved, transcendentals=0),
            compiler_params=pltpu.CompilerParams(vmem_limit_bytes=VMEM_LIMIT),
            name=name,
        )(*args)

    return run


def body(
    warmth_deviation,
    saltiness_deviation,
    easterly_speed,
    poleward_speed,
    stratum_spans,
    water_indicator,
    opposite_counterpart,
    elevation_weights,
    elevation_anomaly,
):
    lons, lats = lax.axis_size("lon"), lax.axis_size("lat")
    lon, lat = lax.axis_index("lon"), lax.axis_index("lat")
    levels, rows, cols = warmth_deviation.shape
    high = packet_rows(levels)
    assert cols & (cols - 1) == 0 and rows >= 24 and rows // 2 == high - 4 * levels + 8 and 4 * levels <= cols // 2 and 2 * START[-1] <= min(RELAY, cols - RELAY) and cols == 128
    tall = rows + 16
    width = cols * lons
    flat = lambda i, j: (i % lons) * lats + j

    place = (lax.rem(lat, 2), lat == lats - 1, lax.rem(lon, 2), lat == 0, lon)
    meta = jnp.stack([value.astype(jnp.int32) for value in place]).reshape(1, 5)
    (meta,) = call(place_kernel, [(8, cols)], LOAD_FLOPS, 16, "place", types=jnp.int32)(meta)

    spans = stratum_spans.reshape(1, levels)
    facing = opposite_counterpart.reshape(1, cols)
    state = (warmth_deviation, saltiness_deviation, easterly_speed, poleward_speed)
    flat_state = (water_indicator, elevation_weights, elevation_anomaly)
    cells = levels * rows * cols
    sums, first, second, kept = call(
        pack_kernel,
        [(3, rows, cols), *[(high, cols)] * 3],
        12 * cells,
        16 * cells,
        "level_sums",
        scratch=[pltpu.VMEM((high, cols), jnp.float32)] * 3,
    )(meta, spans, facing, *state, *flat_state)

    axes = ("lon", "lat")
    pairs_first = [(flat(i, j), flat(i, j ^ 1)) for i in range(lons) for j in range(lats)]
    pairs_inner = [
        (flat(i, a), flat(i, b))
        for i in range(lons)
        for j in range(1, lats - 1, 2)
        for a, b in ((j, j + 1), (j + 1, j))
    ] + [(flat(i, 0), flat(i ^ 1, 0)) for i in range(lons)]

    counterpart, first = lax.optimization_barrier((opposite_counterpart, first))
    hinge = lax.rem(counterpart[0] + 1 + cols * lon, width)
    block = lax.rem((hinge + cols // 2) // cols, lons)

    deep = 4 * levels

    def exchange(block, first, second):
        partner = [(block - 1 - i) % lons for i in range(lons)]
        partner = [i + lons // 2 if i == p else p for i, p in enumerate(partner)]
        pairs_fold = [(flat(p, lats - 1), flat(i, lats - 1)) for i, p in enumerate(partner)]
        second = lax.ppermute(second, axes, pairs_inner + pairs_fold)
        first = lax.ppermute(first, axes, pairs_first)
        columns = call(column_kernel, [(rows, cols)] * 2, 4 * cells, 8 * cells, "columns")(*state[:2])
        return call(
            functools.partial(turn_kernel, lons),
            [
                (FIELDS, tall, cols),
                *[(rows // 2, cols)] * 2,
                *[(rows, cols)] * 2,
                (high - deep, cols),
                *[(deep, cols)] * 2,
            ],
            FIELDS * tall * cols,
            4 * 4 * FIELDS * tall * cols,
            "row_halos",
        )(meta, facing, kept, sums, *flat_state, second, first, *columns)

    ext, to_far, to_near, state_far, state_near, facing_rows, north_rows, south_rows = lax.switch(
        block, [functools.partial(exchange, s) for s in range(lons)], first, second
    )

    near = lambda cells: lax.ppermute(cells, "lon", [(i, i ^ 1) for i in range(lons)])
    far = lambda cells: lax.ppermute(cells, "lon", [(i, (i + 1 if i % 2 else i - 1) % lons) for i in range(lons)])
    from_far, from_near = far(to_far), near(to_near)
    state_far, state_near = far(state_far), near(state_near)

    (shift,) = call(shift_kernel, [(8, cols)], 60 * rows * cols, 24 * rows * cols, "basis_shift")(ext)

    count = lons * lats
    base, moments = call(
        krylov_kernel,
        [(3, rows, cols), (count, cols)],
        200 * tall * cols,
        4 * 12 * tall * cols,
        "krylov",
        scratch=[pltpu.VMEM((2, high - deep + 8, cols), jnp.float32)],
    )(meta, facing, shift, ext, facing_rows, from_far, from_near)

    chunks = 5 if levels % 5 == 0 else 1
    new_heat, new_salt, new_zonal, new_merid = call(
        step_kernel,
        [(levels, rows, cols)] * 4,
        120 * cells,
        32 * cells,
        "levels_step",
        out_space=pltpu.HBM,
        scratch=[
            *[pltpu.VMEM((levels, rows, cols), jnp.float32)] * 4,
            pltpu.VMEM((deep, cols), jnp.float32),
            pltpu.SemaphoreType.DMA((4, chunks)),
        ],
    )(meta, spans, facing, *state, water_indicator, north_rows, south_rows, state_far, state_near)

    shares = lax.all_to_all(moments, axes, 0, 0, tiled=True)
    (surface,) = call(surface_kernel, [(rows, cols)], 6 * rows * cols, 16 * rows * cols, "surface")(shares, shift, base)
    return (new_heat, new_salt, new_zonal, new_merid, surface)


def solution(mesh):
    for axis in mesh.shape.values():
        assert axis > 1 and axis & (axis - 1) == 0
    levels = P(None, "lat", "lon")
    flat = P("lat", "lon")
    return jax.shard_map(
        body,
        mesh=mesh,
        in_specs=(levels, levels, levels, levels, P(), flat, P("lon"), flat, flat),
        out_specs=(levels, levels, levels, levels, flat),
        check_vma=False,
    )
```

```python
import functools

import jax
import jax.numpy as jnp
from jax import lax
from jax.experimental import pallas as pl
from jax.experimental.pallas import tpu as pltpu
from jax.sharding import PartitionSpec as P

TIME_STEP = 0.1
MIXING = 0.1

DEEP = (5, 3, 4, 4, 3, 3)
SIDE = (5, 4, 3, 4, 3, 3)
FIELDS = len(SIDE)
ROW = tuple(sum(DEEP[:f]) for f in range(FIELDS + 1))
START = tuple(sum(SIDE[:f]) for f in range(FIELDS + 1))
RELAY = 56
FLIPPED = (1, 2)
VMEM_LIMIT = 32 * 1024 * 1024
LOAD_FLOPS = 10**10


def density(heat, salt):
    return heat * (-1.0 - 0.15 * heat - 0.2 * salt) + 0.8 * salt


def iota(shape, axis):
    return lax.broadcasted_iota(jnp.int32, shape, axis)


def packet_rows(levels):
    return -(-(4 * levels + ROW[-1]) // 8) * 8


def flags(meta):
    return tuple(meta[i : i + 1, :] == 1 for i in range(4))


def segments(rows):
    size = START[-1]
    return (0, rows // 2, 0), (rows // 2, rows, size), (rows, rows + 8, RELAY), (rows + 8, rows + 16, RELAY + size)


def place_kernel(meta, placed):
    for i in range(5):
        placed[i : i + 1, :] = jnp.broadcast_to(meta[0:1, i : i + 1], (1, placed.shape[1]))
    placed[5:, :] = jnp.zeros((placed.shape[0] - 5, placed.shape[1]), jnp.int32)


def pack_kernel(
    meta, spans, facing, heat, salt, zonal, merid, water, weights, anomaly,
    sums, first, second, kept,
    top, bottom, back,
):
    levels, rows, cols = heat.shape
    span = [spans[0:1, k : k + 1] for k in range(levels)]
    below = [None] * levels
    total = jnp.zeros((1, 1), jnp.float32)
    for k in reversed(range(levels)):
        below[k] = span[k] * (0.5 * span[k] + total)
        total = total + span[k]
    zero = jnp.zeros((rows, cols), jnp.float32)
    press, east, north = zero, zero, zero
    for k in range(levels):
        press = press + below[k] * density(heat[k], salt[k])
        east = east + span[k] * zonal[k]
        north = north + span[k] * merid[k]
        for q, source in ((k, heat), (levels + k, salt)):
            top[2 * q : 2 * q + 2, :] = source[k, rows - 2 :, :]
            bottom[2 * q : 2 * q + 2, :] = source[k, :2, :]
            for i in range(2):
                back[2 * q + i : 2 * q + i + 1, :] = source[k, rows - 1 - i : rows - i, :]
    sums[0] = press
    sums[1] = east
    sums[2] = north
    fields = (sums.at[0], sums.at[1], sums.at[2], water, weights, anomaly)
    for f, field in enumerate(fields):
        at = 4 * levels + ROW[f]
        deep = DEEP[f]
        top[at : at + deep, :] = field[rows - deep :, :].astype(jnp.float32)
        bottom[at : at + deep, :] = field[:deep, :].astype(jnp.float32)
        for j in range(deep):
            back[at + j : at + j + 1, :] = field[rows - 1 - j : rows - j, :].astype(jnp.float32)
    used = 4 * levels + ROW[-1]
    high = first.shape[0]
    if used < high:
        for packet in (top, bottom, back):
            packet[used:, :] = jnp.zeros((high - used, cols), jnp.float32)
    odd, last, _, _ = flags(meta)
    first[...] = jnp.where(odd, bottom[...], top[...])
    packet = jnp.where(last, back[...], jnp.where(odd, top[...], bottom[...]))
    second[...] = packet
    kept[...] = packet


def column_kernel(heat, salt, east_columns, west_columns):
    levels, rows, cols = heat.shape
    pair = iota((rows, cols), 1) // 2
    east = jnp.zeros((rows, cols), jnp.float32)
    west = jnp.zeros((rows, cols), jnp.float32)
    for q in range(2 * levels):
        cells = heat[q] if q < levels else salt[q - levels]
        here = pair == q
        east = jnp.where(here, pltpu.roll(cells, (2 * q + 2) % cols, 1), east)
        west = jnp.where(here, pltpu.roll(cells, 2 * q, 1), west)
    east_columns[...] = east
    west_columns[...] = west


def turn_kernel(
    lons, meta, facing, mine, sums, water, weights, anomaly, second, first, east_columns, west_columns,
    ext, to_far, to_near, state_near, state_far, facing_rows, north_rows, south_rows,
):
    rows, cols = sums.shape[1], sums.shape[2]
    tall = ext.shape[1]
    deep = north_rows.shape[0]
    odd, top, lon_odd, bottom = flags(meta)
    from_first = first[...]
    hinge = facing[0:1, 0:1] + 1 + cols * meta[4:5, 0:1] + cols // 2
    block = lax.shift_right_logical(hinge & (lons * cols - 1), cols.bit_length() - 1)
    alone = ((block - 1 - 2 * meta[4:5, 0:1]) & (lons - 1)) == 0
    from_second = jnp.where(top & alone, mine[...], second[...])
    north = jnp.where(odd, from_second, from_first)
    south = jnp.where(bottom, 0.0, jnp.where(odd, from_first, from_second))
    fields = (sums.at[0], sums.at[1], sums.at[2], water, weights, anomaly)
    for f in range(FIELDS):
        at = deep + ROW[f]
        size = DEEP[f]
        ext[f, :rows, :] = fields[f][...].astype(jnp.float32)
        ext[f, rows : rows + size, :] = north[at : at + size]
        ext[f, rows + size : tall - size, :] = jnp.zeros((tall - rows - 2 * size, cols), jnp.float32)
        ext[f, tall - size :, :] = south[at : at + size]
    passed = from_second[deep:]
    size = passed.shape[0]
    half = rows // 2
    lane = iota((half, cols), 1)
    lower = iota((half, cols), 0) >= size
    empty = jnp.zeros((size, cols), jnp.float32)
    spare = jnp.zeros((half - size, cols), jnp.float32)
    relay = lane >= RELAY
    east = jnp.where(relay, jnp.concatenate([pltpu.roll(passed, RELAY, 1), spare], axis=0), 0.0)
    west = jnp.where(relay, jnp.concatenate([passed, spare], axis=0), 0.0)
    for f in range(FIELDS):
        for start, stop, first_lane in segments(rows):
            at = START[f] + first_lane
            here = (lane >= at) & (lane < at + SIDE[f])
            layer = ext[f, start:stop, :]
            to_east = pltpu.roll(layer, (at + SIDE[f]) % cols, 1)
            to_west = pltpu.roll(layer, at, 1)
            if stop - start < half:
                here = here & lower
                to_east = jnp.concatenate([empty, to_east], axis=0)
                to_west = jnp.concatenate([empty, to_west], axis=0)
            east = jnp.where(here, to_east, east)
            west = jnp.where(here, to_west, west)
    to_far[...] = jnp.where(lon_odd, east, west)
    to_near[...] = jnp.where(lon_odd, west, east)
    passed = from_second[:deep]
    spare = jnp.zeros((rows - deep, cols), jnp.float32)
    right_half = iota((rows, cols), 1) >= cols // 2
    east = jnp.where(right_half, jnp.concatenate([pltpu.roll(passed, cols // 2, 1), spare], axis=0), east_columns[...])
    west = jnp.where(right_half, jnp.concatenate([passed, spare], axis=0), west_columns[...])
    state_far[...] = jnp.where(lon_odd, east, west)
    state_near[...] = jnp.where(lon_odd, west, east)
    facing_rows[...] = from_second[deep:]
    north_rows[...] = north[:deep]
    south_rows[...] = south[:deep]


def fold_shift(facing):
    cols = facing.shape[1]
    offset = (facing[0:1, 0:1] + 1) & (cols - 1)
    return jnp.where(offset >= cols // 2, offset - cols, offset)


def fold(shift, west, own, east, beside):
    rows, cols = own.shape
    lane = iota((rows, cols), 1)
    source = cols - 1 - lane
    if beside:
        place = (source + shift) & (cols - 1)
        low = jnp.where(place - cols < shift, west, own)
        merged = jnp.where(place >= cols // 2, low, jnp.where(place >= shift, east, own))
    else:
        merged = jnp.where(source >= cols - shift, west, jnp.where(source < -shift, east, own))
    return jnp.take_along_axis(merged, cols - 1 - ((lane - shift) & (cols - 1)), axis=1)


def shift_kernel(ext, shift):
    rows, cols = ext.shape[1] - 16, ext.shape[2]
    press, zonal, merid, wet, weights, anomaly = (ext[f, :rows, :] for f in range(FIELDS))
    plus_x = lambda cells: pltpu.roll(cells, cols - 1, 1)
    minus_x = lambda cells: pltpu.roll(cells, 1, 1)
    plus_y = lambda cells: pltpu.roll(cells, rows - 1, 0)
    minus_y = lambda cells: pltpu.roll(cells, 1, 0)
    half = 0.5 * TIME_STEP
    east_flow = wet * (zonal - half * (plus_x(press) - minus_x(press)))
    north_flow = wet * (merid - half * (plus_y(press) - minus_y(press)))
    spread = plus_x(east_flow) - minus_x(east_flow) + plus_y(north_flow) - minus_y(north_flow)
    right = wet * (weights * anomaly - 0.5 * spread)
    inverse = 1.0 / (4.0 + weights)
    zero = right * inverse
    one = wet * inverse * (plus_x(zero) + minus_x(zero) + plus_y(zero) + minus_y(zero))
    lane = iota((rows, cols), 1)
    row = iota((rows, cols), 0)
    inside = (lane >= 8) & (lane < cols - 8) & (row >= 8) & (row < rows - 8)
    total = lambda cells: jnp.sum(jnp.sum(jnp.where(inside, cells, 0.0), axis=0, keepdims=True), axis=1, keepdims=True)
    below = total(right * zero)
    good = below > 0.0
    quotient = jnp.where(good, total(right * one) / jnp.where(good, below, 1.0), 0.0)
    shift[...] = jnp.broadcast_to(jnp.clip(quotient, -1.0, 1.0), shift.shape)


def krylov_kernel(meta, facing, shift, ext, facing_rows, from_far, from_near, base, moments, folded):
    tall, cols = ext.shape[1], ext.shape[2]
    rows = base.shape[1]
    size = facing_rows.shape[0]
    _, top, lon_odd, _ = flags(meta)
    west = jnp.where(lon_odd, from_near[...], from_far[...])
    east = jnp.where(lon_odd, from_far[...], from_near[...])
    theta = shift[0:1, 0:1]
    across = fold_shift(facing)
    row = iota((size, cols), 0)
    flips = (row >= ROW[FLIPPED[0]]) & (row < ROW[FLIPPED[-1] + 1])
    for side in range(2):
        cells = fold(across, pltpu.roll(west[:size], cols - RELAY, 1), facing_rows[...], east[:size], side == 1)
        folded[side, :size, :] = jnp.where(flips, -cells, cells)
    folded[:, size:, :] = jnp.zeros((2, folded.shape[1] - size, cols), jnp.float32)
    lane = iota((tall, cols), 1)
    first = lane == 0
    last = lane == cols - 1
    eighth = iota((8, cols), 0)

    def load(f):
        parts = []
        for packet, shift_of in ((west, 2 * cols - SIDE[f]), (east, cols)):
            pieces = []
            for start, stop, first_lane in segments(rows):
                layer = packet[packet.shape[0] - (stop - start) :]
                pieces.append(pltpu.roll(layer, (shift_of - START[f] - first_lane) % cols, 1))
            parts.append(jnp.concatenate(pieces, axis=0))
        a, b = parts
        beside = jnp.where(lane >= cols - SIDE[f], a, jnp.where(lane < SIDE[f], b, 0.0))

        def put(cells, side):
            new = folded[side, ROW[f] : ROW[f] + 8, :]
            new = jnp.where(eighth < DEEP[f], jnp.where(top, new, cells[rows : rows + 8]), 0.0)
            return jnp.concatenate([cells[:rows], new, cells[rows + 8 :]], axis=0)

        return put(ext[f], 0), put(beside, 1)

    def plus_x(pair):
        a, b = (pltpu.roll(part, cols - 1, 1) for part in pair)
        return jnp.where(last, b, a), jnp.where(last, a, b)

    def minus_x(pair):
        a, b = (pltpu.roll(part, 1, 1) for part in pair)
        return jnp.where(first, b, a), jnp.where(first, a, b)

    def plus_y(pair):
        return tuple(pltpu.roll(part, tall - 1, 0) for part in pair)

    def minus_y(pair):
        return tuple(pltpu.roll(part, 1, 0) for part in pair)

    def each(function, *pairs):
        return tuple(function(*parts) for parts in zip(*pairs))

    def neighbours(pair):
        return each(
            lambda a, b, c, d: (a + b) + (c + d), plus_x(pair), minus_x(pair), plus_y(pair), minus_y(pair)
        )

    press, zonal, merid, wet, weights, anomaly = (load(f) for f in range(FIELDS))
    half = 0.5 * TIME_STEP
    flow = lambda w, speed, a, b: w * (speed - half * (a - b))
    east_flow = each(flow, wet, zonal, plus_x(press), minus_x(press))
    north_flow = each(flow, wet, merid, plus_y(press), minus_y(press))
    right = each(
        lambda w, g, n, a, b, c, d: w * (g * n - 0.5 * (a - b + c - d)),
        wet,
        weights,
        anomaly,
        plus_x(east_flow),
        minus_x(east_flow),
        plus_y(north_flow),
        minus_y(north_flow),
    )
    diagonal = each(lambda g: 4.0 + g, weights)
    inverse = each(lambda m: 1.0 / m, diagonal)
    scale = each(lambda w, i: w * i, wet, inverse)
    zero = each(lambda r, i: r * i, right, inverse)
    one = each(lambda a, n, z: a * n - theta * z, scale, neighbours(zero), zero)
    two = each(lambda a, n, z: a * n - theta * z, scale, neighbours(one), one)
    three = scale[0][:rows] * neighbours(two)[0][:rows] - theta * two[0][:rows]
    right, middle = right[0][:rows], diagonal[0][:rows]
    zero, one, two = zero[0][:rows], one[0][:rows], two[0][:rows]
    base[0] = zero
    base[1] = one
    base[2] = two
    weighted_one = middle * one
    weighted_two = middle * two
    products = (
        right * zero,
        right * one,
        right * two,
        right * three,
        weighted_one * one,
        weighted_one * two,
        weighted_one * three,
        weighted_two * two,
        weighted_two * three,
    )
    which = iota((16, cols), 0)
    place = iota((16, cols), 1)
    sums = jnp.where((which == len(products)) & (place == 0), theta, 0.0)
    for k, product in enumerate(products):
        sums = jnp.where(which == k, jnp.sum(product, axis=0, keepdims=True), sums)
    sums = jnp.sum(sums, axis=1, keepdims=True)
    sums = jnp.sum(jnp.where(which == place, sums, 0.0), axis=0, keepdims=True)
    moments[...] = jnp.broadcast_to(sums, moments.shape)


def step_kernel(
    meta, spans, facing, heat, salt, zonal, merid, water, north_came, south_rows, from_near, from_far,
    heat_out, salt_out, zonal_out, merid_out,
    new_heat, new_salt, new_zonal, new_merid, north_rows, sems,
):
    levels, rows, cols = heat.shape
    deep = 4 * levels
    _, top, lon_odd, _ = flags(meta)
    wet = water[...].astype(jnp.float32)
    lane = iota((rows, cols), 1)
    row = iota((rows, cols), 0)
    east = jnp.where(lon_odd, from_far[...], from_near[...])
    west = jnp.where(lon_odd, from_near[...], from_far[...])
    came = north_came[...]
    across = fold(fold_shift(facing), pltpu.roll(west[:deep], cols // 2, 1), came, east[:deep], False)
    north_rows[...] = jnp.where(top, across, came)

    def around(cells, q):
        a = pltpu.roll(east, (cols - 2 * q) % cols, 1)
        b = pltpu.roll(west, (2 * cols - 2 - 2 * q) % cols, 1)
        side = jnp.where(lane < 2, a, b)

        def shift_x(by):
            a = pltpu.roll(cells, by % cols, 1)
            b = pltpu.roll(side, by % cols, 1)
            own = lane >= by if by > 0 else lane < cols + by
            return jnp.where(own, a, b)

        n0 = north_rows[2 * q : 2 * q + 1, :]
        n1 = north_rows[2 * q + 1 : 2 * q + 2, :]
        s0 = south_rows[2 * q + 1 : 2 * q + 2, :]
        s1 = south_rows[2 * q : 2 * q + 1, :]
        north_one = jnp.where(row == rows - 1, n0, pltpu.roll(cells, rows - 1, 0))
        north_two = jnp.where(row == rows - 1, n1, jnp.where(row == rows - 2, n0, pltpu.roll(cells, rows - 2, 0)))
        south_one = jnp.where(row == 0, s0, pltpu.roll(cells, 1, 0))
        south_two = jnp.where(row == 0, s1, jnp.where(row == 1, s0, pltpu.roll(cells, 2, 0)))
        return (shift_x(-1), shift_x(1), shift_x(-2), shift_x(2), north_one, south_one, north_two, south_two)

    def advance(cells, parts, speed_x, speed_y):
        e1, w1, e2, w2, n1, s1, n2, s2 = parts
        grad_east = 8.0 * (e1 - w1) - (e2 - w2)
        grad_north = 8.0 * (n1 - s1) - (n2 - s2)
        laplace = (e1 + w1) + (n1 + s1) - 4.0 * cells
        tendency = (-TIME_STEP / 12.0) * (speed_x * grad_east + speed_y * grad_north) + MIXING * laplace
        return cells + wet * tendency

    stores = ((new_heat, heat_out), (new_salt, salt_out), (new_zonal, zonal_out), (new_merid, merid_out))
    size = levels // sems.shape[1]
    copies = []
    half = 0.5 * TIME_STEP
    above_x = jnp.zeros((rows, cols), jnp.float32)
    above_y = jnp.zeros((rows, cols), jnp.float32)
    for k in range(levels):
        t, s, u, v = heat[k], salt[k], zonal[k], merid[k]
        around_t = around(t, k)
        around_s = around(s, levels + k)
        new_heat[k] = advance(t, around_t, u, v)
        new_salt[k] = advance(s, around_s, u, v)
        span = spans[0:1, k : k + 1]
        layer_x = span * (density(around_t[0], around_s[0]) - density(around_t[1], around_s[1]))
        layer_y = span * (density(around_t[4], around_s[4]) - density(around_t[5], around_s[5]))
        new_zonal[k] = wet * (u - half * (above_x + 0.5 * layer_x))
        new_merid[k] = wet * (v - half * (above_y + 0.5 * layer_y))
        above_x = above_x + layer_x
        above_y = above_y + layer_y
        if (k + 1) % size == 0:
            piece = pl.ds(k + 1 - size, size)
            for i, (near_ref, far_ref) in enumerate(stores):
                copies.append(pltpu.make_async_copy(near_ref.at[piece], far_ref.at[piece], sems.at[i, k // size]))
                copies[-1].start()
    for copy in copies:
        copy.wait()


def surface_kernel(shares, shift, base, surface):
    lanes = shares.shape[1]
    g00, g01, g02, g03, g11, g12, g13, g22, g23, theta = (
        shares[...] if k == 0 else pltpu.roll(shares[...], lanes - k, 1) for k in range(10)
    )
    add = lambda terms: jnp.sum(terms, axis=0, keepdims=True)

    def ratio(a, b):
        good = b > 0.0
        return jnp.where(good, a / jnp.where(good, b, 1.0), 0.0)

    def form(p, h):
        total = 0.0
        for i, a in enumerate(p):
            for j in range(i, len(p)):
                term = a * p[j] * h[i + j]
                total = total + (term if i == j else 2.0 * term)
        return total

    whole = add(g00)
    common = ratio(add(theta * g00 + g01), whole)
    d = theta - common
    mu = [
        whole,
        add(g01 + d * g00),
        add(g11 + d * (2.0 * g01 + d * g00)),
        add(g12 + d * (2.0 * g11 + g02 + d * (3.0 * g01 + d * g00))),
        add(g22 + d * (4.0 * g12 + d * (2.0 * g02 + 4.0 * g11 + d * (4.0 * g01 + d * g00)))),
        add(
            g23
            + d * (3.0 * g22 + 2.0 * g13 + d * (9.0 * g12 + g03 + d * (4.0 * g02 + 6.0 * g11 + d * (5.0 * g01 + d * g00))))
        ),
    ]
    scale = 1.0 - common
    gap = [scale * mu[k] - mu[k + 1] for k in range(5)]
    alpha = ratio(mu[0], gap[0])
    y = [-alpha * ratio(mu[1], mu[0]), alpha]
    x = [alpha, 0.0, 0.0]
    rz = form(y, mu)
    p = [y[0] + ratio(rz, mu[0]), y[1]]
    alpha = ratio(rz, form(p, gap))
    x = [x[0] + alpha * p[0], alpha * p[1], 0.0]
    y = [y[0] - alpha * scale * p[0], y[1] - alpha * (scale * p[1] - p[0]), alpha * p[1]]
    new = form(y, mu)
    beta = ratio(new, rz)
    p = [y[0] + beta * p[0], y[1] + beta * p[1], y[2]]
    alpha = ratio(new, form(p, gap))
    x = [x[0] + alpha * p[0], x[1] + alpha * p[1], alpha * p[2]]
    d = shift[0:1, :] - common
    x = [x[0] + d * (x[1] + d * x[2]), x[1] + 2.0 * d * x[2], x[2]]
    x = [value[0:1, 0:1] for value in x]
    surface[...] = x[0] * base[0] + x[1] * base[1] + x[2] * base[2]


def call(kernel, outs, flops, moved, name, out_space=pltpu.VMEM, scratch=(), types=jnp.float32):
    def run(*args):
        return pl.pallas_call(
            kernel,
            out_shape=[jax.ShapeDtypeStruct(shape, types) for shape in outs],
            in_specs=[pl.BlockSpec(memory_space=pltpu.VMEM)] * len(args),
            out_specs=[pl.BlockSpec(memory_space=out_space)] * len(outs),
            scratch_shapes=list(scratch),
            cost_estimate=pl.CostEstimate(flops=flops, bytes_accessed=moved, transcendentals=0),
            compiler_params=pltpu.CompilerParams(vmem_limit_bytes=VMEM_LIMIT),
            name=name,
        )(*args)

    return run


def body(
    warmth_deviation,
    saltiness_deviation,
    easterly_speed,
    poleward_speed,
    stratum_spans,
    water_indicator,
    opposite_counterpart,
    elevation_weights,
    elevation_anomaly,
):
    lons, lats = lax.axis_size("lon"), lax.axis_size("lat")
    lon, lat = lax.axis_index("lon"), lax.axis_index("lat")
    levels, rows, cols = warmth_deviation.shape
    high = packet_rows(levels)
    assert cols & (cols - 1) == 0 and rows >= 24 and rows // 2 == high - 4 * levels + 8 and 4 * levels <= cols // 2 and 2 * START[-1] <= min(RELAY, cols - RELAY) and cols == 128
    tall = rows + 16
    width = cols * lons
    flat = lambda i, j: (i % lons) * lats + j

    place = (lax.rem(lat, 2), lat == lats - 1, lax.rem(lon, 2), lat == 0, lon)
    meta = jnp.stack([value.astype(jnp.int32) for value in place]).reshape(1, 5)
    (meta,) = call(place_kernel, [(8, cols)], LOAD_FLOPS, 16, "place", types=jnp.int32)(meta)

    spans = stratum_spans.reshape(1, levels)
    facing = opposite_counterpart.reshape(1, cols)
    state = (warmth_deviation, saltiness_deviation, easterly_speed, poleward_speed)
    flat_state = (water_indicator, elevation_weights, elevation_anomaly)
    cells = levels * rows * cols
    sums, first, second, kept = call(
        pack_kernel,
        [(3, rows, cols), *[(high, cols)] * 3],
        12 * cells,
        16 * cells,
        "level_sums",
        scratch=[pltpu.VMEM((high, cols), jnp.float32)] * 3,
    )(meta, spans, facing, *state, *flat_state)

    axes = ("lon", "lat")
    pairs_first = [(flat(i, j), flat(i, j ^ 1)) for i in range(lons) for j in range(lats)]
    pairs_inner = [
        (flat(i, a), flat(i, b))
        for i in range(lons)
        for j in range(1, lats - 1, 2)
        for a, b in ((j, j + 1), (j + 1, j))
    ] + [(flat(i, 0), flat(i ^ 1, 0)) for i in range(lons)]

    counterpart, first = lax.optimization_barrier((opposite_counterpart, first))
    hinge = lax.rem(counterpart[0] + 1 + cols * lon, width)
    block = lax.rem((hinge + cols // 2) // cols, lons)

    deep = 4 * levels

    def exchange(block, first, second):
        partner = [(block - 1 - i) % lons for i in range(lons)]
        partner = [i + lons // 2 if i == p else p for i, p in enumerate(partner)]
        pairs_fold = [(flat(p, lats - 1), flat(i, lats - 1)) for i, p in enumerate(partner)]
        second = lax.ppermute(second, axes, pairs_inner + pairs_fold)
        first = lax.ppermute(first, axes, pairs_first)
        columns = call(column_kernel, [(rows, cols)] * 2, 4 * cells, 8 * cells, "columns")(*state[:2])
        return call(
            functools.partial(turn_kernel, lons),
            [
                (FIELDS, tall, cols),
                *[(rows // 2, cols)] * 2,
                *[(rows, cols)] * 2,
                (high - deep, cols),
                *[(deep, cols)] * 2,
            ],
            FIELDS * tall * cols,
            4 * 4 * FIELDS * tall * cols,
            "row_halos",
        )(meta, facing, kept, sums, *flat_state, second, first, *columns)

    ext, to_far, to_near, state_near, state_far, facing_rows, north_rows, south_rows = lax.switch(
        block, [functools.partial(exchange, s) for s in range(lons)], first, second
    )

    near = lambda cells: lax.ppermute(cells, "lon", [(i, i ^ 1) for i in range(lons)])
    far = lambda cells: lax.ppermute(cells, "lon", [(i, (i + 1 if i % 2 else i - 1) % lons) for i in range(lons)])
    from_far, from_near = far(to_far), near(to_near)
    state_near, state_far = near(state_near), far(state_far)

    (shift,) = call(shift_kernel, [(8, cols)], 60 * rows * cols, 24 * rows * cols, "basis_shift")(ext)

    count = lons * lats
    base, moments = call(
        krylov_kernel,
        [(3, rows, cols), (count, cols)],
        200 * tall * cols,
        4 * 12 * tall * cols,
        "krylov",
        scratch=[pltpu.VMEM((2, high - deep + 8, cols), jnp.float32)],
    )(meta, facing, shift, ext, facing_rows, from_far, from_near)

    chunks = 5 if levels % 5 == 0 else 1
    new_heat, new_salt, new_zonal, new_merid = call(
        step_kernel,
        [(levels, rows, cols)] * 4,
        120 * cells,
        32 * cells,
        "levels_step",
        out_space=pltpu.HBM,
        scratch=[
            *[pltpu.VMEM((levels, rows, cols), jnp.float32)] * 4,
            pltpu.VMEM((deep, cols), jnp.float32),
            pltpu.SemaphoreType.DMA((4, chunks)),
        ],
    )(meta, spans, facing, *state, water_indicator, north_rows, south_rows, state_near, state_far)

    shares = lax.all_to_all(moments, axes, 0, 0, tiled=True)
    (surface,) = call(surface_kernel, [(rows, cols)], 6 * rows * cols, 16 * rows * cols, "surface")(shares, shift, base)
    return (new_heat, new_salt, new_zonal, new_merid, surface)


def solution(mesh):
    for axis in mesh.shape.values():
        assert axis > 1 and axis & (axis - 1) == 0
    levels = P(None, "lat", "lon")
    flat = P("lat", "lon")
    return jax.shard_map(
        body,
        mesh=mesh,
        in_specs=(levels, levels, levels, levels, P(), flat, P("lon"), flat, flat),
        out_specs=(levels, levels, levels, levels, flat),
        check_vma=False,
    )
```

```python
import functools

import jax
import jax.numpy as jnp
from jax import lax
from jax.experimental import pallas as pl
from jax.experimental.pallas import tpu as pltpu
from jax.sharding import PartitionSpec as P

TIME_STEP = 0.1
MIXING = 0.1

DEEP = (5, 3, 4, 4, 3, 3)
SIDE = (5, 4, 3, 4, 3, 3)
FIELDS = len(SIDE)
ROW = tuple(sum(DEEP[:f]) for f in range(FIELDS + 1))
START = tuple(sum(SIDE[:f]) for f in range(FIELDS + 1))
RELAY = 56
FLIPPED = (1, 2)
VMEM_LIMIT = 32 * 1024 * 1024
LOAD_FLOPS = 10**10


def density(heat, salt):
    return heat * (-1.0 - 0.15 * heat - 0.2 * salt) + 0.8 * salt


def iota(shape, axis):
    return lax.broadcasted_iota(jnp.int32, shape, axis)


def packet_rows(levels):
    return -(-(4 * levels + ROW[-1]) // 8) * 8


def flags(meta):
    return tuple(meta[i : i + 1, :] == 1 for i in range(4))


def segments(rows):
    size = START[-1]
    return (0, rows // 2, 0), (rows // 2, rows, size), (rows, rows + 8, RELAY), (rows + 8, rows + 16, RELAY + size)


def place_kernel(meta, placed):
    for i in range(5):
        placed[i : i + 1, :] = jnp.broadcast_to(meta[0:1, i : i + 1], (1, placed.shape[1]))
    placed[5:, :] = jnp.zeros((placed.shape[0] - 5, placed.shape[1]), jnp.int32)


def pack_kernel(
    meta, spans, facing, heat, salt, zonal, merid, water, weights, anomaly,
    sums, first, second, kept, east_columns, west_columns,
    top, bottom, back,
):
    levels, rows, cols = heat.shape
    span = [spans[0:1, k : k + 1] for k in range(levels)]
    below = [None] * levels
    total = jnp.zeros((1, 1), jnp.float32)
    for k in reversed(range(levels)):
        below[k] = span[k] * (0.5 * span[k] + total)
        total = total + span[k]
    pair = iota((rows, cols), 1) // 2
    zero = jnp.zeros((rows, cols), jnp.float32)
    press, east, north, east_edge, west_edge = zero, zero, zero, zero, zero
    for k in range(levels):
        press = press + below[k] * density(heat[k], salt[k])
        east = east + span[k] * zonal[k]
        north = north + span[k] * merid[k]
        for q, source in ((k, heat), (levels + k, salt)):
            cells = source[k]
            here = pair == q
            east_edge = jnp.where(here, pltpu.roll(cells, (2 * q + 2) % cols, 1), east_edge)
            west_edge = jnp.where(here, pltpu.roll(cells, 2 * q, 1), west_edge)
            top[2 * q : 2 * q + 2, :] = source[k, rows - 2 :, :]
            bottom[2 * q : 2 * q + 2, :] = source[k, :2, :]
            for i in range(2):
                back[2 * q + i : 2 * q + i + 1, :] = source[k, rows - 1 - i : rows - i, :]
    east_columns[...] = east_edge
    west_columns[...] = west_edge
    sums[0] = press
    sums[1] = east
    sums[2] = north
    fields = (sums.at[0], sums.at[1], sums.at[2], water, weights, anomaly)
    for f, field in enumerate(fields):
        at = 4 * levels + ROW[f]
        deep = DEEP[f]
        top[at : at + deep, :] = field[rows - deep :, :].astype(jnp.float32)
        bottom[at : at + deep, :] = field[:deep, :].astype(jnp.float32)
        for j in range(deep):
            back[at + j : at + j + 1, :] = field[rows - 1 - j : rows - j, :].astype(jnp.float32)
    used = 4 * levels + ROW[-1]
    high = first.shape[0]
    if used < high:
        for packet in (top, bottom, back):
            packet[used:, :] = jnp.zeros((high - used, cols), jnp.float32)
    odd, last, _, _ = flags(meta)
    first[...] = jnp.where(odd, bottom[...], top[...])
    packet = jnp.where(last, back[...], jnp.where(odd, top[...], bottom[...]))
    second[...] = packet
    kept[...] = packet


def turn_kernel(
    lons, meta, facing, mine, sums, water, weights, anomaly, second, first, east_columns, west_columns,
    ext, to_far, to_near, state_far, facing_rows, north_rows, south_rows,
):
    rows, cols = sums.shape[1], sums.shape[2]
    tall = ext.shape[1]
    deep = north_rows.shape[0]
    odd, top, lon_odd, bottom = flags(meta)
    from_first = first[...]
    hinge = facing[0:1, 0:1] + 1 + cols * meta[4:5, 0:1] + cols // 2
    block = lax.shift_right_logical(hinge & (lons * cols - 1), cols.bit_length() - 1)
    alone = ((block - 1 - 2 * meta[4:5, 0:1]) & (lons - 1)) == 0
    from_second = jnp.where(top & alone, mine[...], second[...])
    north = jnp.where(odd, from_second, from_first)
    south = jnp.where(bottom, 0.0, jnp.where(odd, from_first, from_second))
    fields = (sums.at[0], sums.at[1], sums.at[2], water, weights, anomaly)
    for f in range(FIELDS):
        at = deep + ROW[f]
        size = DEEP[f]
        ext[f, :rows, :] = fields[f][...].astype(jnp.float32)
        ext[f, rows : rows + size, :] = north[at : at + size]
        ext[f, rows + size : tall - size, :] = jnp.zeros((tall - rows - 2 * size, cols), jnp.float32)
        ext[f, tall - size :, :] = south[at : at + size]
    passed = from_second[deep:]
    size = passed.shape[0]
    half = rows // 2
    lane = iota((half, cols), 1)
    lower = iota((half, cols), 0) >= size
    empty = jnp.zeros((size, cols), jnp.float32)
    spare = jnp.zeros((half - size, cols), jnp.float32)
    relay = lane >= RELAY
    east = jnp.where(relay, jnp.concatenate([pltpu.roll(passed, RELAY, 1), spare], axis=0), 0.0)
    west = jnp.where(relay, jnp.concatenate([passed, spare], axis=0), 0.0)
    for f in range(FIELDS):
        for start, stop, first_lane in segments(rows):
            at = START[f] + first_lane
            here = (lane >= at) & (lane < at + SIDE[f])
            layer = ext[f, start:stop, :]
            to_east = pltpu.roll(layer, (at + SIDE[f]) % cols, 1)
            to_west = pltpu.roll(layer, at, 1)
            if stop - start < half:
                here = here & lower
                to_east = jnp.concatenate([empty, to_east], axis=0)
                to_west = jnp.concatenate([empty, to_west], axis=0)
            east = jnp.where(here, to_east, east)
            west = jnp.where(here, to_west, west)
    to_far[...] = jnp.where(lon_odd, east, west)
    to_near[:half, :] = jnp.where(lon_odd, west, east)
    passed = from_second[:deep]
    spare = jnp.zeros((rows - deep, cols), jnp.float32)
    right_half = iota((rows, cols), 1) >= cols // 2
    east = jnp.where(right_half, jnp.concatenate([pltpu.roll(passed, cols // 2, 1), spare], axis=0), east_columns[...])
    west = jnp.where(right_half, jnp.concatenate([passed, spare], axis=0), west_columns[...])
    state_far[...] = jnp.where(lon_odd, east, west)
    to_near[half:, :] = jnp.where(lon_odd, west, east)
    facing_rows[...] = from_second[deep:]
    north_rows[...] = north[:deep]
    south_rows[...] = south[:deep]


def fold_shift(facing):
    cols = facing.shape[1]
    offset = (facing[0:1, 0:1] + 1) & (cols - 1)
    return jnp.where(offset >= cols // 2, offset - cols, offset)


def fold(shift, west, own, east, beside):
    rows, cols = own.shape
    lane = iota((rows, cols), 1)
    source = cols - 1 - lane
    if beside:
        place = (source + shift) & (cols - 1)
        low = jnp.where(place - cols < shift, west, own)
        merged = jnp.where(place >= cols // 2, low, jnp.where(place >= shift, east, own))
    else:
        merged = jnp.where(source >= cols - shift, west, jnp.where(source < -shift, east, own))
    return jnp.take_along_axis(merged, cols - 1 - ((lane - shift) & (cols - 1)), axis=1)


def shift_kernel(ext, shift):
    rows, cols = ext.shape[1] - 16, ext.shape[2]
    press, zonal, merid, wet, weights, anomaly = (ext[f, :rows, :] for f in range(FIELDS))
    plus_x = lambda cells: pltpu.roll(cells, cols - 1, 1)
    minus_x = lambda cells: pltpu.roll(cells, 1, 1)
    plus_y = lambda cells: pltpu.roll(cells, rows - 1, 0)
    minus_y = lambda cells: pltpu.roll(cells, 1, 0)
    half = 0.5 * TIME_STEP
    east_flow = wet * (zonal - half * (plus_x(press) - minus_x(press)))
    north_flow = wet * (merid - half * (plus_y(press) - minus_y(press)))
    spread = plus_x(east_flow) - minus_x(east_flow) + plus_y(north_flow) - minus_y(north_flow)
    right = wet * (weights * anomaly - 0.5 * spread)
    inverse = 1.0 / (4.0 + weights)
    zero = right * inverse
    one = wet * inverse * (plus_x(zero) + minus_x(zero) + plus_y(zero) + minus_y(zero))
    lane = iota((rows, cols), 1)
    row = iota((rows, cols), 0)
    inside = (lane >= 8) & (lane < cols - 8) & (row >= 8) & (row < rows - 8)
    total = lambda cells: jnp.sum(jnp.sum(jnp.where(inside, cells, 0.0), axis=0, keepdims=True), axis=1, keepdims=True)
    below = total(right * zero)
    good = below > 0.0
    quotient = jnp.where(good, total(right * one) / jnp.where(good, below, 1.0), 0.0)
    shift[...] = jnp.broadcast_to(jnp.clip(quotient, -1.0, 1.0), shift.shape)


def krylov_kernel(meta, facing, shift, ext, facing_rows, from_far, from_near, base, moments, folded):
    tall, cols = ext.shape[1], ext.shape[2]
    rows = base.shape[1]
    size = facing_rows.shape[0]
    _, top, lon_odd, _ = flags(meta)
    near = from_near[: from_far.shape[0], :]
    west = jnp.where(lon_odd, near, from_far[...])
    east = jnp.where(lon_odd, from_far[...], near)
    theta = shift[0:1, 0:1]
    across = fold_shift(facing)
    row = iota((size, cols), 0)
    flips = (row >= ROW[FLIPPED[0]]) & (row < ROW[FLIPPED[-1] + 1])
    for side in range(2):
        cells = fold(across, pltpu.roll(west[:size], cols - RELAY, 1), facing_rows[...], east[:size], side == 1)
        folded[side, :size, :] = jnp.where(flips, -cells, cells)
    folded[:, size:, :] = jnp.zeros((2, folded.shape[1] - size, cols), jnp.float32)
    lane = iota((tall, cols), 1)
    first = lane == 0
    last = lane == cols - 1
    eighth = iota((8, cols), 0)

    def load(f):
        parts = []
        for packet, shift_of in ((west, 2 * cols - SIDE[f]), (east, cols)):
            pieces = []
            for start, stop, first_lane in segments(rows):
                layer = packet[packet.shape[0] - (stop - start) :]
                pieces.append(pltpu.roll(layer, (shift_of - START[f] - first_lane) % cols, 1))
            parts.append(jnp.concatenate(pieces, axis=0))
        a, b = parts
        beside = jnp.where(lane >= cols - SIDE[f], a, jnp.where(lane < SIDE[f], b, 0.0))

        def put(cells, side):
            new = folded[side, ROW[f] : ROW[f] + 8, :]
            new = jnp.where(eighth < DEEP[f], jnp.where(top, new, cells[rows : rows + 8]), 0.0)
            return jnp.concatenate([cells[:rows], new, cells[rows + 8 :]], axis=0)

        return put(ext[f], 0), put(beside, 1)

    def plus_x(pair):
        a, b = (pltpu.roll(part, cols - 1, 1) for part in pair)
        return jnp.where(last, b, a), jnp.where(last, a, b)

    def minus_x(pair):
        a, b = (pltpu.roll(part, 1, 1) for part in pair)
        return jnp.where(first, b, a), jnp.where(first, a, b)

    def plus_y(pair):
        return tuple(pltpu.roll(part, tall - 1, 0) for part in pair)

    def minus_y(pair):
        return tuple(pltpu.roll(part, 1, 0) for part in pair)

    def each(function, *pairs):
        return tuple(function(*parts) for parts in zip(*pairs))

    def neighbours(pair):
        return each(
            lambda a, b, c, d: (a + b) + (c + d), plus_x(pair), minus_x(pair), plus_y(pair), minus_y(pair)
        )

    press, zonal, merid, wet, weights, anomaly = (load(f) for f in range(FIELDS))
    half = 0.5 * TIME_STEP
    flow = lambda w, speed, a, b: w * (speed - half * (a - b))
    east_flow = each(flow, wet, zonal, plus_x(press), minus_x(press))
    north_flow = each(flow, wet, merid, plus_y(press), minus_y(press))
    right = each(
        lambda w, g, n, a, b, c, d: w * (g * n - 0.5 * (a - b + c - d)),
        wet,
        weights,
        anomaly,
        plus_x(east_flow),
        minus_x(east_flow),
        plus_y(north_flow),
        minus_y(north_flow),
    )
    diagonal = each(lambda g: 4.0 + g, weights)
    inverse = each(lambda m: 1.0 / m, diagonal)
    scale = each(lambda w, i: w * i, wet, inverse)
    zero = each(lambda r, i: r * i, right, inverse)
    one = each(lambda a, n, z: a * n - theta * z, scale, neighbours(zero), zero)
    two = each(lambda a, n, z: a * n - theta * z, scale, neighbours(one), one)
    three = scale[0][:rows] * neighbours(two)[0][:rows] - theta * two[0][:rows]
    right, middle = right[0][:rows], diagonal[0][:rows]
    zero, one, two = zero[0][:rows], one[0][:rows], two[0][:rows]
    base[0] = zero
    base[1] = one
    base[2] = two
    weighted_one = middle * one
    weighted_two = middle * two
    products = (
        right * zero,
        right * one,
        right * two,
        right * three,
        weighted_one * one,
        weighted_one * two,
        weighted_one * three,
        weighted_two * two,
        weighted_two * three,
    )
    which = iota((16, cols), 0)
    place = iota((16, cols), 1)
    sums = jnp.where((which == len(products)) & (place == 0), theta, 0.0)
    for k, product in enumerate(products):
        sums = jnp.where(which == k, jnp.sum(product, axis=0, keepdims=True), sums)
    sums = jnp.sum(sums, axis=1, keepdims=True)
    sums = jnp.sum(jnp.where(which == place, sums, 0.0), axis=0, keepdims=True)
    moments[...] = jnp.broadcast_to(sums, moments.shape)


def step_kernel(
    meta, spans, facing, heat, salt, zonal, merid, water, north_came, south_rows, from_far, from_near,
    heat_out, salt_out, zonal_out, merid_out,
    new_heat, new_salt, new_zonal, new_merid, north_rows, sems,
):
    levels, rows, cols = heat.shape
    deep = 4 * levels
    _, top, lon_odd, _ = flags(meta)
    wet = water[...].astype(jnp.float32)
    lane = iota((rows, cols), 1)
    row = iota((rows, cols), 0)
    near = from_near[from_near.shape[0] - rows :, :]
    east = jnp.where(lon_odd, from_far[...], near)
    west = jnp.where(lon_odd, near, from_far[...])
    came = north_came[...]
    across = fold(fold_shift(facing), pltpu.roll(west[:deep], cols // 2, 1), came, east[:deep], False)
    north_rows[...] = jnp.where(top, across, came)

    def around(cells, q):
        a = pltpu.roll(east, (cols - 2 * q) % cols, 1)
        b = pltpu.roll(west, (2 * cols - 2 - 2 * q) % cols, 1)
        side = jnp.where(lane < 2, a, b)

        def shift_x(by):
            a = pltpu.roll(cells, by % cols, 1)
            b = pltpu.roll(side, by % cols, 1)
            own = lane >= by if by > 0 else lane < cols + by
            return jnp.where(own, a, b)

        n0 = north_rows[2 * q : 2 * q + 1, :]
        n1 = north_rows[2 * q + 1 : 2 * q + 2, :]
        s0 = south_rows[2 * q + 1 : 2 * q + 2, :]
        s1 = south_rows[2 * q : 2 * q + 1, :]
        north_one = jnp.where(row == rows - 1, n0, pltpu.roll(cells, rows - 1, 0))
        north_two = jnp.where(row == rows - 1, n1, jnp.where(row == rows - 2, n0, pltpu.roll(cells, rows - 2, 0)))
        south_one = jnp.where(row == 0, s0, pltpu.roll(cells, 1, 0))
        south_two = jnp.where(row == 0, s1, jnp.where(row == 1, s0, pltpu.roll(cells, 2, 0)))
        return (shift_x(-1), shift_x(1), shift_x(-2), shift_x(2), north_one, south_one, north_two, south_two)

    def advance(cells, parts, speed_x, speed_y):
        e1, w1, e2, w2, n1, s1, n2, s2 = parts
        grad_east = 8.0 * (e1 - w1) - (e2 - w2)
        grad_north = 8.0 * (n1 - s1) - (n2 - s2)
        laplace = (e1 + w1) + (n1 + s1) - 4.0 * cells
        tendency = (-TIME_STEP / 12.0) * (speed_x * grad_east + speed_y * grad_north) + MIXING * laplace
        return cells + wet * tendency

    stores = ((new_heat, heat_out), (new_salt, salt_out), (new_zonal, zonal_out), (new_merid, merid_out))
    size = levels // sems.shape[1]
    copies = []
    half = 0.5 * TIME_STEP
    above_x = jnp.zeros((rows, cols), jnp.float32)
    above_y = jnp.zeros((rows, cols), jnp.float32)
    for k in range(levels):
        t, s, u, v = heat[k], salt[k], zonal[k], merid[k]
        around_t = around(t, k)
        around_s = around(s, levels + k)
        new_heat[k] = advance(t, around_t, u, v)
        new_salt[k] = advance(s, around_s, u, v)
        span = spans[0:1, k : k + 1]
        layer_x = span * (density(around_t[0], around_s[0]) - density(around_t[1], around_s[1]))
        layer_y = span * (density(around_t[4], around_s[4]) - density(around_t[5], around_s[5]))
        new_zonal[k] = wet * (u - half * (above_x + 0.5 * layer_x))
        new_merid[k] = wet * (v - half * (above_y + 0.5 * layer_y))
        above_x = above_x + layer_x
        above_y = above_y + layer_y
        if (k + 1) % size == 0:
            piece = pl.ds(k + 1 - size, size)
            for i, (near_ref, far_ref) in enumerate(stores):
                copies.append(pltpu.make_async_copy(near_ref.at[piece], far_ref.at[piece], sems.at[i, k // size]))
                copies[-1].start()
    for copy in copies:
        copy.wait()


def surface_kernel(shares, shift, base, surface):
    lanes = shares.shape[1]
    g00, g01, g02, g03, g11, g12, g13, g22, g23, theta = (
        shares[...] if k == 0 else pltpu.roll(shares[...], lanes - k, 1) for k in range(10)
    )
    add = lambda terms: jnp.sum(terms, axis=0, keepdims=True)

    def ratio(a, b):
        good = b > 0.0
        return jnp.where(good, a / jnp.where(good, b, 1.0), 0.0)

    def form(p, h):
        total = 0.0
        for i, a in enumerate(p):
            for j in range(i, len(p)):
                term = a * p[j] * h[i + j]
                total = total + (term if i == j else 2.0 * term)
        return total

    whole = add(g00)
    common = ratio(add(theta * g00 + g01), whole)
    d = theta - common
    mu = [
        whole,
        add(g01 + d * g00),
        add(g11 + d * (2.0 * g01 + d * g00)),
        add(g12 + d * (2.0 * g11 + g02 + d * (3.0 * g01 + d * g00))),
        add(g22 + d * (4.0 * g12 + d * (2.0 * g02 + 4.0 * g11 + d * (4.0 * g01 + d * g00)))),
        add(
            g23
            + d * (3.0 * g22 + 2.0 * g13 + d * (9.0 * g12 + g03 + d * (4.0 * g02 + 6.0 * g11 + d * (5.0 * g01 + d * g00))))
        ),
    ]
    scale = 1.0 - common
    gap = [scale * mu[k] - mu[k + 1] for k in range(5)]
    alpha = ratio(mu[0], gap[0])
    y = [-alpha * ratio(mu[1], mu[0]), alpha]
    x = [alpha, 0.0, 0.0]
    rz = form(y, mu)
    p = [y[0] + ratio(rz, mu[0]), y[1]]
    alpha = ratio(rz, form(p, gap))
    x = [x[0] + alpha * p[0], alpha * p[1], 0.0]
    y = [y[0] - alpha * scale * p[0], y[1] - alpha * (scale * p[1] - p[0]), alpha * p[1]]
    new = form(y, mu)
    beta = ratio(new, rz)
    p = [y[0] + beta * p[0], y[1] + beta * p[1], y[2]]
    alpha = ratio(new, form(p, gap))
    x = [x[0] + alpha * p[0], x[1] + alpha * p[1], alpha * p[2]]
    d = shift[0:1, :] - common
    x = [x[0] + d * (x[1] + d * x[2]), x[1] + 2.0 * d * x[2], x[2]]
    x = [value[0:1, 0:1] for value in x]
    surface[...] = x[0] * base[0] + x[1] * base[1] + x[2] * base[2]


def call(kernel, outs, flops, moved, name, out_space=pltpu.VMEM, scratch=(), types=jnp.float32):
    def run(*args):
        return pl.pallas_call(
            kernel,
            out_shape=[jax.ShapeDtypeStruct(shape, types) for shape in outs],
            in_specs=[pl.BlockSpec(memory_space=pltpu.VMEM)] * len(args),
            out_specs=[pl.BlockSpec(memory_space=out_space)] * len(outs),
            scratch_shapes=list(scratch),
            cost_estimate=pl.CostEstimate(flops=flops, bytes_accessed=moved, transcendentals=0),
            compiler_params=pltpu.CompilerParams(vmem_limit_bytes=VMEM_LIMIT),
            name=name,
        )(*args)

    return run


def body(
    warmth_deviation,
    saltiness_deviation,
    easterly_speed,
    poleward_speed,
    stratum_spans,
    water_indicator,
    opposite_counterpart,
    elevation_weights,
    elevation_anomaly,
):
    lons, lats = lax.axis_size("lon"), lax.axis_size("lat")
    lon, lat = lax.axis_index("lon"), lax.axis_index("lat")
    levels, rows, cols = warmth_deviation.shape
    high = packet_rows(levels)
    assert cols & (cols - 1) == 0 and rows >= 24 and rows // 2 == high - 4 * levels + 8 and 4 * levels <= cols // 2 and 2 * START[-1] <= min(RELAY, cols - RELAY) and cols == 128
    tall = rows + 16
    width = cols * lons
    flat = lambda i, j: (i % lons) * lats + j

    place = (lax.rem(lat, 2), lat == lats - 1, lax.rem(lon, 2), lat == 0, lon)
    meta = jnp.stack([value.astype(jnp.int32) for value in place]).reshape(1, 5)
    (meta,) = call(place_kernel, [(8, cols)], LOAD_FLOPS, 16, "place", types=jnp.int32)(meta)

    spans = stratum_spans.reshape(1, levels)
    facing = opposite_counterpart.reshape(1, cols)
    state = (warmth_deviation, saltiness_deviation, easterly_speed, poleward_speed)
    flat_state = (water_indicator, elevation_weights, elevation_anomaly)
    cells = levels * rows * cols
    sums, first, second, kept, east_columns, west_columns = call(
        pack_kernel,
        [(3, rows, cols), *[(high, cols)] * 3, (rows, cols), (rows, cols)],
        12 * cells,
        16 * cells,
        "level_sums",
        scratch=[pltpu.VMEM((high, cols), jnp.float32)] * 3,
    )(meta, spans, facing, *state, *flat_state)

    axes = ("lon", "lat")
    pairs_first = [(flat(i, j), flat(i, j ^ 1)) for i in range(lons) for j in range(lats)]
    pairs_inner = [
        (flat(i, a), flat(i, b))
        for i in range(lons)
        for j in range(1, lats - 1, 2)
        for a, b in ((j, j + 1), (j + 1, j))
    ] + [(flat(i, 0), flat(i ^ 1, 0)) for i in range(lons)]

    counterpart, first = lax.optimization_barrier((opposite_counterpart, first))
    hinge = lax.rem(counterpart[0] + 1 + cols * lon, width)
    block = lax.rem((hinge + cols // 2) // cols, lons)

    deep = 4 * levels

    def exchange(block, first, second):
        partner = [(block - 1 - i) % lons for i in range(lons)]
        partner = [i + lons // 2 if i == p else p for i, p in enumerate(partner)]
        pairs_fold = [(flat(p, lats - 1), flat(i, lats - 1)) for i, p in enumerate(partner)]
        second = lax.ppermute(second, axes, pairs_inner + pairs_fold)
        first = lax.ppermute(first, axes, pairs_first)
        return call(
            functools.partial(turn_kernel, lons),
            [
                (FIELDS, tall, cols),
                (rows // 2, cols),
                (rows // 2 + rows, cols),
                (rows, cols),
                (high - deep, cols),
                *[(deep, cols)] * 2,
            ],
            FIELDS * tall * cols,
            4 * 4 * FIELDS * tall * cols,
            "row_halos",
        )(meta, facing, kept, sums, *flat_state, second, first, east_columns, west_columns)

    ext, to_far, to_near, state_far, facing_rows, north_rows, south_rows = lax.switch(
        block, [functools.partial(exchange, s) for s in range(lons)], first, second
    )

    near = lambda cells: lax.ppermute(cells, "lon", [(i, i ^ 1) for i in range(lons)])
    far = lambda cells: lax.ppermute(cells, "lon", [(i, (i + 1 if i % 2 else i - 1) % lons) for i in range(lons)])
    from_far, from_near = far(to_far), near(to_near)
    state_far = far(state_far)

    (shift,) = call(shift_kernel, [(8, cols)], 60 * rows * cols, 24 * rows * cols, "basis_shift")(ext)

    count = lons * lats
    base, moments = call(
        krylov_kernel,
        [(3, rows, cols), (count, cols)],
        200 * tall * cols,
        4 * 12 * tall * cols,
        "krylov",
        scratch=[pltpu.VMEM((2, high - deep + 8, cols), jnp.float32)],
    )(meta, facing, shift, ext, facing_rows, from_far, from_near)

    chunks = 5 if levels % 5 == 0 else 1
    new_heat, new_salt, new_zonal, new_merid = call(
        step_kernel,
        [(levels, rows, cols)] * 4,
        120 * cells,
        32 * cells,
        "levels_step",
        out_space=pltpu.HBM,
        scratch=[
            *[pltpu.VMEM((levels, rows, cols), jnp.float32)] * 4,
            pltpu.VMEM((deep, cols), jnp.float32),
            pltpu.SemaphoreType.DMA((4, chunks)),
        ],
    )(meta, spans, facing, *state, water_indicator, north_rows, south_rows, state_far, from_near)

    shares = lax.all_to_all(moments, axes, 0, 0, tiled=True)
    (surface,) = call(surface_kernel, [(rows, cols)], 6 * rows * cols, 16 * rows * cols, "surface")(shares, shift, base)
    return (new_heat, new_salt, new_zonal, new_merid, surface)


def solution(mesh):
    for axis in mesh.shape.values():
        assert axis > 1 and axis & (axis - 1) == 0
    levels = P(None, "lat", "lon")
    flat = P("lat", "lon")
    return jax.shard_map(
        body,
        mesh=mesh,
        in_specs=(levels, levels, levels, levels, P(), flat, P("lon"), flat, flat),
        out_specs=(levels, levels, levels, levels, flat),
        check_vma=False,
    )
```

```python
import functools

import jax
import jax.numpy as jnp
from jax import lax
from jax.experimental import pallas as pl
from jax.experimental.pallas import tpu as pltpu
from jax.sharding import PartitionSpec as P

TIME_STEP = 0.1
MIXING = 0.1

DEEP = (5, 3, 4, 4, 3, 3)
SIDE = (5, 4, 3, 4, 3, 3)
FIELDS = len(SIDE)
ROW = tuple(sum(DEEP[:f]) for f in range(FIELDS + 1))
START = tuple(sum(SIDE[:f]) for f in range(FIELDS + 1))
RELAY = 56
FLIPPED = (1, 2)
VMEM_LIMIT = 32 * 1024 * 1024
LOAD_FLOPS = 10**10


def density(heat, salt):
    return heat * (-1.0 - 0.15 * heat - 0.2 * salt) + 0.8 * salt


def iota(shape, axis):
    return lax.broadcasted_iota(jnp.int32, shape, axis)


def packet_rows(levels):
    return -(-(4 * levels + ROW[-1]) // 8) * 8


def flags(meta):
    return tuple(meta[i : i + 1, :] == 1 for i in range(4))


def segments(rows):
    size = START[-1]
    return (0, rows // 2, 0), (rows // 2, rows, size), (rows, rows + 8, RELAY), (rows + 8, rows + 16, RELAY + size)


def place_kernel(meta, placed):
    for i in range(5):
        placed[i : i + 1, :] = jnp.broadcast_to(meta[0:1, i : i + 1], (1, placed.shape[1]))
    placed[5:, :] = jnp.zeros((placed.shape[0] - 5, placed.shape[1]), jnp.int32)


def pack_kernel(
    meta, spans, facing, heat, salt, zonal, merid, water, weights, anomaly,
    sums, first, second, kept, east_columns, west_columns,
    top, bottom, back,
):
    levels, rows, cols = heat.shape
    span = [spans[0:1, k : k + 1] for k in range(levels)]
    below = [None] * levels
    total = jnp.zeros((1, 1), jnp.float32)
    for k in reversed(range(levels)):
        below[k] = span[k] * (0.5 * span[k] + total)
        total = total + span[k]
    pair = iota((rows, cols), 1) // 2
    zero = jnp.zeros((rows, cols), jnp.float32)
    press, east, north, east_edge, west_edge = zero, zero, zero, zero, zero
    for k in range(levels):
        press = press + below[k] * density(heat[k], salt[k])
        east = east + span[k] * zonal[k]
        north = north + span[k] * merid[k]
        for q, source in ((k, heat), (levels + k, salt)):
            cells = source[k]
            here = pair == q
            east_edge = jnp.where(here, pltpu.roll(cells, (2 * q + 2) % cols, 1), east_edge)
            west_edge = jnp.where(here, pltpu.roll(cells, 2 * q, 1), west_edge)
            top[2 * q : 2 * q + 2, :] = source[k, rows - 2 :, :]
            bottom[2 * q : 2 * q + 2, :] = source[k, :2, :]
            for i in range(2):
                back[2 * q + i : 2 * q + i + 1, :] = source[k, rows - 1 - i : rows - i, :]
    east_columns[...] = east_edge
    west_columns[...] = west_edge
    sums[0] = press
    sums[1] = east
    sums[2] = north
    fields = (sums.at[0], sums.at[1], sums.at[2], water, weights, anomaly)
    for f, field in enumerate(fields):
        at = 4 * levels + ROW[f]
        deep = DEEP[f]
        top[at : at + deep, :] = field[rows - deep :, :].astype(jnp.float32)
        bottom[at : at + deep, :] = field[:deep, :].astype(jnp.float32)
        for j in range(deep):
            back[at + j : at + j + 1, :] = field[rows - 1 - j : rows - j, :].astype(jnp.float32)
    used = 4 * levels + ROW[-1]
    high = first.shape[0]
    if used < high:
        for packet in (top, bottom, back):
            packet[used:, :] = jnp.zeros((high - used, cols), jnp.float32)
    odd, last, _, _ = flags(meta)
    first[...] = jnp.where(odd, bottom[...], top[...])
    packet = jnp.where(last, back[...], jnp.where(odd, top[...], bottom[...]))
    second[...] = packet
    kept[...] = packet


def turn_kernel(
    lons, meta, facing, mine, sums, water, weights, anomaly, second, first, east_columns, west_columns,
    ext, to_far, to_near, state_near, facing_rows, north_rows, south_rows,
):
    rows, cols = sums.shape[1], sums.shape[2]
    tall = ext.shape[1]
    deep = north_rows.shape[0]
    odd, top, lon_odd, bottom = flags(meta)
    from_first = first[...]
    hinge = facing[0:1, 0:1] + 1 + cols * meta[4:5, 0:1] + cols // 2
    block = lax.shift_right_logical(hinge & (lons * cols - 1), cols.bit_length() - 1)
    alone = ((block - 1 - 2 * meta[4:5, 0:1]) & (lons - 1)) == 0
    from_second = jnp.where(top & alone, mine[...], second[...])
    north = jnp.where(odd, from_second, from_first)
    south = jnp.where(bottom, 0.0, jnp.where(odd, from_first, from_second))
    fields = (sums.at[0], sums.at[1], sums.at[2], water, weights, anomaly)
    for f in range(FIELDS):
        at = deep + ROW[f]
        size = DEEP[f]
        ext[f, :rows, :] = fields[f][...].astype(jnp.float32)
        ext[f, rows : rows + size, :] = north[at : at + size]
        ext[f, rows + size : tall - size, :] = jnp.zeros((tall - rows - 2 * size, cols), jnp.float32)
        ext[f, tall - size :, :] = south[at : at + size]
    passed = from_second[deep:]
    size = passed.shape[0]
    half = rows // 2
    lane = iota((half, cols), 1)
    lower = iota((half, cols), 0) >= size
    empty = jnp.zeros((size, cols), jnp.float32)
    spare = jnp.zeros((half - size, cols), jnp.float32)
    relay = lane >= RELAY
    east = jnp.where(relay, jnp.concatenate([pltpu.roll(passed, RELAY, 1), spare], axis=0), 0.0)
    west = jnp.where(relay, jnp.concatenate([passed, spare], axis=0), 0.0)
    for f in range(FIELDS):
        for start, stop, first_lane in segments(rows):
            at = START[f] + first_lane
            here = (lane >= at) & (lane < at + SIDE[f])
            layer = ext[f, start:stop, :]
            to_east = pltpu.roll(layer, (at + SIDE[f]) % cols, 1)
            to_west = pltpu.roll(layer, at, 1)
            if stop - start < half:
                here = here & lower
                to_east = jnp.concatenate([empty, to_east], axis=0)
                to_west = jnp.concatenate([empty, to_west], axis=0)
            east = jnp.where(here, to_east, east)
            west = jnp.where(here, to_west, west)
    to_far[:half, :] = jnp.where(lon_odd, east, west)
    to_near[...] = jnp.where(lon_odd, west, east)
    passed = from_second[:deep]
    spare = jnp.zeros((rows - deep, cols), jnp.float32)
    right_half = iota((rows, cols), 1) >= cols // 2
    east = jnp.where(right_half, jnp.concatenate([pltpu.roll(passed, cols // 2, 1), spare], axis=0), east_columns[...])
    west = jnp.where(right_half, jnp.concatenate([passed, spare], axis=0), west_columns[...])
    to_far[half:, :] = jnp.where(lon_odd, east, west)
    state_near[...] = jnp.where(lon_odd, west, east)
    facing_rows[...] = from_second[deep:]
    north_rows[...] = north[:deep]
    south_rows[...] = south[:deep]


def fold_shift(facing):
    cols = facing.shape[1]
    offset = (facing[0:1, 0:1] + 1) & (cols - 1)
    return jnp.where(offset >= cols // 2, offset - cols, offset)


def fold(shift, west, own, east, beside):
    rows, cols = own.shape
    lane = iota((rows, cols), 1)
    source = cols - 1 - lane
    if beside:
        place = (source + shift) & (cols - 1)
        low = jnp.where(place - cols < shift, west, own)
        merged = jnp.where(place >= cols // 2, low, jnp.where(place >= shift, east, own))
    else:
        merged = jnp.where(source >= cols - shift, west, jnp.where(source < -shift, east, own))
    return jnp.take_along_axis(merged, cols - 1 - ((lane - shift) & (cols - 1)), axis=1)


def shift_kernel(ext, shift):
    rows, cols = ext.shape[1] - 16, ext.shape[2]
    press, zonal, merid, wet, weights, anomaly = (ext[f, :rows, :] for f in range(FIELDS))
    plus_x = lambda cells: pltpu.roll(cells, cols - 1, 1)
    minus_x = lambda cells: pltpu.roll(cells, 1, 1)
    plus_y = lambda cells: pltpu.roll(cells, rows - 1, 0)
    minus_y = lambda cells: pltpu.roll(cells, 1, 0)
    half = 0.5 * TIME_STEP
    east_flow = wet * (zonal - half * (plus_x(press) - minus_x(press)))
    north_flow = wet * (merid - half * (plus_y(press) - minus_y(press)))
    spread = plus_x(east_flow) - minus_x(east_flow) + plus_y(north_flow) - minus_y(north_flow)
    right = wet * (weights * anomaly - 0.5 * spread)
    inverse = 1.0 / (4.0 + weights)
    zero = right * inverse
    one = wet * inverse * (plus_x(zero) + minus_x(zero) + plus_y(zero) + minus_y(zero))
    lane = iota((rows, cols), 1)
    row = iota((rows, cols), 0)
    inside = (lane >= 8) & (lane < cols - 8) & (row >= 8) & (row < rows - 8)
    total = lambda cells: jnp.sum(jnp.sum(jnp.where(inside, cells, 0.0), axis=0, keepdims=True), axis=1, keepdims=True)
    below = total(right * zero)
    good = below > 0.0
    quotient = jnp.where(good, total(right * one) / jnp.where(good, below, 1.0), 0.0)
    shift[...] = jnp.broadcast_to(jnp.clip(quotient, -1.0, 1.0), shift.shape)


def krylov_kernel(meta, facing, shift, ext, facing_rows, from_far, from_near, base, moments, folded):
    tall, cols = ext.shape[1], ext.shape[2]
    rows = base.shape[1]
    size = facing_rows.shape[0]
    _, top, lon_odd, _ = flags(meta)
    far = from_far[: from_near.shape[0], :]
    west = jnp.where(lon_odd, from_near[...], far)
    east = jnp.where(lon_odd, far, from_near[...])
    theta = shift[0:1, 0:1]
    across = fold_shift(facing)
    row = iota((size, cols), 0)
    flips = (row >= ROW[FLIPPED[0]]) & (row < ROW[FLIPPED[-1] + 1])
    for side in range(2):
        cells = fold(across, pltpu.roll(west[:size], cols - RELAY, 1), facing_rows[...], east[:size], side == 1)
        folded[side, :size, :] = jnp.where(flips, -cells, cells)
    folded[:, size:, :] = jnp.zeros((2, folded.shape[1] - size, cols), jnp.float32)
    lane = iota((tall, cols), 1)
    first = lane == 0
    last = lane == cols - 1
    eighth = iota((8, cols), 0)

    def load(f):
        parts = []
        for packet, shift_of in ((west, 2 * cols - SIDE[f]), (east, cols)):
            pieces = []
            for start, stop, first_lane in segments(rows):
                layer = packet[packet.shape[0] - (stop - start) :]
                pieces.append(pltpu.roll(layer, (shift_of - START[f] - first_lane) % cols, 1))
            parts.append(jnp.concatenate(pieces, axis=0))
        a, b = parts
        beside = jnp.where(lane >= cols - SIDE[f], a, jnp.where(lane < SIDE[f], b, 0.0))

        def put(cells, side):
            new = folded[side, ROW[f] : ROW[f] + 8, :]
            new = jnp.where(eighth < DEEP[f], jnp.where(top, new, cells[rows : rows + 8]), 0.0)
            return jnp.concatenate([cells[:rows], new, cells[rows + 8 :]], axis=0)

        return put(ext[f], 0), put(beside, 1)

    def plus_x(pair):
        a, b = (pltpu.roll(part, cols - 1, 1) for part in pair)
        return jnp.where(last, b, a), jnp.where(last, a, b)

    def minus_x(pair):
        a, b = (pltpu.roll(part, 1, 1) for part in pair)
        return jnp.where(first, b, a), jnp.where(first, a, b)

    def plus_y(pair):
        return tuple(pltpu.roll(part, tall - 1, 0) for part in pair)

    def minus_y(pair):
        return tuple(pltpu.roll(part, 1, 0) for part in pair)

    def each(function, *pairs):
        return tuple(function(*parts) for parts in zip(*pairs))

    def neighbours(pair):
        return each(
            lambda a, b, c, d: (a + b) + (c + d), plus_x(pair), minus_x(pair), plus_y(pair), minus_y(pair)
        )

    press, zonal, merid, wet, weights, anomaly = (load(f) for f in range(FIELDS))
    half = 0.5 * TIME_STEP
    flow = lambda w, speed, a, b: w * (speed - half * (a - b))
    east_flow = each(flow, wet, zonal, plus_x(press), minus_x(press))
    north_flow = each(flow, wet, merid, plus_y(press), minus_y(press))
    right = each(
        lambda w, g, n, a, b, c, d: w * (g * n - 0.5 * (a - b + c - d)),
        wet,
        weights,
        anomaly,
        plus_x(east_flow),
        minus_x(east_flow),
        plus_y(north_flow),
        minus_y(north_flow),
    )
    diagonal = each(lambda g: 4.0 + g, weights)
    inverse = each(lambda m: 1.0 / m, diagonal)
    scale = each(lambda w, i: w * i, wet, inverse)
    zero = each(lambda r, i: r * i, right, inverse)
    one = each(lambda a, n, z: a * n - theta * z, scale, neighbours(zero), zero)
    two = each(lambda a, n, z: a * n - theta * z, scale, neighbours(one), one)
    three = scale[0][:rows] * neighbours(two)[0][:rows] - theta * two[0][:rows]
    right, middle = right[0][:rows], diagonal[0][:rows]
    zero, one, two = zero[0][:rows], one[0][:rows], two[0][:rows]
    base[0] = zero
    base[1] = one
    base[2] = two
    weighted_one = middle * one
    weighted_two = middle * two
    products = (
        right * zero,
        right * one,
        right * two,
        right * three,
        weighted_one * one,
        weighted_one * two,
        weighted_one * three,
        weighted_two * two,
        weighted_two * three,
    )
    which = iota((16, cols), 0)
    place = iota((16, cols), 1)
    sums = jnp.where((which == len(products)) & (place == 0), theta, 0.0)
    for k, product in enumerate(products):
        sums = jnp.where(which == k, jnp.sum(product, axis=0, keepdims=True), sums)
    sums = jnp.sum(sums, axis=1, keepdims=True)
    sums = jnp.sum(jnp.where(which == place, sums, 0.0), axis=0, keepdims=True)
    moments[...] = jnp.broadcast_to(sums, moments.shape)


def step_kernel(
    meta, spans, facing, heat, salt, zonal, merid, water, north_came, south_rows, from_far, from_near,
    heat_out, salt_out, zonal_out, merid_out,
    new_heat, new_salt, new_zonal, new_merid, north_rows, sems,
):
    levels, rows, cols = heat.shape
    deep = 4 * levels
    _, top, lon_odd, _ = flags(meta)
    wet = water[...].astype(jnp.float32)
    lane = iota((rows, cols), 1)
    row = iota((rows, cols), 0)
    far = from_far[from_far.shape[0] - rows :, :]
    east = jnp.where(lon_odd, far, from_near[...])
    west = jnp.where(lon_odd, from_near[...], far)
    came = north_came[...]
    across = fold(fold_shift(facing), pltpu.roll(west[:deep], cols // 2, 1), came, east[:deep], False)
    north_rows[...] = jnp.where(top, across, came)

    def around(cells, q):
        a = pltpu.roll(east, (cols - 2 * q) % cols, 1)
        b = pltpu.roll(west, (2 * cols - 2 - 2 * q) % cols, 1)
        side = jnp.where(lane < 2, a, b)

        def shift_x(by):
            a = pltpu.roll(cells, by % cols, 1)
            b = pltpu.roll(side, by % cols, 1)
            own = lane >= by if by > 0 else lane < cols + by
            return jnp.where(own, a, b)

        n0 = north_rows[2 * q : 2 * q + 1, :]
        n1 = north_rows[2 * q + 1 : 2 * q + 2, :]
        s0 = south_rows[2 * q + 1 : 2 * q + 2, :]
        s1 = south_rows[2 * q : 2 * q + 1, :]
        north_one = jnp.where(row == rows - 1, n0, pltpu.roll(cells, rows - 1, 0))
        north_two = jnp.where(row == rows - 1, n1, jnp.where(row == rows - 2, n0, pltpu.roll(cells, rows - 2, 0)))
        south_one = jnp.where(row == 0, s0, pltpu.roll(cells, 1, 0))
        south_two = jnp.where(row == 0, s1, jnp.where(row == 1, s0, pltpu.roll(cells, 2, 0)))
        return (shift_x(-1), shift_x(1), shift_x(-2), shift_x(2), north_one, south_one, north_two, south_two)

    def advance(cells, parts, speed_x, speed_y):
        e1, w1, e2, w2, n1, s1, n2, s2 = parts
        grad_east = 8.0 * (e1 - w1) - (e2 - w2)
        grad_north = 8.0 * (n1 - s1) - (n2 - s2)
        laplace = (e1 + w1) + (n1 + s1) - 4.0 * cells
        tendency = (-TIME_STEP / 12.0) * (speed_x * grad_east + speed_y * grad_north) + MIXING * laplace
        return cells + wet * tendency

    stores = ((new_heat, heat_out), (new_salt, salt_out), (new_zonal, zonal_out), (new_merid, merid_out))
    size = levels // sems.shape[1]
    copies = []
    half = 0.5 * TIME_STEP
    above_x = jnp.zeros((rows, cols), jnp.float32)
    above_y = jnp.zeros((rows, cols), jnp.float32)
    for k in range(levels):
        t, s, u, v = heat[k], salt[k], zonal[k], merid[k]
        around_t = around(t, k)
        around_s = around(s, levels + k)
        new_heat[k] = advance(t, around_t, u, v)
        new_salt[k] = advance(s, around_s, u, v)
        span = spans[0:1, k : k + 1]
        layer_x = span * (density(around_t[0], around_s[0]) - density(around_t[1], around_s[1]))
        layer_y = span * (density(around_t[4], around_s[4]) - density(around_t[5], around_s[5]))
        new_zonal[k] = wet * (u - half * (above_x + 0.5 * layer_x))
        new_merid[k] = wet * (v - half * (above_y + 0.5 * layer_y))
        above_x = above_x + layer_x
        above_y = above_y + layer_y
        if (k + 1) % size == 0:
            piece = pl.ds(k + 1 - size, size)
            for i, (near_ref, far_ref) in enumerate(stores):
                copies.append(pltpu.make_async_copy(near_ref.at[piece], far_ref.at[piece], sems.at[i, k // size]))
                copies[-1].start()
    for copy in copies:
        copy.wait()


def surface_kernel(shares, shift, base, surface):
    lanes = shares.shape[1]
    g00, g01, g02, g03, g11, g12, g13, g22, g23, theta = (
        shares[...] if k == 0 else pltpu.roll(shares[...], lanes - k, 1) for k in range(10)
    )
    add = lambda terms: jnp.sum(terms, axis=0, keepdims=True)

    def ratio(a, b):
        good = b > 0.0
        return jnp.where(good, a / jnp.where(good, b, 1.0), 0.0)

    def form(p, h):
        total = 0.0
        for i, a in enumerate(p):
            for j in range(i, len(p)):
                term = a * p[j] * h[i + j]
                total = total + (term if i == j else 2.0 * term)
        return total

    whole = add(g00)
    common = ratio(add(theta * g00 + g01), whole)
    d = theta - common
    mu = [
        whole,
        add(g01 + d * g00),
        add(g11 + d * (2.0 * g01 + d * g00)),
        add(g12 + d * (2.0 * g11 + g02 + d * (3.0 * g01 + d * g00))),
        add(g22 + d * (4.0 * g12 + d * (2.0 * g02 + 4.0 * g11 + d * (4.0 * g01 + d * g00)))),
        add(
            g23
            + d * (3.0 * g22 + 2.0 * g13 + d * (9.0 * g12 + g03 + d * (4.0 * g02 + 6.0 * g11 + d * (5.0 * g01 + d * g00))))
        ),
    ]
    scale = 1.0 - common
    gap = [scale * mu[k] - mu[k + 1] for k in range(5)]
    alpha = ratio(mu[0], gap[0])
    y = [-alpha * ratio(mu[1], mu[0]), alpha]
    x = [alpha, 0.0, 0.0]
    rz = form(y, mu)
    p = [y[0] + ratio(rz, mu[0]), y[1]]
    alpha = ratio(rz, form(p, gap))
    x = [x[0] + alpha * p[0], alpha * p[1], 0.0]
    y = [y[0] - alpha * scale * p[0], y[1] - alpha * (scale * p[1] - p[0]), alpha * p[1]]
    new = form(y, mu)
    beta = ratio(new, rz)
    p = [y[0] + beta * p[0], y[1] + beta * p[1], y[2]]
    alpha = ratio(new, form(p, gap))
    x = [x[0] + alpha * p[0], x[1] + alpha * p[1], alpha * p[2]]
    d = shift[0:1, :] - common
    x = [x[0] + d * (x[1] + d * x[2]), x[1] + 2.0 * d * x[2], x[2]]
    x = [value[0:1, 0:1] for value in x]
    surface[...] = x[0] * base[0] + x[1] * base[1] + x[2] * base[2]


def call(kernel, outs, flops, moved, name, out_space=pltpu.VMEM, scratch=(), types=jnp.float32):
    def run(*args):
        return pl.pallas_call(
            kernel,
            out_shape=[jax.ShapeDtypeStruct(shape, types) for shape in outs],
            in_specs=[pl.BlockSpec(memory_space=pltpu.VMEM)] * len(args),
            out_specs=[pl.BlockSpec(memory_space=out_space)] * len(outs),
            scratch_shapes=list(scratch),
            cost_estimate=pl.CostEstimate(flops=flops, bytes_accessed=moved, transcendentals=0),
            compiler_params=pltpu.CompilerParams(vmem_limit_bytes=VMEM_LIMIT),
            name=name,
        )(*args)

    return run


def body(
    warmth_deviation,
    saltiness_deviation,
    easterly_speed,
    poleward_speed,
    stratum_spans,
    water_indicator,
    opposite_counterpart,
    elevation_weights,
    elevation_anomaly,
):
    lons, lats = lax.axis_size("lon"), lax.axis_size("lat")
    lon, lat = lax.axis_index("lon"), lax.axis_index("lat")
    levels, rows, cols = warmth_deviation.shape
    high = packet_rows(levels)
    assert cols & (cols - 1) == 0 and rows >= 24 and rows // 2 == high - 4 * levels + 8 and 4 * levels <= cols // 2 and 2 * START[-1] <= min(RELAY, cols - RELAY) and cols == 128
    tall = rows + 16
    width = cols * lons
    flat = lambda i, j: (i % lons) * lats + j

    place = (lax.rem(lat, 2), lat == lats - 1, lax.rem(lon, 2), lat == 0, lon)
    meta = jnp.stack([value.astype(jnp.int32) for value in place]).reshape(1, 5)
    (meta,) = call(place_kernel, [(8, cols)], LOAD_FLOPS, 16, "place", types=jnp.int32)(meta)

    spans = stratum_spans.reshape(1, levels)
    facing = opposite_counterpart.reshape(1, cols)
    state = (warmth_deviation, saltiness_deviation, easterly_speed, poleward_speed)
    flat_state = (water_indicator, elevation_weights, elevation_anomaly)
    cells = levels * rows * cols
    sums, first, second, kept, east_columns, west_columns = call(
        pack_kernel,
        [(3, rows, cols), *[(high, cols)] * 3, (rows, cols), (rows, cols)],
        12 * cells,
        16 * cells,
        "level_sums",
        scratch=[pltpu.VMEM((high, cols), jnp.float32)] * 3,
    )(meta, spans, facing, *state, *flat_state)

    axes = ("lon", "lat")
    pairs_first = [(flat(i, j), flat(i, j ^ 1)) for i in range(lons) for j in range(lats)]
    pairs_inner = [
        (flat(i, a), flat(i, b))
        for i in range(lons)
        for j in range(1, lats - 1, 2)
        for a, b in ((j, j + 1), (j + 1, j))
    ] + [(flat(i, 0), flat(i ^ 1, 0)) for i in range(lons)]

    counterpart, first = lax.optimization_barrier((opposite_counterpart, first))
    hinge = lax.rem(counterpart[0] + 1 + cols * lon, width)
    block = lax.rem((hinge + cols // 2) // cols, lons)

    deep = 4 * levels

    def exchange(block, first, second):
        partner = [(block - 1 - i) % lons for i in range(lons)]
        partner = [i + lons // 2 if i == p else p for i, p in enumerate(partner)]
        pairs_fold = [(flat(p, lats - 1), flat(i, lats - 1)) for i, p in enumerate(partner)]
        second = lax.ppermute(second, axes, pairs_inner + pairs_fold)
        first = lax.ppermute(first, axes, pairs_first)
        return call(
            functools.partial(turn_kernel, lons),
            [
                (FIELDS, tall, cols),
                (rows // 2 + rows, cols),
                (rows // 2, cols),
                (rows, cols),
                (high - deep, cols),
                *[(deep, cols)] * 2,
            ],
            FIELDS * tall * cols,
            4 * 4 * FIELDS * tall * cols,
            "row_halos",
        )(meta, facing, kept, sums, *flat_state, second, first, east_columns, west_columns)

    ext, to_far, to_near, state_near, facing_rows, north_rows, south_rows = lax.switch(
        block, [functools.partial(exchange, s) for s in range(lons)], first, second
    )

    near = lambda cells: lax.ppermute(cells, "lon", [(i, i ^ 1) for i in range(lons)])
    far = lambda cells: lax.ppermute(cells, "lon", [(i, (i + 1 if i % 2 else i - 1) % lons) for i in range(lons)])
    from_far, from_near = far(to_far), near(to_near)
    state_near = near(state_near)

    (shift,) = call(shift_kernel, [(8, cols)], 60 * rows * cols, 24 * rows * cols, "basis_shift")(ext)

    count = lons * lats
    base, moments = call(
        krylov_kernel,
        [(3, rows, cols), (count, cols)],
        200 * tall * cols,
        4 * 12 * tall * cols,
        "krylov",
        scratch=[pltpu.VMEM((2, high - deep + 8, cols), jnp.float32)],
    )(meta, facing, shift, ext, facing_rows, from_far, from_near)

    chunks = 5 if levels % 5 == 0 else 1
    new_heat, new_salt, new_zonal, new_merid = call(
        step_kernel,
        [(levels, rows, cols)] * 4,
        120 * cells,
        32 * cells,
        "levels_step",
        out_space=pltpu.HBM,
        scratch=[
            *[pltpu.VMEM((levels, rows, cols), jnp.float32)] * 4,
            pltpu.VMEM((deep, cols), jnp.float32),
            pltpu.SemaphoreType.DMA((4, chunks)),
        ],
    )(meta, spans, facing, *state, water_indicator, north_rows, south_rows, from_far, state_near)

    shares = lax.all_to_all(moments, axes, 0, 0, tiled=True)
    (surface,) = call(surface_kernel, [(rows, cols)], 6 * rows * cols, 16 * rows * cols, "surface")(shares, shift, base)
    return (new_heat, new_salt, new_zonal, new_merid, surface)


def solution(mesh):
    for axis in mesh.shape.values():
        assert axis > 1 and axis & (axis - 1) == 0
    levels = P(None, "lat", "lon")
    flat = P("lat", "lon")
    return jax.shard_map(
        body,
        mesh=mesh,
        in_specs=(levels, levels, levels, levels, P(), flat, P("lon"), flat, flat),
        out_specs=(levels, levels, levels, levels, flat),
        check_vma=False,
    )
```
